128 devices in a mesh: grp: 16 (over x, y), blk: 8 (over z, core).
Axes of the slice: x: 4, y: 4, z: 4, core: 2. Of those that a mesh axis runs over, the one named last changes fastest.
Arguments:
- embeddings: bfloat16 [65536, 768], P(('grp', 'blk'))
- assign: int32 [65536], P(('grp', 'blk')), may hold values from 0 to 127, as said below
- owner: int32 [128], replicated, may hold values from 0 to 15, as said below
- send_count: int32 [128, 16], P(('grp', 'blk')), may hold values from 0 to 64, as said below
- send_index: int32 [128, 16, 64], P(('grp', 'blk')), may hold values from 0 to 511, as said below
Outputs:
- max_sim: float32 [65536], P(('grp', 'blk'))
- centroid_cos: float32 [65536], P(('grp', 'blk'))
The draws below stay inside these ranges and needn't reach their ends.
Inputs may be any that keep to these rules, and one draw needn't show every extreme that they name: `owner`: every group owns the same number of clusters. `assign`: every document's cluster is owned by the group in whose list of its device the document stands; a device may send many documents of one cluster. `send_count`: A device's counts sum to 512; a count may be anything from 0 to 64, and at least one group receives exactly 64 documents from every device. `send_index`: the used slots of a device's lists hold each of its documents exactly once; unused slots hold 0.
All inputs are finite; a program needn't handle non-finite values.
Results may differ from the reference program's by a relative error of at most 0.00085.
Values may be sent and summed in bfloat16 or wider, within the bound.
A program may use at most 64 MiB of HBM per device.

```python
import math
import jax
import jax.numpy as jnp
from jax import lax

D = 768
K = 128
ROWS_DEV = 512
CAP = 64
ROWS = 65536
N_GRP = 16
N_BLK = 8


def layout(key):
    devices = N_GRP * N_BLK
    per_group = K // N_GRP
    key_owner, key_rank, key_noise, key_shuffle, key_choose = jax.random.split(jax.random.fold_in(key, 101), 5)
    ordering = jax.random.permutation(key_owner, K).astype(jnp.int32)
    owner = (ordering // per_group).astype(jnp.int32)
    members = jnp.argsort(ordering).astype(jnp.int32)
    ranking = jax.random.permutation(key_rank, N_GRP).astype(jnp.int32)
    slot_group = jnp.arange(N_GRP * CAP, dtype=jnp.int32) // CAP
    slot_rank = ranking[slot_group]
    noise_score = jax.random.randint(key_noise, (devices, N_GRP * CAP), 0, 131072)
    score = noise_score + slot_rank[None, :] * 65536 + jnp.where(slot_rank == N_GRP - 1, 16777216, 0)[None, :]
    chosen = jnp.argsort(-score, axis=1, stable=True)[:, :ROWS_DEV].astype(jnp.int32)
    row_group = chosen // CAP
    shuffle_score = jax.random.randint(key_shuffle, (devices, ROWS_DEV), 0, 1073741824)
    shuffled = jnp.argsort(shuffle_score, axis=1, stable=True)
    row_group = jnp.take_along_axis(row_group, shuffled, axis=1)
    onehot = (row_group[:, :, None] == jnp.arange(N_GRP, dtype=jnp.int32)[None, None, :]).astype(jnp.int32)
    position = jnp.sum((jnp.cumsum(onehot, axis=1) - 1) * onehot, axis=2).astype(jnp.int32)
    counts = jnp.sum(onehot, axis=1).astype(jnp.int32)
    device_ids = jnp.broadcast_to(jnp.arange(devices, dtype=jnp.int32)[:, None], (devices, ROWS_DEV))
    local_rows = jnp.broadcast_to(jnp.arange(ROWS_DEV, dtype=jnp.int32)[None, :], (devices, ROWS_DEV))
    listing = jnp.zeros((devices, N_GRP, CAP), jnp.int32).at[device_ids, row_group, position].set(local_rows)
    within = jax.random.randint(key_choose, (devices, ROWS_DEV), 0, per_group).astype(jnp.int32)
    cluster = members[row_group * per_group + within]
    return (owner, cluster.reshape(ROWS).astype(jnp.int32), counts, listing)


def draw_owner(key, part):
    return layout(key)[0]


def draw_assign(key, part):
    return layout(key)[1]


def draw_send_count(key, part):
    return layout(key)[2]


def draw_send_index(key, part):
    return layout(key)[3]


def draw_embeddings(key, part):
    cluster = layout(key)[1]
    key = jax.random.fold_in(key, 7)
    key_centre, key_noise, key_scale = jax.random.split(key, 3)
    centres = jax.random.normal(key_centre, (K, D), jnp.float32)
    noise = jax.random.normal(key_noise, (ROWS, D), jnp.float32)
    scale = jnp.exp(jax.random.uniform(key_scale, (ROWS,), jnp.float32, 0.0, math.log(10.0)))
    values = scale[:, None] * (0.8 * centres[cluster] + noise)
    return values.astype(jnp.bfloat16)


def setup_inputs(seed: int = 0) -> dict:
    keys = jax.random.split(jax.random.key(seed), 6)
    embeddings = draw_embeddings(jax.random.fold_in(keys[5], 71), 0)
    assign = draw_assign(jax.random.fold_in(keys[5], 71), 0)
    owner = draw_owner(jax.random.fold_in(keys[5], 71), 0)
    send_count = draw_send_count(jax.random.fold_in(keys[5], 71), 0)
    send_index = draw_send_index(jax.random.fold_in(keys[5], 71), 0)
    return {"embeddings": embeddings, "assign": assign, "owner": owner, "send_count": send_count, "send_index": send_index}


EPSILON = 1e-06

def normalize(values):
    widened = values.astype(jnp.float32)
    return widened * lax.rsqrt(lax.optimization_barrier(jnp.sum(widened * widened, axis=1, keepdims=True)) + EPSILON)

def reference(embeddings, assign, owner, send_count, send_index):
    devices = N_GRP * N_BLK
    unit_rows = normalize(embeddings)
    unit_low = unit_rows.astype(jnp.bfloat16)
    centre_sum = jax.ops.segment_sum(unit_rows, assign, num_segments=K)
    centre = normalize(centre_sum)
    nearness = lax.optimization_barrier(jnp.sum(unit_low.astype(jnp.float32) * centre[assign], axis=1))
    live_slot = jnp.arange(CAP, dtype=jnp.int32)[None, None, :] < send_count[:, :, None]
    entry_row = (jnp.arange(devices, dtype=jnp.int32)[:, None, None] * ROWS_DEV + send_index).astype(jnp.int32)
    entry_group = jnp.broadcast_to(jnp.arange(N_GRP, dtype=jnp.int32)[None, :, None], send_index.shape)
    entry_cluster = assign[entry_row]
    kept_entry = live_slot & (owner[entry_cluster] == entry_group)
    entry_key = jnp.where(kept_entry, entry_cluster, -1).astype(jnp.int32)
    group_rows = jnp.transpose(entry_row, (1, 0, 2)).reshape(N_GRP, -1)
    group_keys = jnp.transpose(entry_key, (1, 0, 2)).reshape(N_GRP, -1)
    block_size = 2 * ROWS_DEV
    group_len = group_rows.shape[1]
    block_count = group_len // block_size

    def group_best(number):
        rows_here = group_rows[number]
        keys_here = group_keys[number]
        vectors = unit_low[rows_here]

        def block_best(index):
            offset = (index * block_size).astype(jnp.int32)
            own_vector = lax.dynamic_slice_in_dim(vectors, offset, block_size, 0)
            own_key = lax.dynamic_slice_in_dim(keys_here, offset, block_size, 0)
            own_row = lax.dynamic_slice_in_dim(rows_here, offset, block_size, 0)
            scores = jnp.dot(own_vector, vectors.T, preferred_element_type=jnp.float32)
            matched = (own_key[:, None] == keys_here[None, :]) & (own_key[:, None] >= 0) & (own_row[:, None] != rows_here[None, :])
            return lax.optimization_barrier(jnp.max(jnp.where(matched, scores, -1.0), axis=1))
        return lax.map(block_best, jnp.arange(block_count, dtype=jnp.int32)).reshape(-1)
    best_all = lax.map(group_best, jnp.arange(N_GRP, dtype=jnp.int32))
    max_sim = jnp.full((ROWS,), -1.0, jnp.float32).at[group_rows.reshape(-1)].max(best_all.reshape(-1))
    has_entry = jnp.zeros((ROWS,), jnp.int32).at[entry_row.reshape(-1)].max(kept_entry.astype(jnp.int32).reshape(-1))
    centroid_cos = jnp.where(has_entry > 0, nearness, 0.0)
    return (max_sim, centroid_cos)
```

```python
import functools

import jax
import jax.numpy as jnp
from jax import lax
from jax.experimental import pallas as pl
from jax.experimental.pallas import tpu as pltpu
from jax.sharding import PartitionSpec as P

EPSILON = 1e-06
F32 = jnp.float32
BF16 = jnp.bfloat16

CHIPS = 64
ROWS = 512
WIDTH = 768
CLUSTERS = 128
GROUPS = 16
CAP = 64
BASE = 16
EXTRA = 8
HALF = WIDTH // 2
SLOTS = BASE + EXTRA
LANES = CHIPS * BASE
HELD = 640
PACKED = 16


def normalize(values):
    widened = values.astype(F32)
    return widened * lax.rsqrt(jnp.sum(widened * widened, axis=1, keepdims=True) + EPSILON)


def general(embeddings, assign, owner, send_count, send_index):
    rows_local = embeddings.shape[0]
    feature_width = embeddings.shape[1]
    groups = lax.axis_size("grp")
    clusters = owner.shape[0]
    capacity = send_index.shape[2]
    slot_total = groups * capacity
    unit_rows = normalize(embeddings)
    unit_low = unit_rows.astype(BF16)
    counts = send_count[0]
    listed = send_index[0]
    live_slot = jnp.arange(capacity, dtype=jnp.int32)[None, :] < counts[:, None]
    listed_cluster = assign[listed]
    owned_here = owner[listed_cluster] == jnp.arange(groups, dtype=jnp.int32)[:, None]
    kept_slot = live_slot & owned_here
    out_cluster = jnp.where(kept_slot, listed_cluster, -1)
    out_tag = jnp.where(kept_slot, lax.axis_index(("grp", "blk")) * rows_local + listed, -1)
    out_vector = unit_low[listed.reshape(-1)].reshape(groups, capacity, feature_width)
    got_vector, got_cluster, got_tag = (
        lax.all_to_all(out_vector, "grp", split_axis=0, concat_axis=0, tiled=True),
        lax.all_to_all(out_cluster, "grp", split_axis=0, concat_axis=0, tiled=True),
        lax.all_to_all(out_tag, "grp", split_axis=0, concat_axis=0, tiled=True),
    )
    own_vector = got_vector.reshape(slot_total, feature_width)
    own_cluster = got_cluster.reshape(slot_total)
    own_tag = got_tag.reshape(slot_total)

    def tile_best(current, shard_piece):
        other_vector, other_cluster, other_tag = shard_piece
        scores = jnp.einsum("id,jd->ij", own_vector, other_vector, preferred_element_type=F32)
        matched = (
            (own_cluster[:, None] == other_cluster[None, :])
            & (other_cluster[None, :] >= 0)
            & (own_tag[:, None] != other_tag[None, :])
        )
        return jnp.maximum(current, jnp.max(jnp.where(matched, scores, -1.0), axis=1))

    other_vector = lax.all_gather(own_vector, "blk", axis=0, tiled=True)
    other_cluster = lax.all_gather(own_cluster, "blk", axis=0, tiled=True)
    other_tag = lax.all_gather(own_tag, "blk", axis=0, tiled=True)
    length = other_vector.shape[0]
    number = length // slot_total
    stacked = (
        other_vector.reshape(number, slot_total, feature_width),
        other_cluster.reshape(number, slot_total),
        other_tag.reshape(number, slot_total),
    )

    def scan_step(carry, single):
        return (tile_best(carry, single), None)

    result, unused = lax.scan(scan_step, jnp.full((slot_total,), -1.0, F32), stacked)
    target = jnp.where(live_slot, listed, rows_local).reshape(-1)
    partial_sum = jax.ops.segment_sum(unit_rows, assign, num_segments=clusters)
    centre = normalize(lax.psum(partial_sum, ("grp", "blk")))
    nearness = jnp.sum(unit_low.astype(F32) * centre[assign], axis=1)
    returned = lax.all_to_all(
        result.reshape(groups, capacity), "grp", split_axis=0, concat_axis=0, tiled=True
    )
    has_entry = (
        jnp.zeros((rows_local,), jnp.int32)
        .at[target]
        .max(kept_slot.astype(jnp.int32).reshape(-1), mode="drop")
    )
    centroid_cos = jnp.where(has_entry > 0, nearness, 0.0)
    max_sim = jnp.full((rows_local,), -1.0, F32).at[target].max(returned.reshape(-1), mode="drop")
    return (max_sim, centroid_cos)


def iota(shape, axis):
    return lax.broadcasted_iota(jnp.int32, shape, axis)


def down(values):
    return jnp.sum(values, axis=0, keepdims=True)


def across(values):
    return jnp.sum(values, axis=1, keepdims=True)


def pick(mask, values):
    return jnp.where(mask, values, 0.0)


def as_column(row):
    size = row.shape[1]
    return across(pick(iota((size, size), 0) == iota((size, size), 1), row))


def as_row(column):
    size = column.shape[0]
    return down(pick(iota((size, size), 0) == iota((size, size), 1), column))


def dot(a, b):
    return jnp.dot(a, b, preferred_element_type=F32)


def dot_rows(a, b):
    return lax.dot_general(a, b, (((1,), (1,)), ((), ())), preferred_element_type=F32)


def onehot(mask):
    return jnp.where(mask, 1.0, 0.0).astype(BF16)


def thirds(values):
    first = values.astype(BF16).astype(F32)
    rest = values - first
    second = rest.astype(BF16).astype(F32)
    third = (rest - second).astype(BF16).astype(F32)
    return first, second, third


def rank_groups(count_ref):
    count_row = count_ref[...].astype(F32)
    count_column = as_column(count_row)
    sub, lane = iota((GROUPS, 128), 0), iota((GROUPS, 128), 1)
    count_lanes = down(pick(sub == lane, count_column))
    ahead = (count_column > count_lanes) | ((count_column == count_lanes) & (sub < lane))
    rank = down(jnp.where(ahead, 1.0, 0.0))
    return jnp.where(iota((1, 128), 1) < GROUPS, rank, 0.0), count_column


def place_documents(assign_ref, owner_ref, rank):
    owner_row = owner_ref[...].astype(F32)
    owner_column = as_column(owner_row)
    sub, lane = iota((CLUSTERS, CLUSTERS), 0), iota((CLUSTERS, CLUSTERS), 1)
    within = across(jnp.where((owner_column == owner_row) & (lane < sub), 1.0, 0.0))
    group_rank = across(pick(owner_column == lane.astype(F32), rank))
    place_column = group_rank * (CLUSTERS // GROUPS) + within
    member = iota((CLUSTERS, ROWS), 0) == assign_ref[...]
    place = down(pick(member, place_column))
    group = down(pick(member, owner_column))
    order = iota((CLUSTERS, ROWS), 0).astype(F32)
    at_place = order == place
    earlier = onehot(iota((ROWS, ROWS), 0) < iota((ROWS, ROWS), 1))
    before = dot(onehot(at_place), earlier)
    slot = down(pick(at_place, before))
    count_column = across(jnp.where(at_place, 1.0, 0.0))
    partner_count = down(pick(order == (CLUSTERS - 1) - place, count_column))
    slot = slot + jnp.where(place >= CHIPS, partner_count, 0.0)
    chip = jnp.minimum(place, (CLUSTERS - 1) - place)
    return group, chip.astype(jnp.int32), slot.astype(jnp.int32), as_row(count_column)


def missing_documents(index_ref, count_column, group):
    listed = index_ref[...]
    live = iota((GROUPS, CAP), 1).astype(F32) < count_column
    eye = onehot(iota((CAP, CAP), 0) == iota((CAP, CAP), 1))
    high = dot_rows(eye, jnp.where(live, listed >> 4, 0).astype(F32).astype(BF16))
    low = dot_rows(eye, jnp.where(live, listed & 15, 0).astype(F32).astype(BF16))
    alive = dot_rows(eye, onehot(live))
    slots = jnp.where(alive > 0.5, high * 16.0 + low, -1.0)
    document = iota((1, ROWS), 1).astype(F32)
    hits = jnp.zeros((CAP, ROWS), F32)
    for g in range(GROUPS):
        wanted = jnp.where(group == float(g), document, -2.0)
        hits = hits + jnp.where(slots[:, g : g + 1] == wanted, 1.0, 0.0)
    return across(jnp.where(down(hits) > 0.5, 0.0, 1.0))


def receive_plan(table, rank, chip):
    heads = table.astype(jnp.int32)
    counts = (heads & 1023).astype(F32)
    differ = jnp.where((heads >> 10).astype(F32) != rank, 1.0, 0.0)
    sub, lane = iota((CLUSTERS, CLUSTERS), 0), iota((CLUSTERS, CLUSTERS), 1)
    pair = onehot((sub == lane) | (sub == (CLUSTERS - 1) - lane))
    both = dot(counts.astype(BF16), pair)
    fault = across(down(differ))
    fault = fault + across(down(jnp.where(both > SLOTS, 1.0, 0.0)))
    fault = fault + across(jnp.where(down(both) > HELD, 1.0, 0.0))

    lanes = iota((CHIPS, CLUSTERS), 1)
    source, target = iota((CHIPS, CHIPS), 0), iota((CHIPS, CHIPS), 1)
    columns = []
    totals = []
    for place in (chip, (CLUSTERS - 1) - chip):
        number = across(pick(lanes == place, counts))
        start = across(pick(target < source, as_row(number)))
        columns.append((number, start))
        totals.append(down(number))
    spread = iota((CHIPS, LANES), 0) == (iota((CHIPS, LANES), 1) >> 4)
    (first, first_start), (second, second_start) = [
        tuple(down(pick(spread, column)) for column in pair_) for pair_ in columns
    ]
    second_start = second_start + totals[0]

    def row_of(slot):
        slot = slot.astype(F32)
        later = jnp.where(slot < first + second, second_start + (slot - first), -1.0)
        return jnp.where(slot < first, first_start + slot, later)

    position = iota((1, LANES), 1) & (BASE - 1)
    base = row_of(position)
    extra = row_of(BASE + (position & (EXTRA - 1)))
    left = jnp.where(position < EXTRA, extra, -1.0)
    right = jnp.where(position < EXTRA, -1.0, extra)
    return base, left, right, totals[0], totals[0] + totals[1], fault


def kernel(
    x_ref, assign_ref, owner_ref, count_ref, index_ref,
    max_ref, cos_ref, fault_ref,
    send_a, send_b, got_a, got_b, head, heads, pick_a, pick_l, pick_r,
    mine, theirs, stats, their_stats, back, returned,
    send_sem, recv_sem,
):
    grp, blk = lax.axis_index("grp"), lax.axis_index("blk")
    my_x, my_y, my_z, core = grp // 4, grp % 4, blk // 2, blk % 2
    my_chip = grp * 4 + my_z

    def chip_at(step):
        x = (my_x + step // 16) % 4
        y = (my_y + (step // 4) % 4) % 4
        z = (my_z + step % 4) % 4
        return x * 4 + y, z

    def device_at(step):
        g, z = chip_at(step)
        return {"grp": g, "blk": z * 2 + core}

    other_core = {"grp": grp, "blk": my_z * 2 + (1 - core)}
    barrier = pltpu.get_barrier_semaphore()

    @pl.loop(1, CHIPS)
    def _(step):
        pl.semaphore_signal(
            barrier, inc=1, device_id=device_at(step), device_id_type=pl.DeviceIdType.MESH
        )

    pl.semaphore_signal(barrier, inc=1, device_id=other_core, device_id_type=pl.DeviceIdType.MESH)

    def remote(source, target, number, device):
        return pltpu.make_async_remote_copy(
            src_ref=source,
            dst_ref=target,
            send_sem=send_sem.at[number],
            recv_sem=recv_sem.at[number],
            device_id=device,
            device_id_type=pl.DeviceIdType.MESH,
        )

    def await_all(ref, semaphore):
        block = ref.at[pl.ds(0, CHIPS - 1)]
        pltpu.make_async_copy(block, block, semaphore).wait()

    rank, count_column = rank_groups(count_ref)
    group, chip, slot, place_counts = place_documents(assign_ref, owner_ref, rank)
    missing = missing_documents(index_ref, count_column, group)
    head[0] = place_counts + 1024.0 * rank + jnp.where(missing > 0.5, 16384.0, 0.0)
    heads[my_chip] = head[0]

    pl.semaphore_wait(barrier, CHIPS)

    @pl.loop(1, CHIPS)
    def _(step):
        remote(head, heads.at[pl.ds(my_chip, 1)], 0, device_at(step)).start()

    step_of = (
        (((chip >> 4) - my_x) & 3) * 16 + ((((chip >> 2) & 3) - my_y) & 3) * 4 + (((chip & 3) - my_z) & 3)
    )
    in_base = slot < BASE
    base_slot = jnp.where(in_base, step_of * BASE + slot, -1)
    extra_slot = jnp.where(in_base | (slot >= SLOTS), -1, step_of * BASE + (slot - BASE))
    span = PACKED * BASE
    for part in range(CHIPS // PACKED):
        slots = iota((span, ROWS), 0) + part * span
        rows = dot(onehot(slots == base_slot), x_ref[...]).astype(BF16)
        send_a[pl.ds(part * PACKED, PACKED)] = rows.reshape(PACKED, BASE, WIDTH)
        left = dot(onehot(slots == extra_slot), x_ref[:, :HALF])
        right = dot(onehot((slots - EXTRA == extra_slot) & (extra_slot >= 0)), x_ref[:, HALF:])
        send_b[pl.ds(part * PACKED, PACKED)] = (left + right).astype(BF16).reshape(PACKED, BASE, HALF)

        @pl.loop(max(part * PACKED, 1), (part + 1) * PACKED)
        def _(step):
            device = device_at(step)
            remote(send_a.at[step], got_a.at[my_chip], 1, device).start()
            remote(send_b.at[step], got_b.at[my_chip], 2, device).start()

    got_a[my_chip] = send_a[0]
    got_b[my_chip] = send_b[0]

    await_all(heads, recv_sem.at[0])
    table = heads[...].reshape(CHIPS, CLUSTERS)
    base, left, right, first_end, held_end, fault = receive_plan(table, rank, my_chip)
    rows = iota((HELD, LANES), 0).astype(F32)
    pick_a[...] = onehot(rows == base)
    pick_l[...] = onehot(rows == left)
    pick_r[...] = onehot(rows == right)
    code = as_column((chip * 32 + slot).astype(F32)).astype(jnp.int32)

    await_all(got_a, recv_sem.at[1])
    await_all(got_b, recv_sem.at[2])

    all_a = got_a[...].reshape(LANES, WIDTH)
    all_b = got_b[...].reshape(LANES, HALF)
    piece = HELD // 2
    sums = [jnp.zeros((1, WIDTH), F32), jnp.zeros((1, WIDTH), F32)]
    for part in range(2):
        window = pl.ds(part * piece, piece)
        raw = dot(pick_a[window], all_a) + jnp.concatenate(
            [dot(pick_l[window], all_b), dot(pick_r[window], all_b)], axis=1
        )
        unit = raw * lax.rsqrt(across(raw * raw) + EPSILON)
        mine[window] = unit.astype(BF16)
        number = (iota((piece, 1), 0) + part * piece).astype(F32)
        sums[0] = sums[0] + down(pick(number < first_end, unit))
        sums[1] = sums[1] + down(pick(number >= first_end, unit))
    lane = iota((1, WIDTH), 1)
    facts = jnp.where(lane == 0, first_end, 0.0)
    facts = jnp.where(lane == 1, held_end, facts)
    facts = jnp.where(lane == 2, fault, facts)
    facts = jnp.concatenate([facts[:, :128], rank, facts[:, 256:]], axis=1)
    row = iota((8, WIDTH), 0)
    stats[...] = pick(row == 0, sums[0]) + pick(row == 1, sums[1]) + pick(row == 2, facts)
    swap = remote(mine, theirs, 3, other_core)
    swap_stats = remote(stats, their_stats, 4, other_core)
    swap.start()
    swap_stats.start()

    query_number = iota((1, HELD), 1).astype(F32)
    query = jnp.where(query_number < first_end, 0.0, 1.0)

    def best_of(keys, first, held, best, itself):
        for part in range(2):
            window = pl.ds(part * piece, piece)
            scores = dot_rows(keys[window], mine[...])
            number = (iota((piece, 1), 0) + part * piece).astype(F32)
            kind = jnp.where(number < first, 0.0, jnp.where(number < held, 1.0, 2.0))
            matched = kind == query
            if itself:
                matched = matched & (number != query_number)
            best = jnp.maximum(best, jnp.max(jnp.where(matched, scores, -1.0), axis=0, keepdims=True))
        return best

    best = best_of(mine, first_end, held_end, jnp.full((1, HELD), -1.0, F32), True)
    swap.wait()
    swap_stats.wait()
    facts = their_stats[2:3, :]
    best = best_of(theirs, facts[:, 0:1], facts[:, 1:2], best, False)

    total = pick(row < 2, stats[...] + their_stats[...])
    centre = total * lax.rsqrt(across(total * total) + EPSILON)
    near = dot_rows(jnp.concatenate(thirds(centre), axis=0).astype(BF16), mine[...])
    near = near[0:8] + near[8:16] + near[16:24]
    near = jnp.where(query_number < first_end, near[0:1], near[1:2])

    differ = across(jnp.where(facts[:, 128:256] != rank, 1.0, 0.0))
    fault = fault + facts[:, 2:3] + differ
    fault_ref[...] = jnp.where(fault > 0.5, 1, 0) + jnp.zeros((1, 128), jnp.int32)

    parts = thirds(best) + thirds(near)
    row = iota((8, HELD), 0)
    values = jnp.zeros((8, HELD), F32)
    for number, part in enumerate(parts):
        values = jnp.where(row == number, part, values)
    values = values.astype(BF16)
    for first, chosen in ((0, pick_a), (2, pick_l)):
        out = dot(values, chosen[...])
        for kind in range(2):
            line = out[3 * kind : 3 * kind + 1] + out[3 * kind + 1 : 3 * kind + 2] + out[3 * kind + 2 : 3 * kind + 3]
            for tile in range(LANES // 128):
                back[tile, first + kind : first + kind + 1, :] = line[:, tile * 128 : (tile + 1) * 128]
    returned[my_chip] = back[my_chip // 8]

    @pl.loop(1, CHIPS)
    def _(step):
        g, z = chip_at(step)
        remote(back.at[(g * 4 + z) // 8], returned.at[my_chip], 5, device_at(step)).start()

    document_chip, document_slot = code >> 5, code & 31
    chosen = onehot(document_chip == iota((ROWS, CHIPS), 1))
    lane = iota((ROWS, 128), 1) - (my_chip % 8) * BASE
    at_base = (lane == document_slot) & (document_slot < BASE)
    at_extra = (lane == document_slot - BASE) & (document_slot >= BASE)

    await_all(returned, recv_sem.at[5])
    lines = [returned[:, number, :] for number in range(4)]
    terms = jnp.concatenate([term for line in lines for term in thirds(line)], axis=1)
    found = dot(chosen, terms.astype(BF16))
    found = [
        found[:, n * 384 : n * 384 + 128] + found[:, n * 384 + 128 : n * 384 + 256] + found[:, n * 384 + 256 : n * 384 + 384]
        for n in range(4)
    ]
    for out_ref, kind in ((max_ref, 0), (cos_ref, 1)):
        column = across(pick(at_base, found[kind]) + pick(at_extra, found[2 + kind]))
        out_ref[...] = as_row(column)

    await_all(heads, send_sem.at[0])
    await_all(got_a, send_sem.at[1])
    await_all(got_b, send_sem.at[2])
    await_all(returned, send_sem.at[5])


def routed(embeddings, assign, owner, send_count, send_index):
    return pl.pallas_call(
        kernel,
        out_shape=(
            jax.ShapeDtypeStruct((1, ROWS), F32),
            jax.ShapeDtypeStruct((1, ROWS), F32),
            jax.ShapeDtypeStruct((1, 128), jnp.int32),
        ),
        in_specs=[pl.BlockSpec(memory_space=pltpu.VMEM)] * 5,
        out_specs=(pl.BlockSpec(memory_space=pltpu.VMEM),) * 3,
        scratch_shapes=[
            pltpu.VMEM((CHIPS, BASE, WIDTH), BF16),
            pltpu.VMEM((CHIPS, BASE, HALF), BF16),
            pltpu.VMEM((CHIPS, BASE, WIDTH), BF16),
            pltpu.VMEM((CHIPS, BASE, HALF), BF16),
            pltpu.VMEM((1, 1, 128), F32),
            pltpu.VMEM((CHIPS, 1, 128), F32),
            pltpu.VMEM((HELD, LANES), BF16),
            pltpu.VMEM((HELD, LANES), BF16),
            pltpu.VMEM((HELD, LANES), BF16),
            pltpu.VMEM((HELD, WIDTH), BF16),
            pltpu.VMEM((HELD, WIDTH), BF16),
            pltpu.VMEM((8, WIDTH), F32),
            pltpu.VMEM((8, WIDTH), F32),
            pltpu.VMEM((LANES // 128, 4, 128), F32),
            pltpu.VMEM((CHIPS, 4, 128), F32),
            pltpu.SemaphoreType.DMA((6,)),
            pltpu.SemaphoreType.DMA((6,)),
        ],
        compiler_params=pltpu.CompilerParams(
            collective_id=0, has_side_effects=True, vmem_limit_bytes=48 * 1024 * 1024
        ),
    )(
        embeddings,
        assign.reshape(1, ROWS),
        owner.reshape(1, CLUSTERS),
        send_count,
        send_index[0],
    )


def body(embeddings, assign, owner, send_count, send_index):
    arguments = (embeddings, assign, owner, send_count, send_index)
    max_sim, centroid_cos, fault = routed(*arguments)
    return lax.cond(
        fault[0, 0] != 0,
        lambda: general(*arguments),
        lambda: (max_sim.reshape(ROWS), centroid_cos.reshape(ROWS)),
    )


def solution(mesh):
    placed = (
        P(("grp", "blk"), None),
        P(("grp", "blk")),
        P(),
        P(("grp", "blk"), None),
        P(("grp", "blk"), None, None),
    )
    return jax.shard_map(
        body,
        mesh=mesh,
        in_specs=placed,
        out_specs=(P(("grp", "blk")), P(("grp", "blk"))),
        check_vma=False,
    )
```

```python
import functools

import jax
import jax.numpy as jnp
from jax import lax
from jax.experimental import pallas as pl
from jax.experimental.pallas import tpu as pltpu
from jax.sharding import PartitionSpec as P

EPSILON = 1e-06
F32 = jnp.float32
BF16 = jnp.bfloat16

CHIPS = 64
ROWS = 512
WIDTH = 768
CLUSTERS = 128
GROUPS = 16
CAP = 64
BASE = 16
EXTRA = 8
HALF = WIDTH // 2
SLOTS = BASE + EXTRA
LANES = CHIPS * BASE
HELD = 640
PACKED = 16
PARTS = CHIPS // PACKED


def normalize(values):
    widened = values.astype(F32)
    return widened * lax.rsqrt(jnp.sum(widened * widened, axis=1, keepdims=True) + EPSILON)


def general(embeddings, assign, owner, send_count, send_index):
    rows_local = embeddings.shape[0]
    feature_width = embeddings.shape[1]
    groups = lax.axis_size("grp")
    clusters = owner.shape[0]
    capacity = send_index.shape[2]
    slot_total = groups * capacity
    unit_rows = normalize(embeddings)
    unit_low = unit_rows.astype(BF16)
    counts = send_count[0]
    listed = send_index[0]
    live_slot = jnp.arange(capacity, dtype=jnp.int32)[None, :] < counts[:, None]
    listed_cluster = assign[listed]
    owned_here = owner[listed_cluster] == jnp.arange(groups, dtype=jnp.int32)[:, None]
    kept_slot = live_slot & owned_here
    out_cluster = jnp.where(kept_slot, listed_cluster, -1)
    out_tag = jnp.where(kept_slot, lax.axis_index(("grp", "blk")) * rows_local + listed, -1)
    out_vector = unit_low[listed.reshape(-1)].reshape(groups, capacity, feature_width)
    got_vector, got_cluster, got_tag = (
        lax.all_to_all(out_vector, "grp", split_axis=0, concat_axis=0, tiled=True),
        lax.all_to_all(out_cluster, "grp", split_axis=0, concat_axis=0, tiled=True),
        lax.all_to_all(out_tag, "grp", split_axis=0, concat_axis=0, tiled=True),
    )
    own_vector = got_vector.reshape(slot_total, feature_width)
    own_cluster = got_cluster.reshape(slot_total)
    own_tag = got_tag.reshape(slot_total)

    def tile_best(current, shard_piece):
        other_vector, other_cluster, other_tag = shard_piece
        scores = jnp.einsum("id,jd->ij", own_vector, other_vector, preferred_element_type=F32)
        matched = (
            (own_cluster[:, None] == other_cluster[None, :])
            & (other_cluster[None, :] >= 0)
            & (own_tag[:, None] != other_tag[None, :])
        )
        return jnp.maximum(current, jnp.max(jnp.where(matched, scores, -1.0), axis=1))

    other_vector = lax.all_gather(own_vector, "blk", axis=0, tiled=True)
    other_cluster = lax.all_gather(own_cluster, "blk", axis=0, tiled=True)
    other_tag = lax.all_gather(own_tag, "blk", axis=0, tiled=True)
    length = other_vector.shape[0]
    number = length // slot_total
    stacked = (
        other_vector.reshape(number, slot_total, feature_width),
        other_cluster.reshape(number, slot_total),
        other_tag.reshape(number, slot_total),
    )

    def scan_step(carry, single):
        return (tile_best(carry, single), None)

    result, unused = lax.scan(scan_step, jnp.full((slot_total,), -1.0, F32), stacked)
    target = jnp.where(live_slot, listed, rows_local).reshape(-1)
    partial_sum = jax.ops.segment_sum(unit_rows, assign, num_segments=clusters)
    centre = normalize(lax.psum(partial_sum, ("grp", "blk")))
    nearness = jnp.sum(unit_low.astype(F32) * centre[assign], axis=1)
    returned = lax.all_to_all(
        result.reshape(groups, capacity), "grp", split_axis=0, concat_axis=0, tiled=True
    )
    has_entry = (
        jnp.zeros((rows_local,), jnp.int32)
        .at[target]
        .max(kept_slot.astype(jnp.int32).reshape(-1), mode="drop")
    )
    centroid_cos = jnp.where(has_entry > 0, nearness, 0.0)
    max_sim = jnp.full((rows_local,), -1.0, F32).at[target].max(returned.reshape(-1), mode="drop")
    return (max_sim, centroid_cos)


def iota(shape, axis):
    return lax.broadcasted_iota(jnp.int32, shape, axis)


def down(values):
    return jnp.sum(values, axis=0, keepdims=True)


def across(values):
    return jnp.sum(values, axis=1, keepdims=True)


def pick(mask, values):
    return jnp.where(mask, values, 0.0)


def as_column(row):
    size = row.shape[1]
    return across(pick(iota((size, size), 0) == iota((size, size), 1), row))


def as_row(column):
    size = column.shape[0]
    return down(pick(iota((size, size), 0) == iota((size, size), 1), column))


def dot(a, b):
    return jnp.dot(a, b, preferred_element_type=F32)


def dot_rows(a, b):
    return lax.dot_general(a, b, (((1,), (1,)), ((), ())), preferred_element_type=F32)


def onehot(mask):
    return jnp.where(mask, 1.0, 0.0).astype(BF16)


def thirds(values):
    first = values.astype(BF16).astype(F32)
    rest = values - first
    second = rest.astype(BF16).astype(F32)
    third = (rest - second).astype(BF16).astype(F32)
    return first, second, third


def rank_groups(count_ref):
    count_row = count_ref[...].astype(F32)
    count_column = as_column(count_row)
    sub, lane = iota((GROUPS, 128), 0), iota((GROUPS, 128), 1)
    count_lanes = down(pick(sub == lane, count_column))
    ahead = (count_column > count_lanes) | ((count_column == count_lanes) & (sub < lane))
    rank = down(jnp.where(ahead, 1.0, 0.0))
    return jnp.where(iota((1, 128), 1) < GROUPS, rank, 0.0), count_column


def place_documents(assign_ref, owner_ref, rank):
    owner_row = owner_ref[...].astype(F32)
    owner_column = as_column(owner_row)
    sub, lane = iota((CLUSTERS, CLUSTERS), 0), iota((CLUSTERS, CLUSTERS), 1)
    within = across(jnp.where((owner_column == owner_row) & (lane < sub), 1.0, 0.0))
    group_rank = across(pick(owner_column == lane.astype(F32), rank))
    place_column = group_rank * (CLUSTERS // GROUPS) + within
    member = iota((CLUSTERS, ROWS), 0) == assign_ref[...]
    place = down(pick(member, place_column))
    group = down(pick(member, owner_column))
    order = iota((CLUSTERS, ROWS), 0).astype(F32)
    at_place = order == place
    earlier = onehot(iota((ROWS, ROWS), 0) < iota((ROWS, ROWS), 1))
    before = dot(onehot(at_place), earlier)
    slot = down(pick(at_place, before))
    count_column = across(jnp.where(at_place, 1.0, 0.0))
    partner_count = down(pick(order == (CLUSTERS - 1) - place, count_column))
    slot = slot + jnp.where(place >= CHIPS, partner_count, 0.0)
    chip = jnp.minimum(place, (CLUSTERS - 1) - place)
    return group, chip.astype(jnp.int32), slot.astype(jnp.int32), as_row(count_column)


def missing_documents(index_ref, count_column, group):
    listed = index_ref[...]
    live = iota((GROUPS, CAP), 1).astype(F32) < count_column
    eye = onehot(iota((CAP, CAP), 0) == iota((CAP, CAP), 1))
    high = dot_rows(eye, jnp.where(live, listed >> 4, 0).astype(F32).astype(BF16))
    low = dot_rows(eye, jnp.where(live, listed & 15, 0).astype(F32).astype(BF16))
    alive = dot_rows(eye, onehot(live))
    slots = jnp.where(alive > 0.5, high * 16.0 + low, -1.0)
    document = iota((1, ROWS), 1).astype(F32)
    hits = jnp.zeros((CAP, ROWS), F32)
    for g in range(GROUPS):
        wanted = jnp.where(group == float(g), document, -2.0)
        hits = hits + jnp.where(slots[:, g : g + 1] == wanted, 1.0, 0.0)
    return across(jnp.where(down(hits) > 0.5, 0.0, 1.0))


def receive_plan(table, rank, chip):
    heads = table.astype(jnp.int32)
    counts = (heads & 1023).astype(F32)
    differ = jnp.where((heads >> 10).astype(F32) != rank, 1.0, 0.0)
    sub, lane = iota((CLUSTERS, CLUSTERS), 0), iota((CLUSTERS, CLUSTERS), 1)
    pair = onehot((sub == lane) | (sub == (CLUSTERS - 1) - lane))
    both = dot(counts.astype(BF16), pair)
    fault = across(down(differ))
    fault = fault + across(down(jnp.where(both > SLOTS, 1.0, 0.0)))
    fault = fault + across(jnp.where(down(both) > HELD, 1.0, 0.0))

    lanes = iota((CHIPS, CLUSTERS), 1)
    source, target = iota((CHIPS, CHIPS), 0), iota((CHIPS, CHIPS), 1)
    columns = []
    totals = []
    for place in (chip, (CLUSTERS - 1) - chip):
        number = across(pick(lanes == place, counts))
        start = across(pick(target < source, as_row(number)))
        columns.append((number, start))
        totals.append(down(number))
    spread = iota((CHIPS, LANES), 0) == (iota((CHIPS, LANES), 1) >> 4)
    (first, first_start), (second, second_start) = [
        tuple(down(pick(spread, column)) for column in pair_) for pair_ in columns
    ]
    second_start = second_start + totals[0]

    def row_of(slot):
        slot = slot.astype(F32)
        later = jnp.where(slot < first + second, second_start + (slot - first), -1.0)
        return jnp.where(slot < first, first_start + slot, later)

    position = iota((1, LANES), 1) & (BASE - 1)
    base = row_of(position)
    extra = row_of(BASE + (position & (EXTRA - 1)))
    left = jnp.where(position < EXTRA, extra, -1.0)
    right = jnp.where(position < EXTRA, -1.0, extra)
    return base, left, right, totals[0], totals[0] + totals[1], fault


def kernel(
    x_ref, assign_ref, owner_ref, count_ref, index_ref,
    max_ref, cos_ref, fault_ref,
    send_a, send_b, got_a, got_b, head, heads, pick_a, pick_l, pick_r,
    raw, mine, theirs, stats, their_stats, back, returned,
    send_sem, recv_sem, part_send, part_recv,
):
    grp, blk = lax.axis_index("grp"), lax.axis_index("blk")
    my_x, my_y, my_z, core = grp // 4, grp % 4, blk // 2, blk % 2
    my_chip = grp * 4 + my_z

    def shift_of(step):
        high, middle, low = step // 16, (step // 4) % 4, step % 4
        return low, (middle + low) % 4, (high + middle + low) % 4

    def device_at(step, sign):
        dx, dy, dz = shift_of(step)
        x, y, z = (my_x + sign * dx + 4) % 4, (my_y + sign * dy + 4) % 4, (my_z + sign * dz + 4) % 4
        return {"grp": x * 4 + y, "blk": z * 2 + core}

    other_core = {"grp": grp, "blk": my_z * 2 + (1 - core)}
    barrier = pltpu.get_barrier_semaphore()

    @pl.loop(1, CHIPS)
    def _(step):
        pl.semaphore_signal(
            barrier, inc=1, device_id=device_at(step, 1), device_id_type=pl.DeviceIdType.MESH
        )

    pl.semaphore_signal(barrier, inc=1, device_id=other_core, device_id_type=pl.DeviceIdType.MESH)

    def remote(source, target, sent, arrived, device):
        return pltpu.make_async_remote_copy(
            src_ref=source,
            dst_ref=target,
            send_sem=sent,
            recv_sem=arrived,
            device_id=device,
            device_id_type=pl.DeviceIdType.MESH,
        )

    def await_blocks(ref, number, semaphore):
        block = ref.at[pl.ds(0, number)]
        pltpu.make_async_copy(block, block, semaphore).wait()

    def part_size(part):
        return PACKED - 1 if part == 0 else PACKED

    rank, count_column = rank_groups(count_ref)
    group, chip, slot, place_counts = place_documents(assign_ref, owner_ref, rank)
    dx, dy, dz = ((chip >> 4) - my_x) & 3, (((chip >> 2) & 3) - my_y) & 3, ((chip & 3) - my_z) & 3
    step_of = ((dz - dy) & 3) * 16 + ((dy - dx) & 3) * 4 + dx
    in_base = slot < BASE
    base_slot = jnp.where(in_base, step_of * BASE + slot, -1)
    extra_slot = jnp.where(in_base | (slot >= SLOTS), -1, step_of * BASE + (slot - BASE))
    span = PACKED * BASE

    for part in range(PARTS):
        slots = iota((span, ROWS), 0) + part * span
        rows = dot(onehot(slots == base_slot), x_ref[...]).astype(BF16)
        send_a[pl.ds(part * PACKED, PACKED)] = rows.reshape(PACKED, BASE, WIDTH)
        left = dot(onehot(slots == extra_slot), x_ref[:, :HALF])
        right = dot(onehot((slots - EXTRA == extra_slot) & (extra_slot >= 0)), x_ref[:, HALF:])
        send_b[pl.ds(part * PACKED, PACKED)] = (left + right).astype(BF16).reshape(PACKED, BASE, HALF)
        if part == 0:
            pl.semaphore_wait(barrier, CHIPS)

        @pl.loop(max(part * PACKED, 1), (part + 1) * PACKED)
        def _(step):
            device = device_at(step, 1)
            remote(send_a.at[step], got_a.at[step], part_send.at[part], part_recv.at[part], device).start()
            remote(
                send_b.at[step], got_b.at[step], part_send.at[PARTS + part], part_recv.at[PARTS + part], device
            ).start()

        if part == 0:
            missing = missing_documents(index_ref, count_column, group)
            head[0] = place_counts + 1024.0 * rank + jnp.where(missing > 0.5, 16384.0, 0.0)
            heads[0] = head[0]

            @pl.loop(1, CHIPS)
            def _(step):
                remote(
                    head, heads.at[pl.ds(step, 1)], send_sem.at[0], recv_sem.at[0], device_at(step, 1)
                ).start()

    got_a[0] = send_a[0]
    got_b[0] = send_b[0]

    await_blocks(heads, CHIPS - 1, recv_sem.at[0])
    table = heads[...].reshape(CHIPS, CLUSTERS)
    base, left, right, first_end, held_end, fault = receive_plan(table, rank, my_chip)
    rows = iota((HELD, LANES), 0).astype(F32)
    pick_a[...] = onehot(rows == base)
    pick_l[...] = onehot(rows == left)
    pick_r[...] = onehot(rows == right)

    piece = HELD // 2
    sums = [jnp.zeros((1, WIDTH), F32), jnp.zeros((1, WIDTH), F32)]
    swaps = []
    for part in range(PARTS):
        await_blocks(got_a, part_size(part), part_recv.at[part])
        await_blocks(got_b, part_size(part), part_recv.at[PARTS + part])
        lanes = pl.ds(part * span, span)
        some_a = got_a[pl.ds(part * PACKED, PACKED)].reshape(span, WIDTH)
        some_b = got_b[pl.ds(part * PACKED, PACKED)].reshape(span, HALF)
        for half in range(2):
            window = pl.ds(half * piece, piece)
            some = dot(pick_a[window, lanes], some_a) + jnp.concatenate(
                [dot(pick_l[window, lanes], some_b), dot(pick_r[window, lanes], some_b)], axis=1
            )
            if part == 0:
                raw[window] = some
            elif part < PARTS - 1:
                raw[window] += some
            else:
                some = raw[window] + some
                unit = some * lax.rsqrt(across(some * some) + EPSILON)
                mine[window] = unit.astype(BF16)
                swap = remote(
                    mine.at[window], theirs.at[window], send_sem.at[1 + half], recv_sem.at[1 + half], other_core
                )
                swap.start()
                swaps.append(swap)
                number = (iota((piece, 1), 0) + half * piece).astype(F32)
                sums[0] = sums[0] + down(pick(number < first_end, unit))
                sums[1] = sums[1] + down(pick(number >= first_end, unit))
    lane = iota((1, WIDTH), 1)
    facts = jnp.where(lane == 0, first_end, 0.0)
    facts = jnp.where(lane == 1, held_end, facts)
    facts = jnp.where(lane == 2, fault, facts)
    facts = jnp.concatenate([facts[:, :128], rank, facts[:, 256:]], axis=1)
    row = iota((8, WIDTH), 0)
    stats[...] = pick(row == 0, sums[0]) + pick(row == 1, sums[1]) + pick(row == 2, facts)
    swap = remote(stats, their_stats, send_sem.at[3], recv_sem.at[3], other_core)
    swap.start()
    swaps.append(swap)

    query_number = iota((1, HELD), 1).astype(F32)
    query = jnp.where(query_number < first_end, 0.0, 1.0)

    def best_of(keys, first, held, best, itself):
        for part in range(2):
            window = pl.ds(part * piece, piece)
            scores = dot_rows(keys[window], mine[...])
            number = (iota((piece, 1), 0) + part * piece).astype(F32)
            kind = jnp.where(number < first, 0.0, jnp.where(number < held, 1.0, 2.0))
            matched = kind == query
            if itself:
                matched = matched & (number != query_number)
            best = jnp.maximum(best, jnp.max(jnp.where(matched, scores, -1.0), axis=0, keepdims=True))
        return best

    best = best_of(mine, first_end, held_end, jnp.full((1, HELD), -1.0, F32), True)
    for swap in swaps:
        swap.wait()
    facts = their_stats[2:3, :]
    best = best_of(theirs, facts[:, 0:1], facts[:, 1:2], best, False)

    total = pick(row < 2, stats[...] + their_stats[...])
    centre = total * lax.rsqrt(across(total * total) + EPSILON)
    near = dot_rows(jnp.concatenate(thirds(centre), axis=0).astype(BF16), mine[...])
    near = near[0:8] + near[8:16] + near[16:24]
    near = jnp.where(query_number < first_end, near[0:1], near[1:2])

    parts = thirds(best) + thirds(near)
    row = iota((8, HELD), 0)
    values = jnp.zeros((8, HELD), F32)
    for number, part in enumerate(parts):
        values = jnp.where(row == number, part, values)
    values = values.astype(BF16)
    for first, chosen in ((0, pick_a), (2, pick_l)):
        out = dot(values, chosen[...])
        for kind in range(2):
            line = out[3 * kind : 3 * kind + 1] + out[3 * kind + 1 : 3 * kind + 2] + out[3 * kind + 2 : 3 * kind + 3]
            for tile in range(LANES // 128):
                back[tile, first + kind : first + kind + 1, :] = line[:, tile * 128 : (tile + 1) * 128]
    returned[0] = back[0]

    @pl.loop(1, CHIPS)
    def _(step):
        remote(
            back.at[step // 8], returned.at[step], send_sem.at[4], recv_sem.at[4], device_at(step, -1)
        ).start()

    differ = across(jnp.where(facts[:, 128:256] != rank, 1.0, 0.0))
    fault = fault + facts[:, 2:3] + differ
    fault_ref[...] = jnp.where(fault > 0.5, 1, 0) + jnp.zeros((1, 128), jnp.int32)
    chosen = onehot(iota((CHIPS, ROWS), 0) == step_of)
    sub = iota((128, ROWS), 0) - (step_of & 7) * BASE
    at_base = (sub == slot) & in_base
    at_extra = (sub == slot - BASE) & (slot >= BASE)

    await_blocks(returned, CHIPS - 1, recv_sem.at[4])
    found = []
    for number in range(4):
        terms = jnp.concatenate(thirds(returned[:, number, :]), axis=1).astype(BF16)
        out = lax.dot_general(terms, chosen, (((0,), (0,)), ((), ())), preferred_element_type=F32)
        found.append(out[0:128] + out[128:256] + out[256:384])
    max_ref[...] = down(pick(at_base, found[0]) + pick(at_extra, found[2]))
    cos_ref[...] = down(pick(at_base, found[1]) + pick(at_extra, found[3]))

    await_blocks(heads, CHIPS - 1, send_sem.at[0])
    await_blocks(returned, CHIPS - 1, send_sem.at[4])
    for part in range(PARTS):
        await_blocks(got_a, part_size(part), part_send.at[part])
        await_blocks(got_b, part_size(part), part_send.at[PARTS + part])


def routed(embeddings, assign, owner, send_count, send_index):
    return pl.pallas_call(
        kernel,
        out_shape=(
            jax.ShapeDtypeStruct((1, ROWS), F32),
            jax.ShapeDtypeStruct((1, ROWS), F32),
            jax.ShapeDtypeStruct((1, 128), jnp.int32),
        ),
        in_specs=[pl.BlockSpec(memory_space=pltpu.VMEM)] * 5,
        out_specs=(pl.BlockSpec(memory_space=pltpu.VMEM),) * 3,
        scratch_shapes=[
            pltpu.VMEM((CHIPS, BASE, WIDTH), BF16),
            pltpu.VMEM((CHIPS, BASE, HALF), BF16),
            pltpu.VMEM((CHIPS, BASE, WIDTH), BF16),
            pltpu.VMEM((CHIPS, BASE, HALF), BF16),
            pltpu.VMEM((1, 1, 128), F32),
            pltpu.VMEM((CHIPS, 1, 128), F32),
            pltpu.VMEM((HELD, LANES), BF16),
            pltpu.VMEM((HELD, LANES), BF16),
            pltpu.VMEM((HELD, LANES), BF16),
            pltpu.VMEM((HELD, WIDTH), F32),
            pltpu.VMEM((HELD, WIDTH), BF16),
            pltpu.VMEM((HELD, WIDTH), BF16),
            pltpu.VMEM((8, WIDTH), F32),
            pltpu.VMEM((8, WIDTH), F32),
            pltpu.VMEM((LANES // 128, 4, 128), F32),
            pltpu.VMEM((CHIPS, 4, 128), F32),
            pltpu.SemaphoreType.DMA((5,)),
            pltpu.SemaphoreType.DMA((5,)),
            pltpu.SemaphoreType.DMA((2 * PARTS,)),
            pltpu.SemaphoreType.DMA((2 * PARTS,)),
        ],
        compiler_params=pltpu.CompilerParams(
            collective_id=0, has_side_effects=True, vmem_limit_bytes=48 * 1024 * 1024
        ),
    )(
        embeddings,
        assign.reshape(1, ROWS),
        owner.reshape(1, CLUSTERS),
        send_count,
        send_index[0],
    )


def body(embeddings, assign, owner, send_count, send_index):
    arguments = (embeddings, assign, owner, send_count, send_index)
    max_sim, centroid_cos, fault = routed(*arguments)
    return lax.cond(
        fault[0, 0] != 0,
        lambda: general(*arguments),
        lambda: (max_sim.reshape(ROWS), centroid_cos.reshape(ROWS)),
    )


def solution(mesh):
    placed = (
        P(("grp", "blk"), None),
        P(("grp", "blk")),
        P(),
        P(("grp", "blk"), None),
        P(("grp", "blk"), None, None),
    )
    return jax.shard_map(
        body,
        mesh=mesh,
        in_specs=placed,
        out_specs=(P(("grp", "blk")), P(("grp", "blk"))),
        check_vma=False,
    )
```

```python
import functools

import jax
import jax.numpy as jnp
from jax import lax
from jax.experimental import pallas as pl
from jax.experimental.pallas import tpu as pltpu
from jax.sharding import PartitionSpec as P

EPSILON = 1e-06
F32 = jnp.float32
BF16 = jnp.bfloat16

CHIPS = 64
ROWS = 512
WIDTH = 768
CLUSTERS = 128
GROUPS = 16
CAP = 64
BASE = 16
HALF = WIDTH // 2
LINES = 16
DEPTH = 4
POOL = 8
SEGMENT = 256
PARTS = ((0, 24), (24, 24), (48, 16))
LAST = len(PARTS) - 1


def normalize(values):
    widened = values.astype(F32)
    return widened * lax.rsqrt(jnp.sum(widened * widened, axis=1, keepdims=True) + EPSILON)


def general(embeddings, assign, owner, send_count, send_index):
    rows_local = embeddings.shape[0]
    feature_width = embeddings.shape[1]
    groups = lax.axis_size("grp")
    clusters = owner.shape[0]
    capacity = send_index.shape[2]
    slot_total = groups * capacity
    unit_rows = normalize(embeddings)
    unit_low = unit_rows.astype(BF16)
    counts = send_count[0]
    listed = send_index[0]
    live_slot = jnp.arange(capacity, dtype=jnp.int32)[None, :] < counts[:, None]
    listed_cluster = assign[listed]
    owned_here = owner[listed_cluster] == jnp.arange(groups, dtype=jnp.int32)[:, None]
    kept_slot = live_slot & owned_here
    out_cluster = jnp.where(kept_slot, listed_cluster, -1)
    out_tag = jnp.where(kept_slot, lax.axis_index(("grp", "blk")) * rows_local + listed, -1)
    out_vector = unit_low[listed.reshape(-1)].reshape(groups, capacity, feature_width)
    got_vector, got_cluster, got_tag = (
        lax.all_to_all(out_vector, "grp", split_axis=0, concat_axis=0, tiled=True),
        lax.all_to_all(out_cluster, "grp", split_axis=0, concat_axis=0, tiled=True),
        lax.all_to_all(out_tag, "grp", split_axis=0, concat_axis=0, tiled=True),
    )
    own_vector = got_vector.reshape(slot_total, feature_width)
    own_cluster = got_cluster.reshape(slot_total)
    own_tag = got_tag.reshape(slot_total)

    def tile_best(current, shard_piece):
        other_vector, other_cluster, other_tag = shard_piece
        scores = jnp.einsum("id,jd->ij", own_vector, other_vector, preferred_element_type=F32)
        matched = (
            (own_cluster[:, None] == other_cluster[None, :])
            & (other_cluster[None, :] >= 0)
            & (own_tag[:, None] != other_tag[None, :])
        )
        return jnp.maximum(current, jnp.max(jnp.where(matched, scores, -1.0), axis=1))

    other_vector = lax.all_gather(own_vector, "blk", axis=0, tiled=True)
    other_cluster = lax.all_gather(own_cluster, "blk", axis=0, tiled=True)
    other_tag = lax.all_gather(own_tag, "blk", axis=0, tiled=True)
    length = other_vector.shape[0]
    number = length // slot_total
    stacked = (
        other_vector.reshape(number, slot_total, feature_width),
        other_cluster.reshape(number, slot_total),
        other_tag.reshape(number, slot_total),
    )

    def scan_step(carry, single):
        return (tile_best(carry, single), None)

    result, unused = lax.scan(scan_step, jnp.full((slot_total,), -1.0, F32), stacked)
    target = jnp.where(live_slot, listed, rows_local).reshape(-1)
    partial_sum = jax.ops.segment_sum(unit_rows, assign, num_segments=clusters)
    centre = normalize(lax.psum(partial_sum, ("grp", "blk")))
    nearness = jnp.sum(unit_low.astype(F32) * centre[assign], axis=1)
    returned = lax.all_to_all(
        result.reshape(groups, capacity), "grp", split_axis=0, concat_axis=0, tiled=True
    )
    has_entry = (
        jnp.zeros((rows_local,), jnp.int32)
        .at[target]
        .max(kept_slot.astype(jnp.int32).reshape(-1), mode="drop")
    )
    centroid_cos = jnp.where(has_entry > 0, nearness, 0.0)
    max_sim = jnp.full((rows_local,), -1.0, F32).at[target].max(returned.reshape(-1), mode="drop")
    return (max_sim, centroid_cos)


def iota(shape, axis):
    return lax.broadcasted_iota(jnp.int32, shape, axis)


def down(values):
    return jnp.sum(values, axis=0, keepdims=True)


def across(values):
    return jnp.sum(values, axis=1, keepdims=True)


def pick(mask, values):
    return jnp.where(mask, values, 0.0)


def as_column(row):
    size = row.shape[1]
    return across(pick(iota((size, size), 0) == iota((size, size), 1), row))


def as_row(column):
    size = column.shape[0]
    return down(pick(iota((size, size), 0) == iota((size, size), 1), column))


def dot(a, b):
    return jnp.dot(a, b, preferred_element_type=F32)


def dot_rows(a, b):
    return lax.dot_general(a, b, (((1,), (1,)), ((), ())), preferred_element_type=F32)


def onehot(mask):
    return jnp.where(mask, 1.0, 0.0).astype(BF16)


def thirds(values):
    first = values.astype(BF16).astype(F32)
    rest = values - first
    second = rest.astype(BF16).astype(F32)
    third = (rest - second).astype(BF16).astype(F32)
    return first, second, third


def rank_groups(count_ref):
    count_row = count_ref[...].astype(F32)
    count_column = as_column(count_row)
    sub, lane = iota((GROUPS, 128), 0), iota((GROUPS, 128), 1)
    count_lanes = down(pick(sub == lane, count_column))
    ahead = (count_column > count_lanes) | ((count_column == count_lanes) & (sub < lane))
    rank = down(jnp.where(ahead, 1.0, 0.0))
    return jnp.where(iota((1, 128), 1) < GROUPS, rank, 0.0), count_column


def place_documents(assign_ref, owner_ref, rank):
    owner_row = owner_ref[...].astype(F32)
    owner_column = as_column(owner_row)
    sub, lane = iota((CLUSTERS, CLUSTERS), 0), iota((CLUSTERS, CLUSTERS), 1)
    within = across(jnp.where((owner_column == owner_row) & (lane < sub), 1.0, 0.0))
    group_rank = across(pick(owner_column == lane.astype(F32), rank))
    place_column = group_rank * (CLUSTERS // GROUPS) + within
    member = iota((CLUSTERS, ROWS), 0) == assign_ref[...]
    place = down(pick(member, place_column))
    group = down(pick(member, owner_column))
    order = iota((CLUSTERS, ROWS), 0).astype(F32)
    at_place = order == place
    earlier = onehot(iota((ROWS, ROWS), 0) < iota((ROWS, ROWS), 1))
    before = dot(onehot(at_place), earlier)
    slot = down(pick(at_place, before))
    count_column = across(jnp.where(at_place, 1.0, 0.0))
    partner_count = down(pick(order == (CLUSTERS - 1) - place, count_column))
    slot = slot + jnp.where(place >= CHIPS, partner_count, 0.0)
    chip = jnp.minimum(place, (CLUSTERS - 1) - place)
    return group, chip.astype(jnp.int32), slot.astype(jnp.int32), as_row(count_column)


def missing_documents(index_ref, count_column, group):
    listed = index_ref[...]
    live = iota((GROUPS, CAP), 1).astype(F32) < count_column
    eye = onehot(iota((CAP, CAP), 0) == iota((CAP, CAP), 1))
    high = dot_rows(eye, jnp.where(live, listed >> 4, 0).astype(F32).astype(BF16))
    low = dot_rows(eye, jnp.where(live, listed & 15, 0).astype(F32).astype(BF16))
    alive = dot_rows(eye, onehot(live))
    slots = jnp.where(alive > 0.5, high * 16.0 + low, -1.0)
    document = iota((1, ROWS), 1).astype(F32)
    hits = jnp.zeros((CAP, ROWS), F32)
    for g in range(GROUPS):
        wanted = jnp.where(group == float(g), document, -2.0)
        hits = hits + jnp.where(slots[:, g : g + 1] == wanted, 1.0, 0.0)
    return across(jnp.where(down(hits) > 0.5, 0.0, 1.0))


def shift_of(step):
    high, middle, low = step // 16, (step // 4) % 4, step % 4
    return low, (middle + low) % 4, (high + middle + low) % 4


def step_to(dx, dy, dz):
    dx, dy, dz = dx & 3, dy & 3, dz & 3
    return ((dz - dy) & 3) * 16 + ((dy - dx) & 3) * 4 + dx


def in_part(step, part):
    first, number = PARTS[part]
    return (step >= first) & (step < first + number)


def chip_places():
    sub, lane = iota((CLUSTERS, CLUSTERS), 0), iota((CLUSTERS, CLUSTERS), 1)
    return onehot((sub == lane) | (sub == (CLUSTERS - 1) - lane))


def excess(totals):
    lane = iota(totals.shape, 1)
    return jnp.where(lane < CHIPS, jnp.maximum(totals - BASE, 0.0), 0.0)


def receive_plan(table, rank, my_x, my_y, my_z):
    chip = my_x * 16 + my_y * 4 + my_z
    heads = table.astype(jnp.int32)
    counts = (heads & 1023).astype(F32)
    differ = jnp.where((heads >> 10).astype(F32) != rank, 1.0, 0.0)
    fault = across(down(differ))
    both = dot(counts.astype(BF16), chip_places())
    over = excess(both)

    def origin(step):
        low, middle, high = step & 3, (step >> 2) & 3, step >> 4
        return (my_x - low) & 3, (my_y - middle - low) & 3, (my_z - high - middle - low) & 3

    lanes = iota((CHIPS, CLUSTERS), 1)
    own_x, own_y, own_z = origin(iota((CHIPS, 1), 0))
    line = own_x * 4 + own_y
    row_x, row_y, row_z = origin(iota((1, CHIPS), 1))
    same_line = line == row_x * 4 + row_y
    over_total = across(over)
    over_row = as_row(over_total)
    line_start = across(pick(same_line & (row_z < own_z), over_row))
    line_total = across(pick(same_line, over_row))
    fault = fault + down(jnp.where(line_total > POOL, 1.0, 0.0))
    start = line_start + across(pick(lanes < chip, over))
    number = across(pick(lanes == chip, over))

    to_chip = iota((1, CLUSTERS), 1)
    route = step_to((to_chip >> 4) - own_x, ((to_chip >> 2) & 3) - own_y, (to_chip & 3) - own_z)
    based = jnp.where(lanes < CHIPS, jnp.minimum(both, float(BASE)), 0.0)
    for part in range(len(PARTS)):
        held = down(pick(in_part(route, part), based))
        if part == LAST:
            held = held + down(over)
        fault = fault + across(jnp.where(held > SEGMENT, 1.0, 0.0))

    first = across(pick(lanes == chip, counts))
    second = across(pick(lanes == (CLUSTERS - 1) - chip, counts))
    place = (lanes & (POOL - 1)).astype(F32) - start
    mine = (line == (lanes >> 3)) & (place >= 0.0) & (place < number)
    over_first = down(jnp.where(mine & (place + BASE < first), 1.0, 0.0))
    over_second = down(jnp.where(mine & (place + BASE >= first), 1.0, 0.0))
    over_first_total, over_second_total = across(over_first), across(over_second)
    earlier = onehot(iota((CLUSTERS, CLUSTERS), 0) < iota((CLUSTERS, CLUSTERS), 1))
    sub = iota((16, CLUSTERS), 0)
    before = dot((pick(sub == 0, over_first) + pick(sub == 1, over_second)).astype(BF16), earlier)

    base_first = jnp.minimum(first, float(BASE))
    base_second = jnp.minimum(first + second, float(BASE)) - base_first
    source, target = iota((CHIPS, CHIPS), 0), iota((CHIPS, CHIPS), 1)
    first_row, second_row = as_row(base_first), as_row(base_second)
    plans = []
    ends = []
    for part, (begin, steps) in enumerate(PARTS):
        inside = in_part(iota((CHIPS, 1), 0), part)
        ahead = (target < source) & in_part(iota((1, CHIPS), 1), part)
        first_total = down(pick(inside, base_first))
        second_total = down(pick(inside, base_second))
        first_end = first_total + over_first_total if part == LAST else first_total
        first_start = across(pick(ahead, first_row))
        second_start = across(pick(ahead, second_row)) + first_end
        spread = iota((CHIPS, steps * BASE), 0) - begin == (iota((CHIPS, steps * BASE), 1) >> 4)
        head, tail, head_start, tail_start = [
            down(pick(spread, column)) for column in (base_first, base_second, first_start, second_start)
        ]
        slot = (iota((1, steps * BASE), 1) & (BASE - 1)).astype(F32)
        later = jnp.where(slot < head + tail, tail_start + (slot - head), -1.0)
        plans.append(jnp.where(slot < head, head_start + slot, later))
        held_end = first_end + second_total
        if part == LAST:
            over_row_of = jnp.where(over_second > 0.5, held_end + before[1:2], -1.0)
            over_row_of = jnp.where(over_first > 0.5, first_total + before[0:1], over_row_of)
            held_end = held_end + over_second_total
        ends.append((first_end, held_end))
    return plans, over_row_of, ends, line_start, line_total, over_total, fault


def kernel(
    x_hbm, assign_ref, owner_ref, count_ref, index_ref,
    max_ref, cos_ref, fault_ref,
    x_ref, send, got, head, heads, own_over, line_over, send_over, got_over,
    pick_0, pick_1, pick_2, pick_left, pick_right, pick_over,
    mine, theirs, facts, their_facts, sums, their_sums, back, returned,
    x_sem, send_sem, recv_sem,
):
    grp, blk = lax.axis_index("grp"), lax.axis_index("blk")
    my_x, my_y, my_z, core = grp // 4, grp % 4, blk // 2, blk % 2
    picks = (pick_0, pick_1, pick_2)

    def device_at(step, sign):
        dx, dy, dz = shift_of(step)
        x, y, z = (my_x + sign * dx + 4) % 4, (my_y + sign * dy + 4) % 4, (my_z + sign * dz + 4) % 4
        return {"grp": x * 4 + y, "blk": z * 2 + core}

    other_core = {"grp": grp, "blk": my_z * 2 + (1 - core)}
    barrier = pltpu.get_barrier_semaphore()
    load = pltpu.make_async_copy(x_hbm, x_ref, x_sem)
    load.start()

    @pl.loop(1, CHIPS)
    def _(step):
        pl.semaphore_signal(
            barrier, inc=1, device_id=device_at(step, 1), device_id_type=pl.DeviceIdType.MESH
        )

    pl.semaphore_signal(barrier, inc=1, device_id=other_core, device_id_type=pl.DeviceIdType.MESH)

    def remote(source, target, number, device):
        return pltpu.make_async_remote_copy(
            src_ref=source,
            dst_ref=target,
            send_sem=send_sem.at[number],
            recv_sem=recv_sem.at[number],
            device_id=device,
            device_id_type=pl.DeviceIdType.MESH,
        )

    def await_blocks(ref, number, semaphore):
        block = ref.at[pl.ds(0, number)]
        pltpu.make_async_copy(block, block, semaphore).wait()

    HEADS, LINE, OVER, FACTS, SUMS, BACK, SWAP, PART = 0, 1, 2, 3, 4, 5, 6, 9

    def messages(part):
        return PARTS[part][1] - (1 if part == 0 else 0)

    rank, count_column = rank_groups(count_ref)
    group, chip, slot, place_counts = place_documents(assign_ref, owner_ref, rank)
    step_of = step_to((chip >> 4) - my_x, ((chip >> 2) & 3) - my_y, (chip & 3) - my_z)
    in_base = slot < BASE
    base_slot = jnp.where(in_base, step_of * BASE + slot, -1)
    load.wait()

    def pack(part):
        begin, steps = PARTS[part]
        slots = iota((steps * BASE, ROWS), 0) + begin * BASE
        rows = dot(onehot(slots == base_slot), x_ref[...]).astype(BF16)
        send[pl.ds(begin, steps)] = rows.reshape(steps, BASE, WIDTH)

    def post(part):
        begin, steps = PARTS[part]

        @pl.loop(max(begin, 1), begin + steps)
        def _(step):
            remote(send.at[step], got.at[step], PART + part, device_at(step, 1)).start()

    pack(0)
    pl.semaphore_wait(barrier, CHIPS)
    post(0)
    place_counts_8 = place_counts + jnp.zeros((16, CLUSTERS), F32)
    own_excess = excess(dot(place_counts_8.astype(BF16), chip_places())[0:1])
    eye = iota((CHIPS, CLUSTERS), 0) == iota((CHIPS, CLUSTERS), 1)
    excess_column = across(pick(eye, own_excess))
    over_slot = down(pick(iota((CHIPS, ROWS), 0) < chip, excess_column)).astype(jnp.int32) + (slot - BASE)
    over_slot = jnp.where(in_base, -1, over_slot)
    own_over[...] = dot(onehot(iota((BASE, ROWS), 0) == over_slot), x_ref[...]).astype(BF16)
    line_over[my_z] = own_over[...]

    @pl.loop(1, DEPTH)
    def _(step):
        device = {"grp": grp, "blk": ((my_z + step) % DEPTH) * 2 + core}
        remote(own_over, line_over.at[my_z], LINE, device).start()

    missing = missing_documents(index_ref, count_column, group)
    head[0] = place_counts + 1024.0 * rank + jnp.where(missing > 0.5, 16384.0, 0.0)
    heads[0] = head[0]

    @pl.loop(1, CHIPS)
    def _(step):
        remote(head, heads.at[pl.ds(step, 1)], HEADS, device_at(step, 1)).start()

    pack(1)
    post(1)
    pack(2)
    got[0] = send[0]

    await_blocks(heads, CHIPS - 1, recv_sem.at[HEADS])
    table = heads[...].reshape(CHIPS, CLUSTERS)
    plans, over_row_of, ends, line_start, line_total, over_total, fault = receive_plan(
        table, rank, my_x, my_y, my_z
    )

    await_blocks(line_over, DEPTH - 1, recv_sem.at[LINE])
    sender = iota((CHIPS, 1), 0)
    low, middle, high = sender & 3, (sender >> 2) & 3, sender >> 4
    in_line = (low == 0) & (middle == 0)
    depth = (my_z - high) & 3
    entry = iota((CHIPS, DEPTH * BASE), 1)
    at = in_line & (depth == (entry >> 4))
    begin = down(pick(at, line_start))
    number = down(pick(at, over_total))
    order = (iota((1, DEPTH * BASE), 1) & (BASE - 1)).astype(F32)
    order = jnp.where(order < number, begin + order, -1.0)
    my_start = line_start[0:1]
    rows = iota((2 * POOL, DEPTH * BASE), 0).astype(F32)
    blocks = line_over[...].reshape(DEPTH * BASE, WIDTH)
    left = dot(onehot((rows == order) & (rows < POOL)), blocks[:, :HALF])
    right = dot(onehot((rows - POOL == order) & (rows >= POOL)), blocks[:, HALF:])
    send_over[...] = (left + right).astype(BF16)
    got_over[grp] = send_over[...]

    @pl.loop(1, LINES)
    def _(step):
        low, middle = step % 4, step // 4
        x, y = (my_x + low) % 4, (my_y + middle + low) % 4
        remote(send_over, got_over.at[grp], OVER, {"grp": x * 4 + y, "blk": blk}).start()

    post(2)
    lane = iota((1, 128), 1)
    told = jnp.where(lane == 0, fault, 0.0)
    for part, (first_end, held_end) in enumerate(ends):
        told = jnp.where(lane == 1 + 2 * part, first_end, told)
        told = jnp.where(lane == 2 + 2 * part, held_end, told)
    row = iota((8, 128), 0)
    facts[...] = pick(row == 0, told) + pick(row == 1, rank)
    swap_facts = remote(facts, their_facts, FACTS, other_core)
    swap_facts.start()

    for part, plan in enumerate(plans):
        picks[part][...] = onehot(iota((SEGMENT, plan.shape[1]), 0).astype(F32) == plan)
    rows = iota((SEGMENT, LINES * 2 * POOL), 0).astype(F32)
    position = iota((CLUSTERS, LINES * 2 * POOL), 1)
    spread = onehot(iota((CLUSTERS, LINES * 2 * POOL), 0) == (position >> 4) * POOL + (position & (POOL - 1)))
    wide = dot((over_row_of + jnp.zeros((16, CLUSTERS), F32)).astype(BF16), spread)[0:1]
    is_left = (iota((1, LINES * 2 * POOL), 1) & POOL) == 0
    pick_left[...] = onehot((rows == wide) & is_left)
    pick_right[...] = onehot((rows == wide) & (~is_left))
    pick_over[...] = onehot(iota((SEGMENT, CLUSTERS), 0).astype(F32) == over_row_of)

    key_number = iota((SEGMENT, 1), 0).astype(F32)
    query_number = iota((1, SEGMENT), 1).astype(F32)
    best = [jnp.full((1, SEGMENT), -1.0, F32) for _ in PARTS]
    their_ends = []
    totals = [jnp.zeros((1, WIDTH), F32), jnp.zeros((1, WIDTH), F32)]
    swaps = []

    def compare(keys, key_part, query_part, key_ends, itself):
        window = pl.ds(key_part * SEGMENT, SEGMENT)
        scores = dot_rows(keys[window], mine[pl.ds(query_part * SEGMENT, SEGMENT)])
        first, held = key_ends[key_part]
        kind = jnp.where(key_number < first, 0.0, jnp.where(key_number < held, 1.0, 2.0))
        matched = kind == jnp.where(query_number < ends[query_part][0], 0.0, 1.0)
        if itself and key_part == query_part:
            matched = matched & (key_number != query_number)
        scores = jnp.max(jnp.where(matched, scores, -1.0), axis=0, keepdims=True)
        best[query_part] = jnp.maximum(best[query_part], scores)

    def compare_theirs(part, queries):
        for query_part in queries:
            compare(theirs, part, query_part, their_ends, False)

    for part, (begin, steps) in enumerate(PARTS):
        await_blocks(got, messages(part), recv_sem.at[PART + part])
        window = pl.ds(part * SEGMENT, SEGMENT)
        rows = dot(picks[part][...], got[pl.ds(begin, steps)].reshape(steps * BASE, WIDTH))
        if part == LAST:
            await_blocks(got_over, LINES - 1, recv_sem.at[OVER])
            halves = got_over[...].reshape(LINES * 2 * POOL, HALF)
            rows = rows + jnp.concatenate(
                [dot(pick_left[...], halves), dot(pick_right[...], halves)], axis=1
            )
        unit = rows * lax.rsqrt(across(rows * rows) + EPSILON)
        mine[window] = unit.astype(BF16)
        swap = remote(mine.at[window], theirs.at[window], SWAP + part, other_core)
        swap.start()
        swaps.append(swap)
        is_first = key_number < ends[part][0]
        totals[0] = totals[0] + down(pick(is_first, unit))
        totals[1] = totals[1] + down(jnp.where(is_first, 0.0, unit))
        if part == LAST:
            row = iota((8, WIDTH), 0)
            sums[...] = pick(row == 0, totals[0]) + pick(row == 1, totals[1])
            swap_sums = remote(sums, their_sums, SUMS, other_core)
            swap_sums.start()
        for other in range(part + 1):
            compare(mine, part, other, ends, True)
            if other != part:
                compare(mine, other, part, ends, True)
        if part == 0:
            swap_facts.wait()
            their_told = their_facts[...]
            for number in range(len(PARTS)):
                their_ends.append(
                    (their_told[0:1, 1 + 2 * number : 2 + 2 * number], their_told[0:1, 2 + 2 * number : 3 + 2 * number])
                )
        else:
            for other in range(part - 1):
                compare_theirs(other, [part])
            swaps[part - 1].wait()
            compare_theirs(part - 1, range(part + 1))

    swap_sums.wait()
    total = sums[...] + their_sums[...]
    centre = total * lax.rsqrt(across(total * total) + EPSILON)
    near = dot_rows(jnp.concatenate(thirds(centre), axis=0).astype(BF16), mine[...])
    near = near[0:8] + near[8:16] + near[16:24]
    swaps[LAST].wait()
    compare_theirs(LAST, range(len(PARTS)))

    row = iota((8, SEGMENT), 0)
    lines = [[], []]

    def joined(out, kind):
        return out[3 * kind : 3 * kind + 1] + out[3 * kind + 1 : 3 * kind + 2] + out[3 * kind + 2 : 3 * kind + 3]

    for part, (begin, steps) in enumerate(PARTS):
        some = near[:, part * SEGMENT : (part + 1) * SEGMENT]
        some = jnp.where(query_number < ends[part][0], some[0:1], some[1:2])
        values = jnp.zeros((8, SEGMENT), F32)
        for number, term in enumerate(thirds(best[part]) + thirds(some)):
            values = jnp.where(row == number, term, values)
        values = values.astype(BF16)
        out = dot(values, picks[part][...])
        for kind in range(2):
            line = joined(out, kind)
            for tile in range(steps * BASE // 128):
                back[begin * BASE // 128 + tile, kind : kind + 1, :] = line[:, tile * 128 : (tile + 1) * 128]
        if part == LAST:
            out = dot(values, pick_over[...])
            for kind in range(2):
                for tile in range(CHIPS * BASE // 128):
                    back[tile, 2 + kind : 3 + kind, :] = joined(out, kind)
    returned[0] = back[0]

    @pl.loop(1, CHIPS)
    def _(step):
        remote(back.at[step // 8], returned.at[step], BACK, device_at(step, -1)).start()

    differ = across(jnp.where(their_told[1:2] != rank, 1.0, 0.0))
    fault = fault + their_told[0:1, 0:1] + differ
    fault_ref[...] = jnp.where(fault > 0.5, 1, 0) + jnp.zeros((1, 128), jnp.int32)
    chosen = onehot(iota((CHIPS, ROWS), 0) == step_of)
    sub = iota((128, ROWS), 0)
    at_base = (sub == (step_of & 7) * BASE + slot) & in_base
    at_over = (sub == grp * POOL + my_start.astype(jnp.int32) + over_slot) & (~in_base)

    await_blocks(returned, CHIPS - 1, recv_sem.at[BACK])
    found = []
    for number in range(4):
        terms = jnp.concatenate(thirds(returned[:, number, :]), axis=1).astype(BF16)
        out = lax.dot_general(terms, chosen, (((0,), (0,)), ((), ())), preferred_element_type=F32)
        found.append(out[0:128] + out[128:256] + out[256:384])
    max_ref[...] = down(pick(at_base, found[0]) + pick(at_over, found[2]))
    cos_ref[...] = down(pick(at_base, found[1]) + pick(at_over, found[3]))

    await_blocks(heads, CHIPS - 1, send_sem.at[HEADS])
    await_blocks(line_over, DEPTH - 1, send_sem.at[LINE])
    await_blocks(got_over, LINES - 1, send_sem.at[OVER])
    await_blocks(returned, CHIPS - 1, send_sem.at[BACK])
    for part in range(len(PARTS)):
        await_blocks(got, messages(part), send_sem.at[PART + part])


def routed(embeddings, assign, owner, send_count, send_index):
    return pl.pallas_call(
        kernel,
        out_shape=(
            jax.ShapeDtypeStruct((1, ROWS), F32),
            jax.ShapeDtypeStruct((1, ROWS), F32),
            jax.ShapeDtypeStruct((1, 128), jnp.int32),
        ),
        in_specs=[pl.BlockSpec(memory_space=pl.ANY)] + [pl.BlockSpec(memory_space=pltpu.VMEM)] * 4,
        out_specs=(pl.BlockSpec(memory_space=pltpu.VMEM),) * 3,
        scratch_shapes=[
            pltpu.VMEM((ROWS, WIDTH), BF16),
            pltpu.VMEM((CHIPS, BASE, WIDTH), BF16),
            pltpu.VMEM((CHIPS, BASE, WIDTH), BF16),
            pltpu.VMEM((1, 1, 128), F32),
            pltpu.VMEM((CHIPS, 1, 128), F32),
            pltpu.VMEM((BASE, WIDTH), BF16),
            pltpu.VMEM((DEPTH, BASE, WIDTH), BF16),
            pltpu.VMEM((2 * POOL, HALF), BF16),
            pltpu.VMEM((LINES, 2 * POOL, HALF), BF16),
            *[pltpu.VMEM((SEGMENT, steps * BASE), BF16) for _, steps in PARTS],
            pltpu.VMEM((SEGMENT, LINES * 2 * POOL), BF16),
            pltpu.VMEM((SEGMENT, LINES * 2 * POOL), BF16),
            pltpu.VMEM((SEGMENT, LINES * POOL), BF16),
            pltpu.VMEM((len(PARTS) * SEGMENT, WIDTH), BF16),
            pltpu.VMEM((len(PARTS) * SEGMENT, WIDTH), BF16),
            pltpu.VMEM((8, 128), F32),
            pltpu.VMEM((8, 128), F32),
            pltpu.VMEM((8, WIDTH), F32),
            pltpu.VMEM((8, WIDTH), F32),
            pltpu.VMEM((CHIPS * BASE // 128, 4, 128), F32),
            pltpu.VMEM((CHIPS, 4, 128), F32),
            pltpu.SemaphoreType.DMA,
            pltpu.SemaphoreType.DMA((12,)),
            pltpu.SemaphoreType.DMA((12,)),
        ],
        compiler_params=pltpu.CompilerParams(
            collective_id=0, has_side_effects=True, vmem_limit_bytes=48 * 1024 * 1024
        ),
    )(
        embeddings,
        assign.reshape(1, ROWS),
        owner.reshape(1, CLUSTERS),
        send_count,
        send_index[0],
    )


def body(embeddings, assign, owner, send_count, send_index):
    arguments = (embeddings, assign, owner, send_count, send_index)
    max_sim, centroid_cos, fault = routed(*arguments)
    return lax.cond(
        fault[0, 0] != 0,
        lambda: general(*arguments),
        lambda: (max_sim.reshape(ROWS), centroid_cos.reshape(ROWS)),
    )


def solution(mesh):
    placed = (
        P(("grp", "blk"), None),
        P(("grp", "blk")),
        P(),
        P(("grp", "blk"), None),
        P(("grp", "blk"), None, None),
    )
    return jax.shard_map(
        body,
        mesh=mesh,
        in_specs=placed,
        out_specs=(P(("grp", "blk")), P(("grp", "blk"))),
        check_vma=False,
    )
```

```python
import functools

import jax
import jax.numpy as jnp
from jax import lax
from jax.experimental import pallas as pl
from jax.experimental.pallas import tpu as pltpu
from jax.sharding import PartitionSpec as P

EPSILON = 1e-06
F32 = jnp.float32
BF16 = jnp.bfloat16

CHIPS = 64
ROWS = 512
WIDTH = 768
CLUSTERS = 128
GROUPS = 16
CAP = 64
BASE = 16
HALF = WIDTH // 2
LINES = 16
DEPTH = 4
POOL = 8
SEGMENT = 256
PARTS = ((0, 24), (24, 24), (48, 16))
LAST = len(PARTS) - 1


def normalize(values):
    widened = values.astype(F32)
    return widened * lax.rsqrt(jnp.sum(widened * widened, axis=1, keepdims=True) + EPSILON)


def general(embeddings, assign, owner, send_count, send_index):
    rows_local = embeddings.shape[0]
    feature_width = embeddings.shape[1]
    groups = lax.axis_size("grp")
    clusters = owner.shape[0]
    capacity = send_index.shape[2]
    slot_total = groups * capacity
    unit_rows = normalize(embeddings)
    unit_low = unit_rows.astype(BF16)
    counts = send_count[0]
    listed = send_index[0]
    live_slot = jnp.arange(capacity, dtype=jnp.int32)[None, :] < counts[:, None]
    listed_cluster = assign[listed]
    owned_here = owner[listed_cluster] == jnp.arange(groups, dtype=jnp.int32)[:, None]
    kept_slot = live_slot & owned_here
    out_cluster = jnp.where(kept_slot, listed_cluster, -1)
    out_tag = jnp.where(kept_slot, lax.axis_index(("grp", "blk")) * rows_local + listed, -1)
    out_vector = unit_low[listed.reshape(-1)].reshape(groups, capacity, feature_width)
    got_vector, got_cluster, got_tag = (
        lax.all_to_all(out_vector, "grp", split_axis=0, concat_axis=0, tiled=True),
        lax.all_to_all(out_cluster, "grp", split_axis=0, concat_axis=0, tiled=True),
        lax.all_to_all(out_tag, "grp", split_axis=0, concat_axis=0, tiled=True),
    )
    own_vector = got_vector.reshape(slot_total, feature_width)
    own_cluster = got_cluster.reshape(slot_total)
    own_tag = got_tag.reshape(slot_total)

    def tile_best(current, shard_piece):
        other_vector, other_cluster, other_tag = shard_piece
        scores = jnp.einsum("id,jd->ij", own_vector, other_vector, preferred_element_type=F32)
        matched = (
            (own_cluster[:, None] == other_cluster[None, :])
            & (other_cluster[None, :] >= 0)
            & (own_tag[:, None] != other_tag[None, :])
        )
        return jnp.maximum(current, jnp.max(jnp.where(matched, scores, -1.0), axis=1))

    other_vector = lax.all_gather(own_vector, "blk", axis=0, tiled=True)
    other_cluster = lax.all_gather(own_cluster, "blk", axis=0, tiled=True)
    other_tag = lax.all_gather(own_tag, "blk", axis=0, tiled=True)
    length = other_vector.shape[0]
    number = length // slot_total
    stacked = (
        other_vector.reshape(number, slot_total, feature_width),
        other_cluster.reshape(number, slot_total),
        other_tag.reshape(number, slot_total),
    )

    def scan_step(carry, single):
        return (tile_best(carry, single), None)

    result, unused = lax.scan(scan_step, jnp.full((slot_total,), -1.0, F32), stacked)
    target = jnp.where(live_slot, listed, rows_local).reshape(-1)
    partial_sum = jax.ops.segment_sum(unit_rows, assign, num_segments=clusters)
    centre = normalize(lax.psum(partial_sum, ("grp", "blk")))
    nearness = jnp.sum(unit_low.astype(F32) * centre[assign], axis=1)
    returned = lax.all_to_all(
        result.reshape(groups, capacity), "grp", split_axis=0, concat_axis=0, tiled=True
    )
    has_entry = (
        jnp.zeros((rows_local,), jnp.int32)
        .at[target]
        .max(kept_slot.astype(jnp.int32).reshape(-1), mode="drop")
    )
    centroid_cos = jnp.where(has_entry > 0, nearness, 0.0)
    max_sim = jnp.full((rows_local,), -1.0, F32).at[target].max(returned.reshape(-1), mode="drop")
    return (max_sim, centroid_cos)


def iota(shape, axis):
    return lax.broadcasted_iota(jnp.int32, shape, axis)


def down(values):
    return jnp.sum(values, axis=0, keepdims=True)


def across(values):
    return jnp.sum(values, axis=1, keepdims=True)


def pick(mask, values):
    return jnp.where(mask, values, 0.0)


def as_column(row):
    size = row.shape[1]
    return across(pick(iota((size, size), 0) == iota((size, size), 1), row))


def as_row(column):
    size = column.shape[0]
    return down(pick(iota((size, size), 0) == iota((size, size), 1), column))


def dot(a, b):
    return jnp.dot(a, b, preferred_element_type=F32)


def dot_rows(a, b):
    return lax.dot_general(a, b, (((1,), (1,)), ((), ())), preferred_element_type=F32)


def onehot(mask):
    return jnp.where(mask, 1.0, 0.0).astype(BF16)


def thirds(values):
    first = values.astype(BF16).astype(F32)
    rest = values - first
    second = rest.astype(BF16).astype(F32)
    third = (rest - second).astype(BF16).astype(F32)
    return first, second, third


def rank_groups(count_ref):
    count_row = count_ref[...].astype(F32)
    count_column = as_column(count_row)
    sub, lane = iota((GROUPS, 128), 0), iota((GROUPS, 128), 1)
    count_lanes = down(pick(sub == lane, count_column))
    ahead = (count_column > count_lanes) | ((count_column == count_lanes) & (sub < lane))
    rank = down(jnp.where(ahead, 1.0, 0.0))
    return jnp.where(iota((1, 128), 1) < GROUPS, rank, 0.0), count_column


def place_documents(assign_ref, owner_ref, rank):
    owner_row = owner_ref[...].astype(F32)
    owner_column = as_column(owner_row)
    sub, lane = iota((CLUSTERS, CLUSTERS), 0), iota((CLUSTERS, CLUSTERS), 1)
    within = across(jnp.where((owner_column == owner_row) & (lane < sub), 1.0, 0.0))
    group_rank = across(pick(owner_column == lane.astype(F32), rank))
    place_column = group_rank * (CLUSTERS // GROUPS) + within
    member = iota((CLUSTERS, ROWS), 0) == assign_ref[...]
    place = down(pick(member, place_column))
    group = down(pick(member, owner_column))
    order = iota((CLUSTERS, ROWS), 0).astype(F32)
    at_place = order == place
    earlier = onehot(iota((ROWS, ROWS), 0) < iota((ROWS, ROWS), 1))
    before = dot(onehot(at_place), earlier)
    slot = down(pick(at_place, before))
    count_column = across(jnp.where(at_place, 1.0, 0.0))
    partner_count = down(pick(order == (CLUSTERS - 1) - place, count_column))
    slot = slot + jnp.where(place >= CHIPS, partner_count, 0.0)
    chip = jnp.minimum(place, (CLUSTERS - 1) - place)
    return group, chip.astype(jnp.int32), slot.astype(jnp.int32), as_row(count_column)


def missing_documents(index_ref, count_column, group):
    listed = index_ref[...]
    live = iota((GROUPS, CAP), 1).astype(F32) < count_column
    eye = onehot(iota((CAP, CAP), 0) == iota((CAP, CAP), 1))
    high = dot_rows(eye, jnp.where(live, listed >> 4, 0).astype(F32).astype(BF16))
    low = dot_rows(eye, jnp.where(live, listed & 15, 0).astype(F32).astype(BF16))
    alive = dot_rows(eye, onehot(live))
    slots = jnp.where(alive > 0.5, high * 16.0 + low, -1.0)
    document = iota((1, ROWS), 1).astype(F32)
    hits = jnp.zeros((CAP, ROWS), F32)
    for g in range(GROUPS):
        wanted = jnp.where(group == float(g), document, -2.0)
        hits = hits + jnp.where(slots[:, g : g + 1] == wanted, 1.0, 0.0)
    return across(jnp.where(down(hits) > 0.5, 0.0, 1.0))


def shift_of(step):
    high, middle, low = step // 16, (step // 4) % 4, step % 4
    return low, (middle + low) % 4, (high + middle + low) % 4


def step_to(dx, dy, dz):
    dx, dy, dz = dx & 3, dy & 3, dz & 3
    return ((dz - dy) & 3) * 16 + ((dy - dx) & 3) * 4 + dx


def in_part(step, part):
    first, number = PARTS[part]
    return (step >= first) & (step < first + number)


def chip_places():
    sub, lane = iota((CLUSTERS, CLUSTERS), 0), iota((CLUSTERS, CLUSTERS), 1)
    return onehot((sub == lane) | (sub == (CLUSTERS - 1) - lane))


def excess(totals):
    lane = iota(totals.shape, 1)
    return jnp.where(lane < CHIPS, jnp.maximum(totals - BASE, 0.0), 0.0)


def receive_plan(table, rank, my_x, my_y, my_z):
    chip = my_x * 16 + my_y * 4 + my_z
    heads = table.astype(jnp.int32)
    counts = (heads & 1023).astype(F32)
    differ = jnp.where((heads >> 10).astype(F32) != rank, 1.0, 0.0)
    fault = across(down(differ))
    both = dot(counts.astype(BF16), chip_places())
    over = excess(both)

    def origin(step):
        low, middle, high = step & 3, (step >> 2) & 3, step >> 4
        return (my_x - low) & 3, (my_y - middle - low) & 3, (my_z - high - middle - low) & 3

    lanes = iota((CHIPS, CLUSTERS), 1)
    own_x, own_y, own_z = origin(iota((CHIPS, 1), 0))
    line = own_x * 4 + own_y
    row_x, row_y, row_z = origin(iota((1, CHIPS), 1))
    same_line = line == row_x * 4 + row_y
    over_total = across(over)
    over_row = as_row(over_total)
    line_start = across(pick(same_line & (row_z < own_z), over_row))
    line_total = across(pick(same_line, over_row))
    fault = fault + down(jnp.where(line_total > POOL, 1.0, 0.0))
    start = line_start + across(pick(lanes < chip, over))
    number = across(pick(lanes == chip, over))

    to_chip = iota((1, CLUSTERS), 1)
    route = step_to((to_chip >> 4) - own_x, ((to_chip >> 2) & 3) - own_y, (to_chip & 3) - own_z)
    based = jnp.where(lanes < CHIPS, jnp.minimum(both, float(BASE)), 0.0)
    for part in range(len(PARTS)):
        held = down(pick(in_part(route, part), based))
        if part == LAST:
            held = held + down(over)
        fault = fault + across(jnp.where(held > SEGMENT, 1.0, 0.0))

    first = across(pick(lanes == chip, counts))
    second = across(pick(lanes == (CLUSTERS - 1) - chip, counts))
    place = (lanes & (POOL - 1)).astype(F32) - start
    mine = (line == (lanes >> 3)) & (place >= 0.0) & (place < number)
    over_first = down(jnp.where(mine & (place + BASE < first), 1.0, 0.0))
    over_second = down(jnp.where(mine & (place + BASE >= first), 1.0, 0.0))
    over_first_total, over_second_total = across(over_first), across(over_second)
    earlier = onehot(iota((CLUSTERS, CLUSTERS), 0) < iota((CLUSTERS, CLUSTERS), 1))
    sub = iota((16, CLUSTERS), 0)
    before = dot((pick(sub == 0, over_first) + pick(sub == 1, over_second)).astype(BF16), earlier)

    base_first = jnp.minimum(first, float(BASE))
    base_second = jnp.minimum(first + second, float(BASE)) - base_first
    source, target = iota((CHIPS, CHIPS), 0), iota((CHIPS, CHIPS), 1)
    first_row, second_row = as_row(base_first), as_row(base_second)
    plans = []
    ends = []
    for part, (begin, steps) in enumerate(PARTS):
        inside = in_part(iota((CHIPS, 1), 0), part)
        ahead = (target < source) & in_part(iota((1, CHIPS), 1), part)
        first_total = down(pick(inside, base_first))
        second_total = down(pick(inside, base_second))
        first_end = first_total + over_first_total if part == LAST else first_total
        first_start = across(pick(ahead, first_row))
        second_start = across(pick(ahead, second_row)) + first_end
        spread = iota((CHIPS, steps * BASE), 0) - begin == (iota((CHIPS, steps * BASE), 1) >> 4)
        head, tail, head_start, tail_start = [
            down(pick(spread, column)) for column in (base_first, base_second, first_start, second_start)
        ]
        slot = (iota((1, steps * BASE), 1) & (BASE - 1)).astype(F32)
        later = jnp.where(slot < head + tail, tail_start + (slot - head), -1.0)
        plans.append(jnp.where(slot < head, head_start + slot, later))
        held_end = first_end + second_total
        if part == LAST:
            over_row_of = jnp.where(over_second > 0.5, held_end + before[1:2], -1.0)
            over_row_of = jnp.where(over_first > 0.5, first_total + before[0:1], over_row_of)
            held_end = held_end + over_second_total
        ends.append((first_end, held_end))
    return plans, over_row_of, ends, line_start, line_total, over_total, fault


def kernel(
    x_hbm, assign_ref, owner_ref, count_ref, index_ref,
    max_ref, cos_ref, fault_ref,
    x_ref, send, got, head, heads, own_over, line_over, send_over, got_over,
    pick_0, pick_1, pick_2, pick_left, pick_right, pick_over,
    mine, theirs, facts, their_facts, sums, their_sums, back, returned,
    x_sem, send_sem, recv_sem,
):
    grp, blk = lax.axis_index("grp"), lax.axis_index("blk")
    my_x, my_y, my_z, core = grp // 4, grp % 4, blk // 2, blk % 2
    picks = (pick_0, pick_1, pick_2)

    along_x = [((my_x + d) % 4) * 4 for d in range(4)]
    along_y = [(my_y + d) % 4 for d in range(4)]
    along_z = [((my_z + d) % 4) * 2 + core for d in range(4)]

    def device_at(step, sign):
        dx, dy, dz = [(sign * d) % 4 for d in shift_of(step)]
        return {"grp": along_x[dx] + along_y[dy], "blk": along_z[dz]}

    other_core = {"grp": grp, "blk": my_z * 2 + (1 - core)}
    barrier = pltpu.get_barrier_semaphore()
    load = pltpu.make_async_copy(x_hbm, x_ref, x_sem)
    load.start()

    for device in [device_at(step, 1) for step in range(1, CHIPS)] + [other_core]:
        pl.semaphore_signal(barrier, inc=1, device_id=device, device_id_type=pl.DeviceIdType.MESH)

    def remote(source, target, number, device):
        return pltpu.make_async_remote_copy(
            src_ref=source,
            dst_ref=target,
            send_sem=send_sem.at[number],
            recv_sem=recv_sem.at[number],
            device_id=device,
            device_id_type=pl.DeviceIdType.MESH,
        )

    def await_blocks(ref, number, semaphore):
        block = ref.at[pl.ds(0, number)]
        pltpu.make_async_copy(block, block, semaphore).wait()

    HEADS, LINE, OVER, FACTS, SUMS, BACK, SWAP, PART = 0, 1, 2, 3, 4, 5, 6, 9

    def messages(part):
        return PARTS[part][1] - (1 if part == 0 else 0)

    rank, count_column = rank_groups(count_ref)
    group, chip, slot, place_counts = place_documents(assign_ref, owner_ref, rank)
    step_of = step_to((chip >> 4) - my_x, ((chip >> 2) & 3) - my_y, (chip & 3) - my_z)
    in_base = slot < BASE
    base_slot = jnp.where(in_base, step_of * BASE + slot, -1)
    load.wait()

    def pack(part):
        begin, steps = PARTS[part]
        slots = iota((steps * BASE, ROWS), 0) + begin * BASE
        rows = dot(onehot(slots == base_slot), x_ref[...]).astype(BF16)
        send[pl.ds(begin, steps)] = rows.reshape(steps, BASE, WIDTH)

    def post(part):
        begin, steps = PARTS[part]

        for step in range(max(begin, 1), begin + steps):
            remote(send.at[step], got.at[step], PART + part, device_at(step, 1)).start()

    pack(0)
    pl.semaphore_wait(barrier, CHIPS)
    post(0)
    pack(1)
    post(1)
    place_counts_8 = place_counts + jnp.zeros((16, CLUSTERS), F32)
    own_excess = excess(dot(place_counts_8.astype(BF16), chip_places())[0:1])
    eye = iota((CHIPS, CLUSTERS), 0) == iota((CHIPS, CLUSTERS), 1)
    excess_column = across(pick(eye, own_excess))
    over_slot = down(pick(iota((CHIPS, ROWS), 0) < chip, excess_column)).astype(jnp.int32) + (slot - BASE)
    over_slot = jnp.where(in_base, -1, over_slot)
    own_over[...] = dot(onehot(iota((BASE, ROWS), 0) == over_slot), x_ref[...]).astype(BF16)
    line_over[my_z] = own_over[...]
    for step in range(1, DEPTH):
        device = {"grp": grp, "blk": along_z[step]}
        remote(own_over, line_over.at[my_z], LINE, device).start()

    missing = missing_documents(index_ref, count_column, group)
    head[0] = place_counts + 1024.0 * rank + jnp.where(missing > 0.5, 16384.0, 0.0)
    heads[0] = head[0]
    for step in range(1, CHIPS):
        remote(head, heads.at[pl.ds(step, 1)], HEADS, device_at(step, 1)).start()
    pack(2)
    post(2)
    got[0] = send[0]

    await_blocks(heads, CHIPS - 1, recv_sem.at[HEADS])
    table = heads[...].reshape(CHIPS, CLUSTERS)
    plans, over_row_of, ends, line_start, line_total, over_total, fault = receive_plan(
        table, rank, my_x, my_y, my_z
    )

    await_blocks(line_over, DEPTH - 1, recv_sem.at[LINE])
    sender = iota((CHIPS, 1), 0)
    low, middle, high = sender & 3, (sender >> 2) & 3, sender >> 4
    in_line = (low == 0) & (middle == 0)
    depth = (my_z - high) & 3
    entry = iota((CHIPS, DEPTH * BASE), 1)
    at = in_line & (depth == (entry >> 4))
    begin = down(pick(at, line_start))
    number = down(pick(at, over_total))
    order = (iota((1, DEPTH * BASE), 1) & (BASE - 1)).astype(F32)
    order = jnp.where(order < number, begin + order, -1.0)
    my_start = line_start[0:1]
    rows = iota((2 * POOL, DEPTH * BASE), 0).astype(F32)
    blocks = line_over[...].reshape(DEPTH * BASE, WIDTH)
    left = dot(onehot((rows == order) & (rows < POOL)), blocks[:, :HALF])
    right = dot(onehot((rows - POOL == order) & (rows >= POOL)), blocks[:, HALF:])
    send_over[...] = (left + right).astype(BF16)
    got_over[grp] = send_over[...]

    for step in range(1, LINES):
        low, middle = step % 4, step // 4
        device = {"grp": along_x[low] + along_y[(middle + low) % 4], "blk": blk}
        remote(send_over, got_over.at[grp], OVER, device).start()

    lane = iota((1, 128), 1)
    told = jnp.where(lane == 0, fault, 0.0)
    for part, (first_end, held_end) in enumerate(ends):
        told = jnp.where(lane == 1 + 2 * part, first_end, told)
        told = jnp.where(lane == 2 + 2 * part, held_end, told)
    row = iota((8, 128), 0)
    facts[...] = pick(row == 0, told) + pick(row == 1, rank)
    swap_facts = remote(facts, their_facts, FACTS, other_core)
    swap_facts.start()

    for part, plan in enumerate(plans):
        picks[part][...] = onehot(iota((SEGMENT, plan.shape[1]), 0).astype(F32) == plan)
    rows = iota((SEGMENT, LINES * 2 * POOL), 0).astype(F32)
    position = iota((CLUSTERS, LINES * 2 * POOL), 1)
    spread = onehot(iota((CLUSTERS, LINES * 2 * POOL), 0) == (position >> 4) * POOL + (position & (POOL - 1)))
    wide = dot((over_row_of + jnp.zeros((16, CLUSTERS), F32)).astype(BF16), spread)[0:1]
    is_left = (iota((1, LINES * 2 * POOL), 1) & POOL) == 0
    pick_left[...] = onehot((rows == wide) & is_left)
    pick_right[...] = onehot((rows == wide) & (~is_left))
    pick_over[...] = onehot(iota((SEGMENT, CLUSTERS), 0).astype(F32) == over_row_of)

    key_number = iota((SEGMENT, 1), 0).astype(F32)
    query_number = iota((1, SEGMENT), 1).astype(F32)
    best = [jnp.full((1, SEGMENT), -1.0, F32) for _ in PARTS]
    their_ends = []
    totals = [jnp.zeros((1, WIDTH), F32), jnp.zeros((1, WIDTH), F32)]
    swaps = []

    def compare(keys, key_part, query_part, key_ends, itself):
        window = pl.ds(key_part * SEGMENT, SEGMENT)
        scores = dot_rows(keys[window], mine[pl.ds(query_part * SEGMENT, SEGMENT)])
        first, held = key_ends[key_part]
        kind = jnp.where(key_number < first, 0.0, jnp.where(key_number < held, 1.0, 2.0))
        matched = kind == jnp.where(query_number < ends[query_part][0], 0.0, 1.0)
        if itself and key_part == query_part:
            matched = matched & (key_number != query_number)
        scores = jnp.max(jnp.where(matched, scores, -1.0), axis=0, keepdims=True)
        best[query_part] = jnp.maximum(best[query_part], scores)

    def compare_theirs(part, queries):
        for query_part in queries:
            compare(theirs, part, query_part, their_ends, False)

    for part, (begin, steps) in enumerate(PARTS):
        await_blocks(got, messages(part), recv_sem.at[PART + part])
        window = pl.ds(part * SEGMENT, SEGMENT)
        rows = dot(picks[part][...], got[pl.ds(begin, steps)].reshape(steps * BASE, WIDTH))
        if part == LAST:
            await_blocks(got_over, LINES - 1, recv_sem.at[OVER])
            halves = got_over[...].reshape(LINES * 2 * POOL, HALF)
            rows = rows + jnp.concatenate(
                [dot(pick_left[...], halves), dot(pick_right[...], halves)], axis=1
            )
        unit = rows * lax.rsqrt(across(rows * rows) + EPSILON)
        mine[window] = unit.astype(BF16)
        swap = remote(mine.at[window], theirs.at[window], SWAP + part, other_core)
        swap.start()
        swaps.append(swap)
        is_first = key_number < ends[part][0]
        totals[0] = totals[0] + down(pick(is_first, unit))
        totals[1] = totals[1] + down(jnp.where(is_first, 0.0, unit))
        if part == LAST:
            row = iota((8, WIDTH), 0)
            sums[...] = pick(row == 0, totals[0]) + pick(row == 1, totals[1])
            swap_sums = remote(sums, their_sums, SUMS, other_core)
            swap_sums.start()
        for other in range(part + 1):
            compare(mine, part, other, ends, True)
            if other != part:
                compare(mine, other, part, ends, True)
        if part == 0:
            swap_facts.wait()
            their_told = their_facts[...]
            for number in range(len(PARTS)):
                their_ends.append(
                    (their_told[0:1, 1 + 2 * number : 2 + 2 * number], their_told[0:1, 2 + 2 * number : 3 + 2 * number])
                )
        else:
            for other in range(part - 1):
                compare_theirs(other, [part])
            swaps[part - 1].wait()
            compare_theirs(part - 1, range(part + 1))

    swap_sums.wait()
    total = sums[...] + their_sums[...]
    centre = total * lax.rsqrt(across(total * total) + EPSILON)
    near = dot_rows(jnp.concatenate(thirds(centre), axis=0).astype(BF16), mine[...])
    near = near[0:8] + near[8:16] + near[16:24]
    swaps[LAST].wait()
    compare_theirs(LAST, range(len(PARTS)))

    row = iota((8, SEGMENT), 0)
    lines = [[], []]

    def joined(out, kind):
        return out[3 * kind : 3 * kind + 1] + out[3 * kind + 1 : 3 * kind + 2] + out[3 * kind + 2 : 3 * kind + 3]

    for part, (begin, steps) in enumerate(PARTS):
        some = near[:, part * SEGMENT : (part + 1) * SEGMENT]
        some = jnp.where(query_number < ends[part][0], some[0:1], some[1:2])
        values = jnp.zeros((8, SEGMENT), F32)
        for number, term in enumerate(thirds(best[part]) + thirds(some)):
            values = jnp.where(row == number, term, values)
        values = values.astype(BF16)
        out = dot(values, picks[part][...])
        for kind in range(2):
            line = joined(out, kind)
            for tile in range(steps * BASE // 128):
                back[begin * BASE // 128 + tile, kind : kind + 1, :] = line[:, tile * 128 : (tile + 1) * 128]
        if part == LAST:
            out = dot(values, pick_over[...])
            for kind in range(2):
                for tile in range(CHIPS * BASE // 128):
                    back[tile, 2 + kind : 3 + kind, :] = joined(out, kind)
    returned[0] = back[0]

    for step in range(1, CHIPS):
        remote(back.at[step // 8], returned.at[step], BACK, device_at(step, -1)).start()

    differ = across(jnp.where(their_told[1:2] != rank, 1.0, 0.0))
    fault = fault + their_told[0:1, 0:1] + differ
    fault_ref[...] = jnp.where(fault > 0.5, 1, 0) + jnp.zeros((1, 128), jnp.int32)
    chosen = onehot(iota((CHIPS, ROWS), 0) == step_of)
    sub = iota((128, ROWS), 0)
    at_base = (sub == (step_of & 7) * BASE + slot) & in_base
    at_over = (sub == grp * POOL + my_start.astype(jnp.int32) + over_slot) & (~in_base)

    await_blocks(returned, CHIPS - 1, recv_sem.at[BACK])
    found = []
    for number in range(4):
        terms = jnp.concatenate(thirds(returned[:, number, :]), axis=1).astype(BF16)
        out = lax.dot_general(terms, chosen, (((0,), (0,)), ((), ())), preferred_element_type=F32)
        found.append(out[0:128] + out[128:256] + out[256:384])
    max_ref[...] = down(pick(at_base, found[0]) + pick(at_over, found[2]))
    cos_ref[...] = down(pick(at_base, found[1]) + pick(at_over, found[3]))

    await_blocks(heads, CHIPS - 1, send_sem.at[HEADS])
    await_blocks(line_over, DEPTH - 1, send_sem.at[LINE])
    await_blocks(got_over, LINES - 1, send_sem.at[OVER])
    await_blocks(returned, CHIPS - 1, send_sem.at[BACK])
    for part in range(len(PARTS)):
        await_blocks(got, messages(part), send_sem.at[PART + part])


def routed(embeddings, assign, owner, send_count, send_index):
    return pl.pallas_call(
        kernel,
        out_shape=(
            jax.ShapeDtypeStruct((1, ROWS), F32),
            jax.ShapeDtypeStruct((1, ROWS), F32),
            jax.ShapeDtypeStruct((1, 128), jnp.int32),
        ),
        in_specs=[pl.BlockSpec(memory_space=pl.ANY)] + [pl.BlockSpec(memory_space=pltpu.VMEM)] * 4,
        out_specs=(pl.BlockSpec(memory_space=pltpu.VMEM),) * 3,
        scratch_shapes=[
            pltpu.VMEM((ROWS, WIDTH), BF16),
            pltpu.VMEM((CHIPS, BASE, WIDTH), BF16),
            pltpu.VMEM((CHIPS, BASE, WIDTH), BF16),
            pltpu.VMEM((1, 1, 128), F32),
            pltpu.VMEM((CHIPS, 1, 128), F32),
            pltpu.VMEM((BASE, WIDTH), BF16),
            pltpu.VMEM((DEPTH, BASE, WIDTH), BF16),
            pltpu.VMEM((2 * POOL, HALF), BF16),
            pltpu.VMEM((LINES, 2 * POOL, HALF), BF16),
            *[pltpu.VMEM((SEGMENT, steps * BASE), BF16) for _, steps in PARTS],
            pltpu.VMEM((SEGMENT, LINES * 2 * POOL), BF16),
            pltpu.VMEM((SEGMENT, LINES * 2 * POOL), BF16),
            pltpu.VMEM((SEGMENT, LINES * POOL), BF16),
            pltpu.VMEM((len(PARTS) * SEGMENT, WIDTH), BF16),
            pltpu.VMEM((len(PARTS) * SEGMENT, WIDTH), BF16),
            pltpu.VMEM((8, 128), F32),
            pltpu.VMEM((8, 128), F32),
            pltpu.VMEM((8, WIDTH), F32),
            pltpu.VMEM((8, WIDTH), F32),
            pltpu.VMEM((CHIPS * BASE // 128, 4, 128), F32),
            pltpu.VMEM((CHIPS, 4, 128), F32),
            pltpu.SemaphoreType.DMA,
            pltpu.SemaphoreType.DMA((12,)),
            pltpu.SemaphoreType.DMA((12,)),
        ],
        compiler_params=pltpu.CompilerParams(
            collective_id=0, has_side_effects=True, vmem_limit_bytes=48 * 1024 * 1024
        ),
    )(
        embeddings,
        assign.reshape(1, ROWS),
        owner.reshape(1, CLUSTERS),
        send_count,
        send_index[0],
    )


def body(embeddings, assign, owner, send_count, send_index):
    arguments = (embeddings, assign, owner, send_count, send_index)
    max_sim, centroid_cos, fault = routed(*arguments)
    return lax.cond(
        fault[0, 0] != 0,
        lambda: general(*arguments),
        lambda: (max_sim.reshape(ROWS), centroid_cos.reshape(ROWS)),
    )


def solution(mesh):
    placed = (
        P(("grp", "blk"), None),
        P(("grp", "blk")),
        P(),
        P(("grp", "blk"), None),
        P(("grp", "blk"), None, None),
    )
    return jax.shard_map(
        body,
        mesh=mesh,
        in_specs=placed,
        out_specs=(P(("grp", "blk")), P(("grp", "blk"))),
        check_vma=False,
    )
```

```python
import functools

import jax
import jax.numpy as jnp
from jax import lax
from jax.experimental import pallas as pl
from jax.experimental.pallas import tpu as pltpu
from jax.sharding import PartitionSpec as P

EPSILON = 1e-06
F32 = jnp.float32
BF16 = jnp.bfloat16

CHIPS = 64
ROWS = 512
WIDTH = 768
CLUSTERS = 128
GROUPS = 16
CAP = 64
BASE = 16
HALF = WIDTH // 2
LINES = 16
DEPTH = 4
POOL = 8
SEGMENT = 256
PARTS = 3
STEPS = 24
SPAN = STEPS * BASE
TOTAL = PARTS * STEPS
HELD = PARTS * SEGMENT


def normalize(values):
    widened = values.astype(F32)
    return widened * lax.rsqrt(jnp.sum(widened * widened, axis=1, keepdims=True) + EPSILON)


def general(embeddings, assign, owner, send_count, send_index):
    rows_local = embeddings.shape[0]
    feature_width = embeddings.shape[1]
    groups = lax.axis_size("grp")
    clusters = owner.shape[0]
    capacity = send_index.shape[2]
    slot_total = groups * capacity
    unit_rows = normalize(embeddings)
    unit_low = unit_rows.astype(BF16)
    counts = send_count[0]
    listed = send_index[0]
    live_slot = jnp.arange(capacity, dtype=jnp.int32)[None, :] < counts[:, None]
    listed_cluster = assign[listed]
    owned_here = owner[listed_cluster] == jnp.arange(groups, dtype=jnp.int32)[:, None]
    kept_slot = live_slot & owned_here
    out_cluster = jnp.where(kept_slot, listed_cluster, -1)
    out_tag = jnp.where(kept_slot, lax.axis_index(("grp", "blk")) * rows_local + listed, -1)
    out_vector = unit_low[listed.reshape(-1)].reshape(groups, capacity, feature_width)
    got_vector, got_cluster, got_tag = (
        lax.all_to_all(out_vector, "grp", split_axis=0, concat_axis=0, tiled=True),
        lax.all_to_all(out_cluster, "grp", split_axis=0, concat_axis=0, tiled=True),
        lax.all_to_all(out_tag, "grp", split_axis=0, concat_axis=0, tiled=True),
    )
    own_vector = got_vector.reshape(slot_total, feature_width)
    own_cluster = got_cluster.reshape(slot_total)
    own_tag = got_tag.reshape(slot_total)

    def tile_best(current, shard_piece):
        other_vector, other_cluster, other_tag = shard_piece
        scores = jnp.einsum("id,jd->ij", own_vector, other_vector, preferred_element_type=F32)
        matched = (
            (own_cluster[:, None] == other_cluster[None, :])
            & (other_cluster[None, :] >= 0)
            & (own_tag[:, None] != other_tag[None, :])
        )
        return jnp.maximum(current, jnp.max(jnp.where(matched, scores, -1.0), axis=1))

    other_vector = lax.all_gather(own_vector, "blk", axis=0, tiled=True)
    other_cluster = lax.all_gather(own_cluster, "blk", axis=0, tiled=True)
    other_tag = lax.all_gather(own_tag, "blk", axis=0, tiled=True)
    length = other_vector.shape[0]
    number = length // slot_total
    stacked = (
        other_vector.reshape(number, slot_total, feature_width),
        other_cluster.reshape(number, slot_total),
        other_tag.reshape(number, slot_total),
    )

    def scan_step(carry, single):
        return (tile_best(carry, single), None)

    result, unused = lax.scan(scan_step, jnp.full((slot_total,), -1.0, F32), stacked)
    target = jnp.where(live_slot, listed, rows_local).reshape(-1)
    partial_sum = jax.ops.segment_sum(unit_rows, assign, num_segments=clusters)
    centre = normalize(lax.psum(partial_sum, ("grp", "blk")))
    nearness = jnp.sum(unit_low.astype(F32) * centre[assign], axis=1)
    returned = lax.all_to_all(
        result.reshape(groups, capacity), "grp", split_axis=0, concat_axis=0, tiled=True
    )
    has_entry = (
        jnp.zeros((rows_local,), jnp.int32)
        .at[target]
        .max(kept_slot.astype(jnp.int32).reshape(-1), mode="drop")
    )
    centroid_cos = jnp.where(has_entry > 0, nearness, 0.0)
    max_sim = jnp.full((rows_local,), -1.0, F32).at[target].max(returned.reshape(-1), mode="drop")
    return (max_sim, centroid_cos)


def iota(shape, axis):
    return lax.broadcasted_iota(jnp.int32, shape, axis)


def down(values):
    return jnp.sum(values, axis=0, keepdims=True)


def across(values):
    return jnp.sum(values, axis=1, keepdims=True)


def pick(mask, values):
    return jnp.where(mask, values, 0.0)


def as_column(row):
    size = row.shape[1]
    return across(pick(iota((size, size), 0) == iota((size, size), 1), row))


def as_row(column):
    size = column.shape[0]
    return down(pick(iota((size, size), 0) == iota((size, size), 1), column))


def dot(a, b):
    return jnp.dot(a, b, preferred_element_type=F32)


def dot_rows(a, b):
    return lax.dot_general(a, b, (((1,), (1,)), ((), ())), preferred_element_type=F32)


def onehot(mask):
    return jnp.where(mask, 1.0, 0.0).astype(BF16)


def thirds(values):
    first = values.astype(BF16).astype(F32)
    rest = values - first
    second = rest.astype(BF16).astype(F32)
    third = (rest - second).astype(BF16).astype(F32)
    return first, second, third


def rank_groups(count_ref):
    count_row = count_ref[...].astype(F32)
    count_column = as_column(count_row)
    sub, lane = iota((GROUPS, 128), 0), iota((GROUPS, 128), 1)
    count_lanes = down(pick(sub == lane, count_column))
    ahead = (count_column > count_lanes) | ((count_column == count_lanes) & (sub < lane))
    rank = down(jnp.where(ahead, 1.0, 0.0))
    return jnp.where(iota((1, 128), 1) < GROUPS, rank, 0.0), count_column


def place_documents(assign_ref, owner_ref, rank):
    owner_row = owner_ref[...].astype(F32)
    owner_column = as_column(owner_row)
    sub, lane = iota((CLUSTERS, CLUSTERS), 0), iota((CLUSTERS, CLUSTERS), 1)
    within = across(jnp.where((owner_column == owner_row) & (lane < sub), 1.0, 0.0))
    group_rank = across(pick(owner_column == lane.astype(F32), rank))
    place_column = group_rank * (CLUSTERS // GROUPS) + within
    member = iota((CLUSTERS, ROWS), 0) == assign_ref[...]
    place = down(pick(member, place_column))
    group = down(pick(member, owner_column))
    order = iota((CLUSTERS, ROWS), 0).astype(F32)
    at_place = order == place
    earlier = onehot(iota((ROWS, ROWS), 0) < iota((ROWS, ROWS), 1))
    before = dot(onehot(at_place), earlier)
    slot = down(pick(at_place, before))
    count_column = across(jnp.where(at_place, 1.0, 0.0))
    partner_count = down(pick(order == (CLUSTERS - 1) - place, count_column))
    slot = slot + jnp.where(place >= CHIPS, partner_count, 0.0)
    chip = jnp.minimum(place, (CLUSTERS - 1) - place)
    return group, chip.astype(jnp.int32), slot.astype(jnp.int32), as_row(count_column)


def missing_documents(index_ref, count_column, group):
    listed = index_ref[...]
    live = iota((GROUPS, CAP), 1).astype(F32) < count_column
    eye = onehot(iota((CAP, CAP), 0) == iota((CAP, CAP), 1))
    high = dot_rows(eye, jnp.where(live, listed >> 4, 0).astype(F32).astype(BF16))
    low = dot_rows(eye, jnp.where(live, listed & 15, 0).astype(F32).astype(BF16))
    alive = dot_rows(eye, onehot(live))
    slots = jnp.where(alive > 0.5, high * 16.0 + low, -1.0)
    document = iota((1, ROWS), 1).astype(F32)
    lane = iota((CAP, GROUPS), 1)

    def count(g, hits):
        column = across(pick(lane == g, slots))
        wanted = jnp.where(group == g.astype(F32), document, -2.0)
        return hits + jnp.where(column == wanted, 1.0, 0.0)

    hits = lax.fori_loop(0, GROUPS, count, jnp.zeros((CAP, ROWS), F32))
    return across(jnp.where(down(hits) > 0.5, 0.0, 1.0))


def step_to(dx, dy, dz):
    dx, dy, dz = dx & 3, dy & 3, dz & 3
    return ((dz - dy) & 3) * 16 + ((dy - dx) & 3) * 4 + dx


def in_part(step, part):
    return (step >= part * STEPS) & (step < (part + 1) * STEPS)


def chip_places():
    sub, lane = iota((CLUSTERS, CLUSTERS), 0), iota((CLUSTERS, CLUSTERS), 1)
    return onehot((sub == lane) | (sub == (CLUSTERS - 1) - lane))


def excess(totals):
    lane = iota(totals.shape, 1)
    return jnp.where(lane < CHIPS, jnp.maximum(totals - BASE, 0.0), 0.0)


def receive_plan(table, rank, my_x, my_y, my_z):
    chip = my_x * 16 + my_y * 4 + my_z
    heads = table.astype(jnp.int32)
    counts = (heads & 1023).astype(F32)
    differ = jnp.where((heads >> 10).astype(F32) != rank, 1.0, 0.0)
    fault = across(down(differ))
    both = dot(counts.astype(BF16), chip_places())
    over = excess(both)
    lanes = iota((CHIPS, CLUSTERS), 1)
    sender = iota((CHIPS, 1), 0)
    source, target = iota((CHIPS, CHIPS), 0), iota((CHIPS, CHIPS), 1)

    same_line = (source >> 2) == (target >> 2)
    over_total = across(over)
    over_row = as_row(over_total)
    line_start = across(pick(same_line & (target < source), over_row))
    line_total = across(pick(same_line, over_row))
    fault = fault + down(jnp.where(line_total > POOL, 1.0, 0.0))
    start = line_start + across(pick(lanes < chip, over))
    number = across(pick(lanes == chip, over))

    to_chip = iota((1, CLUSTERS), 1)
    route = step_to(
        (to_chip >> 4) - (sender >> 4), ((to_chip >> 2) & 3) - ((sender >> 2) & 3), (to_chip & 3) - (sender & 3)
    )
    based = jnp.where(lanes < CHIPS, jnp.minimum(both, float(BASE)), 0.0)
    for part in range(PARTS):
        held = down(pick(in_part(route, part), based))
        if part == PARTS - 1:
            held = held + down(over)
        fault = fault + across(jnp.where(held > SEGMENT, 1.0, 0.0))

    first = across(pick(lanes == chip, counts))
    second = across(pick(lanes == (CLUSTERS - 1) - chip, counts))
    place = (lanes & (POOL - 1)).astype(F32) - start
    mine = ((sender >> 2) == (lanes >> 3)) & (place >= 0.0) & (place < number)
    over_first = down(jnp.where(mine & (place + BASE < first), 1.0, 0.0))
    over_second = down(jnp.where(mine & (place + BASE >= first), 1.0, 0.0))
    over_first_total, over_second_total = across(over_first), across(over_second)
    earlier = onehot(iota((CLUSTERS, CLUSTERS), 0) < iota((CLUSTERS, CLUSTERS), 1))
    sub = iota((16, CLUSTERS), 0)
    before = dot((pick(sub == 0, over_first) + pick(sub == 1, over_second)).astype(BF16), earlier)

    base_first = jnp.minimum(first, float(BASE))
    base_second = jnp.minimum(first + second, float(BASE)) - base_first
    first_row, second_row = as_row(base_first), as_row(base_second)

    def my_step(other):
        return step_to(my_x - (other >> 4), my_y - ((other >> 2) & 3), my_z - (other & 3))

    step_column, step_row = my_step(sender), my_step(iota((1, CHIPS), 1))
    plans = []
    ends = []
    for part in range(PARTS):
        inside = in_part(step_column, part)
        ahead = (target < source) & in_part(step_row, part)
        first_total = down(pick(inside, base_first))
        second_total = down(pick(inside, base_second))
        last = part == PARTS - 1
        first_end = first_total + over_first_total if last else first_total
        first_start = across(pick(ahead, first_row))
        second_start = across(pick(ahead, second_row)) + first_end
        spread = step_column - part * STEPS == (iota((CHIPS, SPAN), 1) >> 4)
        head, tail, head_start, tail_start = [
            down(pick(spread, column)) for column in (base_first, base_second, first_start, second_start)
        ]
        slot = (iota((1, SPAN), 1) & (BASE - 1)).astype(F32)
        later = jnp.where(slot < head + tail, tail_start + (slot - head), -1.0)
        plan = jnp.where(slot < head, head_start + slot, later)
        held_end = first_end + second_total
        if last:
            over_row_of = jnp.where(over_second > 0.5, held_end + before[1:2], -1.0)
            over_row_of = jnp.where(over_first > 0.5, first_total + before[0:1], over_row_of)
            plan = jnp.concatenate([plan[:, : SPAN - CLUSTERS], over_row_of], axis=1)
            held_end = held_end + over_second_total
        plans.append(plan)
        ends.append((first_end, held_end))
    return plans, ends, line_start, over_total, fault


def kernel(
    x_hbm, assign_ref, owner_ref, count_ref, index_ref,
    max_ref, cos_ref, fault_ref,
    x_ref, send, got, heads, line_over, send_over, got_over, plan_ref, pick_ref,
    keys, facts, sums, their_sums, best_ref, back, returned,
    x_sem, send_sem, recv_sem,
):
    grp, blk = lax.axis_index("grp"), lax.axis_index("blk")
    my_x, my_y, my_z, core = grp // 4, grp % 4, blk // 2, blk % 2
    my_chip = grp * 4 + my_z
    last = PARTS - 1
    along_x = [((my_x + d) % 4) * 4 for d in range(4)]
    along_y = [(my_y + d) % 4 for d in range(4)]
    along_z = [((my_z + d) % 4) * 2 + core for d in range(4)]
    other_core = {"grp": grp, "blk": my_z * 2 + (1 - core)}

    def each_device(first, stop, sign, act):
        @pl.loop(first, stop)
        def _(quad):
            high, middle = quad // 4, quad % 4
            for low in range(4):
                y = (my_y + 8 + sign * (middle + low)) % 4
                z = (my_z + 12 + sign * (high + middle + low)) % 4
                device = {"grp": along_x[(sign * low) % 4] + y, "blk": z * 2 + core}
                if low == 0:

                    @pl.when(quad > 0)
                    def _():
                        act(quad * 4, device)

                else:
                    act(quad * 4 + low, device)

    def remote(source, target, number, device):
        return pltpu.make_async_remote_copy(
            src_ref=source,
            dst_ref=target,
            send_sem=send_sem.at[number],
            recv_sem=recv_sem.at[number],
            device_id=device,
            device_id_type=pl.DeviceIdType.MESH,
        )

    def await_blocks(ref, number, semaphore):
        block = ref.at[pl.ds(0, number)]
        pltpu.make_async_copy(block, block, semaphore).wait()

    HEAD_Z, HEAD_Y, HEAD_X, LINE, OVER, FACTS, SUMS, BACK, SWAP, PART = 0, 1, 2, 3, 4, 5, 6, 7, 8, 11
    messages = (STEPS - 1, STEPS, CHIPS - 2 * STEPS)

    barrier = pltpu.get_barrier_semaphore()
    load = pltpu.make_async_copy(x_hbm, x_ref, x_sem)
    load.start()

    def greet(step, device):
        pl.semaphore_signal(barrier, inc=1, device_id=device, device_id_type=pl.DeviceIdType.MESH)

    each_device(0, 16, 1, greet)
    greet(0, other_core)

    rank, count_column = rank_groups(count_ref)
    group, chip, slot, place_counts = place_documents(assign_ref, owner_ref, rank)
    step_of = step_to((chip >> 4) - my_x, ((chip >> 2) & 3) - my_y, (chip & 3) - my_z)
    in_base = slot < BASE
    place_counts_16 = place_counts + jnp.zeros((16, CLUSTERS), F32)
    own_excess = excess(dot(place_counts_16.astype(BF16), chip_places())[0:1])
    eye = iota((CHIPS, CLUSTERS), 0) == iota((CHIPS, CLUSTERS), 1)
    excess_column = across(pick(eye, own_excess))
    over_slot = down(pick(iota((CHIPS, ROWS), 0) < chip, excess_column)).astype(jnp.int32) + (slot - BASE)
    over_place = jnp.where(over_slot < BASE, CHIPS * BASE + over_slot, -1)
    send_slot = jnp.where(in_base, step_of * BASE + slot, over_place)
    load.wait()

    @pl.loop(0, PARTS)
    def _(part):
        slots = iota((SPAN, ROWS), 0) + part * SPAN
        rows = dot(onehot(slots == send_slot), x_ref[...]).astype(BF16)
        send[pl.ds(part * STEPS, STEPS)] = rows.reshape(STEPS, BASE, WIDTH)

        @pl.when(part == 0)
        def _():
            pl.semaphore_wait(barrier, CHIPS)

        @pl.when(part == last)
        def _():
            line_over[my_z] = send[CHIPS]
            for step in range(1, DEPTH):
                device = {"grp": grp, "blk": along_z[step]}
                remote(send.at[CHIPS], line_over.at[my_z], LINE, device).start()

        def post(step, device):
            remote(send.at[step], got.at[step], PART + part, device).start()

        each_device(part * (STEPS // 4), jnp.minimum((part + 1) * (STEPS // 4), CHIPS // 4), 1, post)

        @pl.when(part == 0)
        def _():
            missing = missing_documents(index_ref, count_column, group)
            heads[my_chip] = place_counts + 1024.0 * rank + jnp.where(missing > 0.5, 16384.0, 0.0)
            for step in range(1, 4):
                block = heads.at[pl.ds(my_chip, 1)]
                remote(block, block, HEAD_Z, {"grp": grp, "blk": along_z[step]}).start()

        @pl.when(part == 1)
        def _():
            await_blocks(heads, 3, recv_sem.at[HEAD_Z])
            for step in range(1, 4):
                block = heads.at[pl.ds(grp * 4, 4)]
                remote(block, block, HEAD_Y, {"grp": along_x[0] + along_y[step], "blk": blk}).start()

        @pl.when(part == last)
        def _():
            await_blocks(heads, 12, recv_sem.at[HEAD_Y])
            for step in range(1, 4):
                block = heads.at[pl.ds(my_x * 16, 16)]
                remote(block, block, HEAD_X, {"grp": along_x[step] + along_y[0], "blk": blk}).start()

    got[0] = send[0]
    got[pl.ds(CHIPS, TOTAL - CHIPS)] = jnp.zeros((TOTAL - CHIPS, BASE, WIDTH), BF16)
    sums[...] = jnp.zeros((8, WIDTH), F32)
    best_ref[...] = jnp.full((1, HELD), -1.0, F32)

    await_blocks(heads, 48, recv_sem.at[HEAD_X])
    table = heads[...].reshape(CHIPS, CLUSTERS)
    plans, ends, line_start, over_total, fault = receive_plan(table, rank, my_x, my_y, my_z)

    await_blocks(line_over, DEPTH - 1, recv_sem.at[LINE])
    sender = iota((CHIPS, 1), 0)
    at = sender == grp * 4 + (iota((CHIPS, DEPTH * BASE), 1) >> 4)
    begin = down(pick(at, line_start))
    number = down(pick(at, over_total))
    order = (iota((1, DEPTH * BASE), 1) & (BASE - 1)).astype(F32)
    order = jnp.where(order < number, begin + order, -1.0)
    my_start = down(pick(sender == my_chip, line_start))
    rows = iota((2 * POOL, DEPTH * BASE), 0).astype(F32)
    blocks = line_over[...].reshape(DEPTH * BASE, WIDTH)
    left = dot(onehot((rows == order) & (rows < POOL)), blocks[:, :HALF])
    right = dot(onehot((rows - POOL == order) & (rows >= POOL)), blocks[:, HALF:])
    send_over[...] = (left + right).astype(BF16)
    got_over[grp] = send_over[...]
    for step in range(1, LINES):
        low, middle = step % 4, step // 4
        device = {"grp": along_x[low] + along_y[(middle + low) % 4], "blk": blk}
        remote(send_over, got_over.at[grp], OVER, device).start()

    row = iota((8, 128), 0)
    told = pick(row == 6, rank) + pick(row == 7, fault)
    for part, (first_end, held_end) in enumerate(ends):
        told = told + pick(row == part, first_end) + pick(row == PARTS + part, held_end)
        plan_ref[part] = plans[part]
    facts[0] = told
    swap_facts = remote(facts.at[0], facts.at[1], FACTS, other_core)
    swap_facts.start()

    key_number = iota((SEGMENT, 1), 0).astype(F32)

    def swap_of(part):
        window = pl.ds(part * SEGMENT, SEGMENT)
        return remote(keys.at[window], keys.at[pl.ds(HELD + part * SEGMENT, SEGMENT)], SWAP + part, other_core)

    @pl.loop(0, PARTS)
    def _(part):
        some = onehot(iota((SEGMENT, SPAN), 0).astype(F32) == plan_ref[part])
        pick_ref[part] = some
        for number in range(PARTS):

            @pl.when(part == number)
            def _():
                await_blocks(got, messages[number], recv_sem.at[PART + number])

        @pl.when(part == last)
        def _():
            await_blocks(got_over, LINES - 1, recv_sem.at[OVER])
            halves = got_over[...].reshape(LINES * 2 * POOL, HALF)
            shape = (LINES * POOL, LINES * 2 * POOL)
            to, at = iota(shape, 0), iota(shape, 1)
            same = ((to >> 3) == (at >> 4)) & ((to & 7) == (at & 7))
            left = dot(onehot(same & ((at & POOL) == 0)), halves)
            right = dot(onehot(same & ((at & POOL) != 0)), halves)
            whole = jnp.concatenate([left, right], axis=1).astype(BF16)
            got[pl.ds(CHIPS, TOTAL - CHIPS)] = whole.reshape(TOTAL - CHIPS, BASE, WIDTH)

        rows = dot(some, got[pl.ds(part * STEPS, STEPS)].reshape(SPAN, WIDTH))
        unit = rows * lax.rsqrt(across(rows * rows) + EPSILON)
        keys[pl.ds(part * SEGMENT, SEGMENT)] = unit.astype(BF16)
        swap_of(part).start()
        is_first = key_number < facts[0, pl.ds(part, 1), 0:1]
        sums[0:1] += down(pick(is_first, unit))
        sums[1:2] += down(jnp.where(is_first, 0.0, unit))

    swap_sums = remote(sums, their_sums, SUMS, other_core)
    swap_sums.start()

    @pl.loop(0, 2 * PARTS)
    def _(block):
        side, part = block // PARTS, block % PARTS

        @pl.when(block == PARTS)
        def _():
            swap_facts.wait()
            for number in range(last):
                swap_of(number).wait()

        @pl.when(block == 2 * PARTS - 1)
        def _():
            swap_of(last).wait()

        first, held = facts[side, pl.ds(part, 1), 0:1], facts[side, pl.ds(PARTS + part, 1), 0:1]
        kind = jnp.where(key_number < first, 0.0, jnp.where(key_number < held, 1.0, 2.0))
        some = keys[pl.ds(block * SEGMENT, SEGMENT)]
        for query_part in range(PARTS):
            window = pl.ds(query_part * SEGMENT, SEGMENT)
            scores = dot_rows(some, keys[window])
            query_number = iota((1, SEGMENT), 1).astype(F32)
            matched = kind == jnp.where(query_number < ends[query_part][0], 0.0, 1.0)
            itself = iota((SEGMENT, 1), 0) + block * SEGMENT == iota((1, SEGMENT), 1) + query_part * SEGMENT
            scores = jnp.where(matched & (~itself), scores, -1.0)
            best_ref[:, window] = jnp.maximum(best_ref[:, window], jnp.max(scores, axis=0, keepdims=True))

    swap_sums.wait()
    total = sums[...] + their_sums[...]
    centre = total * lax.rsqrt(across(total * total) + EPSILON)
    near = dot_rows(jnp.concatenate(thirds(centre), axis=0).astype(BF16), keys[pl.ds(0, HELD)])
    near = near[0:8] + near[8:16] + near[16:24]

    row = iota((8, SEGMENT), 0)
    query_number = iota((1, SEGMENT), 1).astype(F32)
    tiles = CHIPS * BASE // 128
    for part in range(PARTS):
        window = slice(part * SEGMENT, (part + 1) * SEGMENT)
        some = jnp.where(query_number < ends[part][0], near[0:1, window], near[1:2, window])
        values = jnp.zeros((8, SEGMENT), F32)
        for number, term in enumerate(thirds(best_ref[:, window]) + thirds(some)):
            values = jnp.where(row == number, term, values)
        out = dot(values.astype(BF16), pick_ref[part])
        for kind in range(2):
            line = out[3 * kind : 3 * kind + 1] + out[3 * kind + 1 : 3 * kind + 2] + out[3 * kind + 2 : 3 * kind + 3]
            for tile in range(SPAN // 128):
                piece = line[:, tile * 128 : (tile + 1) * 128]
                if part * (SPAN // 128) + tile < tiles:
                    back[part * (SPAN // 128) + tile, kind : kind + 1, :] = piece
                else:
                    for each in range(tiles):
                        back[each, 2 + kind : 3 + kind, :] = piece
    returned[0] = back[0]

    def give(step, device):
        remote(back.at[step // 8], returned.at[step], BACK, device).start()

    each_device(0, 16, -1, give)

    differ = across(jnp.where(facts[1, 6:7, :] != rank, 1.0, 0.0))
    fault = fault + facts[1, 7:8, 0:1] + differ
    fault_ref[...] = jnp.where(fault > 0.5, 1, 0) + jnp.zeros((1, 128), jnp.int32)
    chosen = onehot(iota((CHIPS, ROWS), 0) == step_of)
    sub = iota((128, ROWS), 0)
    at_base = (sub == (step_of & 7) * BASE + slot) & in_base
    at_over = (sub == grp * POOL + my_start.astype(jnp.int32) + over_slot) & (~in_base)

    await_blocks(returned, CHIPS - 1, recv_sem.at[BACK])
    found = []
    for number in range(4):
        terms = jnp.concatenate(thirds(returned[:, number, :]), axis=1).astype(BF16)
        out = lax.dot_general(terms, chosen, (((0,), (0,)), ((), ())), preferred_element_type=F32)
        found.append(out[0:128] + out[128:256] + out[256:384])
    max_ref[...] = down(pick(at_base, found[0]) + pick(at_over, found[2]))
    cos_ref[...] = down(pick(at_base, found[1]) + pick(at_over, found[3]))

    await_blocks(heads, 3, send_sem.at[HEAD_Z])
    await_blocks(heads, 12, send_sem.at[HEAD_Y])
    await_blocks(heads, 48, send_sem.at[HEAD_X])
    await_blocks(line_over, DEPTH - 1, send_sem.at[LINE])
    await_blocks(got_over, LINES - 1, send_sem.at[OVER])
    await_blocks(returned, CHIPS - 1, send_sem.at[BACK])
    for part in range(PARTS):
        await_blocks(got, messages[part], send_sem.at[PART + part])


def routed(embeddings, assign, owner, send_count, send_index):
    return pl.pallas_call(
        kernel,
        out_shape=(
            jax.ShapeDtypeStruct((1, ROWS), F32),
            jax.ShapeDtypeStruct((1, ROWS), F32),
            jax.ShapeDtypeStruct((1, 128), jnp.int32),
        ),
        in_specs=[pl.BlockSpec(memory_space=pl.ANY)] + [pl.BlockSpec(memory_space=pltpu.VMEM)] * 4,
        out_specs=(pl.BlockSpec(memory_space=pltpu.VMEM),) * 3,
        scratch_shapes=[
            pltpu.VMEM((ROWS, WIDTH), BF16),
            pltpu.VMEM((TOTAL, BASE, WIDTH), BF16),
            pltpu.VMEM((TOTAL, BASE, WIDTH), BF16),
            pltpu.VMEM((CHIPS, 1, 128), F32),
            pltpu.VMEM((DEPTH, BASE, WIDTH), BF16),
            pltpu.VMEM((2 * POOL, HALF), BF16),
            pltpu.VMEM((LINES, 2 * POOL, HALF), BF16),
            pltpu.VMEM((PARTS, 1, SPAN), F32),
            pltpu.VMEM((PARTS, SEGMENT, SPAN), BF16),
            pltpu.VMEM((2 * HELD, WIDTH), BF16),
            pltpu.VMEM((2, 8, 128), F32),
            pltpu.VMEM((8, WIDTH), F32),
            pltpu.VMEM((8, WIDTH), F32),
            pltpu.VMEM((1, HELD), F32),
            pltpu.VMEM((CHIPS * BASE // 128, 4, 128), F32),
            pltpu.VMEM((CHIPS, 4, 128), F32),
            pltpu.SemaphoreType.DMA,
            pltpu.SemaphoreType.DMA((14,)),
            pltpu.SemaphoreType.DMA((14,)),
        ],
        compiler_params=pltpu.CompilerParams(
            collective_id=0, has_side_effects=True, vmem_limit_bytes=48 * 1024 * 1024
        ),
    )(
        embeddings,
        assign.reshape(1, ROWS),
        owner.reshape(1, CLUSTERS),
        send_count,
        send_index[0],
    )


def body(embeddings, assign, owner, send_count, send_index):
    arguments = (embeddings, assign, owner, send_count, send_index)
    max_sim, centroid_cos, fault = routed(*arguments)
    return lax.cond(
        fault[0, 0] != 0,
        lambda: general(*arguments),
        lambda: (max_sim.reshape(ROWS), centroid_cos.reshape(ROWS)),
    )


def solution(mesh):
    placed = (
        P(("grp", "blk"), None),
        P(("grp", "blk")),
        P(),
        P(("grp", "blk"), None),
        P(("grp", "blk"), None, None),
    )
    return jax.shard_map(
        body,
        mesh=mesh,
        in_specs=placed,
        out_specs=(P(("grp", "blk")), P(("grp", "blk"))),
        check_vma=False,
    )
```

```python
import functools

import jax
import jax.numpy as jnp
from jax import lax
from jax.experimental import pallas as pl
from jax.experimental.pallas import tpu as pltpu
from jax.sharding import PartitionSpec as P

EPSILON = 1e-06
F32 = jnp.float32
BF16 = jnp.bfloat16

CHIPS = 64
ROWS = 512
WIDTH = 768
CLUSTERS = 128
GROUPS = 16
CAP = 64
BASE = 16
HALF = WIDTH // 2
LINES = 16
DEPTH = 4
POOL = 8
SEGMENT = 256
PARTS = 3
STEPS = 24
SPAN = STEPS * BASE
TOTAL = PARTS * STEPS
HELD = PARTS * SEGMENT


def normalize(values):
    widened = values.astype(F32)
    return widened * lax.rsqrt(jnp.sum(widened * widened, axis=1, keepdims=True) + EPSILON)


def general(embeddings, assign, owner, send_count, send_index):
    rows_local = embeddings.shape[0]
    feature_width = embeddings.shape[1]
    groups = lax.axis_size("grp")
    clusters = owner.shape[0]
    capacity = send_index.shape[2]
    slot_total = groups * capacity
    unit_rows = normalize(embeddings)
    unit_low = unit_rows.astype(BF16)
    counts = send_count[0]
    listed = send_index[0]
    live_slot = jnp.arange(capacity, dtype=jnp.int32)[None, :] < counts[:, None]
    listed_cluster = assign[listed]
    owned_here = owner[listed_cluster] == jnp.arange(groups, dtype=jnp.int32)[:, None]
    kept_slot = live_slot & owned_here
    out_cluster = jnp.where(kept_slot, listed_cluster, -1)
    out_tag = jnp.where(kept_slot, lax.axis_index(("grp", "blk")) * rows_local + listed, -1)
    out_vector = unit_low[listed.reshape(-1)].reshape(groups, capacity, feature_width)
    got_vector, got_cluster, got_tag = (
        lax.all_to_all(out_vector, "grp", split_axis=0, concat_axis=0, tiled=True),
        lax.all_to_all(out_cluster, "grp", split_axis=0, concat_axis=0, tiled=True),
        lax.all_to_all(out_tag, "grp", split_axis=0, concat_axis=0, tiled=True),
    )
    own_vector = got_vector.reshape(slot_total, feature_width)
    own_cluster = got_cluster.reshape(slot_total)
    own_tag = got_tag.reshape(slot_total)

    def tile_best(current, shard_piece):
        other_vector, other_cluster, other_tag = shard_piece
        scores = jnp.einsum("id,jd->ij", own_vector, other_vector, preferred_element_type=F32)
        matched = (
            (own_cluster[:, None] == other_cluster[None, :])
            & (other_cluster[None, :] >= 0)
            & (own_tag[:, None] != other_tag[None, :])
        )
        return jnp.maximum(current, jnp.max(jnp.where(matched, scores, -1.0), axis=1))

    other_vector = lax.all_gather(own_vector, "blk", axis=0, tiled=True)
    other_cluster = lax.all_gather(own_cluster, "blk", axis=0, tiled=True)
    other_tag = lax.all_gather(own_tag, "blk", axis=0, tiled=True)
    length = other_vector.shape[0]
    number = length // slot_total
    stacked = (
        other_vector.reshape(number, slot_total, feature_width),
        other_cluster.reshape(number, slot_total),
        other_tag.reshape(number, slot_total),
    )

    def scan_step(carry, single):
        return (tile_best(carry, single), None)

    result, unused = lax.scan(scan_step, jnp.full((slot_total,), -1.0, F32), stacked)
    target = jnp.where(live_slot, listed, rows_local).reshape(-1)
    partial_sum = jax.ops.segment_sum(unit_rows, assign, num_segments=clusters)
    centre = normalize(lax.psum(partial_sum, ("grp", "blk")))
    nearness = jnp.sum(unit_low.astype(F32) * centre[assign], axis=1)
    returned = lax.all_to_all(
        result.reshape(groups, capacity), "grp", split_axis=0, concat_axis=0, tiled=True
    )
    has_entry = (
        jnp.zeros((rows_local,), jnp.int32)
        .at[target]
        .max(kept_slot.astype(jnp.int32).reshape(-1), mode="drop")
    )
    centroid_cos = jnp.where(has_entry > 0, nearness, 0.0)
    max_sim = jnp.full((rows_local,), -1.0, F32).at[target].max(returned.reshape(-1), mode="drop")
    return (max_sim, centroid_cos)


def iota(shape, axis):
    return lax.broadcasted_iota(jnp.int32, shape, axis)


def down(values):
    return jnp.sum(values, axis=0, keepdims=True)


def across(values):
    return jnp.sum(values, axis=1, keepdims=True)


def pick(mask, values):
    return jnp.where(mask, values, 0.0)


def as_column(row):
    size = row.shape[1]
    return across(pick(iota((size, size), 0) == iota((size, size), 1), row))


def as_row(column):
    size = column.shape[0]
    return down(pick(iota((size, size), 0) == iota((size, size), 1), column))


def dot(a, b):
    return jnp.dot(a, b, preferred_element_type=F32)


def dot_rows(a, b):
    return lax.dot_general(a, b, (((1,), (1,)), ((), ())), preferred_element_type=F32)


def onehot(mask):
    return jnp.where(mask, 1.0, 0.0).astype(BF16)


def thirds(values):
    first = values.astype(BF16).astype(F32)
    rest = values - first
    second = rest.astype(BF16).astype(F32)
    third = (rest - second).astype(BF16).astype(F32)
    return first, second, third


def rank_groups(count_ref):
    count_row = count_ref[...].astype(F32)
    count_column = as_column(count_row)
    sub, lane = iota((GROUPS, 128), 0), iota((GROUPS, 128), 1)
    count_lanes = down(pick(sub == lane, count_column))
    ahead = (count_column > count_lanes) | ((count_column == count_lanes) & (sub < lane))
    rank = down(jnp.where(ahead, 1.0, 0.0))
    return jnp.where(iota((1, 128), 1) < GROUPS, rank, 0.0), count_column


def place_documents(assign_ref, owner_ref, rank):
    owner_row = owner_ref[...].astype(F32)
    owner_column = as_column(owner_row)
    sub, lane = iota((CLUSTERS, CLUSTERS), 0), iota((CLUSTERS, CLUSTERS), 1)
    within = across(jnp.where((owner_column == owner_row) & (lane < sub), 1.0, 0.0))
    group_rank = across(pick(owner_column == lane.astype(F32), rank))
    place_column = group_rank * (CLUSTERS // GROUPS) + within
    member = iota((CLUSTERS, ROWS), 0) == assign_ref[...]
    place = down(pick(member, place_column))
    group = down(pick(member, owner_column))
    order = iota((CLUSTERS, ROWS), 0).astype(F32)
    at_place = order == place
    earlier = onehot(iota((ROWS, ROWS), 0) < iota((ROWS, ROWS), 1))
    before = dot(onehot(at_place), earlier)
    slot = down(pick(at_place, before))
    count_column = across(jnp.where(at_place, 1.0, 0.0))
    partner_count = down(pick(order == (CLUSTERS - 1) - place, count_column))
    slot = slot + jnp.where(place >= CHIPS, partner_count, 0.0)
    chip = jnp.minimum(place, (CLUSTERS - 1) - place)
    return group, chip.astype(jnp.int32), slot.astype(jnp.int32), as_row(count_column)


def missing_documents(index_ref, count_column, group):
    listed = index_ref[...]
    live = iota((GROUPS, CAP), 1).astype(F32) < count_column
    eye = onehot(iota((CAP, CAP), 0) == iota((CAP, CAP), 1))
    high = dot_rows(eye, jnp.where(live, listed >> 4, 0).astype(F32).astype(BF16))
    low = dot_rows(eye, jnp.where(live, listed & 15, 0).astype(F32).astype(BF16))
    alive = dot_rows(eye, onehot(live))
    slots = jnp.where(alive > 0.5, high * 16.0 + low, -1.0)
    document = iota((1, ROWS), 1).astype(F32)
    lane = iota((CAP, GROUPS), 1)

    def count(g, hits):
        column = across(pick(lane == g, slots))
        wanted = jnp.where(group == g.astype(F32), document, -2.0)
        return hits + jnp.where(column == wanted, 1.0, 0.0)

    hits = lax.fori_loop(0, GROUPS, count, jnp.zeros((CAP, ROWS), F32))
    return across(jnp.where(down(hits) > 0.5, 0.0, 1.0))


def hops(shift):
    return sum(min(d, 4 - d) for d in shift)


def send_order():
    left = [(x, y, z) for x in range(4) for y in range(4) for z in range(4)]
    order, load = [], {}

    def loaded(shift):
        use = {}
        for axis, d in enumerate(shift):
            for way, amount in {0: (), 1: ((0, 1),), 2: ((0, 1), (1, 1)), 3: ((1, 1),)}[d]:
                use[axis, way] = load.get((axis, way), 0) + amount
        return use

    while left:
        most = max(hops(shift) for shift in left)
        some = [shift for shift in left if hops(shift) == most]
        best = min(some, key=lambda shift: (max(loaded(shift).values(), default=0), sum(loaded(shift).values()), shift))
        load.update(loaded(best))
        left.remove(best)
        order.append(best)
    return order


ORDER = send_order()
SELF = CHIPS - 1


def step_to(dx, dy, dz):
    shift = (dx & 3) * 16 + (dy & 3) * 4 + (dz & 3)
    step = jnp.full(shift.shape, SELF, jnp.int32)
    for number, (x, y, z) in enumerate(ORDER[:SELF]):
        step = jnp.where(shift == x * 16 + y * 4 + z, number, step)
    return step


def in_part(step, part):
    return (step >= part * STEPS) & (step < (part + 1) * STEPS)


def chip_places():
    sub, lane = iota((CLUSTERS, CLUSTERS), 0), iota((CLUSTERS, CLUSTERS), 1)
    return onehot((sub == lane) | (sub == (CLUSTERS - 1) - lane))


def excess(totals):
    lane = iota(totals.shape, 1)
    return jnp.where(lane < CHIPS, jnp.maximum(totals - BASE, 0.0), 0.0)


def receive_plan(table, rank, my_x, my_y, my_z):
    chip = my_x * 16 + my_y * 4 + my_z
    heads = table.astype(jnp.int32)
    counts = (heads & 1023).astype(F32)
    differ = jnp.where((heads >> 10).astype(F32) != rank, 1.0, 0.0)
    fault = across(down(differ))
    both = dot(counts.astype(BF16), chip_places())
    over = excess(both)
    lanes = iota((CHIPS, CLUSTERS), 1)
    sender = iota((CHIPS, 1), 0)
    source, target = iota((CHIPS, CHIPS), 0), iota((CHIPS, CHIPS), 1)

    same_line = (source >> 2) == (target >> 2)
    over_total = across(over)
    over_row = as_row(over_total)
    line_start = across(pick(same_line & (target < source), over_row))
    line_total = across(pick(same_line, over_row))
    fault = fault + down(jnp.where(line_total > POOL, 1.0, 0.0))
    start = line_start + across(pick(lanes < chip, over))
    number = across(pick(lanes == chip, over))

    to_chip = iota((1, CLUSTERS), 1)
    route = step_to(
        (to_chip >> 4) - (sender >> 4), ((to_chip >> 2) & 3) - ((sender >> 2) & 3), (to_chip & 3) - (sender & 3)
    )
    based = jnp.where(lanes < CHIPS, jnp.minimum(both, float(BASE)), 0.0)
    for part in range(PARTS):
        held = down(pick(in_part(route, part), based))
        if part == PARTS - 1:
            held = held + down(over)
        fault = fault + across(jnp.where(held > SEGMENT, 1.0, 0.0))

    first = across(pick(lanes == chip, counts))
    second = across(pick(lanes == (CLUSTERS - 1) - chip, counts))
    place = (lanes & (POOL - 1)).astype(F32) - start
    mine = ((sender >> 2) == (lanes >> 3)) & (place >= 0.0) & (place < number)
    over_first = down(jnp.where(mine & (place + BASE < first), 1.0, 0.0))
    over_second = down(jnp.where(mine & (place + BASE >= first), 1.0, 0.0))
    over_first_total, over_second_total = across(over_first), across(over_second)
    earlier = onehot(iota((CLUSTERS, CLUSTERS), 0) < iota((CLUSTERS, CLUSTERS), 1))
    sub = iota((16, CLUSTERS), 0)
    before = dot((pick(sub == 0, over_first) + pick(sub == 1, over_second)).astype(BF16), earlier)

    base_first = jnp.minimum(first, float(BASE))
    base_second = jnp.minimum(first + second, float(BASE)) - base_first
    first_row, second_row = as_row(base_first), as_row(base_second)

    def my_step(other):
        return step_to(my_x - (other >> 4), my_y - ((other >> 2) & 3), my_z - (other & 3))

    step_column, step_row = my_step(sender), my_step(iota((1, CHIPS), 1))
    plans = []
    ends = []
    for part in range(PARTS):
        inside = in_part(step_column, part)
        ahead = (target < source) & in_part(step_row, part)
        first_total = down(pick(inside, base_first))
        second_total = down(pick(inside, base_second))
        last = part == PARTS - 1
        first_end = first_total + over_first_total if last else first_total
        first_start = across(pick(ahead, first_row))
        second_start = across(pick(ahead, second_row)) + first_end
        spread = step_column - part * STEPS == (iota((CHIPS, SPAN), 1) >> 4)
        head, tail, head_start, tail_start = [
            down(pick(spread, column)) for column in (base_first, base_second, first_start, second_start)
        ]
        slot = (iota((1, SPAN), 1) & (BASE - 1)).astype(F32)
        later = jnp.where(slot < head + tail, tail_start + (slot - head), -1.0)
        plan = jnp.where(slot < head, head_start + slot, later)
        held_end = first_end + second_total
        if last:
            over_row_of = jnp.where(over_second > 0.5, held_end + before[1:2], -1.0)
            over_row_of = jnp.where(over_first > 0.5, first_total + before[0:1], over_row_of)
            plan = jnp.concatenate([plan[:, : SPAN - CLUSTERS], over_row_of], axis=1)
            held_end = held_end + over_second_total
        plans.append(plan)
        ends.append((first_end, held_end))
    return plans, ends, line_start, over_total, fault


def kernel(
    x_hbm, assign_ref, owner_ref, count_ref, index_ref,
    max_ref, cos_ref, fault_ref,
    x_ref, send, got, heads, line_over, send_over, got_over, plan_ref, pick_ref,
    keys, facts, sums, their_sums, best_ref, back, returned,
    x_sem, send_sem, recv_sem,
):
    grp, blk = lax.axis_index("grp"), lax.axis_index("blk")
    my_x, my_y, my_z, core = grp // 4, grp % 4, blk // 2, blk % 2
    my_chip = grp * 4 + my_z
    last = PARTS - 1
    along_x = [((my_x + d) % 4) * 4 for d in range(4)]
    along_y = [(my_y + d) % 4 for d in range(4)]
    along_z = [((my_z + d) % 4) * 2 + core for d in range(4)]
    other_core = {"grp": grp, "blk": my_z * 2 + (1 - core)}

    def each_device(steps, sign, act):
        for step in steps:
            dx, dy, dz = [(sign * d) % 4 for d in ORDER[step]]
            act(step, {"grp": along_x[dx] + along_y[dy], "blk": along_z[dz]})

    def remote(source, target, number, device):
        return pltpu.make_async_remote_copy(
            src_ref=source,
            dst_ref=target,
            send_sem=send_sem.at[number],
            recv_sem=recv_sem.at[number],
            device_id=device,
            device_id_type=pl.DeviceIdType.MESH,
        )

    def await_blocks(ref, number, semaphore):
        block = ref.at[pl.ds(0, number)]
        pltpu.make_async_copy(block, block, semaphore).wait()

    HEAD_Z, HEAD_Y, HEAD_X, LINE, OVER, FACTS, SUMS, BACK, SWAP, PART = 0, 1, 2, 3, 4, 5, 6, 7, 8, 11
    messages = (STEPS, STEPS, SELF - 2 * STEPS)

    barrier = pltpu.get_barrier_semaphore()
    load = pltpu.make_async_copy(x_hbm, x_ref, x_sem)
    load.start()

    def greet(step, device):
        pl.semaphore_signal(barrier, inc=1, device_id=device, device_id_type=pl.DeviceIdType.MESH)

    each_device(range(SELF), 1, greet)
    greet(0, other_core)

    rank, count_column = rank_groups(count_ref)
    group, chip, slot, place_counts = place_documents(assign_ref, owner_ref, rank)
    step_of = step_to((chip >> 4) - my_x, ((chip >> 2) & 3) - my_y, (chip & 3) - my_z)
    in_base = slot < BASE
    place_counts_16 = place_counts + jnp.zeros((16, CLUSTERS), F32)
    own_excess = excess(dot(place_counts_16.astype(BF16), chip_places())[0:1])
    eye = iota((CHIPS, CLUSTERS), 0) == iota((CHIPS, CLUSTERS), 1)
    excess_column = across(pick(eye, own_excess))
    over_slot = down(pick(iota((CHIPS, ROWS), 0) < chip, excess_column)).astype(jnp.int32) + (slot - BASE)
    over_place = jnp.where(over_slot < BASE, CHIPS * BASE + over_slot, -1)
    send_slot = jnp.where(in_base, step_of * BASE + slot, over_place)
    load.wait()

    @pl.loop(0, PARTS)
    def _(part):
        slots = iota((SPAN, ROWS), 0) + part * SPAN
        rows = dot(onehot(slots == send_slot), x_ref[...]).astype(BF16)
        send[pl.ds(part * STEPS, STEPS)] = rows.reshape(STEPS, BASE, WIDTH)

        @pl.when(part == 0)
        def _():
            pl.semaphore_wait(barrier, CHIPS)

        @pl.when(part == last)
        def _():
            line_over[my_z] = send[CHIPS]
            for step in range(1, DEPTH):
                device = {"grp": grp, "blk": along_z[step]}
                remote(send.at[CHIPS], line_over.at[my_z], LINE, device).start()

        def post(step, device):
            remote(send.at[step], got.at[step], PART + part, device).start()

        for number in range(PARTS):

            @pl.when(part == number)
            def _():
                each_device(range(number * STEPS, min((number + 1) * STEPS, SELF)), 1, post)

        @pl.when(part == 0)
        def _():
            missing = missing_documents(index_ref, count_column, group)
            heads[my_chip] = place_counts + 1024.0 * rank + jnp.where(missing > 0.5, 16384.0, 0.0)
            for step in range(1, 4):
                block = heads.at[pl.ds(my_chip, 1)]
                remote(block, block, HEAD_Z, {"grp": grp, "blk": along_z[step]}).start()

        @pl.when(part == 1)
        def _():
            await_blocks(heads, 3, recv_sem.at[HEAD_Z])
            for step in range(1, 4):
                block = heads.at[pl.ds(grp * 4, 4)]
                remote(block, block, HEAD_Y, {"grp": along_x[0] + along_y[step], "blk": blk}).start()

        @pl.when(part == last)
        def _():
            await_blocks(heads, 12, recv_sem.at[HEAD_Y])
            for step in range(1, 4):
                block = heads.at[pl.ds(my_x * 16, 16)]
                remote(block, block, HEAD_X, {"grp": along_x[step] + along_y[0], "blk": blk}).start()

    got[SELF] = send[SELF]
    got[pl.ds(CHIPS, TOTAL - CHIPS)] = jnp.zeros((TOTAL - CHIPS, BASE, WIDTH), BF16)
    sums[...] = jnp.zeros((8, WIDTH), F32)
    best_ref[...] = jnp.full((1, HELD), -1.0, F32)

    await_blocks(heads, 48, recv_sem.at[HEAD_X])
    table = heads[...].reshape(CHIPS, CLUSTERS)
    plans, ends, line_start, over_total, fault = receive_plan(table, rank, my_x, my_y, my_z)

    await_blocks(line_over, DEPTH - 1, recv_sem.at[LINE])
    sender = iota((CHIPS, 1), 0)
    at = sender == grp * 4 + (iota((CHIPS, DEPTH * BASE), 1) >> 4)
    begin = down(pick(at, line_start))
    number = down(pick(at, over_total))
    order = (iota((1, DEPTH * BASE), 1) & (BASE - 1)).astype(F32)
    order = jnp.where(order < number, begin + order, -1.0)
    my_start = down(pick(sender == my_chip, line_start))
    rows = iota((2 * POOL, DEPTH * BASE), 0).astype(F32)
    blocks = line_over[...].reshape(DEPTH * BASE, WIDTH)
    left = dot(onehot((rows == order) & (rows < POOL)), blocks[:, :HALF])
    right = dot(onehot((rows - POOL == order) & (rows >= POOL)), blocks[:, HALF:])
    send_over[...] = (left + right).astype(BF16)
    got_over[grp] = send_over[...]
    for step in range(1, LINES):
        low, middle = step % 4, step // 4
        device = {"grp": along_x[low] + along_y[(middle + low) % 4], "blk": blk}
        remote(send_over, got_over.at[grp], OVER, device).start()

    row = iota((8, 128), 0)
    told = pick(row == 6, rank) + pick(row == 7, fault)
    for part, (first_end, held_end) in enumerate(ends):
        told = told + pick(row == part, first_end) + pick(row == PARTS + part, held_end)
        plan_ref[part] = plans[part]
    facts[0] = told
    swap_facts = remote(facts.at[0], facts.at[1], FACTS, other_core)
    swap_facts.start()

    key_number = iota((SEGMENT, 1), 0).astype(F32)

    def swap_of(part):
        window = pl.ds(part * SEGMENT, SEGMENT)
        return remote(keys.at[window], keys.at[pl.ds(HELD + part * SEGMENT, SEGMENT)], SWAP + part, other_core)

    @pl.loop(0, PARTS)
    def _(part):
        some = onehot(iota((SEGMENT, SPAN), 0).astype(F32) == plan_ref[part])
        pick_ref[part] = some
        for number in range(PARTS):

            @pl.when(part == number)
            def _():
                await_blocks(got, messages[number], recv_sem.at[PART + number])

        @pl.when(part == last)
        def _():
            await_blocks(got_over, LINES - 1, recv_sem.at[OVER])
            halves = got_over[...].reshape(LINES * 2 * POOL, HALF)
            shape = (LINES * POOL, LINES * 2 * POOL)
            to, at = iota(shape, 0), iota(shape, 1)
            same = ((to >> 3) == (at >> 4)) & ((to & 7) == (at & 7))
            left = dot(onehot(same & ((at & POOL) == 0)), halves)
            right = dot(onehot(same & ((at & POOL) != 0)), halves)
            whole = jnp.concatenate([left, right], axis=1).astype(BF16)
            got[pl.ds(CHIPS, TOTAL - CHIPS)] = whole.reshape(TOTAL - CHIPS, BASE, WIDTH)

        rows = dot(some, got[pl.ds(part * STEPS, STEPS)].reshape(SPAN, WIDTH))
        unit = rows * lax.rsqrt(across(rows * rows) + EPSILON)
        keys[pl.ds(part * SEGMENT, SEGMENT)] = unit.astype(BF16)
        swap_of(part).start()
        is_first = key_number < facts[0, pl.ds(part, 1), 0:1]
        sums[0:1] += down(pick(is_first, unit))
        sums[1:2] += down(jnp.where(is_first, 0.0, unit))

    swap_sums = remote(sums, their_sums, SUMS, other_core)
    swap_sums.start()

    @pl.loop(0, 2 * PARTS)
    def _(block):
        side, part = block // PARTS, block % PARTS

        @pl.when(block == PARTS)
        def _():
            swap_facts.wait()
            for number in range(last):
                swap_of(number).wait()

        @pl.when(block == 2 * PARTS - 1)
        def _():
            swap_of(last).wait()

        first, held = facts[side, pl.ds(part, 1), 0:1], facts[side, pl.ds(PARTS + part, 1), 0:1]
        kind = jnp.where(key_number < first, 0.0, jnp.where(key_number < held, 1.0, 2.0))
        some = keys[pl.ds(block * SEGMENT, SEGMENT)]
        for query_part in range(PARTS):
            window = pl.ds(query_part * SEGMENT, SEGMENT)
            scores = dot_rows(some, keys[window])
            query_number = iota((1, SEGMENT), 1).astype(F32)
            matched = kind == jnp.where(query_number < ends[query_part][0], 0.0, 1.0)
            itself = iota((SEGMENT, 1), 0) + block * SEGMENT == iota((1, SEGMENT), 1) + query_part * SEGMENT
            scores = jnp.where(matched & (~itself), scores, -1.0)
            best_ref[:, window] = jnp.maximum(best_ref[:, window], jnp.max(scores, axis=0, keepdims=True))

    swap_sums.wait()
    total = sums[...] + their_sums[...]
    centre = total * lax.rsqrt(across(total * total) + EPSILON)
    near = dot_rows(jnp.concatenate(thirds(centre), axis=0).astype(BF16), keys[pl.ds(0, HELD)])
    near = near[0:8] + near[8:16] + near[16:24]

    row = iota((8, SEGMENT), 0)
    query_number = iota((1, SEGMENT), 1).astype(F32)
    tiles = CHIPS * BASE // 128
    for part in range(PARTS):
        window = slice(part * SEGMENT, (part + 1) * SEGMENT)
        some = jnp.where(query_number < ends[part][0], near[0:1, window], near[1:2, window])
        values = jnp.zeros((8, SEGMENT), F32)
        for number, term in enumerate(thirds(best_ref[:, window]) + thirds(some)):
            values = jnp.where(row == number, term, values)
        out = dot(values.astype(BF16), pick_ref[part])
        for kind in range(2):
            line = out[3 * kind : 3 * kind + 1] + out[3 * kind + 1 : 3 * kind + 2] + out[3 * kind + 2 : 3 * kind + 3]
            for tile in range(SPAN // 128):
                piece = line[:, tile * 128 : (tile + 1) * 128]
                if part * (SPAN // 128) + tile < tiles:
                    back[part * (SPAN // 128) + tile, kind : kind + 1, :] = piece
                else:
                    for each in range(tiles):
                        back[each, 2 + kind : 3 + kind, :] = piece
    returned[SELF] = back[SELF // 8]

    def give(step, device):
        remote(back.at[step // 8], returned.at[step], BACK, device).start()

    each_device(range(SELF), -1, give)

    differ = across(jnp.where(facts[1, 6:7, :] != rank, 1.0, 0.0))
    fault = fault + facts[1, 7:8, 0:1] + differ
    fault_ref[...] = jnp.where(fault > 0.5, 1, 0) + jnp.zeros((1, 128), jnp.int32)
    chosen = onehot(iota((CHIPS, ROWS), 0) == step_of)
    sub = iota((128, ROWS), 0)
    at_base = (sub == (step_of & 7) * BASE + slot) & in_base
    at_over = (sub == grp * POOL + my_start.astype(jnp.int32) + over_slot) & (~in_base)

    await_blocks(returned, CHIPS - 1, recv_sem.at[BACK])
    found = []
    for number in range(4):
        terms = jnp.concatenate(thirds(returned[:, number, :]), axis=1).astype(BF16)
        out = lax.dot_general(terms, chosen, (((0,), (0,)), ((), ())), preferred_element_type=F32)
        found.append(out[0:128] + out[128:256] + out[256:384])
    max_ref[...] = down(pick(at_base, found[0]) + pick(at_over, found[2]))
    cos_ref[...] = down(pick(at_base, found[1]) + pick(at_over, found[3]))

    await_blocks(heads, 3, send_sem.at[HEAD_Z])
    await_blocks(heads, 12, send_sem.at[HEAD_Y])
    await_blocks(heads, 48, send_sem.at[HEAD_X])
    await_blocks(line_over, DEPTH - 1, send_sem.at[LINE])
    await_blocks(got_over, LINES - 1, send_sem.at[OVER])
    await_blocks(returned, CHIPS - 1, send_sem.at[BACK])
    for part in range(PARTS):
        await_blocks(got, messages[part], send_sem.at[PART + part])


def routed(embeddings, assign, owner, send_count, send_index):
    return pl.pallas_call(
        kernel,
        out_shape=(
            jax.ShapeDtypeStruct((1, ROWS), F32),
            jax.ShapeDtypeStruct((1, ROWS), F32),
            jax.ShapeDtypeStruct((1, 128), jnp.int32),
        ),
        in_specs=[pl.BlockSpec(memory_space=pl.ANY)] + [pl.BlockSpec(memory_space=pltpu.VMEM)] * 4,
        out_specs=(pl.BlockSpec(memory_space=pltpu.VMEM),) * 3,
        scratch_shapes=[
            pltpu.VMEM((ROWS, WIDTH), BF16),
            pltpu.VMEM((TOTAL, BASE, WIDTH), BF16),
            pltpu.VMEM((TOTAL, BASE, WIDTH), BF16),
            pltpu.VMEM((CHIPS, 1, 128), F32),
            pltpu.VMEM((DEPTH, BASE, WIDTH), BF16),
            pltpu.VMEM((2 * POOL, HALF), BF16),
            pltpu.VMEM((LINES, 2 * POOL, HALF), BF16),
            pltpu.VMEM((PARTS, 1, SPAN), F32),
            pltpu.VMEM((PARTS, SEGMENT, SPAN), BF16),
            pltpu.VMEM((2 * HELD, WIDTH), BF16),
            pltpu.VMEM((2, 8, 128), F32),
            pltpu.VMEM((8, WIDTH), F32),
            pltpu.VMEM((8, WIDTH), F32),
            pltpu.VMEM((1, HELD), F32),
            pltpu.VMEM((CHIPS * BASE // 128, 4, 128), F32),
            pltpu.VMEM((CHIPS, 4, 128), F32),
            pltpu.SemaphoreType.DMA,
            pltpu.SemaphoreType.DMA((14,)),
            pltpu.SemaphoreType.DMA((14,)),
        ],
        compiler_params=pltpu.CompilerParams(
            collective_id=0, has_side_effects=True, vmem_limit_bytes=48 * 1024 * 1024
        ),
    )(
        embeddings,
        assign.reshape(1, ROWS),
        owner.reshape(1, CLUSTERS),
        send_count,
        send_index[0],
    )


def body(embeddings, assign, owner, send_count, send_index):
    arguments = (embeddings, assign, owner, send_count, send_index)
    max_sim, centroid_cos, fault = routed(*arguments)
    return lax.cond(
        fault[0, 0] != 0,
        lambda: general(*arguments),
        lambda: (max_sim.reshape(ROWS), centroid_cos.reshape(ROWS)),
    )


def solution(mesh):
    placed = (
        P(("grp", "blk"), None),
        P(("grp", "blk")),
        P(),
        P(("grp", "blk"), None),
        P(("grp", "blk"), None, None),
    )
    return jax.shard_map(
        body,
        mesh=mesh,
        in_specs=placed,
        out_specs=(P(("grp", "blk")), P(("grp", "blk"))),
        check_vma=False,
    )
```

```python
import functools

import jax
import jax.numpy as jnp
from jax import lax
from jax.experimental import pallas as pl
from jax.experimental.pallas import tpu as pltpu
from jax.sharding import PartitionSpec as P

EPSILON = 1e-06
F32 = jnp.float32
BF16 = jnp.bfloat16

CHIPS = 64
ROWS = 512
WIDTH = 768
CLUSTERS = 128
GROUPS = 16
CAP = 64
BASE = 16
HALF = WIDTH // 2
LINES = 16
DEPTH = 4
POOL = 8
PARTS = ((0, 24, 256), (24, 32, 384), (56, 16, 128))
TOTAL = 72
HELD = 768
STARTS = (0, 256, 640)
LAST = len(PARTS) - 1
NONE = 1e30


def normalize(values):
    widened = values.astype(F32)
    return widened * lax.rsqrt(jnp.sum(widened * widened, axis=1, keepdims=True) + EPSILON)


def general(embeddings, assign, owner, send_count, send_index):
    rows_local = embeddings.shape[0]
    feature_width = embeddings.shape[1]
    groups = lax.axis_size("grp")
    clusters = owner.shape[0]
    capacity = send_index.shape[2]
    slot_total = groups * capacity
    unit_rows = normalize(embeddings)
    unit_low = unit_rows.astype(BF16)
    counts = send_count[0]
    listed = send_index[0]
    live_slot = jnp.arange(capacity, dtype=jnp.int32)[None, :] < counts[:, None]
    listed_cluster = assign[listed]
    owned_here = owner[listed_cluster] == jnp.arange(groups, dtype=jnp.int32)[:, None]
    kept_slot = live_slot & owned_here
    out_cluster = jnp.where(kept_slot, listed_cluster, -1)
    out_tag = jnp.where(kept_slot, lax.axis_index(("grp", "blk")) * rows_local + listed, -1)
    out_vector = unit_low[listed.reshape(-1)].reshape(groups, capacity, feature_width)
    got_vector, got_cluster, got_tag = (
        lax.all_to_all(out_vector, "grp", split_axis=0, concat_axis=0, tiled=True),
        lax.all_to_all(out_cluster, "grp", split_axis=0, concat_axis=0, tiled=True),
        lax.all_to_all(out_tag, "grp", split_axis=0, concat_axis=0, tiled=True),
    )
    own_vector = got_vector.reshape(slot_total, feature_width)
    own_cluster = got_cluster.reshape(slot_total)
    own_tag = got_tag.reshape(slot_total)

    def tile_best(current, shard_piece):
        other_vector, other_cluster, other_tag = shard_piece
        scores = jnp.einsum("id,jd->ij", own_vector, other_vector, preferred_element_type=F32)
        matched = (
            (own_cluster[:, None] == other_cluster[None, :])
            & (other_cluster[None, :] >= 0)
            & (own_tag[:, None] != other_tag[None, :])
        )
        return jnp.maximum(current, jnp.max(jnp.where(matched, scores, -1.0), axis=1))

    other_vector = lax.all_gather(own_vector, "blk", axis=0, tiled=True)
    other_cluster = lax.all_gather(own_cluster, "blk", axis=0, tiled=True)
    other_tag = lax.all_gather(own_tag, "blk", axis=0, tiled=True)
    length = other_vector.shape[0]
    number = length // slot_total
    stacked = (
        other_vector.reshape(number, slot_total, feature_width),
        other_cluster.reshape(number, slot_total),
        other_tag.reshape(number, slot_total),
    )

    def scan_step(carry, single):
        return (tile_best(carry, single), None)

    result, unused = lax.scan(scan_step, jnp.full((slot_total,), -1.0, F32), stacked)
    target = jnp.where(live_slot, listed, rows_local).reshape(-1)
    partial_sum = jax.ops.segment_sum(unit_rows, assign, num_segments=clusters)
    centre = normalize(lax.psum(partial_sum, ("grp", "blk")))
    nearness = jnp.sum(unit_low.astype(F32) * centre[assign], axis=1)
    returned = lax.all_to_all(
        result.reshape(groups, capacity), "grp", split_axis=0, concat_axis=0, tiled=True
    )
    has_entry = (
        jnp.zeros((rows_local,), jnp.int32)
        .at[target]
        .max(kept_slot.astype(jnp.int32).reshape(-1), mode="drop")
    )
    centroid_cos = jnp.where(has_entry > 0, nearness, 0.0)
    max_sim = jnp.full((rows_local,), -1.0, F32).at[target].max(returned.reshape(-1), mode="drop")
    return (max_sim, centroid_cos)


def iota(shape, axis):
    return lax.broadcasted_iota(jnp.int32, shape, axis)


def down(values):
    return jnp.sum(values, axis=0, keepdims=True)


def across(values):
    return jnp.sum(values, axis=1, keepdims=True)


def pick(mask, values):
    return jnp.where(mask, values, 0.0)


def as_column(row):
    size = row.shape[1]
    return across(pick(iota((size, size), 0) == iota((size, size), 1), row))


def as_row(column):
    size = column.shape[0]
    return down(pick(iota((size, size), 0) == iota((size, size), 1), column))


def dot(a, b):
    return jnp.dot(a, b, preferred_element_type=F32)


def dot_rows(a, b):
    return lax.dot_general(a, b, (((1,), (1,)), ((), ())), preferred_element_type=F32)


def onehot(mask):
    return jnp.where(mask, 1.0, 0.0).astype(BF16)


def thirds(values):
    first = values.astype(BF16).astype(F32)
    rest = values - first
    second = rest.astype(BF16).astype(F32)
    third = (rest - second).astype(BF16).astype(F32)
    return first, second, third


def rank_groups(count_ref):
    count_row = count_ref[...].astype(F32)
    count_column = as_column(count_row)
    sub, lane = iota((GROUPS, 128), 0), iota((GROUPS, 128), 1)
    count_lanes = down(pick(sub == lane, count_column))
    ahead = (count_column > count_lanes) | ((count_column == count_lanes) & (sub < lane))
    rank = down(jnp.where(ahead, 1.0, 0.0))
    return jnp.where(iota((1, 128), 1) < GROUPS, rank, 0.0), count_column


def place_documents(assign_ref, owner_ref, rank):
    owner_row = owner_ref[...].astype(F32)
    owner_column = as_column(owner_row)
    sub, lane = iota((CLUSTERS, CLUSTERS), 0), iota((CLUSTERS, CLUSTERS), 1)
    within = across(jnp.where((owner_column == owner_row) & (lane < sub), 1.0, 0.0))
    group_rank = across(pick(owner_column == lane.astype(F32), rank))
    place_column = group_rank * (CLUSTERS // GROUPS) + within
    member = iota((CLUSTERS, ROWS), 0) == assign_ref[...]
    place = down(pick(member, place_column))
    group = down(pick(member, owner_column))
    order = iota((CLUSTERS, ROWS), 0).astype(F32)
    at_place = order == place
    earlier = onehot(iota((ROWS, ROWS), 0) < iota((ROWS, ROWS), 1))
    before = dot(onehot(at_place), earlier)
    slot = down(pick(at_place, before))
    count_column = across(jnp.where(at_place, 1.0, 0.0))
    partner_count = down(pick(order == (CLUSTERS - 1) - place, count_column))
    slot = slot + jnp.where(place >= CHIPS, partner_count, 0.0)
    chip = jnp.minimum(place, (CLUSTERS - 1) - place)
    return group, chip.astype(jnp.int32), slot.astype(jnp.int32), as_row(count_column)


def missing_documents(index_ref, count_column, group):
    listed = index_ref[...]
    live = iota((GROUPS, CAP), 1).astype(F32) < count_column
    eye = onehot(iota((CAP, CAP), 0) == iota((CAP, CAP), 1))
    high = dot_rows(eye, jnp.where(live, listed >> 4, 0).astype(F32).astype(BF16))
    low = dot_rows(eye, jnp.where(live, listed & 15, 0).astype(F32).astype(BF16))
    alive = dot_rows(eye, onehot(live))
    slots = jnp.where(alive > 0.5, high * 16.0 + low, -1.0)
    document = iota((1, ROWS), 1).astype(F32)
    lane = iota((CAP, GROUPS), 1)

    def count(g, hits):
        column = across(pick(lane == g, slots))
        wanted = jnp.where(group == g.astype(F32), document, -2.0)
        return hits + jnp.where(column == wanted, 1.0, 0.0)

    hits = lax.fori_loop(0, GROUPS, count, jnp.zeros((CAP, ROWS), F32))
    return across(jnp.where(down(hits) > 0.5, 0.0, 1.0))


def send_order():
    order = []
    for step in range(CHIPS):
        high, middle, low = step // 16, (step // 4) % 4, step % 4
        order.append((low, (middle + low) % 4, (high + middle + low) % 4))
    near = [shift for shift in order if sum(min(d, 4 - d) for d in shift) <= 1] + [(2, 0, 0)]
    near.sort(key=lambda shift: -sum(min(d, 4 - d) for d in shift))
    return [shift for shift in order if shift not in near] + near


ORDER = send_order()
SELF = CHIPS - 1


def step_to(dx, dy, dz):
    shift = (dx & 3) * 16 + (dy & 3) * 4 + (dz & 3)
    step = jnp.full(shift.shape, SELF, jnp.int32)
    for number, (x, y, z) in enumerate(ORDER[:SELF]):
        step = jnp.where(shift == x * 16 + y * 4 + z, number, step)
    return step


def in_part(step, part):
    begin, steps, _ = PARTS[part]
    return (step >= begin) & (step < begin + steps)


def chip_places():
    sub, lane = iota((CLUSTERS, CLUSTERS), 0), iota((CLUSTERS, CLUSTERS), 1)
    return onehot((sub == lane) | (sub == (CLUSTERS - 1) - lane))


def excess(totals):
    lane = iota(totals.shape, 1)
    return jnp.where(lane < CHIPS, jnp.maximum(totals - BASE, 0.0), 0.0)


def receive_plan(table, rank, my_x, my_y, my_z):
    chip = my_x * 16 + my_y * 4 + my_z
    heads = table.astype(jnp.int32)
    counts = (heads & 1023).astype(F32)
    differ = jnp.where((heads >> 10).astype(F32) != rank, 1.0, 0.0)
    fault = across(down(differ))
    both = dot(counts.astype(BF16), chip_places())
    over = excess(both)
    lanes = iota((CHIPS, CLUSTERS), 1)
    sender = iota((CHIPS, 1), 0)
    source, target = iota((CHIPS, CHIPS), 0), iota((CHIPS, CHIPS), 1)

    same_line = (source >> 2) == (target >> 2)
    over_total = across(over)
    over_row = as_row(over_total)
    line_start = across(pick(same_line & (target < source), over_row))
    line_total = across(pick(same_line, over_row))
    fault = fault + down(jnp.where(line_total > POOL, 1.0, 0.0))
    start = line_start + across(pick(lanes < chip, over))
    number = across(pick(lanes == chip, over))

    to_chip = iota((1, CLUSTERS), 1)
    route = step_to(
        (to_chip >> 4) - (sender >> 4), ((to_chip >> 2) & 3) - ((sender >> 2) & 3), (to_chip & 3) - (sender & 3)
    )
    based = jnp.where(lanes < CHIPS, jnp.minimum(both, float(BASE)), 0.0)
    for part, (_, _, room) in enumerate(PARTS):
        held = down(pick(in_part(route, part), based))
        if part == LAST:
            held = held + down(over)
        fault = fault + across(jnp.where(held > room, 1.0, 0.0))

    first = across(pick(lanes == chip, counts))
    second = across(pick(lanes == (CLUSTERS - 1) - chip, counts))
    place = (lanes & (POOL - 1)).astype(F32) - start
    mine = ((sender >> 2) == (lanes >> 3)) & (place >= 0.0) & (place < number)
    over_first = down(jnp.where(mine & (place + BASE < first), 1.0, 0.0))
    over_second = down(jnp.where(mine & (place + BASE >= first), 1.0, 0.0))
    over_first_total, over_second_total = across(over_first), across(over_second)
    earlier = onehot(iota((CLUSTERS, CLUSTERS), 0) < iota((CLUSTERS, CLUSTERS), 1))
    sub = iota((16, CLUSTERS), 0)
    before = dot((pick(sub == 0, over_first) + pick(sub == 1, over_second)).astype(BF16), earlier)

    base_first = jnp.minimum(first, float(BASE))
    base_second = jnp.minimum(first + second, float(BASE)) - base_first
    first_row, second_row = as_row(base_first), as_row(base_second)

    def my_step(other):
        return step_to(my_x - (other >> 4), my_y - ((other >> 2) & 3), my_z - (other & 3))

    step_column, step_row = my_step(sender), my_step(iota((1, CHIPS), 1))
    plans = []
    ends = []
    for part, (begin, steps, _) in enumerate(PARTS):
        inside = in_part(step_column, part)
        ahead = (target < source) & in_part(step_row, part)
        first_total = down(pick(inside, base_first))
        second_total = down(pick(inside, base_second))
        last = part == LAST
        first_end = first_total + over_first_total if last else first_total
        first_start = across(pick(ahead, first_row))
        second_start = across(pick(ahead, second_row)) + first_end
        spread = step_column - begin == (iota((CHIPS, steps * BASE), 1) >> 4)
        head, tail, head_start, tail_start = [
            down(pick(spread, column)) for column in (base_first, base_second, first_start, second_start)
        ]
        slot = (iota((1, steps * BASE), 1) & (BASE - 1)).astype(F32)
        later = jnp.where(slot < head + tail, tail_start + (slot - head), -1.0)
        plan = jnp.where(slot < head, head_start + slot, later)
        held_end = first_end + second_total
        if last:
            over_row_of = jnp.where(over_second > 0.5, held_end + before[1:2], -1.0)
            over_row_of = jnp.where(over_first > 0.5, first_total + before[0:1], over_row_of)
            plan = jnp.concatenate([plan[:, : steps * BASE - CLUSTERS], over_row_of], axis=1)
            held_end = held_end + over_second_total
        plans.append(plan)
        ends.append((first_end, held_end))
    return plans, ends, line_start, over_total, fault


def kernel(
    x_hbm, assign_hbm, owner_hbm, count_hbm, index_hbm,
    max_ref, cos_ref, fault_ref,
    x_ref, assign_ref, owner_ref, count_ref, index_ref,
    send, got, heads, own_over, line_over, send_over, got_over, pick_0, pick_1, pick_2,
    mine, theirs, facts, sums, their_sums, back, returned,
    load_sem, send_sem, recv_sem,
):
    grp, blk = lax.axis_index("grp"), lax.axis_index("blk")
    my_x, my_y, my_z, core = grp // 4, grp % 4, blk // 2, blk % 2
    my_chip = grp * 4 + my_z
    picks = (pick_0, pick_1, pick_2)
    along_x = [((my_x + d) % 4) * 4 for d in range(4)]
    along_y = [(my_y + d) % 4 for d in range(4)]
    along_z = [((my_z + d) % 4) * 2 + core for d in range(4)]
    other_core = {"grp": grp, "blk": my_z * 2 + (1 - core)}

    def device_at(step, sign):
        dx, dy, dz = [(sign * d) % 4 for d in ORDER[step]]
        return {"grp": along_x[dx] + along_y[dy], "blk": along_z[dz]}

    def remote(source, target, number, device):
        return pltpu.make_async_remote_copy(
            src_ref=source,
            dst_ref=target,
            send_sem=send_sem.at[number],
            recv_sem=recv_sem.at[number],
            device_id=device,
            device_id_type=pl.DeviceIdType.MESH,
        )

    def await_blocks(ref, number, semaphore):
        block = ref.at[pl.ds(0, number)]
        pltpu.make_async_copy(block, block, semaphore).wait()

    HEAD_Z, HEAD_Y, HEAD_X, LINE, OVER, FACTS, SUMS, BACK, SWAP, PART = 0, 1, 2, 3, 4, 5, 6, 7, 8, 11
    messages = [min(begin + steps, SELF) - begin for begin, steps, _ in PARTS]

    loads = [
        pltpu.make_async_copy(source, target, load_sem.at[number])
        for number, (source, target) in enumerate(
            (
                (assign_hbm, assign_ref),
                (owner_hbm, owner_ref),
                (count_hbm, count_ref),
                (index_hbm, index_ref),
                (x_hbm, x_ref),
            )
        )
    ]
    for load in loads:
        load.start()
    barrier = pltpu.get_barrier_semaphore()
    for device in [device_at(step, 1) for step in range(SELF)] + [other_core]:
        pl.semaphore_signal(barrier, inc=1, device_id=device, device_id_type=pl.DeviceIdType.MESH)
    for load in loads[:-1]:
        load.wait()

    rank, count_column = rank_groups(count_ref)
    group, chip, slot, place_counts = place_documents(assign_ref, owner_ref, rank)
    step_of = step_to((chip >> 4) - my_x, ((chip >> 2) & 3) - my_y, (chip & 3) - my_z)
    in_base = slot < BASE
    send_slot = jnp.where(in_base, step_of * BASE + slot, -1)
    heads[my_chip] = place_counts + 1024.0 * rank
    loads[-1].wait()

    def pack(first, stop):
        slots = iota(((stop - first) * BASE, ROWS), 0) + first * BASE
        rows = dot(onehot(slots == send_slot), x_ref[...]).astype(BF16)
        send[pl.ds(first, stop - first)] = rows.reshape(stop - first, BASE, WIDTH)

    def post(first, stop):
        for step in range(first, min(stop, SELF)):
            number = max(part for part in range(len(PARTS)) if PARTS[part][0] <= step)
            remote(send.at[step], got.at[step], PART + number, device_at(step, 1)).start()

    def share_heads(first, number, semaphore, devices):
        block = heads.at[pl.ds(first, number)]
        for device in devices:
            remote(block, block, semaphore, device).start()

    pack(0, 24)
    pl.semaphore_wait(barrier, CHIPS)
    share_heads(my_chip, 1, HEAD_Z, [{"grp": grp, "blk": along_z[d]} for d in range(1, 4)])
    post(0, 8)
    place_counts_16 = place_counts + jnp.zeros((16, CLUSTERS), F32)
    own_excess = excess(dot(place_counts_16.astype(BF16), chip_places())[0:1])
    eye = iota((CHIPS, CLUSTERS), 0) == iota((CHIPS, CLUSTERS), 1)
    excess_column = across(pick(eye, own_excess))
    over_slot = down(pick(iota((CHIPS, ROWS), 0) < chip, excess_column)).astype(jnp.int32) + (slot - BASE)
    over_slot = jnp.where(in_base, -1, over_slot)
    own_over[...] = dot(onehot(iota((BASE, ROWS), 0) == over_slot), x_ref[...]).astype(BF16)
    line_over[my_z] = own_over[...]
    for d in range(1, DEPTH):
        remote(own_over, line_over.at[my_z], LINE, {"grp": grp, "blk": along_z[d]}).start()
    await_blocks(heads, 3, recv_sem.at[HEAD_Z])
    share_heads(grp * 4, 4, HEAD_Y, [{"grp": along_x[0] + along_y[d], "blk": blk} for d in range(1, 4)])
    post(8, 16)
    pack(24, 48)
    await_blocks(heads, 12, recv_sem.at[HEAD_Y])
    share_heads(my_x * 16, 16, HEAD_X, [{"grp": along_x[d] + along_y[0], "blk": blk} for d in range(1, 4)])
    post(16, 40)
    pack(48, CHIPS)
    got[SELF] = send[SELF]

    await_blocks(heads, 48, recv_sem.at[HEAD_X])
    table = heads[...].reshape(CHIPS, CLUSTERS)
    plans, ends, line_start, over_total, fault = receive_plan(table, rank, my_x, my_y, my_z)

    await_blocks(line_over, DEPTH - 1, recv_sem.at[LINE])
    sender = iota((CHIPS, 1), 0)
    at = sender == grp * 4 + (iota((CHIPS, DEPTH * BASE), 1) >> 4)
    begin = down(pick(at, line_start))
    number = down(pick(at, over_total))
    order = (iota((1, DEPTH * BASE), 1) & (BASE - 1)).astype(F32)
    order = jnp.where(order < number, begin + order, -1.0)
    my_start = down(pick(sender == my_chip, line_start))
    rows = iota((2 * POOL, DEPTH * BASE), 0).astype(F32)
    blocks = line_over[...].reshape(DEPTH * BASE, WIDTH)
    left = dot(onehot((rows == order) & (rows < POOL)), blocks[:, :HALF])
    right = dot(onehot((rows - POOL == order) & (rows >= POOL)), blocks[:, HALF:])
    send_over[...] = (left + right).astype(BF16)
    got_over[grp] = send_over[...]
    for step in range(1, LINES):
        low, middle = step % 4, step // 4
        device = {"grp": along_x[low] + along_y[(middle + low) % 4], "blk": blk}
        remote(send_over, got_over.at[grp], OVER, device).start()
    post(40, CHIPS)

    missing = missing_documents(index_ref, count_column, group)
    row = iota((8, 128), 0)
    told = pick(row == 6, rank) + pick(row == 7, jnp.where(iota((1, 128), 1) == 0, fault, missing))
    for part, (first_end, held_end) in enumerate(ends):
        told = told + pick(row == part, first_end) + pick(row == 3 + part, held_end)
        picks[part][...] = onehot(iota(picks[part].shape, 0).astype(F32) == plans[part])
    facts[0] = told
    swap_facts = remote(facts.at[0], facts.at[1], FACTS, other_core)
    swap_facts.start()

    best = [jnp.full((1, room), -1.0, F32) for _, _, room in PARTS]
    their_ends = []
    totals = [jnp.zeros((1, WIDTH), F32), jnp.zeros((1, WIDTH), F32)]
    swaps = []

    def window(part):
        return pl.ds(STARTS[part], PARTS[part][2])

    def compare(keys, key_part, query_part, key_ends, itself):
        scores = dot_rows(keys[window(key_part)], mine[window(query_part)])
        first, held = key_ends[key_part]
        key_number = iota((PARTS[key_part][2], 1), 0).astype(F32)
        query_number = iota((1, PARTS[query_part][2]), 1).astype(F32)
        kind = jnp.where(key_number < first, 0.0, jnp.where(key_number < held, 1.0, 2.0))
        matched = kind == jnp.where(query_number < ends[query_part][0], 0.0, 1.0)
        if itself and key_part == query_part:
            matched = matched & (key_number != query_number)
        scores = jnp.max(jnp.where(matched, scores, -1.0), axis=0, keepdims=True)
        best[query_part] = jnp.maximum(best[query_part], scores)

    for part, (begin, steps, room) in enumerate(PARTS):
        if part == LAST:
            await_blocks(got_over, LINES - 1, recv_sem.at[OVER])
            halves = got_over[...].reshape(LINES * 2 * POOL, HALF)
            shape = (LINES * POOL, LINES * 2 * POOL)
            to, at = iota(shape, 0), iota(shape, 1)
            same = ((to >> 3) == (at >> 4)) & ((to & 7) == (at & 7))
            left = dot(onehot(same & ((at & POOL) == 0)), halves)
            right = dot(onehot(same & ((at & POOL) != 0)), halves)
            whole = jnp.concatenate([left, right], axis=1).astype(BF16)
            got[pl.ds(CHIPS, TOTAL - CHIPS)] = whole.reshape(TOTAL - CHIPS, BASE, WIDTH)
        await_blocks(got, messages[part], recv_sem.at[PART + part])
        rows = dot(picks[part][...], got[pl.ds(begin, steps)].reshape(steps * BASE, WIDTH))
        unit = rows * lax.rsqrt(across(rows * rows) + EPSILON)
        mine[window(part)] = unit.astype(BF16)
        swap = remote(mine.at[window(part)], theirs.at[window(part)], SWAP + part, other_core)
        swap.start()
        swaps.append(swap)
        is_first = iota((room, 1), 0).astype(F32) < ends[part][0]
        totals[0] = totals[0] + down(pick(is_first, unit))
        totals[1] = totals[1] + down(jnp.where(is_first, 0.0, unit))
        if part == LAST:
            row = iota((8, WIDTH), 0)
            sums[...] = pick(row == 0, totals[0]) + pick(row == 1, totals[1])
            swap_sums = remote(sums, their_sums, SUMS, other_core)
            swap_sums.start()
        for other in range(part + 1):
            compare(mine, part, other, ends, True)
            if other != part:
                compare(mine, other, part, ends, True)
        if part == 0:
            swap_facts.wait()
            their_told = facts[1]
            for number in range(len(PARTS)):
                their_ends.append((their_told[number : number + 1, 0:1], their_told[3 + number : 4 + number, 0:1]))
        else:
            for other in range(part - 1):
                compare(theirs, other, part, their_ends, False)
            swaps[part - 1].wait()
            for other in range(part + 1):
                compare(theirs, part - 1, other, their_ends, False)

    swap_sums.wait()
    total = sums[...] + their_sums[...]
    centre = total * lax.rsqrt(across(total * total) + EPSILON)
    near = dot_rows(jnp.concatenate(thirds(centre), axis=0).astype(BF16), mine[...])
    near = near[0:8] + near[8:16] + near[16:24]
    swaps[LAST].wait()
    for other in range(len(PARTS)):
        compare(theirs, LAST, other, their_ends, False)

    poison = missing + their_told[7:8, 1:2] > 0.5
    tiles = CHIPS * BASE // 128
    for part, (begin, steps, room) in enumerate(PARTS):
        row = iota((8, room), 0)
        query_number = iota((1, room), 1).astype(F32)
        some = near[:, STARTS[part] : STARTS[part] + room]
        some = jnp.where(query_number < ends[part][0], some[0:1], some[1:2])
        values = jnp.zeros((8, room), F32)
        for number, term in enumerate(thirds(best[part]) + thirds(some)):
            values = jnp.where(row == number, term, values)
        out = dot(values.astype(BF16), picks[part][...])
        for kind in range(2):
            line = out[3 * kind : 3 * kind + 1] + out[3 * kind + 1 : 3 * kind + 2] + out[3 * kind + 2 : 3 * kind + 3]
            line = jnp.where(poison, NONE, line)
            for tile in range(steps * BASE // 128):
                piece = line[:, tile * 128 : (tile + 1) * 128]
                to = begin * BASE // 128 + tile
                if to < tiles:
                    back[to, kind : kind + 1, :] = piece
                else:
                    for each in range(tiles):
                        back[each, 2 + kind : 3 + kind, :] = piece
    returned[SELF] = back[SELF // 8]
    for step in range(SELF):
        remote(back.at[step // 8], returned.at[step], BACK, device_at(step, -1)).start()

    differ = across(jnp.where(their_told[6:7] != rank, 1.0, 0.0))
    fault = fault + their_told[7:8, 0:1] + differ
    chosen = onehot(iota((CHIPS, ROWS), 0) == step_of)
    sub = iota((128, ROWS), 0)
    at_base = (sub == (step_of & 7) * BASE + slot) & in_base
    at_over = (sub == grp * POOL + my_start.astype(jnp.int32) + over_slot) & (~in_base)

    await_blocks(returned, CHIPS - 1, recv_sem.at[BACK])
    found = []
    for number in range(4):
        line = returned[:, number, :]
        if number == 0:
            poisoned = across(down(jnp.where(line > 0.5 * NONE, 1.0, 0.0)))
            fault_ref[...] = jnp.where(fault + poisoned > 0.5, 1, 0) + jnp.zeros((1, 128), jnp.int32)
        terms = jnp.concatenate(thirds(line), axis=1).astype(BF16)
        out = lax.dot_general(terms, chosen, (((0,), (0,)), ((), ())), preferred_element_type=F32)
        found.append(out[0:128] + out[128:256] + out[256:384])
    max_ref[...] = down(pick(at_base, found[0]) + pick(at_over, found[2]))
    cos_ref[...] = down(pick(at_base, found[1]) + pick(at_over, found[3]))

    await_blocks(heads, 3, send_sem.at[HEAD_Z])
    await_blocks(heads, 12, send_sem.at[HEAD_Y])
    await_blocks(heads, 48, send_sem.at[HEAD_X])
    await_blocks(line_over, DEPTH - 1, send_sem.at[LINE])
    await_blocks(got_over, LINES - 1, send_sem.at[OVER])
    await_blocks(returned, CHIPS - 1, send_sem.at[BACK])
    for part in range(len(PARTS)):
        await_blocks(got, messages[part], send_sem.at[PART + part])


def routed(embeddings, assign, owner, send_count, send_index):
    return pl.pallas_call(
        kernel,
        out_shape=(
            jax.ShapeDtypeStruct((1, ROWS), F32),
            jax.ShapeDtypeStruct((1, ROWS), F32),
            jax.ShapeDtypeStruct((1, 128), jnp.int32),
        ),
        in_specs=[pl.BlockSpec(memory_space=pl.ANY)] * 5,
        out_specs=(pl.BlockSpec(memory_space=pltpu.VMEM),) * 3,
        scratch_shapes=[
            pltpu.VMEM((ROWS, WIDTH), BF16),
            pltpu.VMEM((1, ROWS), jnp.int32),
            pltpu.VMEM((1, CLUSTERS), jnp.int32),
            pltpu.VMEM((1, GROUPS), jnp.int32),
            pltpu.VMEM((GROUPS, CAP), jnp.int32),
            pltpu.VMEM((CHIPS, BASE, WIDTH), BF16),
            pltpu.VMEM((TOTAL, BASE, WIDTH), BF16),
            pltpu.VMEM((CHIPS, 1, 128), F32),
            pltpu.VMEM((BASE, WIDTH), BF16),
            pltpu.VMEM((DEPTH, BASE, WIDTH), BF16),
            pltpu.VMEM((2 * POOL, HALF), BF16),
            pltpu.VMEM((LINES, 2 * POOL, HALF), BF16),
            *[pltpu.VMEM((room, steps * BASE), BF16) for _, steps, room in PARTS],
            pltpu.VMEM((HELD, WIDTH), BF16),
            pltpu.VMEM((HELD, WIDTH), BF16),
            pltpu.VMEM((2, 8, 128), F32),
            pltpu.VMEM((8, WIDTH), F32),
            pltpu.VMEM((8, WIDTH), F32),
            pltpu.VMEM((CHIPS * BASE // 128, 4, 128), F32),
            pltpu.VMEM((CHIPS, 4, 128), F32),
            pltpu.SemaphoreType.DMA((5,)),
            pltpu.SemaphoreType.DMA((14,)),
            pltpu.SemaphoreType.DMA((14,)),
        ],
        compiler_params=pltpu.CompilerParams(
            collective_id=0, has_side_effects=True, vmem_limit_bytes=48 * 1024 * 1024
        ),
    )(
        embeddings,
        assign.reshape(1, ROWS),
        owner.reshape(1, CLUSTERS),
        send_count,
        send_index[0],
    )


def body(embeddings, assign, owner, send_count, send_index):
    arguments = (embeddings, assign, owner, send_count, send_index)
    max_sim, centroid_cos, fault = routed(*arguments)
    return lax.cond(
        fault[0, 0] != 0,
        lambda: general(*arguments),
        lambda: (max_sim.reshape(ROWS), centroid_cos.reshape(ROWS)),
    )


def solution(mesh):
    placed = (
        P(("grp", "blk"), None),
        P(("grp", "blk")),
        P(),
        P(("grp", "blk"), None),
        P(("grp", "blk"), None, None),
    )
    return jax.shard_map(
        body,
        mesh=mesh,
        in_specs=placed,
        out_specs=(P(("grp", "blk")), P(("grp", "blk"))),
        check_vma=False,
    )
```

```python
import functools

import jax
import jax.numpy as jnp
from jax import lax
from jax.experimental import pallas as pl
from jax.experimental.pallas import tpu as pltpu
from jax.sharding import PartitionSpec as P

EPSILON = 1e-06
F32 = jnp.float32
BF16 = jnp.bfloat16

CHIPS = 64
ROWS = 512
WIDTH = 768
CLUSTERS = 128
GROUPS = 16
CAP = 64
BASE = 16
HALF = WIDTH // 2
LINES = 16
DEPTH = 4
POOL = 8
PARTS = ((0, 24, 256), (24, 32, 384), (56, 16, 128))
TOTAL = 72
HELD = 768
STARTS = (0, 256, 640)
LAST = len(PARTS) - 1
NONE = 1e30


def normalize(values):
    widened = values.astype(F32)
    return widened * lax.rsqrt(jnp.sum(widened * widened, axis=1, keepdims=True) + EPSILON)


def general(embeddings, assign, owner, send_count, send_index):
    rows_local = embeddings.shape[0]
    feature_width = embeddings.shape[1]
    groups = lax.axis_size("grp")
    clusters = owner.shape[0]
    capacity = send_index.shape[2]
    slot_total = groups * capacity
    unit_rows = normalize(embeddings)
    unit_low = unit_rows.astype(BF16)
    counts = send_count[0]
    listed = send_index[0]
    live_slot = jnp.arange(capacity, dtype=jnp.int32)[None, :] < counts[:, None]
    listed_cluster = assign[listed]
    owned_here = owner[listed_cluster] == jnp.arange(groups, dtype=jnp.int32)[:, None]
    kept_slot = live_slot & owned_here
    out_cluster = jnp.where(kept_slot, listed_cluster, -1)
    out_tag = jnp.where(kept_slot, lax.axis_index(("grp", "blk")) * rows_local + listed, -1)
    out_vector = unit_low[listed.reshape(-1)].reshape(groups, capacity, feature_width)
    got_vector, got_cluster, got_tag = (
        lax.all_to_all(out_vector, "grp", split_axis=0, concat_axis=0, tiled=True),
        lax.all_to_all(out_cluster, "grp", split_axis=0, concat_axis=0, tiled=True),
        lax.all_to_all(out_tag, "grp", split_axis=0, concat_axis=0, tiled=True),
    )
    own_vector = got_vector.reshape(slot_total, feature_width)
    own_cluster = got_cluster.reshape(slot_total)
    own_tag = got_tag.reshape(slot_total)

    def tile_best(current, shard_piece):
        other_vector, other_cluster, other_tag = shard_piece
        scores = jnp.einsum("id,jd->ij", own_vector, other_vector, preferred_element_type=F32)
        matched = (
            (own_cluster[:, None] == other_cluster[None, :])
            & (other_cluster[None, :] >= 0)
            & (own_tag[:, None] != other_tag[None, :])
        )
        return jnp.maximum(current, jnp.max(jnp.where(matched, scores, -1.0), axis=1))

    other_vector = lax.all_gather(own_vector, "blk", axis=0, tiled=True)
    other_cluster = lax.all_gather(own_cluster, "blk", axis=0, tiled=True)
    other_tag = lax.all_gather(own_tag, "blk", axis=0, tiled=True)
    length = other_vector.shape[0]
    number = length // slot_total
    stacked = (
        other_vector.reshape(number, slot_total, feature_width),
        other_cluster.reshape(number, slot_total),
        other_tag.reshape(number, slot_total),
    )

    def scan_step(carry, single):
        return (tile_best(carry, single), None)

    result, unused = lax.scan(scan_step, jnp.full((slot_total,), -1.0, F32), stacked)
    target = jnp.where(live_slot, listed, rows_local).reshape(-1)
    partial_sum = jax.ops.segment_sum(unit_rows, assign, num_segments=clusters)
    centre = normalize(lax.psum(partial_sum, ("grp", "blk")))
    nearness = jnp.sum(unit_low.astype(F32) * centre[assign], axis=1)
    returned = lax.all_to_all(
        result.reshape(groups, capacity), "grp", split_axis=0, concat_axis=0, tiled=True
    )
    has_entry = (
        jnp.zeros((rows_local,), jnp.int32)
        .at[target]
        .max(kept_slot.astype(jnp.int32).reshape(-1), mode="drop")
    )
    centroid_cos = jnp.where(has_entry > 0, nearness, 0.0)
    max_sim = jnp.full((rows_local,), -1.0, F32).at[target].max(returned.reshape(-1), mode="drop")
    return (max_sim, centroid_cos)


def iota(shape, axis):
    return lax.broadcasted_iota(jnp.int32, shape, axis)


def down(values):
    return jnp.sum(values, axis=0, keepdims=True)


def across(values):
    return jnp.sum(values, axis=1, keepdims=True)


def pick(mask, values):
    return jnp.where(mask, values, 0.0)


def as_column(row):
    size = row.shape[1]
    return across(pick(iota((size, size), 0) == iota((size, size), 1), row))


def as_row(column):
    size = column.shape[0]
    return down(pick(iota((size, size), 0) == iota((size, size), 1), column))


def dot(a, b):
    return jnp.dot(a, b, preferred_element_type=F32)


def dot_rows(a, b):
    return lax.dot_general(a, b, (((1,), (1,)), ((), ())), preferred_element_type=F32)


def onehot(mask):
    return jnp.where(mask, 1.0, 0.0).astype(BF16)


def thirds(values):
    first = values.astype(BF16).astype(F32)
    rest = values - first
    second = rest.astype(BF16).astype(F32)
    third = (rest - second).astype(BF16).astype(F32)
    return first, second, third


def rank_groups(count_ref):
    count_row = count_ref[...].astype(F32)
    count_column = as_column(count_row)
    sub, lane = iota((GROUPS, 128), 0), iota((GROUPS, 128), 1)
    count_lanes = down(pick(sub == lane, count_column))
    ahead = (count_column > count_lanes) | ((count_column == count_lanes) & (sub < lane))
    rank = down(jnp.where(ahead, 1.0, 0.0))
    return jnp.where(iota((1, 128), 1) < GROUPS, rank, 0.0), count_column


def place_documents(assign_ref, owner_ref, rank):
    owner_row = owner_ref[...].astype(F32)
    owner_column = as_column(owner_row)
    sub, lane = iota((CLUSTERS, CLUSTERS), 0), iota((CLUSTERS, CLUSTERS), 1)
    within = across(jnp.where((owner_column == owner_row) & (lane < sub), 1.0, 0.0))
    group_rank = across(pick(owner_column == lane.astype(F32), rank))
    place_column = group_rank * (CLUSTERS // GROUPS) + within
    member = iota((CLUSTERS, ROWS), 0) == assign_ref[...]
    place = down(pick(member, place_column))
    group = down(pick(member, owner_column))
    order = iota((CLUSTERS, ROWS), 0).astype(F32)
    at_place = order == place
    earlier = onehot(iota((ROWS, ROWS), 0) < iota((ROWS, ROWS), 1))
    before = dot(onehot(at_place), earlier)
    slot = down(pick(at_place, before))
    count_column = across(jnp.where(at_place, 1.0, 0.0))
    partner_count = down(pick(order == (CLUSTERS - 1) - place, count_column))
    slot = slot + jnp.where(place >= CHIPS, partner_count, 0.0)
    chip = jnp.minimum(place, (CLUSTERS - 1) - place)
    return group, chip.astype(jnp.int32), slot.astype(jnp.int32), as_row(count_column)


def missing_documents(index_ref, count_column, group):
    listed = index_ref[...]
    live = iota((GROUPS, CAP), 1).astype(F32) < count_column
    eye = onehot(iota((CAP, CAP), 0) == iota((CAP, CAP), 1))
    high = dot_rows(eye, jnp.where(live, listed >> 4, 0).astype(F32).astype(BF16))
    low = dot_rows(eye, jnp.where(live, listed & 15, 0).astype(F32).astype(BF16))
    alive = dot_rows(eye, onehot(live))
    slots = jnp.where(alive > 0.5, high * 16.0 + low, -1.0)
    document = iota((1, ROWS), 1).astype(F32)
    lane = iota((CAP, GROUPS), 1)

    def count(g, hits):
        column = across(pick(lane == g, slots))
        wanted = jnp.where(group == g.astype(F32), document, -2.0)
        return hits + jnp.where(column == wanted, 1.0, 0.0)

    hits = lax.fori_loop(0, GROUPS, count, jnp.zeros((CAP, ROWS), F32))
    return across(jnp.where(down(hits) > 0.5, 0.0, 1.0))


def send_order():
    order = []
    for step in range(CHIPS):
        high, middle, low = step // 16, (step // 4) % 4, step % 4
        order.append((low, (middle + low) % 4, (high + middle + low) % 4))
    near = [shift for shift in order if sum(min(d, 4 - d) for d in shift) <= 1] + [(2, 0, 0)]
    near.sort(key=lambda shift: -sum(min(d, 4 - d) for d in shift))
    return [shift for shift in order if shift not in near] + near


ORDER = send_order()
SELF = CHIPS - 1


def step_to(dx, dy, dz):
    shift = (dx & 3) * 16 + (dy & 3) * 4 + (dz & 3)
    step = jnp.full(shift.shape, SELF, jnp.int32)
    for number, (x, y, z) in enumerate(ORDER[:SELF]):
        step = jnp.where(shift == x * 16 + y * 4 + z, number, step)
    return step


def in_part(step, part):
    begin, steps, _ = PARTS[part]
    return (step >= begin) & (step < begin + steps)


def chip_places():
    sub, lane = iota((CLUSTERS, CLUSTERS), 0), iota((CLUSTERS, CLUSTERS), 1)
    return onehot((sub == lane) | (sub == (CLUSTERS - 1) - lane))


def excess(totals):
    lane = iota(totals.shape, 1)
    return jnp.where(lane < CHIPS, jnp.maximum(totals - BASE, 0.0), 0.0)


def receive_plan(table, rank, my_x, my_y, my_z):
    chip = my_x * 16 + my_y * 4 + my_z
    heads = table.astype(jnp.int32)
    counts = (heads & 1023).astype(F32)
    differ = jnp.where((heads >> 10).astype(F32) != rank, 1.0, 0.0)
    fault = across(down(differ))
    both = dot(counts.astype(BF16), chip_places())
    over = excess(both)
    lanes = iota((CHIPS, CLUSTERS), 1)
    sender = iota((CHIPS, 1), 0)
    source, target = iota((CHIPS, CHIPS), 0), iota((CHIPS, CHIPS), 1)

    same_line = (source >> 2) == (target >> 2)
    over_total = across(over)
    over_row = as_row(over_total)
    line_start = across(pick(same_line & (target < source), over_row))
    line_total = across(pick(same_line, over_row))
    fault = fault + down(jnp.where(line_total > POOL, 1.0, 0.0))
    start = line_start + across(pick(lanes < chip, over))
    number = across(pick(lanes == chip, over))

    to_chip = iota((1, CLUSTERS), 1)
    route = step_to(
        (to_chip >> 4) - (sender >> 4), ((to_chip >> 2) & 3) - ((sender >> 2) & 3), (to_chip & 3) - (sender & 3)
    )
    based = jnp.where(lanes < CHIPS, jnp.minimum(both, float(BASE)), 0.0)
    for part, (_, _, room) in enumerate(PARTS):
        held = down(pick(in_part(route, part), based))
        if part == LAST:
            held = held + down(over)
        fault = fault + across(jnp.where(held > room, 1.0, 0.0))

    first = across(pick(lanes == chip, counts))
    second = across(pick(lanes == (CLUSTERS - 1) - chip, counts))
    place = (lanes & (POOL - 1)).astype(F32) - start
    mine = ((sender >> 2) == (lanes >> 3)) & (place >= 0.0) & (place < number)
    over_first = down(jnp.where(mine & (place + BASE < first), 1.0, 0.0))
    over_second = down(jnp.where(mine & (place + BASE >= first), 1.0, 0.0))
    over_first_total, over_second_total = across(over_first), across(over_second)
    earlier = onehot(iota((CLUSTERS, CLUSTERS), 0) < iota((CLUSTERS, CLUSTERS), 1))
    sub = iota((16, CLUSTERS), 0)
    before = dot((pick(sub == 0, over_first) + pick(sub == 1, over_second)).astype(BF16), earlier)

    base_first = jnp.minimum(first, float(BASE))
    base_second = jnp.minimum(first + second, float(BASE)) - base_first
    first_row, second_row = as_row(base_first), as_row(base_second)

    def my_step(other):
        return step_to(my_x - (other >> 4), my_y - ((other >> 2) & 3), my_z - (other & 3))

    step_column, step_row = my_step(sender), my_step(iota((1, CHIPS), 1))
    plans = []
    ends = []
    all_first_start = jnp.zeros((CHIPS, 1), F32)
    all_second_start = jnp.zeros((CHIPS, 1), F32)
    for part, (begin, steps, _) in enumerate(PARTS):
        inside = in_part(step_column, part)
        ahead = (target < source) & in_part(step_row, part)
        first_total = down(pick(inside, base_first))
        second_total = down(pick(inside, base_second))
        last = part == LAST
        first_end = first_total + over_first_total if last else first_total
        first_start = across(pick(ahead, first_row))
        second_start = across(pick(ahead, second_row)) + first_end
        all_first_start = all_first_start + pick(inside, first_start + STARTS[part])
        all_second_start = all_second_start + pick(inside, second_start + STARTS[part])
        spread = step_column - begin == (iota((CHIPS, steps * BASE), 1) >> 4)
        head, tail, head_start, tail_start = [
            down(pick(spread, column)) for column in (base_first, base_second, first_start, second_start)
        ]
        slot = (iota((1, steps * BASE), 1) & (BASE - 1)).astype(F32)
        later = jnp.where(slot < head + tail, tail_start + (slot - head), -1.0)
        plan = jnp.where(slot < head, head_start + slot, later)
        held_end = first_end + second_total
        if last:
            over_row_of = jnp.where(over_second > 0.5, held_end + before[1:2], -1.0)
            over_row_of = jnp.where(over_first > 0.5, first_total + before[0:1], over_row_of)
            plan = jnp.concatenate([plan[:, : steps * BASE - CLUSTERS], over_row_of], axis=1)
            held_end = held_end + over_second_total
        plans.append(plan)
        ends.append((first_end, held_end))

    dx, dy, dz = (my_x - (sender >> 4)) & 3, (my_y - ((sender >> 2) & 3)) & 3, (my_z - (sender & 3)) & 3
    spread = dz * 16 + dx * 4 + dy == (iota((CHIPS, CHIPS * BASE), 1) >> 4)
    head, tail, head_start, tail_start = [
        down(pick(spread, column)) for column in (base_first, base_second, all_first_start, all_second_start)
    ]
    slot = (iota((1, CHIPS * BASE), 1) & (BASE - 1)).astype(F32)
    later = jnp.where(slot < head + tail, tail_start + (slot - head), -1.0)
    plan_back = jnp.where(slot < head, head_start + slot, later)
    over_back = jnp.where(over_row_of < 0.0, -1.0, over_row_of + STARTS[LAST])
    plan_back = jnp.concatenate([plan_back, over_back], axis=1)
    return plans, plan_back, ends, line_start, over_total, fault


def kernel(
    x_hbm, assign_hbm, owner_hbm, count_hbm, index_hbm,
    max_ref, cos_ref, fault_ref,
    x_ref, assign_ref, owner_ref, count_ref, index_ref,
    send, got, heads, own_over, line_over, send_over, got_over, pick_0, pick_1, pick_2,
    pick_back, mine, theirs, facts, sums, their_sums, back, relay, returned,
    load_sem, send_sem, recv_sem,
):
    grp, blk = lax.axis_index("grp"), lax.axis_index("blk")
    my_x, my_y, my_z, core = grp // 4, grp % 4, blk // 2, blk % 2
    my_chip = grp * 4 + my_z
    picks = (pick_0, pick_1, pick_2)
    along_x = [((my_x + d) % 4) * 4 for d in range(4)]
    along_y = [(my_y + d) % 4 for d in range(4)]
    along_z = [((my_z + d) % 4) * 2 + core for d in range(4)]
    other_core = {"grp": grp, "blk": my_z * 2 + (1 - core)}

    def device_at(step, sign):
        dx, dy, dz = [(sign * d) % 4 for d in ORDER[step]]
        return {"grp": along_x[dx] + along_y[dy], "blk": along_z[dz]}

    def remote(source, target, number, device):
        return pltpu.make_async_remote_copy(
            src_ref=source,
            dst_ref=target,
            send_sem=send_sem.at[number],
            recv_sem=recv_sem.at[number],
            device_id=device,
            device_id_type=pl.DeviceIdType.MESH,
        )

    def await_blocks(ref, number, semaphore):
        block = ref.at[pl.ds(0, number)]
        pltpu.make_async_copy(block, block, semaphore).wait()

    HEAD_Z, HEAD_Y, HEAD_X, LINE, OVER, FACTS, SUMS, BACK_Z, SWAP, PART, BACK = 0, 1, 2, 3, 4, 5, 6, 7, 8, 11, 14
    messages = [min(begin + steps, SELF) - begin for begin, steps, _ in PARTS]

    loads = [
        pltpu.make_async_copy(source, target, load_sem.at[number])
        for number, (source, target) in enumerate(
            (
                (assign_hbm, assign_ref),
                (owner_hbm, owner_ref),
                (count_hbm, count_ref),
                (index_hbm, index_ref),
                (x_hbm, x_ref),
            )
        )
    ]
    for load in loads:
        load.start()
    barrier = pltpu.get_barrier_semaphore()
    for device in [device_at(step, 1) for step in range(SELF)] + [other_core]:
        pl.semaphore_signal(barrier, inc=1, device_id=device, device_id_type=pl.DeviceIdType.MESH)
    for load in loads[:-1]:
        load.wait()

    rank, count_column = rank_groups(count_ref)
    group, chip, slot, place_counts = place_documents(assign_ref, owner_ref, rank)
    step_of = step_to((chip >> 4) - my_x, ((chip >> 2) & 3) - my_y, (chip & 3) - my_z)
    in_base = slot < BASE
    send_slot = jnp.where(in_base, step_of * BASE + slot, -1)
    heads[my_chip] = place_counts + 1024.0 * rank
    loads[-1].wait()

    def pack(first, stop):
        slots = iota(((stop - first) * BASE, ROWS), 0) + first * BASE
        rows = dot(onehot(slots == send_slot), x_ref[...]).astype(BF16)
        send[pl.ds(first, stop - first)] = rows.reshape(stop - first, BASE, WIDTH)

    def post(first, stop):
        for step in range(first, min(stop, SELF)):
            number = max(part for part in range(len(PARTS)) if PARTS[part][0] <= step)
            remote(send.at[step], got.at[step], PART + number, device_at(step, 1)).start()

    def share_heads(first, number, semaphore, devices):
        block = heads.at[pl.ds(first, number)]
        for device in devices:
            remote(block, block, semaphore, device).start()

    pack(0, 24)
    pl.semaphore_wait(barrier, CHIPS)
    share_heads(my_chip, 1, HEAD_Z, [{"grp": grp, "blk": along_z[d]} for d in range(1, 4)])
    post(0, 8)
    place_counts_16 = place_counts + jnp.zeros((16, CLUSTERS), F32)
    own_excess = excess(dot(place_counts_16.astype(BF16), chip_places())[0:1])
    eye = iota((CHIPS, CLUSTERS), 0) == iota((CHIPS, CLUSTERS), 1)
    excess_column = across(pick(eye, own_excess))
    over_slot = down(pick(iota((CHIPS, ROWS), 0) < chip, excess_column)).astype(jnp.int32) + (slot - BASE)
    over_slot = jnp.where(in_base, -1, over_slot)
    own_over[...] = dot(onehot(iota((BASE, ROWS), 0) == over_slot), x_ref[...]).astype(BF16)
    line_over[my_z] = own_over[...]
    for d in range(1, DEPTH):
        remote(own_over, line_over.at[my_z], LINE, {"grp": grp, "blk": along_z[d]}).start()
    await_blocks(heads, 3, recv_sem.at[HEAD_Z])
    share_heads(grp * 4, 4, HEAD_Y, [{"grp": along_x[0] + along_y[d], "blk": blk} for d in range(1, 4)])
    post(8, 16)
    pack(24, 48)
    await_blocks(heads, 12, recv_sem.at[HEAD_Y])
    share_heads(my_x * 16, 16, HEAD_X, [{"grp": along_x[d] + along_y[0], "blk": blk} for d in range(1, 4)])
    post(16, 40)
    pack(48, CHIPS)
    got[SELF] = send[SELF]

    await_blocks(heads, 48, recv_sem.at[HEAD_X])
    table = heads[...].reshape(CHIPS, CLUSTERS)
    plans, plan_back, ends, line_start, over_total, fault = receive_plan(table, rank, my_x, my_y, my_z)

    await_blocks(line_over, DEPTH - 1, recv_sem.at[LINE])
    sender = iota((CHIPS, 1), 0)
    at = sender == grp * 4 + (iota((CHIPS, DEPTH * BASE), 1) >> 4)
    begin = down(pick(at, line_start))
    number = down(pick(at, over_total))
    order = (iota((1, DEPTH * BASE), 1) & (BASE - 1)).astype(F32)
    order = jnp.where(order < number, begin + order, -1.0)
    my_start = down(pick(sender == my_chip, line_start))
    rows = iota((2 * POOL, DEPTH * BASE), 0).astype(F32)
    blocks = line_over[...].reshape(DEPTH * BASE, WIDTH)
    left = dot(onehot((rows == order) & (rows < POOL)), blocks[:, :HALF])
    right = dot(onehot((rows - POOL == order) & (rows >= POOL)), blocks[:, HALF:])
    send_over[...] = (left + right).astype(BF16)
    got_over[grp] = send_over[...]
    for step in range(1, LINES):
        low, middle = step % 4, step // 4
        device = {"grp": along_x[low] + along_y[(middle + low) % 4], "blk": blk}
        remote(send_over, got_over.at[grp], OVER, device).start()
    post(40, CHIPS)

    missing = missing_documents(index_ref, count_column, group)
    row = iota((8, 128), 0)
    told = pick(row == 6, rank) + pick(row == 7, jnp.where(iota((1, 128), 1) == 0, fault, missing))
    for part, (first_end, held_end) in enumerate(ends):
        told = told + pick(row == part, first_end) + pick(row == 3 + part, held_end)
        picks[part][...] = onehot(iota(picks[part].shape, 0).astype(F32) == plans[part])
    pick_back[...] = onehot(iota(pick_back.shape, 0).astype(F32) == plan_back)
    facts[0] = told
    swap_facts = remote(facts.at[0], facts.at[1], FACTS, other_core)
    swap_facts.start()

    best = [jnp.full((1, room), -1.0, F32) for _, _, room in PARTS]
    their_ends = []
    totals = [jnp.zeros((1, WIDTH), F32), jnp.zeros((1, WIDTH), F32)]
    swaps = []

    def window(part):
        return pl.ds(STARTS[part], PARTS[part][2])

    def compare(keys, key_part, query_part, key_ends, itself):
        scores = dot_rows(keys[window(key_part)], mine[window(query_part)])
        first, held = key_ends[key_part]
        key_number = iota((PARTS[key_part][2], 1), 0).astype(F32)
        query_number = iota((1, PARTS[query_part][2]), 1).astype(F32)
        kind = jnp.where(key_number < first, 0.0, jnp.where(key_number < held, 1.0, 2.0))
        matched = kind == jnp.where(query_number < ends[query_part][0], 0.0, 1.0)
        if itself and key_part == query_part:
            matched = matched & (key_number != query_number)
        scores = jnp.max(jnp.where(matched, scores, -1.0), axis=0, keepdims=True)
        best[query_part] = jnp.maximum(best[query_part], scores)

    for part, (begin, steps, room) in enumerate(PARTS):
        if part == LAST:
            await_blocks(got_over, LINES - 1, recv_sem.at[OVER])
            halves = got_over[...].reshape(LINES * 2 * POOL, HALF)
            shape = (LINES * POOL, LINES * 2 * POOL)
            to, at = iota(shape, 0), iota(shape, 1)
            same = ((to >> 3) == (at >> 4)) & ((to & 7) == (at & 7))
            left = dot(onehot(same & ((at & POOL) == 0)), halves)
            right = dot(onehot(same & ((at & POOL) != 0)), halves)
            whole = jnp.concatenate([left, right], axis=1).astype(BF16)
            got[pl.ds(CHIPS, TOTAL - CHIPS)] = whole.reshape(TOTAL - CHIPS, BASE, WIDTH)
        await_blocks(got, messages[part], recv_sem.at[PART + part])
        rows = dot(picks[part][...], got[pl.ds(begin, steps)].reshape(steps * BASE, WIDTH))
        unit = rows * lax.rsqrt(across(rows * rows) + EPSILON)
        mine[window(part)] = unit.astype(BF16)
        swap = remote(mine.at[window(part)], theirs.at[window(part)], SWAP + part, other_core)
        swap.start()
        swaps.append(swap)
        is_first = iota((room, 1), 0).astype(F32) < ends[part][0]
        totals[0] = totals[0] + down(pick(is_first, unit))
        totals[1] = totals[1] + down(jnp.where(is_first, 0.0, unit))
        if part == LAST:
            row = iota((8, WIDTH), 0)
            sums[...] = pick(row == 0, totals[0]) + pick(row == 1, totals[1])
            swap_sums = remote(sums, their_sums, SUMS, other_core)
            swap_sums.start()
        for other in range(part + 1):
            compare(mine, part, other, ends, True)
            if other != part:
                compare(mine, other, part, ends, True)
        if part == 0:
            swap_facts.wait()
            their_told = facts[1]
            for number in range(len(PARTS)):
                their_ends.append((their_told[number : number + 1, 0:1], their_told[3 + number : 4 + number, 0:1]))
        else:
            for other in range(part - 1):
                compare(theirs, other, part, their_ends, False)
            swaps[part - 1].wait()
            for other in range(part + 1):
                compare(theirs, part - 1, other, their_ends, False)

    swap_sums.wait()
    total = sums[...] + their_sums[...]
    centre = total * lax.rsqrt(across(total * total) + EPSILON)
    near = dot_rows(jnp.concatenate(thirds(centre), axis=0).astype(BF16), mine[...])
    near = near[0:8] + near[8:16] + near[16:24]
    swaps[LAST].wait()
    for other in range(len(PARTS)):
        compare(theirs, LAST, other, their_ends, False)

    poison = missing + their_told[7:8, 1:2] > 0.5
    near_mine = []
    for part, (_, _, room) in enumerate(PARTS):
        some = near[:, STARTS[part] : STARTS[part] + room]
        near_mine.append(jnp.where(iota((1, room), 1).astype(F32) < ends[part][0], some[0:1], some[1:2]))
    row = iota((8, HELD), 0)
    values = jnp.zeros((8, HELD), F32)
    for number, term in enumerate(thirds(jnp.concatenate(best, axis=1)) + thirds(jnp.concatenate(near_mine, axis=1))):
        values = jnp.where(row == number, term, values)
    out = dot(values.astype(BF16), pick_back[...])
    for kind in range(2):
        line = out[3 * kind : 3 * kind + 1] + out[3 * kind + 1 : 3 * kind + 2] + out[3 * kind + 2 : 3 * kind + 3]
        line = jnp.where(poison, NONE, line)
        for half in range(2):
            for d in range(DEPTH):
                tile = 2 * d + half
                back[half * DEPTH + d, kind : kind + 1, :] = line[:, tile * 128 : (tile + 1) * 128]
                back[half * DEPTH + d, 2 + kind : 3 + kind, :] = line[:, CHIPS * BASE :]
    for half in range(2):
        for d in range(1, DEPTH):
            block = half * DEPTH + d
            device = {"grp": grp, "blk": along_z[DEPTH - d]}
            remote(back.at[block], relay.at[block], BACK_Z, device).start()
        relay[half * DEPTH] = back[half * DEPTH]
    await_blocks(relay, 2 * (DEPTH - 1), recv_sem.at[BACK_Z])
    for other in range(1, LINES):
        low, high = other // 4, other % 4
        device = {"grp": along_x[(4 - low) % 4] + along_y[(4 - high) % 4], "blk": blk}
        block = relay.at[pl.ds(other // 8 * DEPTH, DEPTH)]
        remote(block, returned.at[other], BACK, device).start()
    returned[0] = relay[pl.ds(0, DEPTH)]

    differ = across(jnp.where(their_told[6:7] != rank, 1.0, 0.0))
    fault = fault + their_told[7:8, 0:1] + differ
    across_lines = (((chip >> 4) - my_x) & 3) * 4 + ((((chip >> 2) & 3) - my_y) & 3)
    chosen = onehot(iota((CHIPS, ROWS), 0) == across_lines * DEPTH + (((chip & 3) - my_z) & 3))
    sub = iota((128, ROWS), 0)
    at_base = (sub == (across_lines & 7) * BASE + slot) & in_base
    at_over = (sub == grp * POOL + my_start.astype(jnp.int32) + over_slot) & (~in_base)

    await_blocks(returned, LINES - 1, recv_sem.at[BACK])
    found = []
    for number in range(4):
        line = returned[:, :, number, :].reshape(CHIPS, 128)
        if number == 0:
            poisoned = across(down(jnp.where(line > 0.5 * NONE, 1.0, 0.0)))
            fault_ref[...] = jnp.where(fault + poisoned > 0.5, 1, 0) + jnp.zeros((1, 128), jnp.int32)
        terms = jnp.concatenate(thirds(line), axis=1).astype(BF16)
        out = lax.dot_general(terms, chosen, (((0,), (0,)), ((), ())), preferred_element_type=F32)
        found.append(out[0:128] + out[128:256] + out[256:384])
    max_ref[...] = down(pick(at_base, found[0]) + pick(at_over, found[2]))
    cos_ref[...] = down(pick(at_base, found[1]) + pick(at_over, found[3]))

    await_blocks(heads, 3, send_sem.at[HEAD_Z])
    await_blocks(heads, 12, send_sem.at[HEAD_Y])
    await_blocks(heads, 48, send_sem.at[HEAD_X])
    await_blocks(line_over, DEPTH - 1, send_sem.at[LINE])
    await_blocks(got_over, LINES - 1, send_sem.at[OVER])
    await_blocks(relay, 2 * (DEPTH - 1), send_sem.at[BACK_Z])
    await_blocks(returned, LINES - 1, send_sem.at[BACK])
    for part in range(len(PARTS)):
        await_blocks(got, messages[part], send_sem.at[PART + part])


def routed(embeddings, assign, owner, send_count, send_index):
    return pl.pallas_call(
        kernel,
        out_shape=(
            jax.ShapeDtypeStruct((1, ROWS), F32),
            jax.ShapeDtypeStruct((1, ROWS), F32),
            jax.ShapeDtypeStruct((1, 128), jnp.int32),
        ),
        in_specs=[pl.BlockSpec(memory_space=pl.ANY)] * 5,
        out_specs=(pl.BlockSpec(memory_space=pltpu.VMEM),) * 3,
        scratch_shapes=[
            pltpu.VMEM((ROWS, WIDTH), BF16),
            pltpu.VMEM((1, ROWS), jnp.int32),
            pltpu.VMEM((1, CLUSTERS), jnp.int32),
            pltpu.VMEM((1, GROUPS), jnp.int32),
            pltpu.VMEM((GROUPS, CAP), jnp.int32),
            pltpu.VMEM((CHIPS, BASE, WIDTH), BF16),
            pltpu.VMEM((TOTAL, BASE, WIDTH), BF16),
            pltpu.VMEM((CHIPS, 1, 128), F32),
            pltpu.VMEM((BASE, WIDTH), BF16),
            pltpu.VMEM((DEPTH, BASE, WIDTH), BF16),
            pltpu.VMEM((2 * POOL, HALF), BF16),
            pltpu.VMEM((LINES, 2 * POOL, HALF), BF16),
            *[pltpu.VMEM((room, steps * BASE), BF16) for _, steps, room in PARTS],
            pltpu.VMEM((HELD, (CHIPS + 8) * BASE), BF16),
            pltpu.VMEM((HELD, WIDTH), BF16),
            pltpu.VMEM((HELD, WIDTH), BF16),
            pltpu.VMEM((2, 8, 128), F32),
            pltpu.VMEM((8, WIDTH), F32),
            pltpu.VMEM((8, WIDTH), F32),
            pltpu.VMEM((2 * DEPTH, 4, 128), F32),
            pltpu.VMEM((2 * DEPTH, 4, 128), F32),
            pltpu.VMEM((LINES, DEPTH, 4, 128), F32),
            pltpu.SemaphoreType.DMA((5,)),
            pltpu.SemaphoreType.DMA((15,)),
            pltpu.SemaphoreType.DMA((15,)),
        ],
        compiler_params=pltpu.CompilerParams(
            collective_id=0, has_side_effects=True, vmem_limit_bytes=48 * 1024 * 1024
        ),
    )(
        embeddings,
        assign.reshape(1, ROWS),
        owner.reshape(1, CLUSTERS),
        send_count,
        send_index[0],
    )


def body(embeddings, assign, owner, send_count, send_index):
    arguments = (embeddings, assign, owner, send_count, send_index)
    max_sim, centroid_cos, fault = routed(*arguments)
    return lax.cond(
        fault[0, 0] != 0,
        lambda: general(*arguments),
        lambda: (max_sim.reshape(ROWS), centroid_cos.reshape(ROWS)),
    )


def solution(mesh):
    placed = (
        P(("grp", "blk"), None),
        P(("grp", "blk")),
        P(),
        P(("grp", "blk"), None),
        P(("grp", "blk"), None, None),
    )
    return jax.shard_map(
        body,
        mesh=mesh,
        in_specs=placed,
        out_specs=(P(("grp", "blk")), P(("grp", "blk"))),
        check_vma=False,
    )
```

```python
import functools

import jax
import jax.numpy as jnp
from jax import lax
from jax.experimental import pallas as pl
from jax.experimental.pallas import tpu as pltpu
from jax.sharding import PartitionSpec as P

EPSILON = 1e-06
F32 = jnp.float32
BF16 = jnp.bfloat16

CHIPS = 64
ROWS = 512
WIDTH = 768
CLUSTERS = 128
GROUPS = 16
CAP = 64
BASE = 16
HALF = WIDTH // 2
LINES = 16
DEPTH = 4
POOL = 8
PARTS = ((0, 24, 256), (24, 32, 384), (56, 16, 128))
TOTAL = 72
HELD = 768
STARTS = (0, 256, 640)
LAST = len(PARTS) - 1
NONE = 1e30


def normalize(values):
    widened = values.astype(F32)
    return widened * lax.rsqrt(jnp.sum(widened * widened, axis=1, keepdims=True) + EPSILON)


def general(embeddings, assign, owner, send_count, send_index):
    rows_local = embeddings.shape[0]
    feature_width = embeddings.shape[1]
    groups = lax.axis_size("grp")
    clusters = owner.shape[0]
    capacity = send_index.shape[2]
    slot_total = groups * capacity
    unit_rows = normalize(embeddings)
    unit_low = unit_rows.astype(BF16)
    counts = send_count[0]
    listed = send_index[0]
    live_slot = jnp.arange(capacity, dtype=jnp.int32)[None, :] < counts[:, None]
    listed_cluster = assign[listed]
    owned_here = owner[listed_cluster] == jnp.arange(groups, dtype=jnp.int32)[:, None]
    kept_slot = live_slot & owned_here
    out_cluster = jnp.where(kept_slot, listed_cluster, -1)
    out_tag = jnp.where(kept_slot, lax.axis_index(("grp", "blk")) * rows_local + listed, -1)
    out_vector = unit_low[listed.reshape(-1)].reshape(groups, capacity, feature_width)
    got_vector, got_cluster, got_tag = (
        lax.all_to_all(out_vector, "grp", split_axis=0, concat_axis=0, tiled=True),
        lax.all_to_all(out_cluster, "grp", split_axis=0, concat_axis=0, tiled=True),
        lax.all_to_all(out_tag, "grp", split_axis=0, concat_axis=0, tiled=True),
    )
    own_vector = got_vector.reshape(slot_total, feature_width)
    own_cluster = got_cluster.reshape(slot_total)
    own_tag = got_tag.reshape(slot_total)

    def tile_best(current, shard_piece):
        other_vector, other_cluster, other_tag = shard_piece
        scores = jnp.einsum("id,jd->ij", own_vector, other_vector, preferred_element_type=F32)
        matched = (
            (own_cluster[:, None] == other_cluster[None, :])
            & (other_cluster[None, :] >= 0)
            & (own_tag[:, None] != other_tag[None, :])
        )
        return jnp.maximum(current, jnp.max(jnp.where(matched, scores, -1.0), axis=1))

    other_vector = lax.all_gather(own_vector, "blk", axis=0, tiled=True)
    other_cluster = lax.all_gather(own_cluster, "blk", axis=0, tiled=True)
    other_tag = lax.all_gather(own_tag, "blk", axis=0, tiled=True)
    length = other_vector.shape[0]
    number = length // slot_total
    stacked = (
        other_vector.reshape(number, slot_total, feature_width),
        other_cluster.reshape(number, slot_total),
        other_tag.reshape(number, slot_total),
    )

    def scan_step(carry, single):
        return (tile_best(carry, single), None)

    result, unused = lax.scan(scan_step, jnp.full((slot_total,), -1.0, F32), stacked)
    target = jnp.where(live_slot, listed, rows_local).reshape(-1)
    partial_sum = jax.ops.segment_sum(unit_rows, assign, num_segments=clusters)
    centre = normalize(lax.psum(partial_sum, ("grp", "blk")))
    nearness = jnp.sum(unit_low.astype(F32) * centre[assign], axis=1)
    returned = lax.all_to_all(
        result.reshape(groups, capacity), "grp", split_axis=0, concat_axis=0, tiled=True
    )
    has_entry = (
        jnp.zeros((rows_local,), jnp.int32)
        .at[target]
        .max(kept_slot.astype(jnp.int32).reshape(-1), mode="drop")
    )
    centroid_cos = jnp.where(has_entry > 0, nearness, 0.0)
    max_sim = jnp.full((rows_local,), -1.0, F32).at[target].max(returned.reshape(-1), mode="drop")
    return (max_sim, centroid_cos)


def iota(shape, axis):
    return lax.broadcasted_iota(jnp.int32, shape, axis)


def down(values):
    return jnp.sum(values, axis=0, keepdims=True)


def across(values):
    return jnp.sum(values, axis=1, keepdims=True)


def pick(mask, values):
    return jnp.where(mask, values, 0.0)


def as_column(row):
    size = row.shape[1]
    return across(pick(iota((size, size), 0) == iota((size, size), 1), row))


def as_row(column):
    size = column.shape[0]
    return down(pick(iota((size, size), 0) == iota((size, size), 1), column))


def dot(a, b):
    return jnp.dot(a, b, preferred_element_type=F32)


def dot_rows(a, b):
    return lax.dot_general(a, b, (((1,), (1,)), ((), ())), preferred_element_type=F32)


def onehot(mask):
    return jnp.where(mask, 1.0, 0.0).astype(BF16)


def thirds(values):
    first = values.astype(BF16).astype(F32)
    rest = values - first
    second = rest.astype(BF16).astype(F32)
    third = (rest - second).astype(BF16).astype(F32)
    return first, second, third


def rank_groups(count_ref):
    count_row = count_ref[...].astype(F32)
    count_column = as_column(count_row)
    sub, lane = iota((GROUPS, 128), 0), iota((GROUPS, 128), 1)
    count_lanes = down(pick(sub == lane, count_column))
    ahead = (count_column > count_lanes) | ((count_column == count_lanes) & (sub < lane))
    rank = down(jnp.where(ahead, 1.0, 0.0))
    return jnp.where(iota((1, 128), 1) < GROUPS, rank, 0.0), count_column


def place_documents(assign_ref, owner_ref, rank):
    owner_row = owner_ref[...].astype(F32)
    owner_column = as_column(owner_row)
    sub, lane = iota((CLUSTERS, CLUSTERS), 0), iota((CLUSTERS, CLUSTERS), 1)
    within = across(jnp.where((owner_column == owner_row) & (lane < sub), 1.0, 0.0))
    group_rank = across(pick(owner_column == lane.astype(F32), rank))
    place_column = group_rank * (CLUSTERS // GROUPS) + within
    member = iota((CLUSTERS, ROWS), 0) == assign_ref[...]
    place = down(pick(member, place_column))
    group = down(pick(member, owner_column))
    order = iota((CLUSTERS, ROWS), 0).astype(F32)
    at_place = order == place
    earlier = onehot(iota((ROWS, ROWS), 0) < iota((ROWS, ROWS), 1))
    before = dot(onehot(at_place), earlier)
    slot = down(pick(at_place, before))
    count_column = across(jnp.where(at_place, 1.0, 0.0))
    partner_count = down(pick(order == (CLUSTERS - 1) - place, count_column))
    slot = slot + jnp.where(place >= CHIPS, partner_count, 0.0)
    chip = jnp.minimum(place, (CLUSTERS - 1) - place)
    return group, chip.astype(jnp.int32), slot.astype(jnp.int32), as_row(count_column)


def missing_documents(index_ref, count_column, group):
    listed = index_ref[...]
    live = iota((GROUPS, CAP), 1).astype(F32) < count_column
    eye = onehot(iota((CAP, CAP), 0) == iota((CAP, CAP), 1))
    high = dot_rows(eye, jnp.where(live, listed >> 4, 0).astype(F32).astype(BF16))
    low = dot_rows(eye, jnp.where(live, listed & 15, 0).astype(F32).astype(BF16))
    alive = dot_rows(eye, onehot(live))
    slots = jnp.where(alive > 0.5, high * 16.0 + low, -1.0)
    document = iota((1, ROWS), 1).astype(F32)
    lane = iota((CAP, GROUPS), 1)

    def count(g, hits):
        column = across(pick(lane == g, slots))
        wanted = jnp.where(group == g.astype(F32), document, -2.0)
        return hits + jnp.where(column == wanted, 1.0, 0.0)

    hits = lax.fori_loop(0, GROUPS, count, jnp.zeros((CAP, ROWS), F32))
    return across(jnp.where(down(hits) > 0.5, 0.0, 1.0))


def send_order():
    order = []
    for step in range(CHIPS):
        high, middle, low = step // 16, (step // 4) % 4, step % 4
        order.append((low, (middle + low) % 4, (high + middle + low) % 4))
    near = [shift for shift in order if sum(min(d, 4 - d) for d in shift) <= 1] + [(2, 0, 0)]
    near.sort(key=lambda shift: -sum(min(d, 4 - d) for d in shift))
    return [shift for shift in order if shift not in near] + near


ORDER = send_order()
SELF = CHIPS - 1
FAR_FIRST = sorted(range(SELF), key=lambda step: -sum(min(d, 4 - d) for d in ORDER[step]))


def step_to(dx, dy, dz):
    shift = (dx & 3) * 16 + (dy & 3) * 4 + (dz & 3)
    step = jnp.full(shift.shape, SELF, jnp.int32)
    for number, (x, y, z) in enumerate(ORDER[:SELF]):
        step = jnp.where(shift == x * 16 + y * 4 + z, number, step)
    return step


def in_part(step, part):
    begin, steps, _ = PARTS[part]
    return (step >= begin) & (step < begin + steps)


def chip_places():
    sub, lane = iota((CLUSTERS, CLUSTERS), 0), iota((CLUSTERS, CLUSTERS), 1)
    return onehot((sub == lane) | (sub == (CLUSTERS - 1) - lane))


def excess(totals):
    lane = iota(totals.shape, 1)
    return jnp.where(lane < CHIPS, jnp.maximum(totals - BASE, 0.0), 0.0)


def receive_plan(table, rank, my_x, my_y, my_z):
    chip = my_x * 16 + my_y * 4 + my_z
    heads = table.astype(jnp.int32)
    counts = (heads & 1023).astype(F32)
    differ = jnp.where((heads >> 10).astype(F32) != rank, 1.0, 0.0)
    fault = across(down(differ))
    both = dot(counts.astype(BF16), chip_places())
    over = excess(both)
    lanes = iota((CHIPS, CLUSTERS), 1)
    sender = iota((CHIPS, 1), 0)
    source, target = iota((CHIPS, CHIPS), 0), iota((CHIPS, CHIPS), 1)

    same_line = (source >> 2) == (target >> 2)
    over_total = across(over)
    over_row = as_row(over_total)
    line_start = across(pick(same_line & (target < source), over_row))
    line_total = across(pick(same_line, over_row))
    fault = fault + down(jnp.where(line_total > POOL, 1.0, 0.0))
    start = line_start + across(pick(lanes < chip, over))
    number = across(pick(lanes == chip, over))

    to_chip = iota((1, CLUSTERS), 1)
    route = step_to(
        (to_chip >> 4) - (sender >> 4), ((to_chip >> 2) & 3) - ((sender >> 2) & 3), (to_chip & 3) - (sender & 3)
    )
    based = jnp.where(lanes < CHIPS, jnp.minimum(both, float(BASE)), 0.0)
    for part, (_, _, room) in enumerate(PARTS):
        held = down(pick(in_part(route, part), based))
        if part == LAST:
            held = held + down(over)
        fault = fault + across(jnp.where(held > room, 1.0, 0.0))

    first = across(pick(lanes == chip, counts))
    second = across(pick(lanes == (CLUSTERS - 1) - chip, counts))
    place = (lanes & (POOL - 1)).astype(F32) - start
    mine = ((sender >> 2) == (lanes >> 3)) & (place >= 0.0) & (place < number)
    over_first = down(jnp.where(mine & (place + BASE < first), 1.0, 0.0))
    over_second = down(jnp.where(mine & (place + BASE >= first), 1.0, 0.0))
    over_first_total, over_second_total = across(over_first), across(over_second)
    earlier = onehot(iota((CLUSTERS, CLUSTERS), 0) < iota((CLUSTERS, CLUSTERS), 1))
    sub = iota((16, CLUSTERS), 0)
    before = dot((pick(sub == 0, over_first) + pick(sub == 1, over_second)).astype(BF16), earlier)

    base_first = jnp.minimum(first, float(BASE))
    base_second = jnp.minimum(first + second, float(BASE)) - base_first
    first_row, second_row = as_row(base_first), as_row(base_second)

    def my_step(other):
        return step_to(my_x - (other >> 4), my_y - ((other >> 2) & 3), my_z - (other & 3))

    step_column, step_row = my_step(sender), my_step(iota((1, CHIPS), 1))
    plans = []
    ends = []
    for part, (begin, steps, _) in enumerate(PARTS):
        inside = in_part(step_column, part)
        ahead = (target < source) & in_part(step_row, part)
        first_total = down(pick(inside, base_first))
        second_total = down(pick(inside, base_second))
        last = part == LAST
        first_end = first_total + over_first_total if last else first_total
        first_start = across(pick(ahead, first_row))
        second_start = across(pick(ahead, second_row)) + first_end
        spread = step_column - begin == (iota((CHIPS, steps * BASE), 1) >> 4)
        head, tail, head_start, tail_start = [
            down(pick(spread, column)) for column in (base_first, base_second, first_start, second_start)
        ]
        slot = (iota((1, steps * BASE), 1) & (BASE - 1)).astype(F32)
        later = jnp.where(slot < head + tail, tail_start + (slot - head), -1.0)
        plan = jnp.where(slot < head, head_start + slot, later)
        held_end = first_end + second_total
        if last:
            over_row_of = jnp.where(over_second > 0.5, held_end + before[1:2], -1.0)
            over_row_of = jnp.where(over_first > 0.5, first_total + before[0:1], over_row_of)
            plan = jnp.concatenate([plan[:, : steps * BASE - CLUSTERS], over_row_of], axis=1)
            held_end = held_end + over_second_total
        plans.append(plan)
        ends.append((first_end, held_end))
    return plans, ends, line_start, over_total, fault


def kernel(
    x_hbm, assign_hbm, owner_hbm, count_hbm, index_hbm,
    out_ref, fault_ref,
    x_ref, assign_ref, owner_ref, count_ref, index_ref,
    send, got, heads, own_over, line_over, send_over, got_over, pick_0, pick_1, pick_2,
    mine, theirs, facts, sums, their_sums, back, returned,
    load_sem, send_sem, recv_sem,
):
    grp, blk = lax.axis_index("grp"), lax.axis_index("blk")
    my_x, my_y, my_z, core = grp // 4, grp % 4, blk // 2, blk % 2
    my_chip = grp * 4 + my_z
    picks = (pick_0, pick_1, pick_2)
    along_x = [((my_x + d) % 4) * 4 for d in range(4)]
    along_y = [(my_y + d) % 4 for d in range(4)]
    along_z = [((my_z + d) % 4) * 2 + core for d in range(4)]
    other_core = {"grp": grp, "blk": my_z * 2 + (1 - core)}

    def device_at(step, sign):
        dx, dy, dz = [(sign * d) % 4 for d in ORDER[step]]
        return {"grp": along_x[dx] + along_y[dy], "blk": along_z[dz]}

    def remote(source, target, number, device):
        return pltpu.make_async_remote_copy(
            src_ref=source,
            dst_ref=target,
            send_sem=send_sem.at[number],
            recv_sem=recv_sem.at[number],
            device_id=device,
            device_id_type=pl.DeviceIdType.MESH,
        )

    def await_blocks(ref, number, semaphore):
        block = ref.at[pl.ds(0, number)]
        pltpu.make_async_copy(block, block, semaphore).wait()

    HEAD, LINE, OVER, FACTS, SUMS, BACK, SWAP, PART = 0, 1, 2, 3, 4, 5, 6, 9
    messages = [min(begin + steps, SELF) - begin for begin, steps, _ in PARTS]

    loads = [
        pltpu.make_async_copy(source, target, load_sem.at[number])
        for number, (source, target) in enumerate(
            (
                (assign_hbm, assign_ref),
                (owner_hbm, owner_ref),
                (count_hbm, count_ref),
                (index_hbm, index_ref),
                (x_hbm, x_ref),
            )
        )
    ]
    for load in loads:
        load.start()
    barrier = pltpu.get_barrier_semaphore()
    for device in [device_at(step, 1) for step in FAR_FIRST] + [other_core]:
        pl.semaphore_signal(barrier, inc=1, device_id=device, device_id_type=pl.DeviceIdType.MESH)
    for load in loads[:-1]:
        load.wait()

    rank, count_column = rank_groups(count_ref)
    group, chip, slot, place_counts = place_documents(assign_ref, owner_ref, rank)
    step_of = step_to((chip >> 4) - my_x, ((chip >> 2) & 3) - my_y, (chip & 3) - my_z)
    in_base = slot < BASE
    send_slot = jnp.where(in_base, step_of * BASE + slot, -1)
    heads[my_chip] = place_counts + 1024.0 * rank
    loads[-1].wait()

    def pack(first, stop):
        slots = iota(((stop - first) * BASE, ROWS), 0) + first * BASE
        rows = dot(onehot(slots == send_slot), x_ref[...]).astype(BF16)
        send[pl.ds(first, stop - first)] = rows.reshape(stop - first, BASE, WIDTH)

    def post(first, stop):
        for step in range(first, min(stop, SELF)):
            number = max(part for part in range(len(PARTS)) if PARTS[part][0] <= step)
            remote(send.at[step], got.at[step], PART + number, device_at(step, 1)).start()

    pack(0, 24)
    pl.semaphore_wait(barrier, CHIPS)
    post(0, 16)
    block = heads.at[pl.ds(my_chip, 1)]
    for step in FAR_FIRST:
        remote(block, block, HEAD, device_at(step, 1)).start()
    place_counts_16 = place_counts + jnp.zeros((16, CLUSTERS), F32)
    own_excess = excess(dot(place_counts_16.astype(BF16), chip_places())[0:1])
    eye = iota((CHIPS, CLUSTERS), 0) == iota((CHIPS, CLUSTERS), 1)
    excess_column = across(pick(eye, own_excess))
    over_slot = down(pick(iota((CHIPS, ROWS), 0) < chip, excess_column)).astype(jnp.int32) + (slot - BASE)
    over_slot = jnp.where(in_base, -1, over_slot)
    own_over[...] = dot(onehot(iota((BASE, ROWS), 0) == over_slot), x_ref[...]).astype(BF16)
    line_over[my_z] = own_over[...]
    for d in range(1, DEPTH):
        remote(own_over, line_over.at[my_z], LINE, {"grp": grp, "blk": along_z[d]}).start()
    post(16, 24)
    pack(24, 48)
    post(24, 40)
    pack(48, CHIPS)
    got[SELF] = send[SELF]

    await_blocks(heads, CHIPS - 1, recv_sem.at[HEAD])
    table = heads[...].reshape(CHIPS, CLUSTERS)
    plans, ends, line_start, over_total, fault = receive_plan(table, rank, my_x, my_y, my_z)

    await_blocks(line_over, DEPTH - 1, recv_sem.at[LINE])
    sender = iota((CHIPS, 1), 0)
    at = sender == grp * 4 + (iota((CHIPS, DEPTH * BASE), 1) >> 4)
    begin = down(pick(at, line_start))
    number = down(pick(at, over_total))
    order = (iota((1, DEPTH * BASE), 1) & (BASE - 1)).astype(F32)
    order = jnp.where(order < number, begin + order, -1.0)
    my_start = down(pick(sender == my_chip, line_start))
    rows = iota((2 * POOL, DEPTH * BASE), 0).astype(F32)
    blocks = line_over[...].reshape(DEPTH * BASE, WIDTH)
    left = dot(onehot((rows == order) & (rows < POOL)), blocks[:, :HALF])
    right = dot(onehot((rows - POOL == order) & (rows >= POOL)), blocks[:, HALF:])
    send_over[...] = (left + right).astype(BF16)
    got_over[grp] = send_over[...]
    for step in range(1, LINES):
        low, middle = step % 4, step // 4
        device = {"grp": along_x[low] + along_y[(middle + low) % 4], "blk": blk}
        remote(send_over, got_over.at[grp], OVER, device).start()
    post(40, CHIPS)

    missing = missing_documents(index_ref, count_column, group)
    row = iota((8, 128), 0)
    told = pick(row == 6, rank) + pick(row == 7, jnp.where(iota((1, 128), 1) == 0, fault, missing))
    for part, (first_end, held_end) in enumerate(ends):
        told = told + pick(row == part, first_end) + pick(row == 3 + part, held_end)
        picks[part][...] = onehot(iota(picks[part].shape, 0).astype(F32) == plans[part])
    facts[0] = told
    swap_facts = remote(facts.at[0], facts.at[1], FACTS, other_core)
    swap_facts.start()

    best = [jnp.full((1, room), -1.0, F32) for _, _, room in PARTS]
    their_ends = []
    totals = [jnp.zeros((1, WIDTH), F32), jnp.zeros((1, WIDTH), F32)]
    swaps = []

    def window(part):
        return pl.ds(STARTS[part], PARTS[part][2])

    def compare(keys, key_part, query_part, key_ends, itself, more=0):
        room = PARTS[key_part][2]
        scores = dot_rows(keys[pl.ds(STARTS[key_part], room + more)], mine[window(query_part)])
        rest, scores = scores[room:], scores[:room]
        first, held = key_ends[key_part]
        key_number = iota((PARTS[key_part][2], 1), 0).astype(F32)
        query_number = iota((1, PARTS[query_part][2]), 1).astype(F32)
        kind = jnp.where(key_number < first, 0.0, jnp.where(key_number < held, 1.0, 2.0))
        matched = kind == jnp.where(query_number < ends[query_part][0], 0.0, 1.0)
        if itself and key_part == query_part:
            matched = matched & (key_number != query_number)
        scores = jnp.max(jnp.where(matched, scores, -1.0), axis=0, keepdims=True)
        best[query_part] = jnp.maximum(best[query_part], scores)
        return rest

    for part, (begin, steps, room) in enumerate(PARTS):
        if part == LAST:
            await_blocks(got_over, LINES - 1, recv_sem.at[OVER])
            halves = got_over[...].reshape(LINES * 2 * POOL, HALF)
            shape = (LINES * POOL, LINES * 2 * POOL)
            to, at = iota(shape, 0), iota(shape, 1)
            same = ((to >> 3) == (at >> 4)) & ((to & 7) == (at & 7))
            left = dot(onehot(same & ((at & POOL) == 0)), halves)
            right = dot(onehot(same & ((at & POOL) != 0)), halves)
            whole = jnp.concatenate([left, right], axis=1).astype(BF16)
            got[pl.ds(CHIPS, TOTAL - CHIPS)] = whole.reshape(TOTAL - CHIPS, BASE, WIDTH)
        await_blocks(got, messages[part], recv_sem.at[PART + part])
        rows = dot(picks[part][...], got[pl.ds(begin, steps)].reshape(steps * BASE, WIDTH))
        unit = rows * lax.rsqrt(across(rows * rows) + EPSILON)
        mine[window(part)] = unit.astype(BF16)
        swap = remote(mine.at[window(part)], theirs.at[window(part)], SWAP + part, other_core)
        swap.start()
        swaps.append(swap)
        is_first = iota((room, 1), 0).astype(F32) < ends[part][0]
        totals[0] = totals[0] + down(pick(is_first, unit))
        totals[1] = totals[1] + down(jnp.where(is_first, 0.0, unit))
        if part == LAST:
            row = iota((8, WIDTH), 0)
            sums[...] = pick(row == 0, totals[0]) + pick(row == 1, totals[1])
            swap_sums = remote(sums, their_sums, SUMS, other_core)
            swap_sums.start()
        for other in range(part + 1):
            compare(mine, part, other, ends, True)
            if other != part:
                compare(mine, other, part, ends, True)
        if part == 0:
            swap_facts.wait()
            their_told = facts[1]
            for number in range(len(PARTS)):
                their_ends.append((their_told[number : number + 1, 0:1], their_told[3 + number : 4 + number, 0:1]))
        for other in range(part):
            compare(theirs, other, part, their_ends, False)
        if part < LAST:
            swaps[part].wait()
            for other in range(part + 1):
                compare(theirs, part, other, their_ends, False)

    swap_sums.wait()
    total = sums[...] + their_sums[...]
    terms = jnp.concatenate(thirds(total) + (jnp.zeros((8, WIDTH), F32),), axis=0)
    theirs[pl.ds(HELD, 32)] = terms.astype(BF16)
    scale = lax.rsqrt(across(total * total) + EPSILON)
    swaps[LAST].wait()
    near = [compare(theirs, LAST, other, their_ends, False, 32) for other in range(len(PARTS))]

    poison = missing + their_told[7:8, 1:2] > 0.5
    tiles = CHIPS * BASE // 128
    for part, (begin, steps, room) in enumerate(PARTS):
        row = iota((8, room), 0)
        query_number = iota((1, room), 1).astype(F32)
        some = (near[part][0:8] + near[part][8:16] + near[part][16:24]) * scale
        some = jnp.where(query_number < ends[part][0], some[0:1], some[1:2])
        values = jnp.zeros((8, room), F32)
        for number, term in enumerate(thirds(best[part]) + thirds(some)):
            values = jnp.where(row == number, term, values)
        out = dot(values.astype(BF16), picks[part][...])
        for kind in range(2):
            line = out[3 * kind : 3 * kind + 1] + out[3 * kind + 1 : 3 * kind + 2] + out[3 * kind + 2 : 3 * kind + 3]
            line = jnp.where(poison, NONE, line)
            for tile in range(steps * BASE // 128):
                piece = line[:, tile * 128 : (tile + 1) * 128]
                to = begin * BASE // 128 + tile
                if to < tiles:
                    back[to, kind : kind + 1, :] = piece
                else:
                    for each in range(tiles):
                        back[each, 2 + kind : 3 + kind, :] = piece
    returned[SELF] = back[SELF // 8]
    for step in FAR_FIRST:
        remote(back.at[step // 8], returned.at[step], BACK, device_at(step, -1)).start()

    differ = across(jnp.where(their_told[6:7] != rank, 1.0, 0.0))
    fault = fault + their_told[7:8, 0:1] + differ
    chosen = onehot(iota((CHIPS, ROWS), 0) == step_of)
    sub = iota((128, ROWS), 0)
    at_base = (sub == (step_of & 7) * BASE + slot) & in_base
    at_over = (sub == grp * POOL + my_start.astype(jnp.int32) + over_slot) & (~in_base)

    await_blocks(returned, CHIPS - 1, recv_sem.at[BACK])
    found = []
    for number in range(4):
        line = returned[:, number, :]
        if number == 0:
            poisoned = across(down(jnp.where(line > 0.5 * NONE, 1.0, 0.0)))
            fault_ref[...] = jnp.where(fault + poisoned > 0.5, 1, 0) + jnp.zeros((1, 128), jnp.int32)
        terms = jnp.concatenate(thirds(line), axis=1).astype(BF16)
        out = lax.dot_general(terms, chosen, (((0,), (0,)), ((), ())), preferred_element_type=F32)
        found.append(out[0:128] + out[128:256] + out[256:384])
    out_ref[0:1] = down(pick(at_base, found[0]) + pick(at_over, found[2]))
    out_ref[1:2] = down(pick(at_base, found[1]) + pick(at_over, found[3]))

    await_blocks(heads, CHIPS - 1, send_sem.at[HEAD])
    await_blocks(line_over, DEPTH - 1, send_sem.at[LINE])
    await_blocks(got_over, LINES - 1, send_sem.at[OVER])
    await_blocks(returned, CHIPS - 1, send_sem.at[BACK])
    for part in range(len(PARTS)):
        await_blocks(got, messages[part], send_sem.at[PART + part])


def routed(embeddings, assign, owner, send_count, send_index):
    return pl.pallas_call(
        kernel,
        out_shape=(
            jax.ShapeDtypeStruct((2, ROWS), F32),
            jax.ShapeDtypeStruct((1, 128), jnp.int32),
        ),
        in_specs=[pl.BlockSpec(memory_space=pl.ANY)] * 5,
        out_specs=(pl.BlockSpec(memory_space=pltpu.VMEM),) * 2,
        scratch_shapes=[
            pltpu.VMEM((ROWS, WIDTH), BF16),
            pltpu.VMEM((1, ROWS), jnp.int32),
            pltpu.VMEM((1, CLUSTERS), jnp.int32),
            pltpu.VMEM((1, GROUPS), jnp.int32),
            pltpu.VMEM((GROUPS, CAP), jnp.int32),
            pltpu.VMEM((CHIPS, BASE, WIDTH), BF16),
            pltpu.VMEM((TOTAL, BASE, WIDTH), BF16),
            pltpu.VMEM((CHIPS, 1, 128), F32),
            pltpu.VMEM((BASE, WIDTH), BF16),
            pltpu.VMEM((DEPTH, BASE, WIDTH), BF16),
            pltpu.VMEM((2 * POOL, HALF), BF16),
            pltpu.VMEM((LINES, 2 * POOL, HALF), BF16),
            *[pltpu.VMEM((room, steps * BASE), BF16) for _, steps, room in PARTS],
            pltpu.VMEM((HELD, WIDTH), BF16),
            pltpu.VMEM((HELD + 32, WIDTH), BF16),
            pltpu.VMEM((2, 8, 128), F32),
            pltpu.VMEM((8, WIDTH), F32),
            pltpu.VMEM((8, WIDTH), F32),
            pltpu.VMEM((CHIPS * BASE // 128, 4, 128), F32),
            pltpu.VMEM((CHIPS, 4, 128), F32),
            pltpu.SemaphoreType.DMA((5,)),
            pltpu.SemaphoreType.DMA((12,)),
            pltpu.SemaphoreType.DMA((12,)),
        ],
        compiler_params=pltpu.CompilerParams(
            collective_id=0, has_side_effects=True, vmem_limit_bytes=48 * 1024 * 1024
        ),
    )(
        embeddings,
        assign.reshape(1, ROWS),
        owner.reshape(1, CLUSTERS),
        send_count,
        send_index[0],
    )


def body(embeddings, assign, owner, send_count, send_index):
    arguments = (embeddings, assign, owner, send_count, send_index)
    results, fault = routed(*arguments)
    results = lax.cond(fault[0, 0] != 0, lambda: jnp.stack(general(*arguments)), lambda: results)
    return results[0], results[1]


def solution(mesh):
    placed = (
        P(("grp", "blk"), None),
        P(("grp", "blk")),
        P(),
        P(("grp", "blk"), None),
        P(("grp", "blk"), None, None),
    )
    return jax.shard_map(
        body,
        mesh=mesh,
        in_specs=placed,
        out_specs=(P(("grp", "blk")), P(("grp", "blk"))),
        check_vma=False,
    )
```

```python
import functools

import jax
import jax.numpy as jnp
from jax import lax
from jax.experimental import pallas as pl
from jax.experimental.pallas import tpu as pltpu
from jax.sharding import PartitionSpec as P

EPSILON = 1e-06
F32 = jnp.float32
BF16 = jnp.bfloat16

CHIPS = 64
ROWS = 512
WIDTH = 768
CLUSTERS = 128
GROUPS = 16
CAP = 64
BASE = 16
HALF = WIDTH // 2
LINES = 16
DEPTH = 4
POOL = 8
PARTS = ((0, 24, 256), (24, 32, 384), (56, 16, 128))
TOTAL = 72
HELD = 768
STARTS = (0, 256, 640)
LAST = len(PARTS) - 1
NONE = 1e30


def normalize(values):
    widened = values.astype(F32)
    return widened * lax.rsqrt(jnp.sum(widened * widened, axis=1, keepdims=True) + EPSILON)


def general(embeddings, assign, owner, send_count, send_index):
    rows_local = embeddings.shape[0]
    feature_width = embeddings.shape[1]
    groups = lax.axis_size("grp")
    clusters = owner.shape[0]
    capacity = send_index.shape[2]
    slot_total = groups * capacity
    unit_rows = normalize(embeddings)
    unit_low = unit_rows.astype(BF16)
    counts = send_count[0]
    listed = send_index[0]
    live_slot = jnp.arange(capacity, dtype=jnp.int32)[None, :] < counts[:, None]
    listed_cluster = assign[listed]
    owned_here = owner[listed_cluster] == jnp.arange(groups, dtype=jnp.int32)[:, None]
    kept_slot = live_slot & owned_here
    out_cluster = jnp.where(kept_slot, listed_cluster, -1)
    out_tag = jnp.where(kept_slot, lax.axis_index(("grp", "blk")) * rows_local + listed, -1)
    out_vector = unit_low[listed.reshape(-1)].reshape(groups, capacity, feature_width)
    got_vector, got_cluster, got_tag = (
        lax.all_to_all(out_vector, "grp", split_axis=0, concat_axis=0, tiled=True),
        lax.all_to_all(out_cluster, "grp", split_axis=0, concat_axis=0, tiled=True),
        lax.all_to_all(out_tag, "grp", split_axis=0, concat_axis=0, tiled=True),
    )
    own_vector = got_vector.reshape(slot_total, feature_width)
    own_cluster = got_cluster.reshape(slot_total)
    own_tag = got_tag.reshape(slot_total)

    def tile_best(current, shard_piece):
        other_vector, other_cluster, other_tag = shard_piece
        scores = jnp.einsum("id,jd->ij", own_vector, other_vector, preferred_element_type=F32)
        matched = (
            (own_cluster[:, None] == other_cluster[None, :])
            & (other_cluster[None, :] >= 0)
            & (own_tag[:, None] != other_tag[None, :])
        )
        return jnp.maximum(current, jnp.max(jnp.where(matched, scores, -1.0), axis=1))

    other_vector = lax.all_gather(own_vector, "blk", axis=0, tiled=True)
    other_cluster = lax.all_gather(own_cluster, "blk", axis=0, tiled=True)
    other_tag = lax.all_gather(own_tag, "blk", axis=0, tiled=True)
    length = other_vector.shape[0]
    number = length // slot_total
    stacked = (
        other_vector.reshape(number, slot_total, feature_width),
        other_cluster.reshape(number, slot_total),
        other_tag.reshape(number, slot_total),
    )

    def scan_step(carry, single):
        return (tile_best(carry, single), None)

    result, unused = lax.scan(scan_step, jnp.full((slot_total,), -1.0, F32), stacked)
    target = jnp.where(live_slot, listed, rows_local).reshape(-1)
    partial_sum = jax.ops.segment_sum(unit_rows, assign, num_segments=clusters)
    centre = normalize(lax.psum(partial_sum, ("grp", "blk")))
    nearness = jnp.sum(unit_low.astype(F32) * centre[assign], axis=1)
    returned = lax.all_to_all(
        result.reshape(groups, capacity), "grp", split_axis=0, concat_axis=0, tiled=True
    )
    has_entry = (
        jnp.zeros((rows_local,), jnp.int32)
        .at[target]
        .max(kept_slot.astype(jnp.int32).reshape(-1), mode="drop")
    )
    centroid_cos = jnp.where(has_entry > 0, nearness, 0.0)
    max_sim = jnp.full((rows_local,), -1.0, F32).at[target].max(returned.reshape(-1), mode="drop")
    return (max_sim, centroid_cos)


def iota(shape, axis):
    return lax.broadcasted_iota(jnp.int32, shape, axis)


def down(values):
    return jnp.sum(values, axis=0, keepdims=True)


def across(values):
    return jnp.sum(values, axis=1, keepdims=True)


def pick(mask, values):
    return jnp.where(mask, values, 0.0)


def as_column(row):
    size = row.shape[1]
    return across(pick(iota((size, size), 0) == iota((size, size), 1), row))


def as_row(column):
    size = column.shape[0]
    return down(pick(iota((size, size), 0) == iota((size, size), 1), column))


def dot(a, b):
    return jnp.dot(a, b, preferred_element_type=F32)


def dot_rows(a, b):
    return lax.dot_general(a, b, (((1,), (1,)), ((), ())), preferred_element_type=F32)


def onehot(mask):
    return jnp.where(mask, 1.0, 0.0).astype(BF16)


def thirds(values):
    first = values.astype(BF16).astype(F32)
    rest = values - first
    second = rest.astype(BF16).astype(F32)
    third = (rest - second).astype(BF16).astype(F32)
    return first, second, third


def rank_groups(count_ref):
    count_row = count_ref[...].astype(F32)
    count_column = as_column(count_row)
    sub, lane = iota((GROUPS, 128), 0), iota((GROUPS, 128), 1)
    count_lanes = down(pick(sub == lane, count_column))
    ahead = (count_column > count_lanes) | ((count_column == count_lanes) & (sub < lane))
    rank = down(jnp.where(ahead, 1.0, 0.0))
    return jnp.where(iota((1, 128), 1) < GROUPS, rank, 0.0), count_column


def place_documents(assign_ref, owner_ref, rank):
    owner_row = owner_ref[...].astype(F32)
    owner_column = as_column(owner_row)
    sub, lane = iota((CLUSTERS, CLUSTERS), 0), iota((CLUSTERS, CLUSTERS), 1)
    within = across(jnp.where((owner_column == owner_row) & (lane < sub), 1.0, 0.0))
    group_rank = across(pick(owner_column == lane.astype(F32), rank))
    place_column = group_rank * (CLUSTERS // GROUPS) + within
    member = iota((CLUSTERS, ROWS), 0) == assign_ref[...]
    place = down(pick(member, place_column))
    group = down(pick(member, owner_column))
    order = iota((CLUSTERS, ROWS), 0).astype(F32)
    at_place = order == place
    earlier = onehot(iota((ROWS, ROWS), 0) < iota((ROWS, ROWS), 1))
    before = dot(onehot(at_place), earlier)
    slot = down(pick(at_place, before))
    count_column = across(jnp.where(at_place, 1.0, 0.0))
    partner_count = down(pick(order == (CLUSTERS - 1) - place, count_column))
    slot = slot + jnp.where(place >= CHIPS, partner_count, 0.0)
    chip = jnp.minimum(place, (CLUSTERS - 1) - place)
    return group, chip.astype(jnp.int32), slot.astype(jnp.int32), as_row(count_column)


def missing_documents(index_ref, count_column, group):
    listed = index_ref[...]
    live = iota((GROUPS, CAP), 1).astype(F32) < count_column
    eye = onehot(iota((CAP, CAP), 0) == iota((CAP, CAP), 1))
    high = dot_rows(eye, jnp.where(live, listed >> 4, 0).astype(F32).astype(BF16))
    low = dot_rows(eye, jnp.where(live, listed & 15, 0).astype(F32).astype(BF16))
    alive = dot_rows(eye, onehot(live))
    slots = jnp.where(alive > 0.5, high * 16.0 + low, -1.0)
    document = iota((1, ROWS), 1).astype(F32)
    lane = iota((CAP, GROUPS), 1)

    def count(g, hits):
        column = across(pick(lane == g, slots))
        wanted = jnp.where(group == g.astype(F32), document, -2.0)
        return hits + jnp.where(column == wanted, 1.0, 0.0)

    hits = lax.fori_loop(0, GROUPS, count, jnp.zeros((CAP, ROWS), F32))
    return across(jnp.where(down(hits) > 0.5, 0.0, 1.0))


def send_order():
    order = []
    for step in range(CHIPS):
        high, middle, low = step // 16, (step // 4) % 4, step % 4
        order.append((low, (middle + low) % 4, (high + middle + low) % 4))
    near = [shift for shift in order if sum(min(d, 4 - d) for d in shift) <= 1] + [(2, 0, 0)]
    near.sort(key=lambda shift: -sum(min(d, 4 - d) for d in shift))
    return [shift for shift in order if shift not in near] + near


ORDER = send_order()
SELF = CHIPS - 1


def step_to(dx, dy, dz):
    shift = (dx & 3) * 16 + (dy & 3) * 4 + (dz & 3)
    step = jnp.full(shift.shape, SELF, jnp.int32)
    for number, (x, y, z) in enumerate(ORDER[:SELF]):
        step = jnp.where(shift == x * 16 + y * 4 + z, number, step)
    return step


def in_part(step, part):
    begin, steps, _ = PARTS[part]
    return (step >= begin) & (step < begin + steps)


def chip_places():
    sub, lane = iota((CLUSTERS, CLUSTERS), 0), iota((CLUSTERS, CLUSTERS), 1)
    return onehot((sub == lane) | (sub == (CLUSTERS - 1) - lane))


def excess(totals):
    lane = iota(totals.shape, 1)
    return jnp.where(lane < CHIPS, jnp.maximum(totals - BASE, 0.0), 0.0)


def receive_plan(table, rank, my_x, my_y, my_z):
    chip = my_x * 16 + my_y * 4 + my_z
    heads = table.astype(jnp.int32)
    counts = (heads & 1023).astype(F32)
    differ = jnp.where((heads >> 10).astype(F32) != rank, 1.0, 0.0)
    fault = across(down(differ))
    both = dot(counts.astype(BF16), chip_places())
    over = excess(both)
    lanes = iota((CHIPS, CLUSTERS), 1)
    sender = iota((CHIPS, 1), 0)
    source, target = iota((CHIPS, CHIPS), 0), iota((CHIPS, CHIPS), 1)

    same_line = (source >> 2) == (target >> 2)
    over_total = across(over)
    over_row = as_row(over_total)
    line_start = across(pick(same_line & (target < source), over_row))
    line_total = across(pick(same_line, over_row))
    fault = fault + down(jnp.where(line_total > POOL, 1.0, 0.0))
    start = line_start + across(pick(lanes < chip, over))
    number = across(pick(lanes == chip, over))

    to_chip = iota((1, CLUSTERS), 1)
    route = step_to(
        (to_chip >> 4) - (sender >> 4), ((to_chip >> 2) & 3) - ((sender >> 2) & 3), (to_chip & 3) - (sender & 3)
    )
    based = jnp.where(lanes < CHIPS, jnp.minimum(both, float(BASE)), 0.0)
    for part, (_, _, room) in enumerate(PARTS):
        held = down(pick(in_part(route, part), based))
        if part == LAST:
            held = held + down(over)
        fault = fault + across(jnp.where(held > room, 1.0, 0.0))

    first = across(pick(lanes == chip, counts))
    second = across(pick(lanes == (CLUSTERS - 1) - chip, counts))
    place = (lanes & (POOL - 1)).astype(F32) - start
    mine = ((sender >> 2) == (lanes >> 3)) & (place >= 0.0) & (place < number)
    over_first = down(jnp.where(mine & (place + BASE < first), 1.0, 0.0))
    over_second = down(jnp.where(mine & (place + BASE >= first), 1.0, 0.0))
    over_first_total, over_second_total = across(over_first), across(over_second)
    earlier = onehot(iota((CLUSTERS, CLUSTERS), 0) < iota((CLUSTERS, CLUSTERS), 1))
    sub = iota((16, CLUSTERS), 0)
    before = dot((pick(sub == 0, over_first) + pick(sub == 1, over_second)).astype(BF16), earlier)

    base_first = jnp.minimum(first, float(BASE))
    base_second = jnp.minimum(first + second, float(BASE)) - base_first
    first_row, second_row = as_row(base_first), as_row(base_second)

    def my_step(other):
        return step_to(my_x - (other >> 4), my_y - ((other >> 2) & 3), my_z - (other & 3))

    step_column, step_row = my_step(sender), my_step(iota((1, CHIPS), 1))
    plans = []
    ends = []
    for part, (begin, steps, _) in enumerate(PARTS):
        inside = in_part(step_column, part)
        ahead = (target < source) & in_part(step_row, part)
        first_total = down(pick(inside, base_first))
        second_total = down(pick(inside, base_second))
        last = part == LAST
        first_end = first_total + over_first_total if last else first_total
        first_start = across(pick(ahead, first_row))
        second_start = across(pick(ahead, second_row)) + first_end
        spread = step_column - begin == (iota((CHIPS, steps * BASE), 1) >> 4)
        head, tail, head_start, tail_start = [
            down(pick(spread, column)) for column in (base_first, base_second, first_start, second_start)
        ]
        slot = (iota((1, steps * BASE), 1) & (BASE - 1)).astype(F32)
        later = jnp.where(slot < head + tail, tail_start + (slot - head), -1.0)
        plan = jnp.where(slot < head, head_start + slot, later)
        held_end = first_end + second_total
        if last:
            over_row_of = jnp.where(over_second > 0.5, held_end + before[1:2], -1.0)
            over_row_of = jnp.where(over_first > 0.5, first_total + before[0:1], over_row_of)
            plan = jnp.concatenate([plan[:, : steps * BASE - CLUSTERS], over_row_of], axis=1)
            held_end = held_end + over_second_total
        plans.append(plan)
        ends.append((first_end, held_end))
    return plans, ends, fault


def kernel(
    x_hbm, assign_hbm, owner_hbm, count_hbm, index_hbm,
    out_ref, fault_ref,
    x_ref, assign_ref, owner_ref, count_ref, index_ref,
    send, got, heads, own_over, line_over, send_over, got_over, pick_0, pick_1, pick_2,
    mine, theirs, facts, sums, their_sums, back, returned,
    load_sem, send_sem, recv_sem,
):
    grp, blk = lax.axis_index("grp"), lax.axis_index("blk")
    my_x, my_y, my_z, core = grp // 4, grp % 4, blk // 2, blk % 2
    my_chip = grp * 4 + my_z
    picks = (pick_0, pick_1, pick_2)
    along_x = [((my_x + d) % 4) * 4 for d in range(4)]
    along_y = [(my_y + d) % 4 for d in range(4)]
    along_z = [((my_z + d) % 4) * 2 + core for d in range(4)]
    other_core = {"grp": grp, "blk": my_z * 2 + (1 - core)}

    def device_at(step, sign):
        dx, dy, dz = [(sign * d) % 4 for d in ORDER[step]]
        return {"grp": along_x[dx] + along_y[dy], "blk": along_z[dz]}

    def remote(source, target, number, device):
        return pltpu.make_async_remote_copy(
            src_ref=source,
            dst_ref=target,
            send_sem=send_sem.at[number],
            recv_sem=recv_sem.at[number],
            device_id=device,
            device_id_type=pl.DeviceIdType.MESH,
        )

    def await_blocks(ref, number, semaphore):
        block = ref.at[pl.ds(0, number)]
        pltpu.make_async_copy(block, block, semaphore).wait()

    HEAD_Z, HEAD_XY, LINE, OVER, FACTS, SUMS, BACK, SWAP, PART = 0, 1, 2, 3, 4, 5, 6, 7, 10
    messages = [min(begin + steps, SELF) - begin for begin, steps, _ in PARTS]

    loads = [
        pltpu.make_async_copy(source, target, load_sem.at[number])
        for number, (source, target) in enumerate(
            (
                (assign_hbm, assign_ref),
                (owner_hbm, owner_ref),
                (count_hbm, count_ref),
                (index_hbm, index_ref),
                (x_hbm, x_ref),
            )
        )
    ]
    for load in loads:
        load.start()
    barrier = pltpu.get_barrier_semaphore()
    for device in [device_at(step, 1) for step in range(SELF)] + [other_core]:
        pl.semaphore_signal(barrier, inc=1, device_id=device, device_id_type=pl.DeviceIdType.MESH)
    for load in loads[:-1]:
        load.wait()

    rank, count_column = rank_groups(count_ref)
    group, chip, slot, place_counts = place_documents(assign_ref, owner_ref, rank)
    step_of = step_to((chip >> 4) - my_x, ((chip >> 2) & 3) - my_y, (chip & 3) - my_z)
    in_base = slot < BASE
    send_slot = jnp.where(in_base, step_of * BASE + slot, -1)
    heads[my_chip] = place_counts + 1024.0 * rank
    loads[-1].wait()

    def pack(first, stop):
        slots = iota(((stop - first) * BASE, ROWS), 0) + first * BASE
        rows = dot(onehot(slots == send_slot), x_ref[...]).astype(BF16)
        send[pl.ds(first, stop - first)] = rows.reshape(stop - first, BASE, WIDTH)

    def post(first, stop):
        for step in range(first, min(stop, SELF)):
            number = max(part for part in range(len(PARTS)) if PARTS[part][0] <= step)
            remote(send.at[step], got.at[step], PART + number, device_at(step, 1)).start()

    pack(0, 24)
    place_counts_16 = place_counts + jnp.zeros((16, CLUSTERS), F32)
    own_excess = excess(dot(place_counts_16.astype(BF16), chip_places())[0:1])
    eye = iota((CHIPS, CLUSTERS), 0) == iota((CHIPS, CLUSTERS), 1)
    excess_column = across(pick(eye, own_excess))
    over_slot = down(pick(iota((CHIPS, ROWS), 0) < chip, excess_column)).astype(jnp.int32) + (slot - BASE)
    over_slot = jnp.where(in_base, -1, over_slot)
    own_over[...] = dot(onehot(iota((BASE, ROWS), 0) == over_slot), x_ref[...]).astype(BF16)
    line_over[my_z] = own_over[...]
    pl.semaphore_wait(barrier, CHIPS)
    for d in range(1, DEPTH):
        device = {"grp": grp, "blk": along_z[d]}
        block = heads.at[pl.ds(my_chip, 1)]
        remote(block, block, HEAD_Z, device).start()
        remote(own_over, line_over.at[my_z], LINE, device).start()
    post(0, 24)

    await_blocks(heads, DEPTH - 1, recv_sem.at[HEAD_Z])
    line_heads = heads[pl.ds(grp * DEPTH, DEPTH)].reshape(DEPTH, CLUSTERS)
    line_counts = (line_heads.astype(jnp.int32) & 1023).astype(F32).astype(BF16)
    line_total = across(excess(dot(line_counts, chip_places())))
    depth = iota((DEPTH, 1), 0)
    line_start = jnp.zeros((DEPTH, 1), F32)
    for d in range(DEPTH - 1):
        line_start = line_start + pick(depth > d, line_total[d : d + 1])
    my_start = down(pick(depth == my_z, line_start))
    at = depth == (iota((DEPTH, DEPTH * BASE), 1) >> 4)
    begin = down(pick(at, line_start))
    number = down(pick(at, line_total))
    order = (iota((1, DEPTH * BASE), 1) & (BASE - 1)).astype(F32)
    order = jnp.where(order < number, begin + order, -1.0)
    rows = iota((2 * POOL, DEPTH * BASE), 0).astype(F32)
    await_blocks(line_over, DEPTH - 1, recv_sem.at[LINE])
    blocks = line_over[...].reshape(DEPTH * BASE, WIDTH)
    left = dot(onehot((rows == order) & (rows < POOL)), blocks[:, :HALF])
    right = dot(onehot((rows - POOL == order) & (rows >= POOL)), blocks[:, HALF:])
    send_over[...] = (left + right).astype(BF16)
    got_over[grp] = send_over[...]
    for step in range(1, LINES):
        low, middle = step % 4, step // 4
        device = {"grp": along_x[low] + along_y[(middle + low) % 4], "blk": blk}
        block = heads.at[pl.ds(grp * DEPTH, DEPTH)]
        remote(block, block, HEAD_XY, device).start()
        remote(send_over, got_over.at[grp], OVER, device).start()
    pack(24, 48)
    post(24, 48)
    pack(48, CHIPS)
    post(48, CHIPS)
    got[SELF] = send[SELF]

    await_blocks(heads, CHIPS - DEPTH, recv_sem.at[HEAD_XY])
    table = heads[...].reshape(CHIPS, CLUSTERS)
    plans, ends, fault = receive_plan(table, rank, my_x, my_y, my_z)

    missing = missing_documents(index_ref, count_column, group)
    row = iota((8, 128), 0)
    told = pick(row == 6, rank) + pick(row == 7, jnp.where(iota((1, 128), 1) == 0, fault, missing))
    for part, (first_end, held_end) in enumerate(ends):
        told = told + pick(row == part, first_end) + pick(row == 3 + part, held_end)
        picks[part][...] = onehot(iota(picks[part].shape, 0).astype(F32) == plans[part])
    facts[0] = told
    swap_facts = remote(facts.at[0], facts.at[1], FACTS, other_core)
    swap_facts.start()

    best = [jnp.full((1, room), -1.0, F32) for _, _, room in PARTS]
    their_ends = []
    totals = [jnp.zeros((1, WIDTH), F32), jnp.zeros((1, WIDTH), F32)]
    swaps = []

    def window(part):
        return pl.ds(STARTS[part], PARTS[part][2])

    def compare(keys, key_part, query_part, key_ends, itself, more=0):
        room = PARTS[key_part][2]
        scores = dot_rows(keys[pl.ds(STARTS[key_part], room + more)], mine[window(query_part)])
        rest, scores = scores[room:], scores[:room]
        first, held = key_ends[key_part]
        key_number = iota((PARTS[key_part][2], 1), 0).astype(F32)
        query_number = iota((1, PARTS[query_part][2]), 1).astype(F32)
        kind = jnp.where(key_number < first, 0.0, jnp.where(key_number < held, 1.0, 2.0))
        matched = kind == jnp.where(query_number < ends[query_part][0], 0.0, 1.0)
        if itself and key_part == query_part:
            matched = matched & (key_number != query_number)
        scores = jnp.max(jnp.where(matched, scores, -1.0), axis=0, keepdims=True)
        best[query_part] = jnp.maximum(best[query_part], scores)
        return rest

    for part, (begin, steps, room) in enumerate(PARTS):
        if part == LAST:
            await_blocks(got_over, LINES - 1, recv_sem.at[OVER])
            halves = got_over[...].reshape(LINES * 2 * POOL, HALF)
            shape = (LINES * POOL, LINES * 2 * POOL)
            to, at = iota(shape, 0), iota(shape, 1)
            same = ((to >> 3) == (at >> 4)) & ((to & 7) == (at & 7))
            left = dot(onehot(same & ((at & POOL) == 0)), halves)
            right = dot(onehot(same & ((at & POOL) != 0)), halves)
            whole = jnp.concatenate([left, right], axis=1).astype(BF16)
            got[pl.ds(CHIPS, TOTAL - CHIPS)] = whole.reshape(TOTAL - CHIPS, BASE, WIDTH)
        await_blocks(got, messages[part], recv_sem.at[PART + part])
        rows = dot(picks[part][...], got[pl.ds(begin, steps)].reshape(steps * BASE, WIDTH))
        unit = rows * lax.rsqrt(across(rows * rows) + EPSILON)
        mine[window(part)] = unit.astype(BF16)
        swap = remote(mine.at[window(part)], theirs.at[window(part)], SWAP + part, other_core)
        swap.start()
        swaps.append(swap)
        is_first = iota((room, 1), 0).astype(F32) < ends[part][0]
        totals[0] = totals[0] + down(pick(is_first, unit))
        totals[1] = totals[1] + down(jnp.where(is_first, 0.0, unit))
        if part == LAST:
            row = iota((8, WIDTH), 0)
            sums[...] = pick(row == 0, totals[0]) + pick(row == 1, totals[1])
            swap_sums = remote(sums, their_sums, SUMS, other_core)
            swap_sums.start()
        for other in range(part + 1):
            compare(mine, part, other, ends, True)
            if other != part:
                compare(mine, other, part, ends, True)
        if part == 0:
            swap_facts.wait()
            their_told = facts[1]
            for number in range(len(PARTS)):
                their_ends.append((their_told[number : number + 1, 0:1], their_told[3 + number : 4 + number, 0:1]))
        for other in range(part):
            compare(theirs, other, part, their_ends, False)
        if part < LAST:
            swaps[part].wait()
            for other in range(part + 1):
                compare(theirs, part, other, their_ends, False)

    swap_sums.wait()
    total = sums[...] + their_sums[...]
    terms = jnp.concatenate(thirds(total) + (jnp.zeros((8, WIDTH), F32),), axis=0)
    theirs[pl.ds(HELD, 32)] = terms.astype(BF16)
    scale = lax.rsqrt(across(total * total) + EPSILON)
    swaps[LAST].wait()
    near = [compare(theirs, LAST, other, their_ends, False, 32) for other in range(len(PARTS))]

    poison = missing + their_told[7:8, 1:2] > 0.5
    tiles = CHIPS * BASE // 128
    for part, (begin, steps, room) in enumerate(PARTS):
        row = iota((8, room), 0)
        query_number = iota((1, room), 1).astype(F32)
        some = (near[part][0:8] + near[part][8:16] + near[part][16:24]) * scale
        some = jnp.where(query_number < ends[part][0], some[0:1], some[1:2])
        values = jnp.zeros((8, room), F32)
        for number, term in enumerate(thirds(best[part]) + thirds(some)):
            values = jnp.where(row == number, term, values)
        out = dot(values.astype(BF16), picks[part][...])
        for kind in range(2):
            line = out[3 * kind : 3 * kind + 1] + out[3 * kind + 1 : 3 * kind + 2] + out[3 * kind + 2 : 3 * kind + 3]
            line = jnp.where(poison, NONE, line)
            for tile in range(steps * BASE // 128):
                piece = line[:, tile * 128 : (tile + 1) * 128]
                to = begin * BASE // 128 + tile
                if to < tiles:
                    back[to, kind : kind + 1, :] = piece
                else:
                    for each in range(tiles):
                        back[each, 2 + kind : 3 + kind, :] = piece
    returned[SELF] = back[SELF // 8]
    for step in range(SELF):
        remote(back.at[step // 8], returned.at[step], BACK, device_at(step, -1)).start()

    differ = across(jnp.where(their_told[6:7] != rank, 1.0, 0.0))
    fault = fault + their_told[7:8, 0:1] + differ
    chosen = onehot(iota((CHIPS, ROWS), 0) == step_of)
    sub = iota((128, ROWS), 0)
    at_base = (sub == (step_of & 7) * BASE + slot) & in_base
    at_over = (sub == grp * POOL + my_start.astype(jnp.int32) + over_slot) & (~in_base)

    await_blocks(returned, CHIPS - 1, recv_sem.at[BACK])
    found = []
    for number in range(4):
        line = returned[:, number, :]
        if number == 0:
            poisoned = across(down(jnp.where(line > 0.5 * NONE, 1.0, 0.0)))
            fault_ref[...] = jnp.where(fault + poisoned > 0.5, 1, 0) + jnp.zeros((1, 128), jnp.int32)
        terms = jnp.concatenate(thirds(line), axis=1).astype(BF16)
        out = lax.dot_general(terms, chosen, (((0,), (0,)), ((), ())), preferred_element_type=F32)
        found.append(out[0:128] + out[128:256] + out[256:384])
    out_ref[0:1] = down(pick(at_base, found[0]) + pick(at_over, found[2]))
    out_ref[1:2] = down(pick(at_base, found[1]) + pick(at_over, found[3]))

    await_blocks(heads, DEPTH - 1, send_sem.at[HEAD_Z])
    await_blocks(heads, CHIPS - DEPTH, send_sem.at[HEAD_XY])
    await_blocks(line_over, DEPTH - 1, send_sem.at[LINE])
    await_blocks(got_over, LINES - 1, send_sem.at[OVER])
    await_blocks(returned, CHIPS - 1, send_sem.at[BACK])
    for part in range(len(PARTS)):
        await_blocks(got, messages[part], send_sem.at[PART + part])


def routed(embeddings, assign, owner, send_count, send_index):
    return pl.pallas_call(
        kernel,
        out_shape=(
            jax.ShapeDtypeStruct((2, ROWS), F32),
            jax.ShapeDtypeStruct((1, 128), jnp.int32),
        ),
        in_specs=[pl.BlockSpec(memory_space=pl.ANY)] * 5,
        out_specs=(pl.BlockSpec(memory_space=pltpu.VMEM),) * 2,
        scratch_shapes=[
            pltpu.VMEM((ROWS, WIDTH), BF16),
            pltpu.VMEM((1, ROWS), jnp.int32),
            pltpu.VMEM((1, CLUSTERS), jnp.int32),
            pltpu.VMEM((1, GROUPS), jnp.int32),
            pltpu.VMEM((GROUPS, CAP), jnp.int32),
            pltpu.VMEM((CHIPS, BASE, WIDTH), BF16),
            pltpu.VMEM((TOTAL, BASE, WIDTH), BF16),
            pltpu.VMEM((CHIPS, 1, 128), F32),
            pltpu.VMEM((BASE, WIDTH), BF16),
            pltpu.VMEM((DEPTH, BASE, WIDTH), BF16),
            pltpu.VMEM((2 * POOL, HALF), BF16),
            pltpu.VMEM((LINES, 2 * POOL, HALF), BF16),
            *[pltpu.VMEM((room, steps * BASE), BF16) for _, steps, room in PARTS],
            pltpu.VMEM((HELD, WIDTH), BF16),
            pltpu.VMEM((HELD + 32, WIDTH), BF16),
            pltpu.VMEM((2, 8, 128), F32),
            pltpu.VMEM((8, WIDTH), F32),
            pltpu.VMEM((8, WIDTH), F32),
            pltpu.VMEM((CHIPS * BASE // 128, 4, 128), F32),
            pltpu.VMEM((CHIPS, 4, 128), F32),
            pltpu.SemaphoreType.DMA((5,)),
            pltpu.SemaphoreType.DMA((13,)),
            pltpu.SemaphoreType.DMA((13,)),
        ],
        compiler_params=pltpu.CompilerParams(
            collective_id=0, has_side_effects=True, vmem_limit_bytes=48 * 1024 * 1024
        ),
    )(
        embeddings,
        assign.reshape(1, ROWS),
        owner.reshape(1, CLUSTERS),
        send_count,
        send_index[0],
    )


def body(embeddings, assign, owner, send_count, send_index):
    arguments = (embeddings, assign, owner, send_count, send_index)
    results, fault = routed(*arguments)
    results = lax.cond(fault[0, 0] != 0, lambda: jnp.stack(general(*arguments)), lambda: results)
    return results[0], results[1]


def solution(mesh):
    placed = (
        P(("grp", "blk"), None),
        P(("grp", "blk")),
        P(),
        P(("grp", "blk"), None),
        P(("grp", "blk"), None, None),
    )
    return jax.shard_map(
        body,
        mesh=mesh,
        in_specs=placed,
        out_specs=(P(("grp", "blk")), P(("grp", "blk"))),
        check_vma=False,
    )
```

```python
import functools

import jax
import jax.numpy as jnp
from jax import lax
from jax.experimental import pallas as pl
from jax.experimental.pallas import tpu as pltpu
from jax.sharding import PartitionSpec as P

EPSILON = 1e-06
F32 = jnp.float32
BF16 = jnp.bfloat16

CHIPS = 64
ROWS = 512
WIDTH = 768
CLUSTERS = 128
GROUPS = 16
CAP = 64
BASE = 16
HALF = WIDTH // 2
LINES = 16
DEPTH = 4
POOL = 8
PARTS = ((0, 32, 384), (32, 24, 256), (56, 16, 128))
TOTAL = 72
HELD = 768
STARTS = (0, 384, 640)
LAST = len(PARTS) - 1
NONE = 1e30


def normalize(values):
    widened = values.astype(F32)
    return widened * lax.rsqrt(jnp.sum(widened * widened, axis=1, keepdims=True) + EPSILON)


def general(embeddings, assign, owner, send_count, send_index):
    rows_local = embeddings.shape[0]
    feature_width = embeddings.shape[1]
    groups = lax.axis_size("grp")
    clusters = owner.shape[0]
    capacity = send_index.shape[2]
    slot_total = groups * capacity
    unit_rows = normalize(embeddings)
    unit_low = unit_rows.astype(BF16)
    counts = send_count[0]
    listed = send_index[0]
    live_slot = jnp.arange(capacity, dtype=jnp.int32)[None, :] < counts[:, None]
    listed_cluster = assign[listed]
    owned_here = owner[listed_cluster] == jnp.arange(groups, dtype=jnp.int32)[:, None]
    kept_slot = live_slot & owned_here
    out_cluster = jnp.where(kept_slot, listed_cluster, -1)
    out_tag = jnp.where(kept_slot, lax.axis_index(("grp", "blk")) * rows_local + listed, -1)
    out_vector = unit_low[listed.reshape(-1)].reshape(groups, capacity, feature_width)
    got_vector, got_cluster, got_tag = (
        lax.all_to_all(out_vector, "grp", split_axis=0, concat_axis=0, tiled=True),
        lax.all_to_all(out_cluster, "grp", split_axis=0, concat_axis=0, tiled=True),
        lax.all_to_all(out_tag, "grp", split_axis=0, concat_axis=0, tiled=True),
    )
    own_vector = got_vector.reshape(slot_total, feature_width)
    own_cluster = got_cluster.reshape(slot_total)
    own_tag = got_tag.reshape(slot_total)

    def tile_best(current, shard_piece):
        other_vector, other_cluster, other_tag = shard_piece
        scores = jnp.einsum("id,jd->ij", own_vector, other_vector, preferred_element_type=F32)
        matched = (
            (own_cluster[:, None] == other_cluster[None, :])
            & (other_cluster[None, :] >= 0)
            & (own_tag[:, None] != other_tag[None, :])
        )
        return jnp.maximum(current, jnp.max(jnp.where(matched, scores, -1.0), axis=1))

    other_vector = lax.all_gather(own_vector, "blk", axis=0, tiled=True)
    other_cluster = lax.all_gather(own_cluster, "blk", axis=0, tiled=True)
    other_tag = lax.all_gather(own_tag, "blk", axis=0, tiled=True)
    length = other_vector.shape[0]
    number = length // slot_total
    stacked = (
        other_vector.reshape(number, slot_total, feature_width),
        other_cluster.reshape(number, slot_total),
        other_tag.reshape(number, slot_total),
    )

    def scan_step(carry, single):
        return (tile_best(carry, single), None)

    result, unused = lax.scan(scan_step, jnp.full((slot_total,), -1.0, F32), stacked)
    target = jnp.where(live_slot, listed, rows_local).reshape(-1)
    partial_sum = jax.ops.segment_sum(unit_rows, assign, num_segments=clusters)
    centre = normalize(lax.psum(partial_sum, ("grp", "blk")))
    nearness = jnp.sum(unit_low.astype(F32) * centre[assign], axis=1)
    returned = lax.all_to_all(
        result.reshape(groups, capacity), "grp", split_axis=0, concat_axis=0, tiled=True
    )
    has_entry = (
        jnp.zeros((rows_local,), jnp.int32)
        .at[target]
        .max(kept_slot.astype(jnp.int32).reshape(-1), mode="drop")
    )
    centroid_cos = jnp.where(has_entry > 0, nearness, 0.0)
    max_sim = jnp.full((rows_local,), -1.0, F32).at[target].max(returned.reshape(-1), mode="drop")
    return (max_sim, centroid_cos)


def iota(shape, axis):
    return lax.broadcasted_iota(jnp.int32, shape, axis)


def down(values):
    return jnp.sum(values, axis=0, keepdims=True)


def across(values):
    return jnp.sum(values, axis=1, keepdims=True)


def pick(mask, values):
    return jnp.where(mask, values, 0.0)


def as_column(row):
    size = row.shape[1]
    return across(pick(iota((size, size), 0) == iota((size, size), 1), row))


def as_row(column):
    size = column.shape[0]
    return down(pick(iota((size, size), 0) == iota((size, size), 1), column))


def dot(a, b):
    return jnp.dot(a, b, preferred_element_type=F32)


def dot_rows(a, b):
    return lax.dot_general(a, b, (((1,), (1,)), ((), ())), preferred_element_type=F32)


def onehot(mask):
    return jnp.where(mask, 1.0, 0.0).astype(BF16)


def thirds(values):
    first = values.astype(BF16).astype(F32)
    rest = values - first
    second = rest.astype(BF16).astype(F32)
    third = (rest - second).astype(BF16).astype(F32)
    return first, second, third


def rank_groups(count_ref):
    count_row = count_ref[...].astype(F32)
    count_column = as_column(count_row)
    sub, lane = iota((GROUPS, 128), 0), iota((GROUPS, 128), 1)
    count_lanes = down(pick(sub == lane, count_column))
    ahead = (count_column > count_lanes) | ((count_column == count_lanes) & (sub < lane))
    rank = down(jnp.where(ahead, 1.0, 0.0))
    return jnp.where(iota((1, 128), 1) < GROUPS, rank, 0.0), count_column


def place_documents(assign_ref, owner_ref, rank):
    owner_row = owner_ref[...].astype(F32)
    owner_column = as_column(owner_row)
    sub, lane = iota((CLUSTERS, CLUSTERS), 0), iota((CLUSTERS, CLUSTERS), 1)
    within = across(jnp.where((owner_column == owner_row) & (lane < sub), 1.0, 0.0))
    group_rank = across(pick(owner_column == lane.astype(F32), rank))
    place_column = group_rank * (CLUSTERS // GROUPS) + within
    member = iota((CLUSTERS, ROWS), 0) == assign_ref[...]
    place = down(pick(member, place_column))
    group = down(pick(member, owner_column))
    order = iota((CLUSTERS, ROWS), 0).astype(F32)
    at_place = order == place
    earlier = onehot(iota((ROWS, ROWS), 0) < iota((ROWS, ROWS), 1))
    before = dot(onehot(at_place), earlier)
    slot = down(pick(at_place, before))
    count_column = across(jnp.where(at_place, 1.0, 0.0))
    partner_count = down(pick(order == (CLUSTERS - 1) - place, count_column))
    slot = slot + jnp.where(place >= CHIPS, partner_count, 0.0)
    chip = jnp.minimum(place, (CLUSTERS - 1) - place)
    return group, chip.astype(jnp.int32), slot.astype(jnp.int32), as_row(count_column)


def missing_documents(index_ref, count_column, group):
    listed = index_ref[...]
    live = iota((GROUPS, CAP), 1).astype(F32) < count_column
    eye = onehot(iota((CAP, CAP), 0) == iota((CAP, CAP), 1))
    high = dot_rows(eye, jnp.where(live, listed >> 4, 0).astype(F32).astype(BF16))
    low = dot_rows(eye, jnp.where(live, listed & 15, 0).astype(F32).astype(BF16))
    alive = dot_rows(eye, onehot(live))
    slots = jnp.where(alive > 0.5, high * 16.0 + low, -1.0)
    document = iota((1, ROWS), 1).astype(F32)
    lane = iota((CAP, GROUPS), 1)

    def count(g, hits):
        column = across(pick(lane == g, slots))
        wanted = jnp.where(group == g.astype(F32), document, -2.0)
        return hits + jnp.where(column == wanted, 1.0, 0.0)

    hits = lax.fori_loop(0, GROUPS, count, jnp.zeros((CAP, ROWS), F32))
    return across(jnp.where(down(hits) > 0.5, 0.0, 1.0))


def send_order():
    order = []
    for step in range(CHIPS):
        high, middle, low = step // 16, (step // 4) % 4, step % 4
        order.append((low, (middle + low) % 4, (high + middle + low) % 4))
    near = [shift for shift in order if sum(min(d, 4 - d) for d in shift) <= 1] + [(2, 0, 0)]
    near.sort(key=lambda shift: -sum(min(d, 4 - d) for d in shift))
    return [shift for shift in order if shift not in near] + near


ORDER = send_order()
SELF = CHIPS - 1


def step_to(dx, dy, dz):
    shift = (dx & 3) * 16 + (dy & 3) * 4 + (dz & 3)
    step = jnp.full(shift.shape, SELF, jnp.int32)
    for number, (x, y, z) in enumerate(ORDER[:SELF]):
        step = jnp.where(shift == x * 16 + y * 4 + z, number, step)
    return step


def in_part(step, part):
    begin, steps, _ = PARTS[part]
    return (step >= begin) & (step < begin + steps)


def chip_places():
    sub, lane = iota((CLUSTERS, CLUSTERS), 0), iota((CLUSTERS, CLUSTERS), 1)
    return onehot((sub == lane) | (sub == (CLUSTERS - 1) - lane))


def excess(totals):
    lane = iota(totals.shape, 1)
    return jnp.where(lane < CHIPS, jnp.maximum(totals - BASE, 0.0), 0.0)


def receive_plan(table, rank, my_x, my_y, my_z):
    chip = my_x * 16 + my_y * 4 + my_z
    heads = table.astype(jnp.int32)
    counts = (heads & 1023).astype(F32)
    differ = jnp.where((heads >> 10).astype(F32) != rank, 1.0, 0.0)
    fault = across(down(differ))
    both = dot(counts.astype(BF16), chip_places())
    over = excess(both)
    lanes = iota((CHIPS, CLUSTERS), 1)
    sender = iota((CHIPS, 1), 0)
    source, target = iota((CHIPS, CHIPS), 0), iota((CHIPS, CHIPS), 1)

    same_line = (source >> 2) == (target >> 2)
    over_total = across(over)
    over_row = as_row(over_total)
    line_start = across(pick(same_line & (target < source), over_row))
    line_total = across(pick(same_line, over_row))
    fault = fault + down(jnp.where(line_total > POOL, 1.0, 0.0))
    start = line_start + across(pick(lanes < chip, over))
    number = across(pick(lanes == chip, over))

    to_chip = iota((1, CLUSTERS), 1)
    route = step_to(
        (to_chip >> 4) - (sender >> 4), ((to_chip >> 2) & 3) - ((sender >> 2) & 3), (to_chip & 3) - (sender & 3)
    )
    based = jnp.where(lanes < CHIPS, jnp.minimum(both, float(BASE)), 0.0)
    for part, (_, _, room) in enumerate(PARTS):
        held = down(pick(in_part(route, part), based))
        if part == LAST:
            held = held + down(over)
        fault = fault + across(jnp.where(held > room, 1.0, 0.0))

    first = across(pick(lanes == chip, counts))
    second = across(pick(lanes == (CLUSTERS - 1) - chip, counts))
    place = (lanes & (POOL - 1)).astype(F32) - start
    mine = ((sender >> 2) == (lanes >> 3)) & (place >= 0.0) & (place < number)
    over_first = down(jnp.where(mine & (place + BASE < first), 1.0, 0.0))
    over_second = down(jnp.where(mine & (place + BASE >= first), 1.0, 0.0))
    over_first_total, over_second_total = across(over_first), across(over_second)
    earlier = onehot(iota((CLUSTERS, CLUSTERS), 0) < iota((CLUSTERS, CLUSTERS), 1))
    sub = iota((16, CLUSTERS), 0)
    before = dot((pick(sub == 0, over_first) + pick(sub == 1, over_second)).astype(BF16), earlier)

    base_first = jnp.minimum(first, float(BASE))
    base_second = jnp.minimum(first + second, float(BASE)) - base_first
    first_row, second_row = as_row(base_first), as_row(base_second)

    def my_step(other):
        return step_to(my_x - (other >> 4), my_y - ((other >> 2) & 3), my_z - (other & 3))

    step_column, step_row = my_step(sender), my_step(iota((1, CHIPS), 1))
    plans = []
    ends = []
    for part, (begin, steps, _) in enumerate(PARTS):
        inside = in_part(step_column, part)
        ahead = (target < source) & in_part(step_row, part)
        first_total = down(pick(inside, base_first))
        second_total = down(pick(inside, base_second))
        last = part == LAST
        first_end = first_total + over_first_total if last else first_total
        first_start = across(pick(ahead, first_row))
        second_start = across(pick(ahead, second_row)) + first_end
        spread = step_column - begin == (iota((CHIPS, steps * BASE), 1) >> 4)
        head, tail, head_start, tail_start = [
            down(pick(spread, column)) for column in (base_first, base_second, first_start, second_start)
        ]
        slot = (iota((1, steps * BASE), 1) & (BASE - 1)).astype(F32)
        later = jnp.where(slot < head + tail, tail_start + (slot - head), -1.0)
        plan = jnp.where(slot < head, head_start + slot, later)
        held_end = first_end + second_total
        if last:
            over_row_of = jnp.where(over_second > 0.5, held_end + before[1:2], -1.0)
            over_row_of = jnp.where(over_first > 0.5, first_total + before[0:1], over_row_of)
            plan = jnp.concatenate([plan[:, : steps * BASE - CLUSTERS], over_row_of], axis=1)
            held_end = held_end + over_second_total
        plans.append(plan)
        ends.append((first_end, held_end))
    return plans, ends, fault


def kernel(
    x_hbm, assign_hbm, owner_hbm, count_hbm, index_hbm,
    out_ref, fault_ref,
    x_ref, assign_ref, owner_ref, count_ref, index_ref,
    send, got, heads, own_over, line_over, send_over, got_over, pick_0, pick_1, pick_2,
    mine, theirs, facts, sums, their_sums, back, returned,
    load_sem, send_sem, recv_sem,
):
    grp, blk = lax.axis_index("grp"), lax.axis_index("blk")
    my_x, my_y, my_z, core = grp // 4, grp % 4, blk // 2, blk % 2
    my_chip = grp * 4 + my_z
    picks = (pick_0, pick_1, pick_2)
    along_x = [((my_x + d) % 4) * 4 for d in range(4)]
    along_y = [(my_y + d) % 4 for d in range(4)]
    along_z = [((my_z + d) % 4) * 2 + core for d in range(4)]
    other_core = {"grp": grp, "blk": my_z * 2 + (1 - core)}

    def device_at(step, sign):
        dx, dy, dz = [(sign * d) % 4 for d in ORDER[step]]
        return {"grp": along_x[dx] + along_y[dy], "blk": along_z[dz]}

    def remote(source, target, number, device):
        return pltpu.make_async_remote_copy(
            src_ref=source,
            dst_ref=target,
            send_sem=send_sem.at[number],
            recv_sem=recv_sem.at[number],
            device_id=device,
            device_id_type=pl.DeviceIdType.MESH,
        )

    def await_blocks(ref, number, semaphore):
        block = ref.at[pl.ds(0, number)]
        pltpu.make_async_copy(block, block, semaphore).wait()

    HEAD_Z, HEAD_XY, LINE, OVER, FACTS, SUMS, BACK, SWAP, PART = 0, 1, 2, 3, 4, 5, 6, 7, 10
    messages = [min(begin + steps, SELF) - begin for begin, steps, _ in PARTS]

    loads = [
        pltpu.make_async_copy(source, target, load_sem.at[number])
        for number, (source, target) in enumerate(
            (
                (assign_hbm, assign_ref),
                (owner_hbm, owner_ref),
                (count_hbm, count_ref),
                (index_hbm, index_ref),
                (x_hbm, x_ref),
            )
        )
    ]
    for load in loads:
        load.start()
    barrier = pltpu.get_barrier_semaphore()
    for device in [device_at(step, 1) for step in range(SELF)] + [other_core]:
        pl.semaphore_signal(barrier, inc=1, device_id=device, device_id_type=pl.DeviceIdType.MESH)
    for load in loads[:-1]:
        load.wait()

    rank, count_column = rank_groups(count_ref)
    group, chip, slot, place_counts = place_documents(assign_ref, owner_ref, rank)
    step_of = step_to((chip >> 4) - my_x, ((chip >> 2) & 3) - my_y, (chip & 3) - my_z)
    in_base = slot < BASE
    send_slot = jnp.where(in_base, step_of * BASE + slot, -1)
    heads[my_chip] = place_counts + 1024.0 * rank
    loads[-1].wait()

    def pack(first, stop):
        slots = iota(((stop - first) * BASE, ROWS), 0) + first * BASE
        rows = dot(onehot(slots == send_slot), x_ref[...]).astype(BF16)
        send[pl.ds(first, stop - first)] = rows.reshape(stop - first, BASE, WIDTH)

    def post(first, stop):
        for step in range(first, min(stop, SELF)):
            number = max(part for part in range(len(PARTS)) if PARTS[part][0] <= step)
            remote(send.at[step], got.at[step], PART + number, device_at(step, 1)).start()

    pack(0, 24)
    pl.semaphore_wait(barrier, CHIPS)
    for d in range(1, DEPTH):
        device = {"grp": grp, "blk": along_z[d]}
        block = heads.at[pl.ds(my_chip, 1)]
        remote(block, block, HEAD_Z, device).start()
    post(0, 8)
    place_counts_16 = place_counts + jnp.zeros((16, CLUSTERS), F32)
    own_excess = excess(dot(place_counts_16.astype(BF16), chip_places())[0:1])
    eye = iota((CHIPS, CLUSTERS), 0) == iota((CHIPS, CLUSTERS), 1)
    excess_column = across(pick(eye, own_excess))
    over_slot = down(pick(iota((CHIPS, ROWS), 0) < chip, excess_column)).astype(jnp.int32) + (slot - BASE)
    over_slot = jnp.where(in_base, -1, over_slot)
    own_over[...] = dot(onehot(iota((BASE, ROWS), 0) == over_slot), x_ref[...]).astype(BF16)
    line_over[my_z] = own_over[...]
    for d in range(1, DEPTH):
        remote(own_over, line_over.at[my_z], LINE, {"grp": grp, "blk": along_z[d]}).start()
    post(8, 24)

    await_blocks(heads, DEPTH - 1, recv_sem.at[HEAD_Z])
    line_heads = heads[pl.ds(grp * DEPTH, DEPTH)].reshape(DEPTH, CLUSTERS)
    line_counts = (line_heads.astype(jnp.int32) & 1023).astype(F32).astype(BF16)
    line_total = across(excess(dot(line_counts, chip_places())))
    depth = iota((DEPTH, 1), 0)
    line_start = jnp.zeros((DEPTH, 1), F32)
    for d in range(DEPTH - 1):
        line_start = line_start + pick(depth > d, line_total[d : d + 1])
    my_start = down(pick(depth == my_z, line_start))
    at = depth == (iota((DEPTH, DEPTH * BASE), 1) >> 4)
    begin = down(pick(at, line_start))
    number = down(pick(at, line_total))
    order = (iota((1, DEPTH * BASE), 1) & (BASE - 1)).astype(F32)
    order = jnp.where(order < number, begin + order, -1.0)
    rows = iota((2 * POOL, DEPTH * BASE), 0).astype(F32)
    await_blocks(line_over, DEPTH - 1, recv_sem.at[LINE])
    blocks = line_over[...].reshape(DEPTH * BASE, WIDTH)
    left = dot(onehot((rows == order) & (rows < POOL)), blocks[:, :HALF])
    right = dot(onehot((rows - POOL == order) & (rows >= POOL)), blocks[:, HALF:])
    send_over[...] = (left + right).astype(BF16)
    got_over[grp] = send_over[...]
    for step in range(1, LINES):
        low, middle = step % 4, step // 4
        device = {"grp": along_x[low] + along_y[(middle + low) % 4], "blk": blk}
        block = heads.at[pl.ds(grp * DEPTH, DEPTH)]
        remote(block, block, HEAD_XY, device).start()
        remote(send_over, got_over.at[grp], OVER, device).start()
    pack(24, 48)
    post(24, 48)
    pack(48, CHIPS)
    post(48, CHIPS)
    got[SELF] = send[SELF]

    await_blocks(heads, CHIPS - DEPTH, recv_sem.at[HEAD_XY])
    table = heads[...].reshape(CHIPS, CLUSTERS)
    plans, ends, fault = receive_plan(table, rank, my_x, my_y, my_z)

    missing = missing_documents(index_ref, count_column, group)
    row = iota((8, 128), 0)
    told = pick(row == 6, rank) + pick(row == 7, jnp.where(iota((1, 128), 1) == 0, fault, missing))
    for part, (first_end, held_end) in enumerate(ends):
        told = told + pick(row == part, first_end) + pick(row == 3 + part, held_end)
        picks[part][...] = onehot(iota(picks[part].shape, 0).astype(F32) == plans[part])
    facts[0] = told
    swap_facts = remote(facts.at[0], facts.at[1], FACTS, other_core)
    swap_facts.start()

    best = [jnp.full((1, room), -1.0, F32) for _, _, room in PARTS]
    their_ends = []
    totals = [jnp.zeros((1, WIDTH), F32), jnp.zeros((1, WIDTH), F32)]
    swaps = []

    def window(part):
        return pl.ds(STARTS[part], PARTS[part][2])

    def compare(keys, key_part, query_part, key_ends, itself, more=0):
        room = PARTS[key_part][2]
        scores = dot_rows(keys[pl.ds(STARTS[key_part], room + more)], mine[window(query_part)])
        rest, scores = scores[room:], scores[:room]
        first, held = key_ends[key_part]
        key_number = iota((PARTS[key_part][2], 1), 0).astype(F32)
        query_number = iota((1, PARTS[query_part][2]), 1).astype(F32)
        kind = jnp.where(key_number < first, 0.0, jnp.where(key_number < held, 1.0, 2.0))
        matched = kind == jnp.where(query_number < ends[query_part][0], 0.0, 1.0)
        if itself and key_part == query_part:
            matched = matched & (key_number != query_number)
        scores = jnp.max(jnp.where(matched, scores, -1.0), axis=0, keepdims=True)
        best[query_part] = jnp.maximum(best[query_part], scores)
        return rest

    for part, (begin, steps, room) in enumerate(PARTS):
        if part == LAST:
            await_blocks(got_over, LINES - 1, recv_sem.at[OVER])
            halves = got_over[...].reshape(LINES * 2 * POOL, HALF)
            shape = (LINES * POOL, LINES * 2 * POOL)
            to, at = iota(shape, 0), iota(shape, 1)
            same = ((to >> 3) == (at >> 4)) & ((to & 7) == (at & 7))
            left = dot(onehot(same & ((at & POOL) == 0)), halves)
            right = dot(onehot(same & ((at & POOL) != 0)), halves)
            whole = jnp.concatenate([left, right], axis=1).astype(BF16)
            got[pl.ds(CHIPS, TOTAL - CHIPS)] = whole.reshape(TOTAL - CHIPS, BASE, WIDTH)
        await_blocks(got, messages[part], recv_sem.at[PART + part])
        rows = dot(picks[part][...], got[pl.ds(begin, steps)].reshape(steps * BASE, WIDTH))
        unit = rows * lax.rsqrt(across(rows * rows) + EPSILON)
        mine[window(part)] = unit.astype(BF16)
        swap = remote(mine.at[window(part)], theirs.at[window(part)], SWAP + part, other_core)
        swap.start()
        swaps.append(swap)
        is_first = iota((room, 1), 0).astype(F32) < ends[part][0]
        totals[0] = totals[0] + down(pick(is_first, unit))
        totals[1] = totals[1] + down(jnp.where(is_first, 0.0, unit))
        if part == LAST:
            row = iota((8, WIDTH), 0)
            sums[...] = pick(row == 0, totals[0]) + pick(row == 1, totals[1])
            swap_sums = remote(sums, their_sums, SUMS, other_core)
            swap_sums.start()
        if part == 0:
            compare(mine, 0, 0, ends, True)
            swap_facts.wait()
            their_told = facts[1]
            for number in range(len(PARTS)):
                their_ends.append((their_told[number : number + 1, 0:1], their_told[3 + number : 4 + number, 0:1]))
            swap.wait()
            compare(theirs, 0, 0, their_ends, False)
    for part in range(1, len(PARTS)):
        for other in range(part + 1):
            compare(mine, part, other, ends, True)
            if other != part:
                compare(mine, other, part, ends, True)
        compare(theirs, 0, part, their_ends, False)
    swaps[1].wait()
    for part in range(len(PARTS)):
        compare(theirs, 1, part, their_ends, False)

    swap_sums.wait()
    total = sums[...] + their_sums[...]
    terms = jnp.concatenate(thirds(total) + (jnp.zeros((8, WIDTH), F32),), axis=0)
    theirs[pl.ds(HELD, 32)] = terms.astype(BF16)
    scale = lax.rsqrt(across(total * total) + EPSILON)
    swaps[LAST].wait()
    near = [compare(theirs, LAST, other, their_ends, False, 32) for other in range(len(PARTS))]

    poison = missing + their_told[7:8, 1:2] > 0.5
    tiles = CHIPS * BASE // 128
    for part, (begin, steps, room) in enumerate(PARTS):
        row = iota((8, room), 0)
        query_number = iota((1, room), 1).astype(F32)
        some = (near[part][0:8] + near[part][8:16] + near[part][16:24]) * scale
        some = jnp.where(query_number < ends[part][0], some[0:1], some[1:2])
        values = jnp.zeros((8, room), F32)
        for number, term in enumerate(thirds(best[part]) + thirds(some)):
            values = jnp.where(row == number, term, values)
        out = dot(values.astype(BF16), picks[part][...])
        for kind in range(2):
            line = out[3 * kind : 3 * kind + 1] + out[3 * kind + 1 : 3 * kind + 2] + out[3 * kind + 2 : 3 * kind + 3]
            line = jnp.where(poison, NONE, line)
            for tile in range(steps * BASE // 128):
                piece = line[:, tile * 128 : (tile + 1) * 128]
                to = begin * BASE // 128 + tile
                if to < tiles:
                    back[to, kind : kind + 1, :] = piece
                else:
                    for each in range(tiles):
                        back[each, 2 + kind : 3 + kind, :] = piece
    returned[SELF] = back[SELF // 8]
    for step in range(SELF):
        remote(back.at[step // 8], returned.at[step], BACK, device_at(step, -1)).start()

    differ = across(jnp.where(their_told[6:7] != rank, 1.0, 0.0))
    fault = fault + their_told[7:8, 0:1] + differ
    chosen = onehot(iota((CHIPS, ROWS), 0) == step_of)
    sub = iota((128, ROWS), 0)
    at_base = (sub == (step_of & 7) * BASE + slot) & in_base
    at_over = (sub == grp * POOL + my_start.astype(jnp.int32) + over_slot) & (~in_base)

    await_blocks(returned, CHIPS - 1, recv_sem.at[BACK])
    found = []
    for number in range(4):
        line = returned[:, number, :]
        if number == 0:
            poisoned = across(down(jnp.where(line > 0.5 * NONE, 1.0, 0.0)))
            fault_ref[...] = jnp.where(fault + poisoned > 0.5, 1, 0) + jnp.zeros((1, 128), jnp.int32)
        terms = jnp.concatenate(thirds(line), axis=1).astype(BF16)
        out = lax.dot_general(terms, chosen, (((0,), (0,)), ((), ())), preferred_element_type=F32)
        found.append(out[0:128] + out[128:256] + out[256:384])
    out_ref[0:1] = down(pick(at_base, found[0]) + pick(at_over, found[2]))
    out_ref[1:2] = down(pick(at_base, found[1]) + pick(at_over, found[3]))

    await_blocks(heads, DEPTH - 1, send_sem.at[HEAD_Z])
    await_blocks(heads, CHIPS - DEPTH, send_sem.at[HEAD_XY])
    await_blocks(line_over, DEPTH - 1, send_sem.at[LINE])
    await_blocks(got_over, LINES - 1, send_sem.at[OVER])
    await_blocks(returned, CHIPS - 1, send_sem.at[BACK])
    for part in range(len(PARTS)):
        await_blocks(got, messages[part], send_sem.at[PART + part])


def routed(embeddings, assign, owner, send_count, send_index):
    return pl.pallas_call(
        kernel,
        out_shape=(
            jax.ShapeDtypeStruct((2, ROWS), F32),
            jax.ShapeDtypeStruct((1, 128), jnp.int32),
        ),
        in_specs=[pl.BlockSpec(memory_space=pl.ANY)] * 5,
        out_specs=(pl.BlockSpec(memory_space=pltpu.VMEM),) * 2,
        scratch_shapes=[
            pltpu.VMEM((ROWS, WIDTH), BF16),
            pltpu.VMEM((1, ROWS), jnp.int32),
            pltpu.VMEM((1, CLUSTERS), jnp.int32),
            pltpu.VMEM((1, GROUPS), jnp.int32),
            pltpu.VMEM((GROUPS, CAP), jnp.int32),
            pltpu.VMEM((CHIPS, BASE, WIDTH), BF16),
            pltpu.VMEM((TOTAL, BASE, WIDTH), BF16),
            pltpu.VMEM((CHIPS, 1, 128), F32),
            pltpu.VMEM((BASE, WIDTH), BF16),
            pltpu.VMEM((DEPTH, BASE, WIDTH), BF16),
            pltpu.VMEM((2 * POOL, HALF), BF16),
            pltpu.VMEM((LINES, 2 * POOL, HALF), BF16),
            *[pltpu.VMEM((room, steps * BASE), BF16) for _, steps, room in PARTS],
            pltpu.VMEM((HELD, WIDTH), BF16),
            pltpu.VMEM((HELD + 32, WIDTH), BF16),
            pltpu.VMEM((2, 8, 128), F32),
            pltpu.VMEM((8, WIDTH), F32),
            pltpu.VMEM((8, WIDTH), F32),
            pltpu.VMEM((CHIPS * BASE // 128, 4, 128), F32),
            pltpu.VMEM((CHIPS, 4, 128), F32),
            pltpu.SemaphoreType.DMA((5,)),
            pltpu.SemaphoreType.DMA((13,)),
            pltpu.SemaphoreType.DMA((13,)),
        ],
        compiler_params=pltpu.CompilerParams(
            collective_id=0, has_side_effects=True, vmem_limit_bytes=48 * 1024 * 1024
        ),
    )(
        embeddings,
        assign.reshape(1, ROWS),
        owner.reshape(1, CLUSTERS),
        send_count,
        send_index[0],
    )


def body(embeddings, assign, owner, send_count, send_index):
    arguments = (embeddings, assign, owner, send_count, send_index)
    results, fault = routed(*arguments)
    results = lax.cond(fault[0, 0] != 0, lambda: jnp.stack(general(*arguments)), lambda: results)
    return results[0], results[1]


def solution(mesh):
    placed = (
        P(("grp", "blk"), None),
        P(("grp", "blk")),
        P(),
        P(("grp", "blk"), None),
        P(("grp", "blk"), None, None),
    )
    return jax.shard_map(
        body,
        mesh=mesh,
        in_specs=placed,
        out_specs=(P(("grp", "blk")), P(("grp", "blk"))),
        check_vma=False,
    )
```

```python
import functools

import jax
import jax.numpy as jnp
from jax import lax
from jax.experimental import pallas as pl
from jax.experimental.pallas import tpu as pltpu
from jax.sharding import PartitionSpec as P

EPSILON = 1e-06
F32 = jnp.float32
BF16 = jnp.bfloat16

CHIPS = 64
ROWS = 512
WIDTH = 768
CLUSTERS = 128
GROUPS = 16
CAP = 64
BASE = 16
HALF = WIDTH // 2
LINES = 16
DEPTH = 4
POOL = 8
PARTS = ((0, 32, 384), (32, 24, 256), (56, 16, 128))
BATCH = 8
TOTAL = 72
HELD = 768
STARTS = (0, 384, 640)
LAST = len(PARTS) - 1
NONE = 1e30


def normalize(values):
    widened = values.astype(F32)
    return widened * lax.rsqrt(jnp.sum(widened * widened, axis=1, keepdims=True) + EPSILON)


def general(embeddings, assign, owner, send_count, send_index):
    rows_local = embeddings.shape[0]
    feature_width = embeddings.shape[1]
    groups = lax.axis_size("grp")
    clusters = owner.shape[0]
    capacity = send_index.shape[2]
    slot_total = groups * capacity
    unit_rows = normalize(embeddings)
    unit_low = unit_rows.astype(BF16)
    counts = send_count[0]
    listed = send_index[0]
    live_slot = jnp.arange(capacity, dtype=jnp.int32)[None, :] < counts[:, None]
    listed_cluster = assign[listed]
    owned_here = owner[listed_cluster] == jnp.arange(groups, dtype=jnp.int32)[:, None]
    kept_slot = live_slot & owned_here
    out_cluster = jnp.where(kept_slot, listed_cluster, -1)
    out_tag = jnp.where(kept_slot, lax.axis_index(("grp", "blk")) * rows_local + listed, -1)
    out_vector = unit_low[listed.reshape(-1)].reshape(groups, capacity, feature_width)
    got_vector, got_cluster, got_tag = (
        lax.all_to_all(out_vector, "grp", split_axis=0, concat_axis=0, tiled=True),
        lax.all_to_all(out_cluster, "grp", split_axis=0, concat_axis=0, tiled=True),
        lax.all_to_all(out_tag, "grp", split_axis=0, concat_axis=0, tiled=True),
    )
    own_vector = got_vector.reshape(slot_total, feature_width)
    own_cluster = got_cluster.reshape(slot_total)
    own_tag = got_tag.reshape(slot_total)

    def tile_best(current, shard_piece):
        other_vector, other_cluster, other_tag = shard_piece
        scores = jnp.einsum("id,jd->ij", own_vector, other_vector, preferred_element_type=F32)
        matched = (
            (own_cluster[:, None] == other_cluster[None, :])
            & (other_cluster[None, :] >= 0)
            & (own_tag[:, None] != other_tag[None, :])
        )
        return jnp.maximum(current, jnp.max(jnp.where(matched, scores, -1.0), axis=1))

    other_vector = lax.all_gather(own_vector, "blk", axis=0, tiled=True)
    other_cluster = lax.all_gather(own_cluster, "blk", axis=0, tiled=True)
    other_tag = lax.all_gather(own_tag, "blk", axis=0, tiled=True)
    length = other_vector.shape[0]
    number = length // slot_total
    stacked = (
        other_vector.reshape(number, slot_total, feature_width),
        other_cluster.reshape(number, slot_total),
        other_tag.reshape(number, slot_total),
    )

    def scan_step(carry, single):
        return (tile_best(carry, single), None)

    result, unused = lax.scan(scan_step, jnp.full((slot_total,), -1.0, F32), stacked)
    target = jnp.where(live_slot, listed, rows_local).reshape(-1)
    partial_sum = jax.ops.segment_sum(unit_rows, assign, num_segments=clusters)
    centre = normalize(lax.psum(partial_sum, ("grp", "blk")))
    nearness = jnp.sum(unit_low.astype(F32) * centre[assign], axis=1)
    returned = lax.all_to_all(
        result.reshape(groups, capacity), "grp", split_axis=0, concat_axis=0, tiled=True
    )
    has_entry = (
        jnp.zeros((rows_local,), jnp.int32)
        .at[target]
        .max(kept_slot.astype(jnp.int32).reshape(-1), mode="drop")
    )
    centroid_cos = jnp.where(has_entry > 0, nearness, 0.0)
    max_sim = jnp.full((rows_local,), -1.0, F32).at[target].max(returned.reshape(-1), mode="drop")
    return (max_sim, centroid_cos)


def iota(shape, axis):
    return lax.broadcasted_iota(jnp.int32, shape, axis)


def down(values):
    return jnp.sum(values, axis=0, keepdims=True)


def across(values):
    return jnp.sum(values, axis=1, keepdims=True)


def pick(mask, values):
    return jnp.where(mask, values, 0.0)


def as_column(row):
    size = row.shape[1]
    return across(pick(iota((size, size), 0) == iota((size, size), 1), row))


def as_row(column):
    size = column.shape[0]
    return down(pick(iota((size, size), 0) == iota((size, size), 1), column))


def dot(a, b):
    return jnp.dot(a, b, preferred_element_type=F32)


def dot_rows(a, b):
    return lax.dot_general(a, b, (((1,), (1,)), ((), ())), preferred_element_type=F32)


def onehot(mask):
    return jnp.where(mask, 1.0, 0.0).astype(BF16)


def thirds(values):
    first = values.astype(BF16).astype(F32)
    rest = values - first
    second = rest.astype(BF16).astype(F32)
    third = (rest - second).astype(BF16).astype(F32)
    return first, second, third


def rank_groups(count_ref):
    count_row = count_ref[...].astype(F32)
    count_column = as_column(count_row)
    sub, lane = iota((GROUPS, 128), 0), iota((GROUPS, 128), 1)
    count_lanes = down(pick(sub == lane, count_column))
    ahead = (count_column > count_lanes) | ((count_column == count_lanes) & (sub < lane))
    rank = down(jnp.where(ahead, 1.0, 0.0))
    return jnp.where(iota((1, 128), 1) < GROUPS, rank, 0.0), count_column


def place_documents(assign_ref, owner_ref, rank):
    owner_row = owner_ref[...].astype(F32)
    owner_column = as_column(owner_row)
    sub, lane = iota((CLUSTERS, CLUSTERS), 0), iota((CLUSTERS, CLUSTERS), 1)
    within = across(jnp.where((owner_column == owner_row) & (lane < sub), 1.0, 0.0))
    group_rank = across(pick(owner_column == lane.astype(F32), rank))
    place_column = group_rank * (CLUSTERS // GROUPS) + within
    member = iota((CLUSTERS, ROWS), 0) == assign_ref[...]
    place = down(pick(member, place_column))
    group = down(pick(member, owner_column))
    order = iota((CLUSTERS, ROWS), 0).astype(F32)
    at_place = order == place
    earlier = onehot(iota((ROWS, ROWS), 0) < iota((ROWS, ROWS), 1))
    before = dot(onehot(at_place), earlier)
    slot = down(pick(at_place, before))
    count_column = across(jnp.where(at_place, 1.0, 0.0))
    partner_count = down(pick(order == (CLUSTERS - 1) - place, count_column))
    slot = slot + jnp.where(place >= CHIPS, partner_count, 0.0)
    chip = jnp.minimum(place, (CLUSTERS - 1) - place)
    return group, chip.astype(jnp.int32), slot.astype(jnp.int32), as_row(count_column)


def missing_documents(index_ref, count_column, group):
    listed = index_ref[...]
    live = iota((GROUPS, CAP), 1).astype(F32) < count_column
    eye = onehot(iota((CAP, CAP), 0) == iota((CAP, CAP), 1))
    high = dot_rows(eye, jnp.where(live, listed >> 4, 0).astype(F32).astype(BF16))
    low = dot_rows(eye, jnp.where(live, listed & 15, 0).astype(F32).astype(BF16))
    alive = dot_rows(eye, onehot(live))
    slots = jnp.where(alive > 0.5, high * 16.0 + low, -1.0)
    document = iota((1, ROWS), 1).astype(F32)
    lane = iota((CAP, GROUPS), 1)

    def count(g, hits):
        column = across(pick(lane == g, slots))
        wanted = jnp.where(group == g.astype(F32), document, -2.0)
        return hits + jnp.where(column == wanted, 1.0, 0.0)

    hits = lax.fori_loop(0, GROUPS, count, jnp.zeros((CAP, ROWS), F32))
    return across(jnp.where(down(hits) > 0.5, 0.0, 1.0))


def send_order():
    order = []
    for step in range(CHIPS):
        high, middle, low = step // 16, (step // 4) % 4, step % 4
        order.append((low, (middle + low) % 4, (high + middle + low) % 4))
    near = [shift for shift in order if sum(min(d, 4 - d) for d in shift) <= 1] + [(2, 0, 0)]
    near.sort(key=lambda shift: -sum(min(d, 4 - d) for d in shift))
    return [shift for shift in order if shift not in near] + near


ORDER = send_order()
SELF = CHIPS - 1


def step_to(dx, dy, dz):
    shift = (dx & 3) * 16 + (dy & 3) * 4 + (dz & 3)
    step = jnp.full(shift.shape, SELF, jnp.int32)
    for number, (x, y, z) in enumerate(ORDER[:SELF]):
        step = jnp.where(shift == x * 16 + y * 4 + z, number, step)
    return step


def in_part(step, part):
    begin, steps, _ = PARTS[part]
    return (step >= begin) & (step < begin + steps)


def chip_places():
    sub, lane = iota((CLUSTERS, CLUSTERS), 0), iota((CLUSTERS, CLUSTERS), 1)
    return onehot((sub == lane) | (sub == (CLUSTERS - 1) - lane))


def excess(totals):
    lane = iota(totals.shape, 1)
    return jnp.where(lane < CHIPS, jnp.maximum(totals - BASE, 0.0), 0.0)


def receive_plan(table, rank, my_x, my_y, my_z):
    chip = my_x * 16 + my_y * 4 + my_z
    heads = table.astype(jnp.int32)
    counts = (heads & 1023).astype(F32)
    differ = jnp.where((heads >> 10).astype(F32) != rank, 1.0, 0.0)
    fault = across(down(differ))
    both = dot(counts.astype(BF16), chip_places())
    over = excess(both)
    lanes = iota((CHIPS, CLUSTERS), 1)
    sender = iota((CHIPS, 1), 0)
    source, target = iota((CHIPS, CHIPS), 0), iota((CHIPS, CHIPS), 1)

    same_line = (source >> 2) == (target >> 2)
    over_total = across(over)
    over_row = as_row(over_total)
    line_start = across(pick(same_line & (target < source), over_row))
    line_total = across(pick(same_line, over_row))
    fault = fault + down(jnp.where(line_total > POOL, 1.0, 0.0))
    start = line_start + across(pick(lanes < chip, over))
    number = across(pick(lanes == chip, over))

    to_chip = iota((1, CLUSTERS), 1)
    route = step_to(
        (to_chip >> 4) - (sender >> 4), ((to_chip >> 2) & 3) - ((sender >> 2) & 3), (to_chip & 3) - (sender & 3)
    )
    based = jnp.where(lanes < CHIPS, jnp.minimum(both, float(BASE)), 0.0)
    for part, (_, _, room) in enumerate(PARTS):
        held = down(pick(in_part(route, part), based))
        if part == LAST:
            held = held + down(over)
        fault = fault + across(jnp.where(held > room, 1.0, 0.0))

    first = across(pick(lanes == chip, counts))
    second = across(pick(lanes == (CLUSTERS - 1) - chip, counts))
    place = (lanes & (POOL - 1)).astype(F32) - start
    mine = ((sender >> 2) == (lanes >> 3)) & (place >= 0.0) & (place < number)
    over_first = down(jnp.where(mine & (place + BASE < first), 1.0, 0.0))
    over_second = down(jnp.where(mine & (place + BASE >= first), 1.0, 0.0))
    over_first_total, over_second_total = across(over_first), across(over_second)
    earlier = onehot(iota((CLUSTERS, CLUSTERS), 0) < iota((CLUSTERS, CLUSTERS), 1))
    sub = iota((16, CLUSTERS), 0)
    before = dot((pick(sub == 0, over_first) + pick(sub == 1, over_second)).astype(BF16), earlier)

    base_first = jnp.minimum(first, float(BASE))
    base_second = jnp.minimum(first + second, float(BASE)) - base_first
    first_row, second_row = as_row(base_first), as_row(base_second)

    def my_step(other):
        return step_to(my_x - (other >> 4), my_y - ((other >> 2) & 3), my_z - (other & 3))

    step_column, step_row = my_step(sender), my_step(iota((1, CHIPS), 1))
    plans = []
    ends = []
    for part, (begin, steps, _) in enumerate(PARTS):
        inside = in_part(step_column, part)
        ahead = (target < source) & in_part(step_row, part)
        first_total = down(pick(inside, base_first))
        second_total = down(pick(inside, base_second))
        last = part == LAST
        first_end = first_total + over_first_total if last else first_total
        first_start = across(pick(ahead, first_row))
        second_start = across(pick(ahead, second_row)) + first_end
        spread = step_column - begin == (iota((CHIPS, steps * BASE), 1) >> 4)
        head, tail, head_start, tail_start = [
            down(pick(spread, column)) for column in (base_first, base_second, first_start, second_start)
        ]
        slot = (iota((1, steps * BASE), 1) & (BASE - 1)).astype(F32)
        later = jnp.where(slot < head + tail, tail_start + (slot - head), -1.0)
        plan = jnp.where(slot < head, head_start + slot, later)
        held_end = first_end + second_total
        if last:
            over_row_of = jnp.where(over_second > 0.5, held_end + before[1:2], -1.0)
            over_row_of = jnp.where(over_first > 0.5, first_total + before[0:1], over_row_of)
            plan = jnp.concatenate([plan[:, : steps * BASE - CLUSTERS], over_row_of], axis=1)
            held_end = held_end + over_second_total
        plans.append(plan)
        ends.append((first_end, held_end))
    return plans, ends, fault


def kernel(
    x_hbm, assign_hbm, owner_hbm, count_hbm, index_hbm,
    out_ref, fault_ref,
    x_ref, assign_ref, owner_ref, count_ref, index_ref,
    send, got, heads, own_over, line_over, send_over, got_over, pick_0, pick_1, pick_2,
    mine, theirs, facts, sums, their_sums, back, returned,
    load_sem, send_sem, recv_sem,
):
    grp, blk = lax.axis_index("grp"), lax.axis_index("blk")
    my_x, my_y, my_z, core = grp // 4, grp % 4, blk // 2, blk % 2
    my_chip = grp * 4 + my_z
    picks = (pick_0, pick_1, pick_2)
    along_x = [((my_x + d) % 4) * 4 for d in range(4)]
    along_y = [(my_y + d) % 4 for d in range(4)]
    along_z = [((my_z + d) % 4) * 2 + core for d in range(4)]
    other_core = {"grp": grp, "blk": my_z * 2 + (1 - core)}

    def device_at(step, sign):
        dx, dy, dz = [(sign * d) % 4 for d in ORDER[step]]
        return {"grp": along_x[dx] + along_y[dy], "blk": along_z[dz]}

    def remote(source, target, number, device, sent=None):
        return pltpu.make_async_remote_copy(
            src_ref=source,
            dst_ref=target,
            send_sem=send_sem.at[number if sent is None else sent],
            recv_sem=recv_sem.at[number],
            device_id=device,
            device_id_type=pl.DeviceIdType.MESH,
        )

    def await_blocks(ref, number, semaphore):
        block = ref.at[pl.ds(0, number)]
        pltpu.make_async_copy(block, block, semaphore).wait()

    HEAD_Z, HEAD_XY, LINE, OVER, FACTS, SUMS, BACK, SWAP, PART, SENT = 0, 1, 2, 3, 4, 5, 6, 7, 10, 13
    messages = [min(begin + steps, SELF) - begin for begin, steps, _ in PARTS]

    loads = [
        pltpu.make_async_copy(source, target, load_sem.at[number])
        for number, (source, target) in enumerate(
            (
                (assign_hbm, assign_ref),
                (owner_hbm, owner_ref),
                (count_hbm, count_ref),
                (index_hbm, index_ref),
                (x_hbm, x_ref),
            )
        )
    ]
    for load in loads:
        load.start()
    barrier = pltpu.get_barrier_semaphore()
    for device in [device_at(step, 1) for step in range(SELF)] + [other_core]:
        pl.semaphore_signal(barrier, inc=1, device_id=device, device_id_type=pl.DeviceIdType.MESH)
    for load in loads[:-1]:
        load.wait()

    rank, count_column = rank_groups(count_ref)
    group, chip, slot, place_counts = place_documents(assign_ref, owner_ref, rank)
    step_of = step_to((chip >> 4) - my_x, ((chip >> 2) & 3) - my_y, (chip & 3) - my_z)
    in_base = slot < BASE
    send_slot = jnp.where(in_base, step_of * BASE + slot, -1)
    heads[my_chip] = place_counts + 1024.0 * rank
    loads[-1].wait()

    def pack(first, stop):
        slots = iota(((stop - first) * BASE, ROWS), 0) + first * BASE
        rows = dot(onehot(slots == send_slot), x_ref[...]).astype(BF16)
        send[pl.ds(first, stop - first)] = rows.reshape(stop - first, BASE, WIDTH)

    def post(batch):
        if batch >= 2:
            await_blocks(send, BATCH, send_sem.at[SENT + batch - 2])
        for step in range(batch * BATCH, min((batch + 1) * BATCH, SELF)):
            number = max(part for part in range(len(PARTS)) if PARTS[part][0] <= step)
            remote(send.at[step], got.at[step], PART + number, device_at(step, 1), SENT + batch).start()

    pack(0, 24)
    pl.semaphore_wait(barrier, CHIPS)
    for d in range(1, DEPTH):
        device = {"grp": grp, "blk": along_z[d]}
        block = heads.at[pl.ds(my_chip, 1)]
        remote(block, block, HEAD_Z, device).start()
    post(0)
    post(1)
    place_counts_16 = place_counts + jnp.zeros((16, CLUSTERS), F32)
    own_excess = excess(dot(place_counts_16.astype(BF16), chip_places())[0:1])
    eye = iota((CHIPS, CLUSTERS), 0) == iota((CHIPS, CLUSTERS), 1)
    excess_column = across(pick(eye, own_excess))
    over_slot = down(pick(iota((CHIPS, ROWS), 0) < chip, excess_column)).astype(jnp.int32) + (slot - BASE)
    over_slot = jnp.where(in_base, -1, over_slot)
    own_over[...] = dot(onehot(iota((BASE, ROWS), 0) == over_slot), x_ref[...]).astype(BF16)
    line_over[my_z] = own_over[...]
    for d in range(1, DEPTH):
        remote(own_over, line_over.at[my_z], LINE, {"grp": grp, "blk": along_z[d]}).start()

    await_blocks(heads, DEPTH - 1, recv_sem.at[HEAD_Z])
    line_heads = heads[pl.ds(grp * DEPTH, DEPTH)].reshape(DEPTH, CLUSTERS)
    line_counts = (line_heads.astype(jnp.int32) & 1023).astype(F32).astype(BF16)
    line_total = across(excess(dot(line_counts, chip_places())))
    depth = iota((DEPTH, 1), 0)
    line_start = jnp.zeros((DEPTH, 1), F32)
    for d in range(DEPTH - 1):
        line_start = line_start + pick(depth > d, line_total[d : d + 1])
    my_start = down(pick(depth == my_z, line_start))
    at = depth == (iota((DEPTH, DEPTH * BASE), 1) >> 4)
    begin = down(pick(at, line_start))
    number = down(pick(at, line_total))
    order = (iota((1, DEPTH * BASE), 1) & (BASE - 1)).astype(F32)
    order = jnp.where(order < number, begin + order, -1.0)
    rows = iota((2 * POOL, DEPTH * BASE), 0).astype(F32)
    await_blocks(line_over, DEPTH - 1, recv_sem.at[LINE])
    blocks = line_over[...].reshape(DEPTH * BASE, WIDTH)
    left = dot(onehot((rows == order) & (rows < POOL)), blocks[:, :HALF])
    right = dot(onehot((rows - POOL == order) & (rows >= POOL)), blocks[:, HALF:])
    send_over[...] = (left + right).astype(BF16)
    got_over[grp] = send_over[...]
    for step in range(1, LINES):
        low, middle = step % 4, step // 4
        device = {"grp": along_x[low] + along_y[(middle + low) % 4], "blk": blk}
        block = heads.at[pl.ds(grp * DEPTH, DEPTH)]
        remote(block, block, HEAD_XY, device).start()
        remote(send_over, got_over.at[grp], OVER, device).start()
    pack(24, 48)
    post(2)
    post(3)
    pack(48, CHIPS)
    got[SELF] = send[SELF]
    post(4)

    await_blocks(heads, CHIPS - DEPTH, recv_sem.at[HEAD_XY])
    table = heads[...].reshape(CHIPS, CLUSTERS)
    plans, ends, fault = receive_plan(table, rank, my_x, my_y, my_z)

    post(5)

    missing = missing_documents(index_ref, count_column, group)
    row = iota((8, 128), 0)
    told = pick(row == 6, rank) + pick(row == 7, jnp.where(iota((1, 128), 1) == 0, fault, missing))
    for part, (first_end, held_end) in enumerate(ends):
        told = told + pick(row == part, first_end) + pick(row == 3 + part, held_end)
        picks[part][...] = onehot(iota(picks[part].shape, 0).astype(F32) == plans[part])
    facts[0] = told
    swap_facts = remote(facts.at[0], facts.at[1], FACTS, other_core)
    swap_facts.start()
    post(6)
    post(7)

    best = [jnp.full((1, room), -1.0, F32) for _, _, room in PARTS]
    their_ends = []
    totals = [jnp.zeros((1, WIDTH), F32), jnp.zeros((1, WIDTH), F32)]
    swaps = []

    def window(part):
        return pl.ds(STARTS[part], PARTS[part][2])

    def compare(keys, key_part, query_part, key_ends, itself, more=0):
        room = PARTS[key_part][2]
        scores = dot_rows(keys[pl.ds(STARTS[key_part], room + more)], mine[window(query_part)])
        rest, scores = scores[room:], scores[:room]
        first, held = key_ends[key_part]
        key_number = iota((PARTS[key_part][2], 1), 0).astype(F32)
        query_number = iota((1, PARTS[query_part][2]), 1).astype(F32)
        kind = jnp.where(key_number < first, 0.0, jnp.where(key_number < held, 1.0, 2.0))
        matched = kind == jnp.where(query_number < ends[query_part][0], 0.0, 1.0)
        if itself and key_part == query_part:
            matched = matched & (key_number != query_number)
        scores = jnp.max(jnp.where(matched, scores, -1.0), axis=0, keepdims=True)
        best[query_part] = jnp.maximum(best[query_part], scores)
        return rest

    for part, (begin, steps, room) in enumerate(PARTS):
        if part == LAST:
            await_blocks(got_over, LINES - 1, recv_sem.at[OVER])
            halves = got_over[...].reshape(LINES * 2 * POOL, HALF)
            shape = (LINES * POOL, LINES * 2 * POOL)
            to, at = iota(shape, 0), iota(shape, 1)
            same = ((to >> 3) == (at >> 4)) & ((to & 7) == (at & 7))
            left = dot(onehot(same & ((at & POOL) == 0)), halves)
            right = dot(onehot(same & ((at & POOL) != 0)), halves)
            whole = jnp.concatenate([left, right], axis=1).astype(BF16)
            got[pl.ds(CHIPS, TOTAL - CHIPS)] = whole.reshape(TOTAL - CHIPS, BASE, WIDTH)
        await_blocks(got, messages[part], recv_sem.at[PART + part])
        rows = dot(picks[part][...], got[pl.ds(begin, steps)].reshape(steps * BASE, WIDTH))
        unit = rows * lax.rsqrt(across(rows * rows) + EPSILON)
        mine[window(part)] = unit.astype(BF16)
        swap = remote(mine.at[window(part)], theirs.at[window(part)], SWAP + part, other_core)
        swap.start()
        swaps.append(swap)
        is_first = iota((room, 1), 0).astype(F32) < ends[part][0]
        totals[0] = totals[0] + down(pick(is_first, unit))
        totals[1] = totals[1] + down(jnp.where(is_first, 0.0, unit))
        if part == LAST:
            row = iota((8, WIDTH), 0)
            sums[...] = pick(row == 0, totals[0]) + pick(row == 1, totals[1])
            swap_sums = remote(sums, their_sums, SUMS, other_core)
            swap_sums.start()
        if part == 0:
            compare(mine, 0, 0, ends, True)
            swap_facts.wait()
            their_told = facts[1]
            for number in range(len(PARTS)):
                their_ends.append((their_told[number : number + 1, 0:1], their_told[3 + number : 4 + number, 0:1]))
            swap.wait()
            compare(theirs, 0, 0, their_ends, False)
    for part in range(1, len(PARTS)):
        for other in range(part + 1):
            compare(mine, part, other, ends, True)
            if other != part:
                compare(mine, other, part, ends, True)
        compare(theirs, 0, part, their_ends, False)
    swaps[1].wait()
    for part in range(len(PARTS)):
        compare(theirs, 1, part, their_ends, False)

    swap_sums.wait()
    total = sums[...] + their_sums[...]
    terms = jnp.concatenate(thirds(total) + (jnp.zeros((8, WIDTH), F32),), axis=0)
    theirs[pl.ds(HELD, 32)] = terms.astype(BF16)
    scale = lax.rsqrt(across(total * total) + EPSILON)
    swaps[LAST].wait()
    near = [compare(theirs, LAST, other, their_ends, False, 32) for other in range(len(PARTS))]

    poison = missing + their_told[7:8, 1:2] > 0.5
    tiles = CHIPS * BASE // 128
    for part, (begin, steps, room) in enumerate(PARTS):
        row = iota((8, room), 0)
        query_number = iota((1, room), 1).astype(F32)
        some = (near[part][0:8] + near[part][8:16] + near[part][16:24]) * scale
        some = jnp.where(query_number < ends[part][0], some[0:1], some[1:2])
        values = jnp.zeros((8, room), F32)
        for number, term in enumerate(thirds(best[part]) + thirds(some)):
            values = jnp.where(row == number, term, values)
        out = dot(values.astype(BF16), picks[part][...])
        for kind in range(2):
            line = out[3 * kind : 3 * kind + 1] + out[3 * kind + 1 : 3 * kind + 2] + out[3 * kind + 2 : 3 * kind + 3]
            line = jnp.where(poison, NONE, line)
            for tile in range(steps * BASE // 128):
                piece = line[:, tile * 128 : (tile + 1) * 128]
                to = begin * BASE // 128 + tile
                if to < tiles:
                    back[to, kind : kind + 1, :] = piece
                else:
                    for each in range(tiles):
                        back[each, 2 + kind : 3 + kind, :] = piece
    returned[SELF] = back[SELF // 8]
    for step in range(SELF):
        remote(back.at[step // 8], returned.at[step], BACK, device_at(step, -1)).start()

    differ = across(jnp.where(their_told[6:7] != rank, 1.0, 0.0))
    fault = fault + their_told[7:8, 0:1] + differ
    chosen = onehot(iota((CHIPS, ROWS), 0) == step_of)
    sub = iota((128, ROWS), 0)
    at_base = (sub == (step_of & 7) * BASE + slot) & in_base
    at_over = (sub == grp * POOL + my_start.astype(jnp.int32) + over_slot) & (~in_base)

    await_blocks(returned, CHIPS - 1, recv_sem.at[BACK])
    found = []
    for number in range(4):
        line = returned[:, number, :]
        if number == 0:
            poisoned = across(down(jnp.where(line > 0.5 * NONE, 1.0, 0.0)))
            fault_ref[...] = jnp.where(fault + poisoned > 0.5, 1, 0) + jnp.zeros((1, 128), jnp.int32)
        terms = jnp.concatenate(thirds(line), axis=1).astype(BF16)
        out = lax.dot_general(terms, chosen, (((0,), (0,)), ((), ())), preferred_element_type=F32)
        found.append(out[0:128] + out[128:256] + out[256:384])
    out_ref[0:1] = down(pick(at_base, found[0]) + pick(at_over, found[2]))
    out_ref[1:2] = down(pick(at_base, found[1]) + pick(at_over, found[3]))

    await_blocks(heads, DEPTH - 1, send_sem.at[HEAD_Z])
    await_blocks(heads, CHIPS - DEPTH, send_sem.at[HEAD_XY])
    await_blocks(line_over, DEPTH - 1, send_sem.at[LINE])
    await_blocks(got_over, LINES - 1, send_sem.at[OVER])
    await_blocks(returned, CHIPS - 1, send_sem.at[BACK])
    await_blocks(send, BATCH, send_sem.at[SENT + 6])
    await_blocks(send, BATCH - 1, send_sem.at[SENT + 7])


def routed(embeddings, assign, owner, send_count, send_index):
    return pl.pallas_call(
        kernel,
        out_shape=(
            jax.ShapeDtypeStruct((2, ROWS), F32),
            jax.ShapeDtypeStruct((1, 128), jnp.int32),
        ),
        in_specs=[pl.BlockSpec(memory_space=pl.ANY)] * 5,
        out_specs=(pl.BlockSpec(memory_space=pltpu.VMEM),) * 2,
        scratch_shapes=[
            pltpu.VMEM((ROWS, WIDTH), BF16),
            pltpu.VMEM((1, ROWS), jnp.int32),
            pltpu.VMEM((1, CLUSTERS), jnp.int32),
            pltpu.VMEM((1, GROUPS), jnp.int32),
            pltpu.VMEM((GROUPS, CAP), jnp.int32),
            pltpu.VMEM((CHIPS, BASE, WIDTH), BF16),
            pltpu.VMEM((TOTAL, BASE, WIDTH), BF16),
            pltpu.VMEM((CHIPS, 1, 128), F32),
            pltpu.VMEM((BASE, WIDTH), BF16),
            pltpu.VMEM((DEPTH, BASE, WIDTH), BF16),
            pltpu.VMEM((2 * POOL, HALF), BF16),
            pltpu.VMEM((LINES, 2 * POOL, HALF), BF16),
            *[pltpu.VMEM((room, steps * BASE), BF16) for _, steps, room in PARTS],
            pltpu.VMEM((HELD, WIDTH), BF16),
            pltpu.VMEM((HELD + 32, WIDTH), BF16),
            pltpu.VMEM((2, 8, 128), F32),
            pltpu.VMEM((8, WIDTH), F32),
            pltpu.VMEM((8, WIDTH), F32),
            pltpu.VMEM((CHIPS * BASE // 128, 4, 128), F32),
            pltpu.VMEM((CHIPS, 4, 128), F32),
            pltpu.SemaphoreType.DMA((5,)),
            pltpu.SemaphoreType.DMA((21,)),
            pltpu.SemaphoreType.DMA((13,)),
        ],
        compiler_params=pltpu.CompilerParams(
            collective_id=0, has_side_effects=True, vmem_limit_bytes=48 * 1024 * 1024
        ),
    )(
        embeddings,
        assign.reshape(1, ROWS),
        owner.reshape(1, CLUSTERS),
        send_count,
        send_index[0],
    )


def body(embeddings, assign, owner, send_count, send_index):
    arguments = (embeddings, assign, owner, send_count, send_index)
    results, fault = routed(*arguments)
    results = lax.cond(fault[0, 0] != 0, lambda: jnp.stack(general(*arguments)), lambda: results)
    return results[0], results[1]


def solution(mesh):
    placed = (
        P(("grp", "blk"), None),
        P(("grp", "blk")),
        P(),
        P(("grp", "blk"), None),
        P(("grp", "blk"), None, None),
    )
    return jax.shard_map(
        body,
        mesh=mesh,
        in_specs=placed,
        out_specs=(P(("grp", "blk")), P(("grp", "blk"))),
        check_vma=False,
    )
```

```python
import functools

import jax
import jax.numpy as jnp
from jax import lax
from jax.experimental import pallas as pl
from jax.experimental.pallas import tpu as pltpu
from jax.sharding import PartitionSpec as P

EPSILON = 1e-06
F32 = jnp.float32
BF16 = jnp.bfloat16

CHIPS = 64
ROWS = 512
WIDTH = 768
CLUSTERS = 128
GROUPS = 16
CAP = 64
BASE = 16
HALF = WIDTH // 2
LINES = 16
DEPTH = 4
POOL = 8
PARTS = ((0, 32, 384), (32, 24, 256), (56, 16, 128))
TOTAL = 72
HELD = 768
STARTS = (0, 384, 640)
LAST = len(PARTS) - 1
NONE = 1e30


def normalize(values):
    widened = values.astype(F32)
    return widened * lax.rsqrt(jnp.sum(widened * widened, axis=1, keepdims=True) + EPSILON)


def general(embeddings, assign, owner, send_count, send_index):
    rows_local = embeddings.shape[0]
    feature_width = embeddings.shape[1]
    groups = lax.axis_size("grp")
    clusters = owner.shape[0]
    capacity = send_index.shape[2]
    slot_total = groups * capacity
    unit_rows = normalize(embeddings)
    unit_low = unit_rows.astype(BF16)
    counts = send_count[0]
    listed = send_index[0]
    live_slot = jnp.arange(capacity, dtype=jnp.int32)[None, :] < counts[:, None]
    listed_cluster = assign[listed]
    owned_here = owner[listed_cluster] == jnp.arange(groups, dtype=jnp.int32)[:, None]
    kept_slot = live_slot & owned_here
    out_cluster = jnp.where(kept_slot, listed_cluster, -1)
    out_tag = jnp.where(kept_slot, lax.axis_index(("grp", "blk")) * rows_local + listed, -1)
    out_vector = unit_low[listed.reshape(-1)].reshape(groups, capacity, feature_width)
    got_vector, got_cluster, got_tag = (
        lax.all_to_all(out_vector, "grp", split_axis=0, concat_axis=0, tiled=True),
        lax.all_to_all(out_cluster, "grp", split_axis=0, concat_axis=0, tiled=True),
        lax.all_to_all(out_tag, "grp", split_axis=0, concat_axis=0, tiled=True),
    )
    own_vector = got_vector.reshape(slot_total, feature_width)
    own_cluster = got_cluster.reshape(slot_total)
    own_tag = got_tag.reshape(slot_total)

    def tile_best(current, shard_piece):
        other_vector, other_cluster, other_tag = shard_piece
        scores = jnp.einsum("id,jd->ij", own_vector, other_vector, preferred_element_type=F32)
        matched = (
            (own_cluster[:, None] == other_cluster[None, :])
            & (other_cluster[None, :] >= 0)
            & (own_tag[:, None] != other_tag[None, :])
        )
        return jnp.maximum(current, jnp.max(jnp.where(matched, scores, -1.0), axis=1))

    other_vector = lax.all_gather(own_vector, "blk", axis=0, tiled=True)
    other_cluster = lax.all_gather(own_cluster, "blk", axis=0, tiled=True)
    other_tag = lax.all_gather(own_tag, "blk", axis=0, tiled=True)
    length = other_vector.shape[0]
    number = length // slot_total
    stacked = (
        other_vector.reshape(number, slot_total, feature_width),
        other_cluster.reshape(number, slot_total),
        other_tag.reshape(number, slot_total),
    )

    def scan_step(carry, single):
        return (tile_best(carry, single), None)

    result, unused = lax.scan(scan_step, jnp.full((slot_total,), -1.0, F32), stacked)
    target = jnp.where(live_slot, listed, rows_local).reshape(-1)
    partial_sum = jax.ops.segment_sum(unit_rows, assign, num_segments=clusters)
    centre = normalize(lax.psum(partial_sum, ("grp", "blk")))
    nearness = jnp.sum(unit_low.astype(F32) * centre[assign], axis=1)
    returned = lax.all_to_all(
        result.reshape(groups, capacity), "grp", split_axis=0, concat_axis=0, tiled=True
    )
    has_entry = (
        jnp.zeros((rows_local,), jnp.int32)
        .at[target]
        .max(kept_slot.astype(jnp.int32).reshape(-1), mode="drop")
    )
    centroid_cos = jnp.where(has_entry > 0, nearness, 0.0)
    max_sim = jnp.full((rows_local,), -1.0, F32).at[target].max(returned.reshape(-1), mode="drop")
    return (max_sim, centroid_cos)


def iota(shape, axis):
    return lax.broadcasted_iota(jnp.int32, shape, axis)


def down(values):
    return jnp.sum(values, axis=0, keepdims=True)


def across(values):
    return jnp.sum(values, axis=1, keepdims=True)


def pick(mask, values):
    return jnp.where(mask, values, 0.0)


def as_column(row):
    size = row.shape[1]
    return across(pick(iota((size, size), 0) == iota((size, size), 1), row))


def as_row(column):
    size = column.shape[0]
    return down(pick(iota((size, size), 0) == iota((size, size), 1), column))


def dot(a, b):
    return jnp.dot(a, b, preferred_element_type=F32)


def dot_rows(a, b):
    return lax.dot_general(a, b, (((1,), (1,)), ((), ())), preferred_element_type=F32)


def onehot(mask):
    return jnp.where(mask, 1.0, 0.0).astype(BF16)


def halves(values):
    first = values.astype(BF16).astype(F32)
    return first, (values - first).astype(BF16).astype(F32)


def rank_groups(count_ref):
    count_row = count_ref[...].astype(F32)
    count_column = as_column(count_row)
    sub, lane = iota((GROUPS, 128), 0), iota((GROUPS, 128), 1)
    count_lanes = down(pick(sub == lane, count_column))
    ahead = (count_column > count_lanes) | ((count_column == count_lanes) & (sub < lane))
    rank = down(jnp.where(ahead, 1.0, 0.0))
    return jnp.where(iota((1, 128), 1) < GROUPS, rank, 0.0), count_column


def place_documents(assign_ref, owner_ref, rank):
    owner_row = owner_ref[...].astype(F32)
    owner_column = as_column(owner_row)
    sub, lane = iota((CLUSTERS, CLUSTERS), 0), iota((CLUSTERS, CLUSTERS), 1)
    within = across(jnp.where((owner_column == owner_row) & (lane < sub), 1.0, 0.0))
    group_rank = across(pick(owner_column == lane.astype(F32), rank))
    place_column = group_rank * (CLUSTERS // GROUPS) + within
    member = iota((CLUSTERS, ROWS), 0) == assign_ref[...]
    place = down(pick(member, place_column))
    group = down(pick(member, owner_column))
    order = iota((CLUSTERS, ROWS), 0).astype(F32)
    at_place = order == place
    earlier = onehot(iota((ROWS, ROWS), 0) < iota((ROWS, ROWS), 1))
    before = dot(onehot(at_place), earlier)
    slot = down(pick(at_place, before))
    count_column = across(jnp.where(at_place, 1.0, 0.0))
    partner_count = down(pick(order == (CLUSTERS - 1) - place, count_column))
    slot = slot + jnp.where(place >= CHIPS, partner_count, 0.0)
    chip = jnp.minimum(place, (CLUSTERS - 1) - place)
    return group, chip.astype(jnp.int32), slot.astype(jnp.int32), as_row(count_column)


def missing_documents(index_ref, count_column, group):
    listed = index_ref[...]
    live = iota((GROUPS, CAP), 1).astype(F32) < count_column
    eye = onehot(iota((CAP, CAP), 0) == iota((CAP, CAP), 1))
    high = dot_rows(eye, jnp.where(live, listed >> 4, 0).astype(F32).astype(BF16))
    low = dot_rows(eye, jnp.where(live, listed & 15, 0).astype(F32).astype(BF16))
    alive = dot_rows(eye, onehot(live))
    slots = jnp.where(alive > 0.5, high * 16.0 + low, -1.0)
    document = iota((1, ROWS), 1).astype(F32)
    lane = iota((CAP, GROUPS), 1)

    def count(g, hits):
        column = across(pick(lane == g, slots))
        wanted = jnp.where(group == g.astype(F32), document, -2.0)
        return hits + jnp.where(column == wanted, 1.0, 0.0)

    hits = lax.fori_loop(0, GROUPS, count, jnp.zeros((CAP, ROWS), F32))
    return across(jnp.where(down(hits) > 0.5, 0.0, 1.0))


def send_order():
    order = []
    for step in range(CHIPS):
        high, middle, low = step // 16, (step // 4) % 4, step % 4
        order.append((low, (middle + low) % 4, (high + middle + low) % 4))
    near = [shift for shift in order if sum(min(d, 4 - d) for d in shift) <= 1] + [(2, 0, 0)]
    near.sort(key=lambda shift: -sum(min(d, 4 - d) for d in shift))
    return [shift for shift in order if shift not in near] + near


ORDER = send_order()
SELF = CHIPS - 1


def step_to(dx, dy, dz):
    shift = (dx & 3) * 16 + (dy & 3) * 4 + (dz & 3)
    step = jnp.full(shift.shape, SELF, jnp.int32)
    for number, (x, y, z) in enumerate(ORDER[:SELF]):
        step = jnp.where(shift == x * 16 + y * 4 + z, number, step)
    return step


def in_part(step, part):
    begin, steps, _ = PARTS[part]
    return (step >= begin) & (step < begin + steps)


def chip_places():
    sub, lane = iota((CLUSTERS, CLUSTERS), 0), iota((CLUSTERS, CLUSTERS), 1)
    return onehot((sub == lane) | (sub == (CLUSTERS - 1) - lane))


def excess(totals):
    lane = iota(totals.shape, 1)
    return jnp.where(lane < CHIPS, jnp.maximum(totals - BASE, 0.0), 0.0)


def receive_plan(table, rank, my_x, my_y, my_z):
    chip = my_x * 16 + my_y * 4 + my_z
    heads = table.astype(jnp.int32)
    counts = (heads & 1023).astype(F32)
    differ = jnp.where((heads >> 10).astype(F32) != rank, 1.0, 0.0)
    fault = across(down(differ))
    both = dot(counts.astype(BF16), chip_places())
    over = excess(both)
    lanes = iota((CHIPS, CLUSTERS), 1)
    sender = iota((CHIPS, 1), 0)
    source, target = iota((CHIPS, CHIPS), 0), iota((CHIPS, CHIPS), 1)

    same_line = (source >> 2) == (target >> 2)
    over_total = across(over)
    over_row = as_row(over_total)
    line_start = across(pick(same_line & (target < source), over_row))
    line_total = across(pick(same_line, over_row))
    fault = fault + down(jnp.where(line_total > POOL, 1.0, 0.0))
    start = line_start + across(pick(lanes < chip, over))
    number = across(pick(lanes == chip, over))

    to_chip = iota((1, CLUSTERS), 1)
    route = step_to(
        (to_chip >> 4) - (sender >> 4), ((to_chip >> 2) & 3) - ((sender >> 2) & 3), (to_chip & 3) - (sender & 3)
    )
    based = jnp.where(lanes < CHIPS, jnp.minimum(both, float(BASE)), 0.0)
    for part, (_, _, room) in enumerate(PARTS):
        held = down(pick(in_part(route, part), based))
        if part == LAST:
            held = held + down(over)
        fault = fault + across(jnp.where(held > room, 1.0, 0.0))

    first = across(pick(lanes == chip, counts))
    second = across(pick(lanes == (CLUSTERS - 1) - chip, counts))
    place = (lanes & (POOL - 1)).astype(F32) - start
    mine = ((sender >> 2) == (lanes >> 3)) & (place >= 0.0) & (place < number)
    over_first = down(jnp.where(mine & (place + BASE < first), 1.0, 0.0))
    over_second = down(jnp.where(mine & (place + BASE >= first), 1.0, 0.0))
    over_first_total, over_second_total = across(over_first), across(over_second)
    earlier = onehot(iota((CLUSTERS, CLUSTERS), 0) < iota((CLUSTERS, CLUSTERS), 1))
    sub = iota((16, CLUSTERS), 0)
    before = dot((pick(sub == 0, over_first) + pick(sub == 1, over_second)).astype(BF16), earlier)

    base_first = jnp.minimum(first, float(BASE))
    base_second = jnp.minimum(first + second, float(BASE)) - base_first
    first_row, second_row = as_row(base_first), as_row(base_second)

    def my_step(other):
        return step_to(my_x - (other >> 4), my_y - ((other >> 2) & 3), my_z - (other & 3))

    step_column, step_row = my_step(sender), my_step(iota((1, CHIPS), 1))
    plans = []
    ends = []
    for part, (begin, steps, _) in enumerate(PARTS):
        inside = in_part(step_column, part)
        ahead = (target < source) & in_part(step_row, part)
        first_total = down(pick(inside, base_first))
        second_total = down(pick(inside, base_second))
        last = part == LAST
        first_end = first_total + over_first_total if last else first_total
        first_start = across(pick(ahead, first_row))
        second_start = across(pick(ahead, second_row)) + first_end
        spread = step_column - begin == (iota((CHIPS, steps * BASE), 1) >> 4)
        head, tail, head_start, tail_start = [
            down(pick(spread, column)) for column in (base_first, base_second, first_start, second_start)
        ]
        slot = (iota((1, steps * BASE), 1) & (BASE - 1)).astype(F32)
        later = jnp.where(slot < head + tail, tail_start + (slot - head), -1.0)
        plan = jnp.where(slot < head, head_start + slot, later)
        held_end = first_end + second_total
        if last:
            over_row_of = jnp.where(over_second > 0.5, held_end + before[1:2], -1.0)
            over_row_of = jnp.where(over_first > 0.5, first_total + before[0:1], over_row_of)
            plan = jnp.concatenate([plan[:, : steps * BASE - CLUSTERS], over_row_of], axis=1)
            held_end = held_end + over_second_total
        plans.append(plan)
        ends.append((first_end, held_end))
    return plans, ends, fault


def kernel(
    x_hbm, assign_hbm, owner_hbm, count_hbm, index_hbm,
    out_ref, fault_ref,
    x_ref, assign_ref, owner_ref, count_ref, index_ref,
    send, got, heads, own_over, line_over, send_over, got_over, pick_0, pick_1, pick_2,
    keys, facts, sums, their_sums, back, returned,
    load_sem, send_sem, recv_sem,
):
    grp, blk = lax.axis_index("grp"), lax.axis_index("blk")
    my_x, my_y, my_z, core = grp // 4, grp % 4, blk // 2, blk % 2
    my_chip = grp * 4 + my_z
    picks = (pick_0, pick_1, pick_2)
    along_x = [((my_x + d) % 4) * 4 for d in range(4)]
    along_y = [(my_y + d) % 4 for d in range(4)]
    along_z = [((my_z + d) % 4) * 2 + core for d in range(4)]
    other_core = {"grp": grp, "blk": my_z * 2 + (1 - core)}

    def device_at(step, sign):
        dx, dy, dz = [(sign * d) % 4 for d in ORDER[step]]
        return {"grp": along_x[dx] + along_y[dy], "blk": along_z[dz]}

    def remote(source, target, number, device):
        return pltpu.make_async_remote_copy(
            src_ref=source,
            dst_ref=target,
            send_sem=send_sem.at[number],
            recv_sem=recv_sem.at[number],
            device_id=device,
            device_id_type=pl.DeviceIdType.MESH,
        )

    def await_blocks(ref, number, semaphore):
        block = ref.at[pl.ds(0, number)]
        pltpu.make_async_copy(block, block, semaphore).wait()

    HEAD_Z, HEAD_XY, LINE, OVER, FACTS, SUMS, BACK, SWAP, PART = 0, 1, 2, 3, 4, 5, 6, 7, 10
    messages = [min(begin + steps, SELF) - begin for begin, steps, _ in PARTS]

    loads = [
        pltpu.make_async_copy(source, target, load_sem.at[number])
        for number, (source, target) in enumerate(
            (
                (assign_hbm, assign_ref),
                (owner_hbm, owner_ref),
                (count_hbm, count_ref),
                (index_hbm, index_ref),
                (x_hbm, x_ref),
            )
        )
    ]
    for load in loads:
        load.start()
    barrier = pltpu.get_barrier_semaphore()
    for device in [device_at(step, 1) for step in range(SELF)] + [other_core]:
        pl.semaphore_signal(barrier, inc=1, device_id=device, device_id_type=pl.DeviceIdType.MESH)
    for load in loads[:-1]:
        load.wait()

    rank, count_column = rank_groups(count_ref)
    group, chip, slot, place_counts = place_documents(assign_ref, owner_ref, rank)
    step_of = step_to((chip >> 4) - my_x, ((chip >> 2) & 3) - my_y, (chip & 3) - my_z)
    in_base = slot < BASE
    send_slot = jnp.where(in_base, step_of * BASE + slot, -1)
    heads[my_chip] = place_counts + 1024.0 * rank
    loads[-1].wait()

    def pack(first, stop):
        slots = iota(((stop - first) * BASE, ROWS), 0) + first * BASE
        rows = dot(onehot(slots == send_slot), x_ref[...]).astype(BF16)
        send[pl.ds(first, stop - first)] = rows.reshape(stop - first, BASE, WIDTH)

    def post(first, stop):
        for step in range(first, min(stop, SELF)):
            number = max(part for part in range(len(PARTS)) if PARTS[part][0] <= step)
            remote(send.at[step], got.at[step], PART + number, device_at(step, 1)).start()

    pack(0, 24)
    pl.semaphore_wait(barrier, CHIPS)
    for d in range(1, DEPTH):
        device = {"grp": grp, "blk": along_z[d]}
        block = heads.at[pl.ds(my_chip, 1)]
        remote(block, block, HEAD_Z, device).start()
    post(0, 8)
    place_counts_16 = place_counts + jnp.zeros((16, CLUSTERS), F32)
    own_excess = excess(dot(place_counts_16.astype(BF16), chip_places())[0:1])
    eye = iota((CHIPS, CLUSTERS), 0) == iota((CHIPS, CLUSTERS), 1)
    excess_column = across(pick(eye, own_excess))
    over_slot = down(pick(iota((CHIPS, ROWS), 0) < chip, excess_column)).astype(jnp.int32) + (slot - BASE)
    over_slot = jnp.where(in_base, -1, over_slot)
    own_over[...] = dot(onehot(iota((BASE, ROWS), 0) == over_slot), x_ref[...]).astype(BF16)
    line_over[my_z] = own_over[...]
    for d in range(1, DEPTH):
        remote(own_over, line_over.at[my_z], LINE, {"grp": grp, "blk": along_z[d]}).start()
    post(8, 24)

    await_blocks(heads, DEPTH - 1, recv_sem.at[HEAD_Z])
    line_heads = heads[pl.ds(grp * DEPTH, DEPTH)].reshape(DEPTH, CLUSTERS)
    line_counts = (line_heads.astype(jnp.int32) & 1023).astype(F32).astype(BF16)
    line_total = across(excess(dot(line_counts, chip_places())))
    depth = iota((DEPTH, 1), 0)
    line_start = jnp.zeros((DEPTH, 1), F32)
    for d in range(DEPTH - 1):
        line_start = line_start + pick(depth > d, line_total[d : d + 1])
    my_start = down(pick(depth == my_z, line_start))
    at = depth == (iota((DEPTH, DEPTH * BASE), 1) >> 4)
    begin = down(pick(at, line_start))
    number = down(pick(at, line_total))
    order = (iota((1, DEPTH * BASE), 1) & (BASE - 1)).astype(F32)
    order = jnp.where(order < number, begin + order, -1.0)
    rows = iota((2 * POOL, DEPTH * BASE), 0).astype(F32)
    await_blocks(line_over, DEPTH - 1, recv_sem.at[LINE])
    blocks = line_over[...].reshape(DEPTH * BASE, WIDTH)
    left = dot(onehot((rows == order) & (rows < POOL)), blocks[:, :HALF])
    right = dot(onehot((rows - POOL == order) & (rows >= POOL)), blocks[:, HALF:])
    send_over[...] = (left + right).astype(BF16)
    got_over[grp] = send_over[...]
    for step in range(1, LINES):
        low, middle = step % 4, step // 4
        device = {"grp": along_x[low] + along_y[(middle + low) % 4], "blk": blk}
        block = heads.at[pl.ds(grp * DEPTH, DEPTH)]
        remote(block, block, HEAD_XY, device).start()
        remote(send_over, got_over.at[grp], OVER, device).start()
    pack(24, 48)
    post(24, 48)
    pack(48, CHIPS)
    post(48, CHIPS)
    got[SELF] = send[SELF]

    await_blocks(heads, CHIPS - DEPTH, recv_sem.at[HEAD_XY])
    table = heads[...].reshape(CHIPS, CLUSTERS)
    plans, ends, fault = receive_plan(table, rank, my_x, my_y, my_z)

    missing = missing_documents(index_ref, count_column, group)
    row = iota((8, 128), 0)
    told = pick(row == 6, rank) + pick(row == 7, jnp.where(iota((1, 128), 1) == 0, fault, missing))
    for part, (first_end, held_end) in enumerate(ends):
        told = told + pick(row == part, first_end) + pick(row == 3 + part, held_end)
        picks[part][...] = onehot(iota(picks[part].shape, 0).astype(F32) == plans[part])
    facts[0] = told
    swap_facts = remote(facts.at[0], facts.at[1], FACTS, other_core)
    swap_facts.start()

    best = [jnp.full((1, room), -1.0, F32) for _, _, room in PARTS]
    key_kinds = []
    query_kinds = []
    totals = [jnp.zeros((1, WIDTH), F32), jnp.zeros((1, WIDTH), F32)]
    swaps = []

    def add_kinds(first, held, room):
        number = iota((room, 1), 0).astype(F32)
        key_kinds.append(jnp.where(number < first, 0.0, jnp.where(number < held, 1.0, 2.0)))

    for (first_end, held_end), (_, _, room) in zip(ends, PARTS):
        add_kinds(first_end, held_end, room)
        query_kinds.append(jnp.where(iota((1, room), 1).astype(F32) < first_end, 0.0, 1.0))

    def compare(first_key, last_key, first_query, last_query, more=0):
        begin, stop = [(STARTS + tuple(HELD + start for start in STARTS) + (2 * HELD,))[n] for n in (first_key, last_key + 1)]
        start, end = (STARTS + (HELD,))[first_query], (STARTS + (HELD,))[last_query + 1]
        scores = dot_rows(keys[begin : stop + more], keys[start:end])
        rest, scores = scores[stop - begin :], scores[: stop - begin]
        kind = jnp.concatenate(key_kinds[first_key : last_key + 1], axis=0)
        matched = kind == jnp.concatenate(query_kinds[first_query : last_query + 1], axis=1)
        if begin < end and start < stop:
            matched = matched & (iota(kind.shape, 0) + (begin - start) != iota((1, end - start), 1))
        scores = jnp.max(jnp.where(matched, scores, -1.0), axis=0, keepdims=True)
        for part in range(first_query, last_query + 1):
            piece = scores[:, STARTS[part] - start : STARTS[part] - start + PARTS[part][2]]
            best[part] = jnp.maximum(best[part], piece)
        return rest

    def arrive(part):
        begin, steps, room = PARTS[part]
        await_blocks(got, messages[part], recv_sem.at[PART + part])
        rows = dot(picks[part][...], got[pl.ds(begin, steps)].reshape(steps * BASE, WIDTH))
        unit = rows * lax.rsqrt(across(rows * rows) + EPSILON)
        keys[pl.ds(STARTS[part], room)] = unit.astype(BF16)
        swap = remote(
            keys.at[pl.ds(STARTS[part], room)], keys.at[pl.ds(HELD + STARTS[part], room)], SWAP + part, other_core
        )
        swap.start()
        swaps.append(swap)
        is_first = iota((room, 1), 0).astype(F32) < ends[part][0]
        totals[0] = totals[0] + down(pick(is_first, unit))
        totals[1] = totals[1] + down(jnp.where(is_first, 0.0, unit))

    arrive(0)
    compare(0, 0, 0, 0)
    swap_facts.wait()
    their_told = facts[1]
    for part, (_, _, room) in enumerate(PARTS):
        add_kinds(their_told[part : part + 1, 0:1], their_told[3 + part : 4 + part, 0:1], room)
    swaps[0].wait()
    compare(3, 3, 0, 0)
    await_blocks(got_over, LINES - 1, recv_sem.at[OVER])
    half_rows = got_over[...].reshape(LINES * 2 * POOL, HALF)
    shape = (LINES * POOL, LINES * 2 * POOL)
    to, at = iota(shape, 0), iota(shape, 1)
    same = ((to >> 3) == (at >> 4)) & ((to & 7) == (at & 7))
    left = dot(onehot(same & ((at & POOL) == 0)), half_rows)
    right = dot(onehot(same & ((at & POOL) != 0)), half_rows)
    whole = jnp.concatenate([left, right], axis=1).astype(BF16)
    got[pl.ds(CHIPS, TOTAL - CHIPS)] = whole.reshape(TOTAL - CHIPS, BASE, WIDTH)

    arrive(1)
    compare(0, 1, 1, 1)
    compare(1, 1, 0, 0)
    compare(3, 3, 1, 1)

    arrive(2)
    row = iota((8, WIDTH), 0)
    sums[...] = pick(row == 0, totals[0]) + pick(row == 1, totals[1])
    swap_sums = remote(sums, their_sums, SUMS, other_core)
    swap_sums.start()
    swaps[1].wait()
    compare(4, 4, 0, 1)
    compare(0, 4, 2, 2)
    compare(2, 2, 0, 1)

    swap_sums.wait()
    total = sums[...] + their_sums[...]
    keys[pl.ds(2 * HELD, 16)] = jnp.concatenate(halves(total), axis=0).astype(BF16)
    scale = lax.rsqrt(across(total * total) + EPSILON)
    swaps[2].wait()
    near = compare(5, 5, 0, 2, 16)
    near = (near[0:8] + near[8:16]) * scale

    poison = missing + their_told[7:8, 1:2] > 0.5
    tiles = CHIPS * BASE // 128
    for part, (begin, steps, room) in enumerate(PARTS):
        row = iota((8, room), 0)
        query_number = iota((1, room), 1).astype(F32)
        some = near[:, STARTS[part] : STARTS[part] + room]
        some = jnp.where(query_number < ends[part][0], some[0:1], some[1:2])
        values = jnp.zeros((8, room), F32)
        for number, term in enumerate(halves(best[part]) + halves(some)):
            values = jnp.where(row == number, term, values)
        out = dot(values.astype(BF16), picks[part][...])
        for kind in range(2):
            line = out[2 * kind : 2 * kind + 1] + out[2 * kind + 1 : 2 * kind + 2]
            line = jnp.where(poison, NONE, line)
            for tile in range(steps * BASE // 128):
                piece = line[:, tile * 128 : (tile + 1) * 128]
                to = begin * BASE // 128 + tile
                if to < tiles:
                    back[to, kind : kind + 1, :] = piece
                else:
                    for each in range(tiles):
                        back[each, 2 + kind : 3 + kind, :] = piece
    returned[SELF] = back[SELF // 8]
    for step in range(SELF):
        remote(back.at[step // 8], returned.at[step], BACK, device_at(step, -1)).start()

    differ = across(jnp.where(their_told[6:7] != rank, 1.0, 0.0))
    fault = fault + their_told[7:8, 0:1] + differ
    chosen = onehot(iota((CHIPS, ROWS), 0) == step_of)
    sub = iota((128, ROWS), 0)
    at_base = (sub == (step_of & 7) * BASE + slot) & in_base
    at_over = (sub == grp * POOL + my_start.astype(jnp.int32) + over_slot) & (~in_base)

    await_blocks(returned, CHIPS - 1, recv_sem.at[BACK])
    found = []
    for number in range(4):
        line = returned[:, number, :]
        if number == 0:
            poisoned = across(down(jnp.where(line > 0.5 * NONE, 1.0, 0.0)))
            fault_ref[...] = jnp.where(fault + poisoned > 0.5, 1, 0) + jnp.zeros((1, 128), jnp.int32)
        terms = jnp.concatenate(halves(line), axis=1).astype(BF16)
        out = lax.dot_general(terms, chosen, (((0,), (0,)), ((), ())), preferred_element_type=F32)
        found.append(out[0:128] + out[128:256])
    out_ref[0:1] = down(pick(at_base, found[0]) + pick(at_over, found[2]))
    out_ref[1:2] = down(pick(at_base, found[1]) + pick(at_over, found[3]))

    await_blocks(heads, DEPTH - 1, send_sem.at[HEAD_Z])
    await_blocks(heads, CHIPS - DEPTH, send_sem.at[HEAD_XY])
    await_blocks(line_over, DEPTH - 1, send_sem.at[LINE])
    await_blocks(got_over, LINES - 1, send_sem.at[OVER])
    await_blocks(returned, CHIPS - 1, send_sem.at[BACK])
    for part in range(len(PARTS)):
        await_blocks(got, messages[part], send_sem.at[PART + part])


def routed(embeddings, assign, owner, send_count, send_index):
    return pl.pallas_call(
        kernel,
        out_shape=(
            jax.ShapeDtypeStruct((2, ROWS), F32),
            jax.ShapeDtypeStruct((1, 128), jnp.int32),
        ),
        in_specs=[pl.BlockSpec(memory_space=pl.ANY)] * 5,
        out_specs=(pl.BlockSpec(memory_space=pltpu.VMEM),) * 2,
        scratch_shapes=[
            pltpu.VMEM((ROWS, WIDTH), BF16),
            pltpu.VMEM((1, ROWS), jnp.int32),
            pltpu.VMEM((1, CLUSTERS), jnp.int32),
            pltpu.VMEM((1, GROUPS), jnp.int32),
            pltpu.VMEM((GROUPS, CAP), jnp.int32),
            pltpu.VMEM((CHIPS, BASE, WIDTH), BF16),
            pltpu.VMEM((TOTAL, BASE, WIDTH), BF16),
            pltpu.VMEM((CHIPS, 1, 128), F32),
            pltpu.VMEM((BASE, WIDTH), BF16),
            pltpu.VMEM((DEPTH, BASE, WIDTH), BF16),
            pltpu.VMEM((2 * POOL, HALF), BF16),
            pltpu.VMEM((LINES, 2 * POOL, HALF), BF16),
            *[pltpu.VMEM((room, steps * BASE), BF16) for _, steps, room in PARTS],
            pltpu.VMEM((2 * HELD + 16, WIDTH), BF16),
            pltpu.VMEM((2, 8, 128), F32),
            pltpu.VMEM((8, WIDTH), F32),
            pltpu.VMEM((8, WIDTH), F32),
            pltpu.VMEM((CHIPS * BASE // 128, 4, 128), F32),
            pltpu.VMEM((CHIPS, 4, 128), F32),
            pltpu.SemaphoreType.DMA((5,)),
            pltpu.SemaphoreType.DMA((13,)),
            pltpu.SemaphoreType.DMA((13,)),
        ],
        compiler_params=pltpu.CompilerParams(
            collective_id=0, has_side_effects=True, vmem_limit_bytes=48 * 1024 * 1024
        ),
    )(
        embeddings,
        assign.reshape(1, ROWS),
        owner.reshape(1, CLUSTERS),
        send_count,
        send_index[0],
    )


def body(embeddings, assign, owner, send_count, send_index):
    arguments = (embeddings, assign, owner, send_count, send_index)
    results, fault = routed(*arguments)
    results = lax.cond(fault[0, 0] != 0, lambda: jnp.stack(general(*arguments)), lambda: results)
    return results[0], results[1]


def solution(mesh):
    placed = (
        P(("grp", "blk"), None),
        P(("grp", "blk")),
        P(),
        P(("grp", "blk"), None),
        P(("grp", "blk"), None, None),
    )
    return jax.shard_map(
        body,
        mesh=mesh,
        in_specs=placed,
        out_specs=(P(("grp", "blk")), P(("grp", "blk"))),
        check_vma=False,
    )
```

```python
import functools

import jax
import jax.numpy as jnp
from jax import lax
from jax.experimental import pallas as pl
from jax.experimental.pallas import tpu as pltpu
from jax.sharding import PartitionSpec as P

EPSILON = 1e-06
F32 = jnp.float32
BF16 = jnp.bfloat16

CHIPS = 64
ROWS = 512
WIDTH = 768
CLUSTERS = 128
GROUPS = 16
CAP = 64
BASE = 16
HALF = WIDTH // 2
LINES = 16
DEPTH = 4
POOL = 8
PARTS = ((0, 24, 256), (24, 32, 384), (56, 16, 128))
TOTAL = 72
HELD = 768
STARTS = (0, 256, 640)
LAST = len(PARTS) - 1
NONE = 1e30


def normalize(values):
    widened = values.astype(F32)
    return widened * lax.rsqrt(jnp.sum(widened * widened, axis=1, keepdims=True) + EPSILON)


def general(embeddings, assign, owner, send_count, send_index):
    rows_local = embeddings.shape[0]
    feature_width = embeddings.shape[1]
    groups = lax.axis_size("grp")
    clusters = owner.shape[0]
    capacity = send_index.shape[2]
    slot_total = groups * capacity
    unit_rows = normalize(embeddings)
    unit_low = unit_rows.astype(BF16)
    counts = send_count[0]
    listed = send_index[0]
    live_slot = jnp.arange(capacity, dtype=jnp.int32)[None, :] < counts[:, None]
    listed_cluster = assign[listed]
    owned_here = owner[listed_cluster] == jnp.arange(groups, dtype=jnp.int32)[:, None]
    kept_slot = live_slot & owned_here
    out_cluster = jnp.where(kept_slot, listed_cluster, -1)
    out_tag = jnp.where(kept_slot, lax.axis_index(("grp", "blk")) * rows_local + listed, -1)
    out_vector = unit_low[listed.reshape(-1)].reshape(groups, capacity, feature_width)
    got_vector, got_cluster, got_tag = (
        lax.all_to_all(out_vector, "grp", split_axis=0, concat_axis=0, tiled=True),
        lax.all_to_all(out_cluster, "grp", split_axis=0, concat_axis=0, tiled=True),
        lax.all_to_all(out_tag, "grp", split_axis=0, concat_axis=0, tiled=True),
    )
    own_vector = got_vector.reshape(slot_total, feature_width)
    own_cluster = got_cluster.reshape(slot_total)
    own_tag = got_tag.reshape(slot_total)

    def tile_best(current, shard_piece):
        other_vector, other_cluster, other_tag = shard_piece
        scores = jnp.einsum("id,jd->ij", own_vector, other_vector, preferred_element_type=F32)
        matched = (
            (own_cluster[:, None] == other_cluster[None, :])
            & (other_cluster[None, :] >= 0)
            & (own_tag[:, None] != other_tag[None, :])
        )
        return jnp.maximum(current, jnp.max(jnp.where(matched, scores, -1.0), axis=1))

    other_vector = lax.all_gather(own_vector, "blk", axis=0, tiled=True)
    other_cluster = lax.all_gather(own_cluster, "blk", axis=0, tiled=True)
    other_tag = lax.all_gather(own_tag, "blk", axis=0, tiled=True)
    length = other_vector.shape[0]
    number = length // slot_total
    stacked = (
        other_vector.reshape(number, slot_total, feature_width),
        other_cluster.reshape(number, slot_total),
        other_tag.reshape(number, slot_total),
    )

    def scan_step(carry, single):
        return (tile_best(carry, single), None)

    result, unused = lax.scan(scan_step, jnp.full((slot_total,), -1.0, F32), stacked)
    target = jnp.where(live_slot, listed, rows_local).reshape(-1)
    partial_sum = jax.ops.segment_sum(unit_rows, assign, num_segments=clusters)
    centre = normalize(lax.psum(partial_sum, ("grp", "blk")))
    nearness = jnp.sum(unit_low.astype(F32) * centre[assign], axis=1)
    returned = lax.all_to_all(
        result.reshape(groups, capacity), "grp", split_axis=0, concat_axis=0, tiled=True
    )
    has_entry = (
        jnp.zeros((rows_local,), jnp.int32)
        .at[target]
        .max(kept_slot.astype(jnp.int32).reshape(-1), mode="drop")
    )
    centroid_cos = jnp.where(has_entry > 0, nearness, 0.0)
    max_sim = jnp.full((rows_local,), -1.0, F32).at[target].max(returned.reshape(-1), mode="drop")
    return (max_sim, centroid_cos)


def iota(shape, axis):
    return lax.broadcasted_iota(jnp.int32, shape, axis)


def down(values):
    return jnp.sum(values, axis=0, keepdims=True)


def across(values):
    return jnp.sum(values, axis=1, keepdims=True)


def pick(mask, values):
    return jnp.where(mask, values, 0.0)


def as_column(row):
    size = row.shape[1]
    return across(pick(iota((size, size), 0) == iota((size, size), 1), row))


def as_row(column):
    size = column.shape[0]
    return down(pick(iota((size, size), 0) == iota((size, size), 1), column))


def dot(a, b):
    return jnp.dot(a, b, preferred_element_type=F32)


def dot_rows(a, b):
    return lax.dot_general(a, b, (((1,), (1,)), ((), ())), preferred_element_type=F32)


def onehot(mask):
    return jnp.where(mask, 1.0, 0.0).astype(BF16)


def thirds(values):
    first = values.astype(BF16).astype(F32)
    rest = values - first
    second = rest.astype(BF16).astype(F32)
    third = (rest - second).astype(BF16).astype(F32)
    return first, second, third


def rank_groups(count_ref):
    count_row = count_ref[...].astype(F32)
    count_column = as_column(count_row)
    sub, lane = iota((GROUPS, 128), 0), iota((GROUPS, 128), 1)
    count_lanes = down(pick(sub == lane, count_column))
    ahead = (count_column > count_lanes) | ((count_column == count_lanes) & (sub < lane))
    rank = down(jnp.where(ahead, 1.0, 0.0))
    return jnp.where(iota((1, 128), 1) < GROUPS, rank, 0.0), count_column


def place_documents(assign_ref, owner_ref, rank):
    owner_row = owner_ref[...].astype(F32)
    owner_column = as_column(owner_row)
    sub, lane = iota((CLUSTERS, CLUSTERS), 0), iota((CLUSTERS, CLUSTERS), 1)
    within = across(jnp.where((owner_column == owner_row) & (lane < sub), 1.0, 0.0))
    group_rank = across(pick(owner_column == lane.astype(F32), rank))
    place_column = group_rank * (CLUSTERS // GROUPS) + within
    member = iota((CLUSTERS, ROWS), 0) == assign_ref[...]
    place = down(pick(member, place_column))
    group = down(pick(member, owner_column))
    order = iota((CLUSTERS, ROWS), 0).astype(F32)
    at_place = order == place
    earlier = onehot(iota((ROWS, ROWS), 0) < iota((ROWS, ROWS), 1))
    before = dot(onehot(at_place), earlier)
    slot = down(pick(at_place, before))
    count_column = across(jnp.where(at_place, 1.0, 0.0))
    partner_count = down(pick(order == (CLUSTERS - 1) - place, count_column))
    slot = slot + jnp.where(place >= CHIPS, partner_count, 0.0)
    chip = jnp.minimum(place, (CLUSTERS - 1) - place)
    return group, chip.astype(jnp.int32), slot.astype(jnp.int32), as_row(count_column)


def missing_documents(index_ref, count_column, group):
    listed = index_ref[...]
    live = iota((GROUPS, CAP), 1).astype(F32) < count_column
    eye = onehot(iota((CAP, CAP), 0) == iota((CAP, CAP), 1))
    high = dot_rows(eye, jnp.where(live, listed >> 4, 0).astype(F32).astype(BF16))
    low = dot_rows(eye, jnp.where(live, listed & 15, 0).astype(F32).astype(BF16))
    alive = dot_rows(eye, onehot(live))
    slots = jnp.where(alive > 0.5, high * 16.0 + low, -1.0)
    document = iota((1, ROWS), 1).astype(F32)
    lane = iota((CAP, GROUPS), 1)

    def count(g, hits):
        column = across(pick(lane == g, slots))
        wanted = jnp.where(group == g.astype(F32), document, -2.0)
        return hits + jnp.where(column == wanted, 1.0, 0.0)

    hits = lax.fori_loop(0, GROUPS, count, jnp.zeros((CAP, ROWS), F32))
    return across(jnp.where(down(hits) > 0.5, 0.0, 1.0))


ORDERS = (
    (
        (2, 2, 0), (3, 3, 1), (3, 3, 3), (0, 2, 0), (3, 1, 1), (1, 1, 1), (1, 3, 3), (0, 2, 2), (0, 0, 2),
        (1, 1, 3), (1, 3, 1), (3, 1, 3), (0, 2, 3), (1, 1, 2), (0, 2, 1), (1, 3, 2), (2, 0, 3), (3, 1, 2),
        (2, 0, 1), (3, 3, 2), (1, 0, 1), (0, 3, 2), (1, 2, 3), (2, 3, 0), (3, 0, 1), (2, 1, 0), (1, 2, 1),
        (0, 1, 2), (1, 0, 3), (3, 1, 0), (0, 1, 3), (1, 2, 0), (0, 1, 1), (1, 0, 2), (0, 3, 3), (3, 0, 2),
        (2, 3, 3), (3, 2, 0), (2, 1, 3), (3, 2, 3), (0, 3, 1), (3, 3, 0), (2, 1, 1), (1, 1, 0), (3, 2, 1),
        (1, 3, 0), (2, 3, 1), (3, 0, 3), (2, 1, 2), (3, 2, 2), (2, 2, 2), (2, 3, 2), (2, 2, 3), (1, 2, 2),
        (2, 2, 1), (2, 0, 2), (2, 0, 0), (0, 0, 3), (0, 0, 1), (0, 3, 0), (3, 0, 0), (1, 0, 0), (0, 1, 0),
    ),
    (
        (0, 0, 2), (1, 1, 3), (1, 1, 1), (2, 0, 2), (1, 3, 3), (3, 3, 3), (3, 1, 1), (2, 0, 0), (2, 2, 0),
        (3, 3, 1), (3, 1, 3), (1, 3, 1), (2, 0, 1), (3, 3, 0), (2, 0, 3), (3, 1, 0), (0, 2, 1), (1, 3, 0),
        (0, 2, 3), (1, 1, 0), (3, 2, 3), (2, 1, 0), (3, 0, 1), (0, 1, 2), (1, 2, 3), (0, 3, 2), (3, 0, 3),
        (2, 3, 0), (3, 2, 1), (1, 3, 2), (2, 3, 1), (3, 0, 2), (2, 3, 3), (3, 2, 0), (2, 1, 1), (1, 2, 0),
        (0, 1, 1), (1, 0, 2), (0, 3, 1), (1, 0, 1), (2, 1, 3), (1, 1, 2), (0, 3, 3), (3, 3, 2), (1, 0, 3),
        (3, 1, 2), (0, 1, 3), (1, 2, 1), (2, 2, 1), (2, 2, 2), (2, 2, 3), (1, 2, 2), (3, 2, 2), (2, 3, 2),
        (0, 2, 2), (2, 1, 2), (0, 2, 0), (3, 0, 0), (0, 1, 0), (1, 0, 0), (0, 0, 3), (0, 0, 1), (0, 3, 0),
    ),
)
SELF = CHIPS - 1


def by_core(first, second, core):
    return first + core * (second - first) if first != second else first


def step_to(dx, dy, dz, core):
    shift = (dx & 3) * 16 + (dy & 3) * 4 + (dz & 3)
    step = jnp.full(shift.shape, SELF, jnp.int32)
    for number in range(SELF):
        codes = [x * 16 + y * 4 + z for x, y, z in (order[number] for order in ORDERS)]
        step = jnp.where(shift == by_core(*codes, core), number, step)
    return step


def in_part(step, part):
    begin, steps, _ = PARTS[part]
    return (step >= begin) & (step < begin + steps)


def chip_places():
    sub, lane = iota((CLUSTERS, CLUSTERS), 0), iota((CLUSTERS, CLUSTERS), 1)
    return onehot((sub == lane) | (sub == (CLUSTERS - 1) - lane))


def excess(totals):
    lane = iota(totals.shape, 1)
    return jnp.where(lane < CHIPS, jnp.maximum(totals - BASE, 0.0), 0.0)


def receive_plan(table, rank, my_x, my_y, my_z, core):
    chip = my_x * 16 + my_y * 4 + my_z
    heads = table.astype(jnp.int32)
    counts = (heads & 1023).astype(F32)
    differ = jnp.where((heads >> 10).astype(F32) != rank, 1.0, 0.0)
    fault = across(down(differ))
    both = dot(counts.astype(BF16), chip_places())
    over = excess(both)
    lanes = iota((CHIPS, CLUSTERS), 1)
    sender = iota((CHIPS, 1), 0)
    source, target = iota((CHIPS, CHIPS), 0), iota((CHIPS, CHIPS), 1)

    same_line = (source >> 2) == (target >> 2)
    over_total = across(over)
    over_row = as_row(over_total)
    line_start = across(pick(same_line & (target < source), over_row))
    line_total = across(pick(same_line, over_row))
    fault = fault + down(jnp.where(line_total > POOL, 1.0, 0.0))
    start = line_start + across(pick(lanes < chip, over))
    number = across(pick(lanes == chip, over))

    to_chip = iota((1, CLUSTERS), 1)
    route = step_to(
        (to_chip >> 4) - (sender >> 4), ((to_chip >> 2) & 3) - ((sender >> 2) & 3), (to_chip & 3) - (sender & 3), core
    )
    based = jnp.where(lanes < CHIPS, jnp.minimum(both, float(BASE)), 0.0)
    for part, (_, _, room) in enumerate(PARTS):
        held = down(pick(in_part(route, part), based))
        if part == LAST:
            held = held + down(over)
        fault = fault + across(jnp.where(held > room, 1.0, 0.0))

    first = across(pick(lanes == chip, counts))
    second = across(pick(lanes == (CLUSTERS - 1) - chip, counts))
    place = (lanes & (POOL - 1)).astype(F32) - start
    mine = ((sender >> 2) == (lanes >> 3)) & (place >= 0.0) & (place < number)
    over_first = down(jnp.where(mine & (place + BASE < first), 1.0, 0.0))
    over_second = down(jnp.where(mine & (place + BASE >= first), 1.0, 0.0))
    over_first_total, over_second_total = across(over_first), across(over_second)
    earlier = onehot(iota((CLUSTERS, CLUSTERS), 0) < iota((CLUSTERS, CLUSTERS), 1))
    sub = iota((16, CLUSTERS), 0)
    before = dot((pick(sub == 0, over_first) + pick(sub == 1, over_second)).astype(BF16), earlier)

    base_first = jnp.minimum(first, float(BASE))
    base_second = jnp.minimum(first + second, float(BASE)) - base_first
    first_row, second_row = as_row(base_first), as_row(base_second)

    def my_step(other):
        return step_to(my_x - (other >> 4), my_y - ((other >> 2) & 3), my_z - (other & 3), core)

    step_column, step_row = my_step(sender), my_step(iota((1, CHIPS), 1))
    plans = []
    ends = []
    for part, (begin, steps, _) in enumerate(PARTS):
        inside = in_part(step_column, part)
        ahead = (target < source) & in_part(step_row, part)
        first_total = down(pick(inside, base_first))
        second_total = down(pick(inside, base_second))
        last = part == LAST
        first_end = first_total + over_first_total if last else first_total
        first_start = across(pick(ahead, first_row))
        second_start = across(pick(ahead, second_row)) + first_end
        spread = step_column - begin == (iota((CHIPS, steps * BASE), 1) >> 4)
        head, tail, head_start, tail_start = [
            down(pick(spread, column)) for column in (base_first, base_second, first_start, second_start)
        ]
        slot = (iota((1, steps * BASE), 1) & (BASE - 1)).astype(F32)
        later = jnp.where(slot < head + tail, tail_start + (slot - head), -1.0)
        plan = jnp.where(slot < head, head_start + slot, later)
        held_end = first_end + second_total
        if last:
            over_row_of = jnp.where(over_second > 0.5, held_end + before[1:2], -1.0)
            over_row_of = jnp.where(over_first > 0.5, first_total + before[0:1], over_row_of)
            plan = jnp.concatenate([plan[:, : steps * BASE - CLUSTERS], over_row_of], axis=1)
            held_end = held_end + over_second_total
        plans.append(plan)
        ends.append((first_end, held_end))
    return plans, ends, line_start, over_total, fault


def kernel(
    x_hbm, assign_hbm, owner_hbm, count_hbm, index_hbm,
    out_ref, fault_ref,
    x_ref, assign_ref, owner_ref, count_ref, index_ref,
    send, got, heads, own_over, line_over, send_over, got_over, pick_0, pick_1, pick_2,
    mine, theirs, facts, sums, their_sums, back, returned,
    load_sem, send_sem, recv_sem,
):
    grp, blk = lax.axis_index("grp"), lax.axis_index("blk")
    my_x, my_y, my_z, core = grp // 4, grp % 4, blk // 2, blk % 2
    my_chip = grp * 4 + my_z
    picks = (pick_0, pick_1, pick_2)
    along_x = [((my_x + d) % 4) * 4 for d in range(4)]
    along_y = [(my_y + d) % 4 for d in range(4)]
    along_z = [((my_z + d) % 4) * 2 + core for d in range(4)]
    other_core = {"grp": grp, "blk": my_z * 2 + (1 - core)}

    def device_at(step, sign):
        shifts = [[(sign * d) % 4 for d in order[step]] for order in ORDERS]
        x, y, z = [(my + by_core(d0, d1, core)) % 4 for my, d0, d1 in zip((my_x, my_y, my_z), *shifts)]
        return {"grp": x * 4 + y, "blk": z * 2 + core}

    def remote(source, target, number, device):
        return pltpu.make_async_remote_copy(
            src_ref=source,
            dst_ref=target,
            send_sem=send_sem.at[number],
            recv_sem=recv_sem.at[number],
            device_id=device,
            device_id_type=pl.DeviceIdType.MESH,
        )

    def await_blocks(ref, number, semaphore):
        block = ref.at[pl.ds(0, number)]
        pltpu.make_async_copy(block, block, semaphore).wait()

    HEAD_Z, HEAD_Y, HEAD_X, LINE, OVER, FACTS, SUMS, BACK, SWAP, PART = 0, 1, 2, 3, 4, 5, 6, 7, 8, 11
    messages = [min(begin + steps, SELF) - begin for begin, steps, _ in PARTS]

    loads = [
        pltpu.make_async_copy(source, target, load_sem.at[number])
        for number, (source, target) in enumerate(
            (
                (assign_hbm, assign_ref),
                (owner_hbm, owner_ref),
                (count_hbm, count_ref),
                (index_hbm, index_ref),
                (x_hbm, x_ref),
            )
        )
    ]
    for load in loads:
        load.start()
    barrier = pltpu.get_barrier_semaphore()
    for device in [device_at(step, 1) for step in range(SELF)] + [other_core]:
        pl.semaphore_signal(barrier, inc=1, device_id=device, device_id_type=pl.DeviceIdType.MESH)
    for load in loads[:-1]:
        load.wait()

    rank, count_column = rank_groups(count_ref)
    group, chip, slot, place_counts = place_documents(assign_ref, owner_ref, rank)
    step_of = step_to((chip >> 4) - my_x, ((chip >> 2) & 3) - my_y, (chip & 3) - my_z, core)
    in_base = slot < BASE
    send_slot = jnp.where(in_base, step_of * BASE + slot, -1)
    heads[my_chip] = place_counts + 1024.0 * rank
    loads[-1].wait()

    def pack(first, stop):
        slots = iota(((stop - first) * BASE, ROWS), 0) + first * BASE
        rows = dot(onehot(slots == send_slot), x_ref[...]).astype(BF16)
        send[pl.ds(first, stop - first)] = rows.reshape(stop - first, BASE, WIDTH)

    def post(first, stop):
        for step in range(first, min(stop, SELF)):
            number = max(part for part in range(len(PARTS)) if PARTS[part][0] <= step)
            remote(send.at[step], got.at[step], PART + number, device_at(step, 1)).start()

    def share_heads(first, number, semaphore, devices):
        block = heads.at[pl.ds(first, number)]
        for device in devices:
            remote(block, block, semaphore, device).start()

    pack(0, 24)
    pl.semaphore_wait(barrier, CHIPS)
    share_heads(my_chip, 1, HEAD_Z, [{"grp": grp, "blk": along_z[d]} for d in range(1, 4)])
    post(0, 8)
    place_counts_16 = place_counts + jnp.zeros((16, CLUSTERS), F32)
    own_excess = excess(dot(place_counts_16.astype(BF16), chip_places())[0:1])
    eye = iota((CHIPS, CLUSTERS), 0) == iota((CHIPS, CLUSTERS), 1)
    excess_column = across(pick(eye, own_excess))
    over_slot = down(pick(iota((CHIPS, ROWS), 0) < chip, excess_column)).astype(jnp.int32) + (slot - BASE)
    over_slot = jnp.where(in_base, -1, over_slot)
    own_over[...] = dot(onehot(iota((BASE, ROWS), 0) == over_slot), x_ref[...]).astype(BF16)
    line_over[my_z] = own_over[...]
    for d in range(1, DEPTH):
        remote(own_over, line_over.at[my_z], LINE, {"grp": grp, "blk": along_z[d]}).start()
    await_blocks(heads, 3, recv_sem.at[HEAD_Z])
    share_heads(grp * 4, 4, HEAD_Y, [{"grp": along_x[0] + along_y[d], "blk": blk} for d in range(1, 4)])
    post(8, 16)
    pack(24, 48)
    await_blocks(heads, 12, recv_sem.at[HEAD_Y])
    share_heads(my_x * 16, 16, HEAD_X, [{"grp": along_x[d] + along_y[0], "blk": blk} for d in range(1, 4)])
    post(16, 40)
    pack(48, CHIPS)
    got[SELF] = send[SELF]

    await_blocks(heads, 48, recv_sem.at[HEAD_X])
    table = heads[...].reshape(CHIPS, CLUSTERS)
    plans, ends, line_start, over_total, fault = receive_plan(table, rank, my_x, my_y, my_z, core)

    await_blocks(line_over, DEPTH - 1, recv_sem.at[LINE])
    sender = iota((CHIPS, 1), 0)
    at = sender == grp * 4 + (iota((CHIPS, DEPTH * BASE), 1) >> 4)
    begin = down(pick(at, line_start))
    number = down(pick(at, over_total))
    order = (iota((1, DEPTH * BASE), 1) & (BASE - 1)).astype(F32)
    order = jnp.where(order < number, begin + order, -1.0)
    my_start = down(pick(sender == my_chip, line_start))
    rows = iota((2 * POOL, DEPTH * BASE), 0).astype(F32)
    blocks = line_over[...].reshape(DEPTH * BASE, WIDTH)
    left = dot(onehot((rows == order) & (rows < POOL)), blocks[:, :HALF])
    right = dot(onehot((rows - POOL == order) & (rows >= POOL)), blocks[:, HALF:])
    send_over[...] = (left + right).astype(BF16)
    got_over[grp] = send_over[...]
    for step in range(1, LINES):
        low, middle = step % 4, step // 4
        device = {"grp": along_x[low] + along_y[(middle + low) % 4], "blk": blk}
        remote(send_over, got_over.at[grp], OVER, device).start()
    post(40, CHIPS)

    missing = missing_documents(index_ref, count_column, group)
    row = iota((8, 128), 0)
    told = pick(row == 6, rank) + pick(row == 7, jnp.where(iota((1, 128), 1) == 0, fault, missing))
    for part, (first_end, held_end) in enumerate(ends):
        told = told + pick(row == part, first_end) + pick(row == 3 + part, held_end)
        picks[part][...] = onehot(iota(picks[part].shape, 0).astype(F32) == plans[part])
    facts[0] = told
    swap_facts = remote(facts.at[0], facts.at[1], FACTS, other_core)
    swap_facts.start()

    best = [jnp.full((1, room), -1.0, F32) for _, _, room in PARTS]
    their_ends = []
    totals = [jnp.zeros((1, WIDTH), F32), jnp.zeros((1, WIDTH), F32)]
    swaps = []

    def window(part):
        return pl.ds(STARTS[part], PARTS[part][2])

    def compare(keys, key_part, query_part, key_ends, itself):
        scores = dot_rows(keys[window(key_part)], mine[window(query_part)])
        first, held = key_ends[key_part]
        key_number = iota((PARTS[key_part][2], 1), 0).astype(F32)
        query_number = iota((1, PARTS[query_part][2]), 1).astype(F32)
        kind = jnp.where(key_number < first, 0.0, jnp.where(key_number < held, 1.0, 2.0))
        matched = kind == jnp.where(query_number < ends[query_part][0], 0.0, 1.0)
        if itself and key_part == query_part:
            matched = matched & (key_number != query_number)
        scores = jnp.max(jnp.where(matched, scores, -1.0), axis=0, keepdims=True)
        best[query_part] = jnp.maximum(best[query_part], scores)

    for part, (begin, steps, room) in enumerate(PARTS):
        if part == LAST:
            await_blocks(got_over, LINES - 1, recv_sem.at[OVER])
            halves = got_over[...].reshape(LINES * 2 * POOL, HALF)
            shape = (LINES * POOL, LINES * 2 * POOL)
            to, at = iota(shape, 0), iota(shape, 1)
            same = ((to >> 3) == (at >> 4)) & ((to & 7) == (at & 7))
            left = dot(onehot(same & ((at & POOL) == 0)), halves)
            right = dot(onehot(same & ((at & POOL) != 0)), halves)
            whole = jnp.concatenate([left, right], axis=1).astype(BF16)
            got[pl.ds(CHIPS, TOTAL - CHIPS)] = whole.reshape(TOTAL - CHIPS, BASE, WIDTH)
        await_blocks(got, messages[part], recv_sem.at[PART + part])
        rows = dot(picks[part][...], got[pl.ds(begin, steps)].reshape(steps * BASE, WIDTH))
        unit = rows * lax.rsqrt(across(rows * rows) + EPSILON)
        mine[window(part)] = unit.astype(BF16)
        swap = remote(mine.at[window(part)], theirs.at[window(part)], SWAP + part, other_core)
        swap.start()
        swaps.append(swap)
        is_first = iota((room, 1), 0).astype(F32) < ends[part][0]
        totals[0] = totals[0] + down(pick(is_first, unit))
        totals[1] = totals[1] + down(jnp.where(is_first, 0.0, unit))
        if part == LAST:
            row = iota((8, WIDTH), 0)
            sums[...] = pick(row == 0, totals[0]) + pick(row == 1, totals[1])
            swap_sums = remote(sums, their_sums, SUMS, other_core)
            swap_sums.start()
        for other in range(part + 1):
            compare(mine, part, other, ends, True)
            if other != part:
                compare(mine, other, part, ends, True)
        if part == 0:
            swap_facts.wait()
            their_told = facts[1]
            for number in range(len(PARTS)):
                their_ends.append((their_told[number : number + 1, 0:1], their_told[3 + number : 4 + number, 0:1]))
        else:
            for other in range(part - 1):
                compare(theirs, other, part, their_ends, False)
            swaps[part - 1].wait()
            for other in range(part + 1):
                compare(theirs, part - 1, other, their_ends, False)

    swap_sums.wait()
    total = sums[...] + their_sums[...]
    centre = total * lax.rsqrt(across(total * total) + EPSILON)
    near = dot_rows(jnp.concatenate(thirds(centre), axis=0).astype(BF16), mine[...])
    near = near[0:8] + near[8:16] + near[16:24]
    swaps[LAST].wait()
    for other in range(len(PARTS)):
        compare(theirs, LAST, other, their_ends, False)

    poison = missing + their_told[7:8, 1:2] > 0.5
    tiles = CHIPS * BASE // 128
    for part, (begin, steps, room) in enumerate(PARTS):
        row = iota((8, room), 0)
        query_number = iota((1, room), 1).astype(F32)
        some = near[:, STARTS[part] : STARTS[part] + room]
        some = jnp.where(query_number < ends[part][0], some[0:1], some[1:2])
        values = jnp.zeros((8, room), F32)
        for number, term in enumerate(thirds(best[part]) + thirds(some)):
            values = jnp.where(row == number, term, values)
        out = dot(values.astype(BF16), picks[part][...])
        for kind in range(2):
            line = out[3 * kind : 3 * kind + 1] + out[3 * kind + 1 : 3 * kind + 2] + out[3 * kind + 2 : 3 * kind + 3]
            line = jnp.where(poison, NONE, line)
            for tile in range(steps * BASE // 128):
                piece = line[:, tile * 128 : (tile + 1) * 128]
                to = begin * BASE // 128 + tile
                if to < tiles:
                    back[to, kind : kind + 1, :] = piece
                else:
                    for each in range(tiles):
                        back[each, 2 + kind : 3 + kind, :] = piece
    returned[SELF] = back[SELF // 8]
    for step in range(SELF):
        remote(back.at[step // 8], returned.at[step], BACK, device_at(step, -1)).start()

    differ = across(jnp.where(their_told[6:7] != rank, 1.0, 0.0))
    fault = fault + their_told[7:8, 0:1] + differ
    chosen = onehot(iota((CHIPS, ROWS), 0) == step_of)
    sub = iota((128, ROWS), 0)
    at_base = (sub == (step_of & 7) * BASE + slot) & in_base
    at_over = (sub == grp * POOL + my_start.astype(jnp.int32) + over_slot) & (~in_base)

    await_blocks(returned, CHIPS - 1, recv_sem.at[BACK])
    found = []
    for number in range(4):
        line = returned[:, number, :]
        if number == 0:
            poisoned = across(down(jnp.where(line > 0.5 * NONE, 1.0, 0.0)))
            fault_ref[...] = jnp.where(fault + poisoned > 0.5, 1, 0) + jnp.zeros((1, 128), jnp.int32)
        terms = jnp.concatenate(thirds(line), axis=1).astype(BF16)
        out = lax.dot_general(terms, chosen, (((0,), (0,)), ((), ())), preferred_element_type=F32)
        found.append(out[0:128] + out[128:256] + out[256:384])
    out_ref[0:1] = down(pick(at_base, found[0]) + pick(at_over, found[2]))
    out_ref[1:2] = down(pick(at_base, found[1]) + pick(at_over, found[3]))

    await_blocks(heads, 3, send_sem.at[HEAD_Z])
    await_blocks(heads, 12, send_sem.at[HEAD_Y])
    await_blocks(heads, 48, send_sem.at[HEAD_X])
    await_blocks(line_over, DEPTH - 1, send_sem.at[LINE])
    await_blocks(got_over, LINES - 1, send_sem.at[OVER])
    await_blocks(returned, CHIPS - 1, send_sem.at[BACK])
    for part in range(len(PARTS)):
        await_blocks(got, messages[part], send_sem.at[PART + part])


def routed(embeddings, assign, owner, send_count, send_index):
    return pl.pallas_call(
        kernel,
        out_shape=(
            jax.ShapeDtypeStruct((2, ROWS), F32),
            jax.ShapeDtypeStruct((1, 128), jnp.int32),
        ),
        in_specs=[pl.BlockSpec(memory_space=pl.ANY)] * 5,
        out_specs=(pl.BlockSpec(memory_space=pltpu.VMEM),) * 2,
        scratch_shapes=[
            pltpu.VMEM((ROWS, WIDTH), BF16),
            pltpu.VMEM((1, ROWS), jnp.int32),
            pltpu.VMEM((1, CLUSTERS), jnp.int32),
            pltpu.VMEM((1, GROUPS), jnp.int32),
            pltpu.VMEM((GROUPS, CAP), jnp.int32),
            pltpu.VMEM((CHIPS, BASE, WIDTH), BF16),
            pltpu.VMEM((TOTAL, BASE, WIDTH), BF16),
            pltpu.VMEM((CHIPS, 1, 128), F32),
            pltpu.VMEM((BASE, WIDTH), BF16),
            pltpu.VMEM((DEPTH, BASE, WIDTH), BF16),
            pltpu.VMEM((2 * POOL, HALF), BF16),
            pltpu.VMEM((LINES, 2 * POOL, HALF), BF16),
            *[pltpu.VMEM((room, steps * BASE), BF16) for _, steps, room in PARTS],
            pltpu.VMEM((HELD, WIDTH), BF16),
            pltpu.VMEM((HELD, WIDTH), BF16),
            pltpu.VMEM((2, 8, 128), F32),
            pltpu.VMEM((8, WIDTH), F32),
            pltpu.VMEM((8, WIDTH), F32),
            pltpu.VMEM((CHIPS * BASE // 128, 4, 128), F32),
            pltpu.VMEM((CHIPS, 4, 128), F32),
            pltpu.SemaphoreType.DMA((5,)),
            pltpu.SemaphoreType.DMA((14,)),
            pltpu.SemaphoreType.DMA((14,)),
        ],
        compiler_params=pltpu.CompilerParams(
            collective_id=0, has_side_effects=True, vmem_limit_bytes=48 * 1024 * 1024
        ),
    )(
        embeddings,
        assign.reshape(1, ROWS),
        owner.reshape(1, CLUSTERS),
        send_count,
        send_index[0],
    )


def body(embeddings, assign, owner, send_count, send_index):
    arguments = (embeddings, assign, owner, send_count, send_index)
    results, fault = routed(*arguments)
    results = lax.cond(fault[0, 0] != 0, lambda: jnp.stack(general(*arguments)), lambda: results)
    return results[0], results[1]


def solution(mesh):
    placed = (
        P(("grp", "blk"), None),
        P(("grp", "blk")),
        P(),
        P(("grp", "blk"), None),
        P(("grp", "blk"), None, None),
    )
    return jax.shard_map(
        body,
        mesh=mesh,
        in_specs=placed,
        out_specs=(P(("grp", "blk")), P(("grp", "blk"))),
        check_vma=False,
    )
```

```python
import functools

import jax
import jax.numpy as jnp
from jax import lax
from jax.experimental import pallas as pl
from jax.experimental.pallas import tpu as pltpu
from jax.sharding import PartitionSpec as P

EPSILON = 1e-06
F32 = jnp.float32
BF16 = jnp.bfloat16

CHIPS = 64
ROWS = 512
WIDTH = 768
CLUSTERS = 128
GROUPS = 16
CAP = 64
TILE = 16
PIECE = 256
BASE = 10
LINES = 16
DEPTH = 4
SPARE = 64
PARTS = ((0, 24, 256), (24, 32, 384), (56, 24, 128))
HELD = 768
STARTS = (0, 256, 640)
LAST = len(PARTS) - 1
NONE = 1e30


def normalize(values):
    widened = values.astype(F32)
    return widened * lax.rsqrt(jnp.sum(widened * widened, axis=1, keepdims=True) + EPSILON)


def general(embeddings, assign, owner, send_count, send_index):
    rows_local = embeddings.shape[0]
    feature_width = embeddings.shape[1]
    groups = lax.axis_size("grp")
    clusters = owner.shape[0]
    capacity = send_index.shape[2]
    slot_total = groups * capacity
    unit_rows = normalize(embeddings)
    unit_low = unit_rows.astype(BF16)
    counts = send_count[0]
    listed = send_index[0]
    live_slot = jnp.arange(capacity, dtype=jnp.int32)[None, :] < counts[:, None]
    listed_cluster = assign[listed]
    owned_here = owner[listed_cluster] == jnp.arange(groups, dtype=jnp.int32)[:, None]
    kept_slot = live_slot & owned_here
    out_cluster = jnp.where(kept_slot, listed_cluster, -1)
    out_tag = jnp.where(kept_slot, lax.axis_index(("grp", "blk")) * rows_local + listed, -1)
    out_vector = unit_low[listed.reshape(-1)].reshape(groups, capacity, feature_width)
    got_vector, got_cluster, got_tag = (
        lax.all_to_all(out_vector, "grp", split_axis=0, concat_axis=0, tiled=True),
        lax.all_to_all(out_cluster, "grp", split_axis=0, concat_axis=0, tiled=True),
        lax.all_to_all(out_tag, "grp", split_axis=0, concat_axis=0, tiled=True),
    )
    own_vector = got_vector.reshape(slot_total, feature_width)
    own_cluster = got_cluster.reshape(slot_total)
    own_tag = got_tag.reshape(slot_total)

    def tile_best(current, shard_piece):
        other_vector, other_cluster, other_tag = shard_piece
        scores = jnp.einsum("id,jd->ij", own_vector, other_vector, preferred_element_type=F32)
        matched = (
            (own_cluster[:, None] == other_cluster[None, :])
            & (other_cluster[None, :] >= 0)
            & (own_tag[:, None] != other_tag[None, :])
        )
        return jnp.maximum(current, jnp.max(jnp.where(matched, scores, -1.0), axis=1))

    other_vector = lax.all_gather(own_vector, "blk", axis=0, tiled=True)
    other_cluster = lax.all_gather(own_cluster, "blk", axis=0, tiled=True)
    other_tag = lax.all_gather(own_tag, "blk", axis=0, tiled=True)
    length = other_vector.shape[0]
    number = length // slot_total
    stacked = (
        other_vector.reshape(number, slot_total, feature_width),
        other_cluster.reshape(number, slot_total),
        other_tag.reshape(number, slot_total),
    )

    def scan_step(carry, single):
        return (tile_best(carry, single), None)

    result, unused = lax.scan(scan_step, jnp.full((slot_total,), -1.0, F32), stacked)
    target = jnp.where(live_slot, listed, rows_local).reshape(-1)
    partial_sum = jax.ops.segment_sum(unit_rows, assign, num_segments=clusters)
    centre = normalize(lax.psum(partial_sum, ("grp", "blk")))
    nearness = jnp.sum(unit_low.astype(F32) * centre[assign], axis=1)
    returned = lax.all_to_all(
        result.reshape(groups, capacity), "grp", split_axis=0, concat_axis=0, tiled=True
    )
    has_entry = (
        jnp.zeros((rows_local,), jnp.int32)
        .at[target]
        .max(kept_slot.astype(jnp.int32).reshape(-1), mode="drop")
    )
    centroid_cos = jnp.where(has_entry > 0, nearness, 0.0)
    max_sim = jnp.full((rows_local,), -1.0, F32).at[target].max(returned.reshape(-1), mode="drop")
    return (max_sim, centroid_cos)


def iota(shape, axis):
    return lax.broadcasted_iota(jnp.int32, shape, axis)


def down(values):
    return jnp.sum(values, axis=0, keepdims=True)


def across(values):
    return jnp.sum(values, axis=1, keepdims=True)


def pick(mask, values):
    return jnp.where(mask, values, 0.0)


def as_column(row):
    size = row.shape[1]
    return across(pick(iota((size, size), 0) == iota((size, size), 1), row))


def as_row(column):
    size = column.shape[0]
    return down(pick(iota((size, size), 0) == iota((size, size), 1), column))


def dot(a, b):
    return jnp.dot(a, b, preferred_element_type=F32)


def dot_rows(a, b):
    return lax.dot_general(a, b, (((1,), (1,)), ((), ())), preferred_element_type=F32)


def onehot(mask):
    return jnp.where(mask, 1.0, 0.0).astype(BF16)


def thirds(values):
    first = values.astype(BF16).astype(F32)
    rest = values - first
    second = rest.astype(BF16).astype(F32)
    third = (rest - second).astype(BF16).astype(F32)
    return first, second, third


def rank_groups(count_ref):
    count_row = count_ref[...].astype(F32)
    count_column = as_column(count_row)
    sub, lane = iota((GROUPS, 128), 0), iota((GROUPS, 128), 1)
    count_lanes = down(pick(sub == lane, count_column))
    ahead = (count_column > count_lanes) | ((count_column == count_lanes) & (sub < lane))
    rank = down(jnp.where(ahead, 1.0, 0.0))
    return jnp.where(iota((1, 128), 1) < GROUPS, rank, 0.0), count_column


def place_documents(assign_ref, owner_ref, rank):
    owner_row = owner_ref[...].astype(F32)
    owner_column = as_column(owner_row)
    sub, lane = iota((CLUSTERS, CLUSTERS), 0), iota((CLUSTERS, CLUSTERS), 1)
    within = across(jnp.where((owner_column == owner_row) & (lane < sub), 1.0, 0.0))
    group_rank = across(pick(owner_column == lane.astype(F32), rank))
    place_column = group_rank * (CLUSTERS // GROUPS) + within
    member = iota((CLUSTERS, ROWS), 0) == assign_ref[...]
    place = down(pick(member, place_column))
    group = down(pick(member, owner_column))
    order = iota((CLUSTERS, ROWS), 0).astype(F32)
    at_place = order == place
    earlier = onehot(iota((ROWS, ROWS), 0) < iota((ROWS, ROWS), 1))
    before = dot(onehot(at_place), earlier)
    slot = down(pick(at_place, before))
    count_column = across(jnp.where(at_place, 1.0, 0.0))
    partner_count = down(pick(order == (CLUSTERS - 1) - place, count_column))
    slot = slot + jnp.where(place >= CHIPS, partner_count, 0.0)
    chip = jnp.minimum(place, (CLUSTERS - 1) - place)
    return group, chip.astype(jnp.int32), slot.astype(jnp.int32), as_row(count_column)


def missing_documents(index_ref, count_column, group):
    listed = index_ref[...]
    live = iota((GROUPS, CAP), 1).astype(F32) < count_column
    eye = onehot(iota((CAP, CAP), 0) == iota((CAP, CAP), 1))
    high = dot_rows(eye, jnp.where(live, listed >> 4, 0).astype(F32).astype(BF16))
    low = dot_rows(eye, jnp.where(live, listed & 15, 0).astype(F32).astype(BF16))
    alive = dot_rows(eye, onehot(live))
    slots = jnp.where(alive > 0.5, high * 16.0 + low, -1.0)
    document = iota((1, ROWS), 1).astype(F32)
    lane = iota((CAP, GROUPS), 1)

    def count(g, hits):
        column = across(pick(lane == g, slots))
        wanted = jnp.where(group == g.astype(F32), document, -2.0)
        return hits + jnp.where(column == wanted, 1.0, 0.0)

    hits = lax.fori_loop(0, GROUPS, count, jnp.zeros((CAP, ROWS), F32))
    return across(jnp.where(down(hits) > 0.5, 0.0, 1.0))


def send_order():
    order = []
    for step in range(CHIPS):
        high, middle, low = step // 16, (step // 4) % 4, step % 4
        order.append((low, (middle + low) % 4, (high + middle + low) % 4))
    near = [shift for shift in order if sum(min(d, 4 - d) for d in shift) <= 1] + [(2, 0, 0)]
    near.sort(key=lambda shift: -sum(min(d, 4 - d) for d in shift))
    return [shift for shift in order if shift not in near] + near


ORDER = send_order()
SELF = CHIPS - 1


def step_to(dx, dy, dz):
    shift = (dx & 3) * 16 + (dy & 3) * 4 + (dz & 3)
    step = jnp.full(shift.shape, SELF, jnp.int32)
    for number, (x, y, z) in enumerate(ORDER[:SELF]):
        step = jnp.where(shift == x * 16 + y * 4 + z, number, step)
    return step


def in_part(step, part):
    begin, steps, _ = PARTS[part]
    return (step >= begin) & (step < begin + steps)


def piece_of(sublane, side):
    number = side * TILE + sublane
    row = (number * 11) >> 5
    return row, number - 3 * row


def split_rows(rows, third):
    one, two, three = rows[:, :PIECE], rows[:, PIECE : 2 * PIECE], rows[:, 2 * PIECE :]
    return jnp.where(third == 0, one, jnp.where(third == 1, two, three)).astype(BF16)


def chip_places():
    sub, lane = iota((CLUSTERS, CLUSTERS), 0), iota((CLUSTERS, CLUSTERS), 1)
    return onehot((sub == lane) | (sub == (CLUSTERS - 1) - lane))


def excess(totals):
    lane = iota(totals.shape, 1)
    return jnp.where(lane < CHIPS, jnp.maximum(totals - BASE, 0.0), 0.0)


def receive_plan(table, rank, my_x, my_y, my_z):
    chip = my_x * 16 + my_y * 4 + my_z
    heads = table.astype(jnp.int32)
    counts = (heads & 1023).astype(F32)
    differ = jnp.where((heads >> 10).astype(F32) != rank, 1.0, 0.0)
    fault = across(down(differ))
    both = dot(counts.astype(BF16), chip_places())
    over = excess(both)
    lanes = iota((CHIPS, CLUSTERS), 1)
    sender = iota((CHIPS, 1), 0)
    source, target = iota((CHIPS, CHIPS), 0), iota((CHIPS, CHIPS), 1)

    same_line = (source >> 2) == (target >> 2)
    fault = fault + down(jnp.where(across(over) > SPARE, 1.0, 0.0))
    of_line = dot(onehot(same_line), over.astype(BF16))
    fault = fault + across(down(jnp.where(of_line > TILE, 1.0, 0.0)))
    number = across(pick(lanes == chip, over))
    start = across(pick(same_line & (target < source), as_row(number)))

    to_chip = iota((1, CLUSTERS), 1)
    route = step_to(
        (to_chip >> 4) - (sender >> 4), ((to_chip >> 2) & 3) - ((sender >> 2) & 3), (to_chip & 3) - (sender & 3)
    )
    based = jnp.where(lanes < CHIPS, jnp.minimum(both, float(BASE)), 0.0)
    for part, (_, _, room) in enumerate(PARTS):
        held = down(pick(in_part(route, part), based))
        if part == LAST:
            held = held + down(over)
        fault = fault + across(jnp.where(held > room, 1.0, 0.0))

    first = across(pick(lanes == chip, counts))
    second = across(pick(lanes == (CLUSTERS - 1) - chip, counts))
    over_lanes = iota((CHIPS, LINES * TILE), 1)
    way = ((my_x - (sender >> 4)) & 3) * 4 + ((my_y - ((sender >> 2) & 3)) & 3)
    place = (over_lanes & (TILE - 1)).astype(F32) - start
    mine = (way == (over_lanes >> 4)) & (place >= 0.0) & (place < number)
    over_first = down(jnp.where(mine & (place + BASE < first), 1.0, 0.0))
    over_second = down(jnp.where(mine & (place + BASE >= first), 1.0, 0.0))
    over_first_total, over_second_total = across(over_first), across(over_second)
    square = (LINES * TILE, LINES * TILE)
    earlier = onehot(iota(square, 0) < iota(square, 1))
    sub = iota((16, LINES * TILE), 0)
    before = dot((pick(sub == 0, over_first) + pick(sub == 1, over_second)).astype(BF16), earlier)

    base_first = jnp.minimum(first, float(BASE))
    base_second = jnp.minimum(first + second, float(BASE)) - base_first
    first_row, second_row = as_row(base_first), as_row(base_second)

    def my_step(other):
        return step_to(my_x - (other >> 4), my_y - ((other >> 2) & 3), my_z - (other & 3))

    step_column, step_row = my_step(sender), my_step(iota((1, CHIPS), 1))
    plans = []
    ends = []
    for part, (begin, steps, _) in enumerate(PARTS):
        steps = min(begin + steps, CHIPS) - begin
        inside = in_part(step_column, part)
        ahead = (target < source) & in_part(step_row, part)
        first_total = down(pick(inside, base_first))
        second_total = down(pick(inside, base_second))
        last = part == LAST
        first_end = first_total + over_first_total if last else first_total
        first_start = across(pick(ahead, first_row))
        second_start = across(pick(ahead, second_row)) + first_end
        spread = step_column - begin == (iota((CHIPS, steps * TILE), 1) >> 4)
        head, tail, head_start, tail_start = [
            down(pick(spread, column)) for column in (base_first, base_second, first_start, second_start)
        ]

        def row_of(slot):
            slot = slot.astype(F32)
            later = jnp.where(slot < head + tail, tail_start + (slot - head), -1.0)
            return jnp.where(slot < head, head_start + slot, later)

        sublane = iota((1, steps * TILE), 1) & (TILE - 1)
        plan = [row_of(piece_of(sublane, 0)[0]), row_of(piece_of(sublane, 1)[0]), row_of(sublane)]
        held_end = first_end + second_total
        if last:
            over_row_of = jnp.where(over_second > 0.5, held_end + before[1:2], -1.0)
            over_row_of = jnp.where(over_first > 0.5, first_total + before[0:1], over_row_of)
            plan[2] = jnp.concatenate([plan[2], over_row_of], axis=1)
            held_end = held_end + over_second_total
        plans.append(plan)
        ends.append((first_end, held_end))
    return plans, ends, fault


def kernel(
    x_hbm, assign_hbm, owner_hbm, count_hbm, index_hbm,
    out_ref, fault_ref,
    x_ref, assign_ref, owner_ref, count_ref, index_ref,
    send, got, heads, own_over, line_over, send_over, got_over, picks,
    mine, theirs, facts, sums, their_sums, back, returned,
    load_sem, send_sem, recv_sem,
):
    grp, blk = lax.axis_index("grp"), lax.axis_index("blk")
    my_x, my_y, my_z, core = grp // 4, grp % 4, blk // 2, blk % 2
    my_chip = grp * 4 + my_z
    along_x = [((my_x + d) % 4) * 4 for d in range(4)]
    along_y = [(my_y + d) % 4 for d in range(4)]
    along_z = [((my_z + d) % 4) * 2 + core for d in range(4)]
    other_core = {"grp": grp, "blk": my_z * 2 + (1 - core)}

    def device_at(step, sign):
        dx, dy, dz = [(sign * d) % 4 for d in ORDER[step]]
        return {"grp": along_x[dx] + along_y[dy], "blk": along_z[dz]}

    def remote(source, target, number, device):
        return pltpu.make_async_remote_copy(
            src_ref=source,
            dst_ref=target,
            send_sem=send_sem.at[number],
            recv_sem=recv_sem.at[number],
            device_id=device,
            device_id_type=pl.DeviceIdType.MESH,
        )

    def await_blocks(ref, number, semaphore):
        block = ref.at[pl.ds(0, number)]
        pltpu.make_async_copy(block, block, semaphore).wait()

    HEAD_Z, HEAD_Y, HEAD_X, LINE, OVER, FACTS, SUMS, BACK, SWAP, PART = 0, 1, 2, 3, 4, 5, 6, 7, 8, 11
    messages = [min(begin + steps, SELF) - begin for begin, steps, _ in PARTS]
    shifts = [(d // 4, d % 4) for d in range(LINES)]

    loads = [
        pltpu.make_async_copy(source, target, load_sem.at[number])
        for number, (source, target) in enumerate(
            (
                (assign_hbm, assign_ref),
                (owner_hbm, owner_ref),
                (count_hbm, count_ref),
                (index_hbm, index_ref),
                (x_hbm, x_ref),
            )
        )
    ]
    for load in loads:
        load.start()
    barrier = pltpu.get_barrier_semaphore()
    for device in [device_at(step, 1) for step in range(SELF)] + [other_core]:
        pl.semaphore_signal(barrier, inc=1, device_id=device, device_id_type=pl.DeviceIdType.MESH)
    for load in loads[:-1]:
        load.wait()

    rank, count_column = rank_groups(count_ref)
    group, chip, slot, place_counts = place_documents(assign_ref, owner_ref, rank)
    step_of = step_to((chip >> 4) - my_x, ((chip >> 2) & 3) - my_y, (chip & 3) - my_z)
    in_base = slot < BASE
    send_slot = jnp.where(in_base, step_of * TILE + slot, -1)
    heads[my_chip] = place_counts + 1024.0 * rank
    loads[-1].wait()

    def pack(first, stop):
        sublane = iota(((stop - first) * TILE, 1), 0)
        sides = []
        for side in range(2):
            row, third = piece_of(sublane & (TILE - 1), side)
            wanted = (sublane >> 4) * TILE + row + first * TILE
            sides.append(split_rows(dot(onehot(wanted == send_slot), x_ref[...]), third))
        packed = jnp.concatenate(sides, axis=1)
        send[pl.ds(first, stop - first)] = packed.reshape(stop - first, TILE, 2 * PIECE)

    def post(first, stop):
        for step in range(first, min(stop, SELF)):
            number = max(part for part in range(len(PARTS)) if PARTS[part][0] <= step)
            remote(send.at[step], got.at[step], PART + number, device_at(step, 1)).start()

    def share_heads(first, number, semaphore, devices):
        block = heads.at[pl.ds(first, number)]
        for device in devices:
            remote(block, block, semaphore, device).start()

    pack(0, 24)
    pl.semaphore_wait(barrier, CHIPS)
    share_heads(my_chip, 1, HEAD_Z, [{"grp": grp, "blk": along_z[d]} for d in range(1, 4)])
    post(0, 8)
    place_counts_16 = place_counts + jnp.zeros((16, CLUSTERS), F32)
    own_excess = excess(dot(place_counts_16.astype(BF16), chip_places())[0:1])
    eye = iota((CHIPS, CLUSTERS), 0) == iota((CHIPS, CLUSTERS), 1)
    excess_column = across(pick(eye, own_excess))
    over_slot = down(pick(iota((CHIPS, ROWS), 0) < chip, excess_column)).astype(jnp.int32) + (slot - BASE)
    over_slot = jnp.where(in_base, -1, over_slot)
    own_over[...] = dot(onehot(iota((SPARE, ROWS), 0) == over_slot), x_ref[...]).astype(BF16)
    line_over[my_z] = own_over[...]
    for d in range(1, DEPTH):
        remote(own_over, line_over.at[my_z], LINE, {"grp": grp, "blk": along_z[d]}).start()
    post(8, 16)
    pack(24, 48)
    await_blocks(heads, 3, recv_sem.at[HEAD_Z])
    share_heads(grp * 4, 4, HEAD_Y, [{"grp": along_x[0] + along_y[d], "blk": blk} for d in range(1, 4)])
    post(16, 32)

    line_heads = heads[pl.ds(grp * DEPTH, DEPTH)].reshape(DEPTH, CLUSTERS)
    line_counts = (line_heads.astype(jnp.int32) & 1023).astype(F32).astype(BF16)
    over = excess(dot(line_counts, chip_places()))
    earlier = onehot(iota((CLUSTERS, CLUSTERS), 0) < iota((CLUSTERS, CLUSTERS), 1))
    ahead = dot(over.astype(BF16), earlier)
    sums_before = [jnp.zeros((1, CLUSTERS), F32)]
    for d in range(DEPTH - 1):
        sums_before.append(sums_before[-1] + over[d : d + 1])
    before = jnp.concatenate(sums_before, axis=0)
    depth = iota((DEPTH, 1), 0)
    before_mine = down(pick(depth == my_z, before))
    facts_of = jnp.concatenate([over, ahead, before, jnp.zeros((DEPTH, CLUSTERS), F32)], axis=0).astype(BF16)
    sublane = iota((LINES * TILE, 1), 0)
    way = sublane >> 4
    to_chip = ((my_x + (way >> 2)) & 3) * 16 + ((my_y + way) & 3) * 4 + my_z
    facts_of = dot_rows(onehot(iota((LINES * TILE, CLUSTERS), 1) == to_chip), facts_of)
    entry = iota((LINES * TILE, DEPTH * SPARE), 1)

    def of_depth(kind):
        values = facts_of[:, kind * DEPTH + DEPTH - 1 : (kind + 1) * DEPTH]
        for d in range(DEPTH - 2, -1, -1):
            values = jnp.where(entry < (d + 1) * SPARE, facts_of[:, kind * DEPTH + d : kind * DEPTH + d + 1], values)
        return values

    offset = entry
    for d in range(1, DEPTH):
        offset = jnp.where(entry >= d * SPARE, entry - d * SPARE, offset)
    offset = offset.astype(F32) - of_depth(1)
    position = jnp.where((offset >= 0.0) & (offset < of_depth(0)), offset + of_depth(2), -1.0)
    await_blocks(line_over, DEPTH - 1, recv_sem.at[LINE])
    blocks = line_over[...].reshape(DEPTH * SPARE, WIDTH)
    rows = dot(onehot((sublane & (TILE - 1)).astype(F32) == position), blocks)
    send_over[...] = rows.astype(BF16).reshape(LINES, TILE, WIDTH)
    got_over[0] = send_over[0]
    for d, (dx, dy) in enumerate(shifts):
        if d > 0:
            remote(send_over.at[d], got_over.at[d], OVER, {"grp": along_x[dx] + along_y[dy], "blk": blk}).start()

    await_blocks(heads, 12, recv_sem.at[HEAD_Y])
    share_heads(my_x * 16, 16, HEAD_X, [{"grp": along_x[d] + along_y[0], "blk": blk} for d in range(1, 4)])
    post(32, 48)
    pack(48, CHIPS)
    post(48, CHIPS)
    got[SELF] = send[SELF]

    await_blocks(heads, 48, recv_sem.at[HEAD_X])
    table = heads[...].reshape(CHIPS, CLUSTERS)
    plans, ends, fault = receive_plan(table, rank, my_x, my_y, my_z)

    missing = missing_documents(index_ref, count_column, group)
    row = iota((8, 128), 0)
    told = pick(row == 6, rank) + pick(row == 7, jnp.where(iota((1, 128), 1) == 0, fault, missing))
    for part, (first_end, held_end) in enumerate(ends):
        told = told + pick(row == part, first_end) + pick(row == 3 + part, held_end)
        room = PARTS[part][2]
        for kind, plan in enumerate(plans[part]):
            width = plan.shape[1]
            picks[kind, pl.ds(STARTS[part], room), pl.ds(0, width)] = onehot(
                iota((room, width), 0).astype(F32) == plan
            )
    facts[0] = told
    swap_facts = remote(facts.at[0], facts.at[1], FACTS, other_core)
    swap_facts.start()

    best = [jnp.full((1, room), -1.0, F32) for _, _, room in PARTS]
    their_ends = []
    totals = [jnp.zeros((1, WIDTH), F32), jnp.zeros((1, WIDTH), F32)]
    swaps = []

    def window(part):
        return pl.ds(STARTS[part], PARTS[part][2])

    def compare(keys, key_part, query_part, key_ends, itself):
        scores = dot_rows(keys[window(key_part)], mine[window(query_part)])
        first, held = key_ends[key_part]
        key_number = iota((PARTS[key_part][2], 1), 0).astype(F32)
        query_number = iota((1, PARTS[query_part][2]), 1).astype(F32)
        kind = jnp.where(key_number < first, 0.0, jnp.where(key_number < held, 1.0, 2.0))
        matched = kind == jnp.where(query_number < ends[query_part][0], 0.0, 1.0)
        if itself and key_part == query_part:
            matched = matched & (key_number != query_number)
        scores = jnp.max(jnp.where(matched, scores, -1.0), axis=0, keepdims=True)
        best[query_part] = jnp.maximum(best[query_part], scores)

    for part, (begin, steps, room) in enumerate(PARTS):
        base_steps = min(begin + steps, CHIPS) - begin
        rows = jnp.zeros((room, WIDTH), F32)
        if part == LAST:
            await_blocks(got_over, LINES - 1, recv_sem.at[OVER])
            spares = got_over[...].reshape(LINES * TILE, WIDTH)
            rows = dot(picks[2, window(part), pl.ds(base_steps * TILE, LINES * TILE)], spares)
        await_blocks(got, messages[part], recv_sem.at[PART + part])
        packed = got[pl.ds(begin, base_steps)].reshape(base_steps * TILE, 2 * PIECE)
        sublane = iota((base_steps * TILE, 1), 0) & (TILE - 1)
        for side in range(2):
            third = piece_of(sublane, side)[1]
            pieces = packed[:, side * PIECE : (side + 1) * PIECE]
            placed = jnp.concatenate([pieces * onehot(third == number) for number in range(3)], axis=1)
            rows = rows + dot(picks[side, window(part), pl.ds(0, base_steps * TILE)], placed)
        unit = rows * lax.rsqrt(across(rows * rows) + EPSILON)
        mine[window(part)] = unit.astype(BF16)
        swap = remote(mine.at[window(part)], theirs.at[window(part)], SWAP + part, other_core)
        swap.start()
        swaps.append(swap)
        is_first = iota((room, 1), 0).astype(F32) < ends[part][0]
        totals[0] = totals[0] + down(pick(is_first, unit))
        totals[1] = totals[1] + down(jnp.where(is_first, 0.0, unit))
        if part == LAST:
            row = iota((8, WIDTH), 0)
            sums[...] = pick(row == 0, totals[0]) + pick(row == 1, totals[1])
            swap_sums = remote(sums, their_sums, SUMS, other_core)
            swap_sums.start()
        for other in range(part + 1):
            compare(mine, part, other, ends, True)
            if other != part:
                compare(mine, other, part, ends, True)
        if part == 0:
            swap_facts.wait()
            their_told = facts[1]
            for number in range(len(PARTS)):
                their_ends.append((their_told[number : number + 1, 0:1], their_told[3 + number : 4 + number, 0:1]))
        else:
            for other in range(part - 1):
                compare(theirs, other, part, their_ends, False)
            swaps[part - 1].wait()
            for other in range(part + 1):
                compare(theirs, part - 1, other, their_ends, False)

    swap_sums.wait()
    total = sums[...] + their_sums[...]
    centre = total * lax.rsqrt(across(total * total) + EPSILON)
    near = dot_rows(jnp.concatenate(thirds(centre), axis=0).astype(BF16), mine[...])
    near = near[0:8] + near[8:16] + near[16:24]
    swaps[LAST].wait()
    for other in range(len(PARTS)):
        compare(theirs, LAST, other, their_ends, False)

    poison = missing + their_told[7:8, 1:2] > 0.5
    for part, (begin, steps, room) in enumerate(PARTS):
        row = iota((8, room), 0)
        query_number = iota((1, room), 1).astype(F32)
        some = near[:, STARTS[part] : STARTS[part] + room]
        some = jnp.where(query_number < ends[part][0], some[0:1], some[1:2])
        values = jnp.zeros((8, room), F32)
        for number, term in enumerate(thirds(best[part]) + thirds(some)):
            values = jnp.where(row == number, term, values)
        out = dot(values.astype(BF16), picks[2, window(part), pl.ds(0, steps * TILE)])
        for kind in range(2):
            line = out[3 * kind : 3 * kind + 1] + out[3 * kind + 1 : 3 * kind + 2] + out[3 * kind + 2 : 3 * kind + 3]
            line = jnp.where(poison, NONE, line)
            for number in range(steps * TILE // 128):
                piece = line[:, number * 128 : (number + 1) * 128]
                tile = begin * TILE // 128 + number
                for other in range(2 if tile < 8 else 8):
                    if tile < 8:
                        back[tile * 2 + other, kind : kind + 1, :] = piece
                    else:
                        back[other * 2 + tile - 8, 2 + kind : 3 + kind, :] = piece

    def back_of(step):
        dx, dy, _ = ORDER[step]
        return step // 8 * 2 + (dx * 4 + dy) // 8

    returned[SELF] = back[back_of(SELF)]
    for step in range(SELF):
        remote(back.at[back_of(step)], returned.at[step], BACK, device_at(step, -1)).start()

    differ = across(jnp.where(their_told[6:7] != rank, 1.0, 0.0))
    fault = fault + their_told[7:8, 0:1] + differ
    chosen = onehot(iota((CHIPS, ROWS), 0) == step_of)
    sub = iota((128, ROWS), 0)
    at_base = (sub == (step_of & 7) * TILE + slot) & in_base
    before_column = across(pick(eye, before_mine))
    line_slot = down(pick(iota((CHIPS, ROWS), 0) == chip, before_column))
    way = (((chip >> 4) - my_x) & 3) * 4 + ((((chip >> 2) & 3) - my_y) & 3)
    at_over = (sub == (way & 7) * TILE + line_slot.astype(jnp.int32) + (slot - BASE)) & (~in_base)

    await_blocks(returned, CHIPS - 1, recv_sem.at[BACK])
    found = []
    for number in range(4):
        line = returned[:, number, :]
        if number == 0:
            poisoned = across(down(jnp.where(line > 0.5 * NONE, 1.0, 0.0)))
            fault_ref[...] = jnp.where(fault + poisoned > 0.5, 1, 0) + jnp.zeros((1, 128), jnp.int32)
        terms = jnp.concatenate(thirds(line), axis=1).astype(BF16)
        out = lax.dot_general(terms, chosen, (((0,), (0,)), ((), ())), preferred_element_type=F32)
        found.append(out[0:128] + out[128:256] + out[256:384])
    out_ref[0:1] = down(pick(at_base, found[0]) + pick(at_over, found[2]))
    out_ref[1:2] = down(pick(at_base, found[1]) + pick(at_over, found[3]))

    await_blocks(heads, 3, send_sem.at[HEAD_Z])
    await_blocks(heads, 12, send_sem.at[HEAD_Y])
    await_blocks(heads, 48, send_sem.at[HEAD_X])
    await_blocks(line_over, DEPTH - 1, send_sem.at[LINE])
    await_blocks(got_over, LINES - 1, send_sem.at[OVER])
    await_blocks(returned, CHIPS - 1, send_sem.at[BACK])
    for part in range(len(PARTS)):
        await_blocks(got, messages[part], send_sem.at[PART + part])


def routed(embeddings, assign, owner, send_count, send_index):
    return pl.pallas_call(
        kernel,
        out_shape=(
            jax.ShapeDtypeStruct((2, ROWS), F32),
            jax.ShapeDtypeStruct((1, 128), jnp.int32),
        ),
        in_specs=[pl.BlockSpec(memory_space=pl.ANY)] * 5,
        out_specs=(pl.BlockSpec(memory_space=pltpu.VMEM),) * 2,
        scratch_shapes=[
            pltpu.VMEM((ROWS, WIDTH), BF16),
            pltpu.VMEM((1, ROWS), jnp.int32),
            pltpu.VMEM((1, CLUSTERS), jnp.int32),
            pltpu.VMEM((1, GROUPS), jnp.int32),
            pltpu.VMEM((GROUPS, CAP), jnp.int32),
            pltpu.VMEM((CHIPS, TILE, 2 * PIECE), BF16),
            pltpu.VMEM((CHIPS, TILE, 2 * PIECE), BF16),
            pltpu.VMEM((CHIPS, 1, 128), F32),
            pltpu.VMEM((SPARE, WIDTH), BF16),
            pltpu.VMEM((DEPTH, SPARE, WIDTH), BF16),
            pltpu.VMEM((LINES, TILE, WIDTH), BF16),
            pltpu.VMEM((LINES, TILE, WIDTH), BF16),
            pltpu.VMEM((3, HELD, 512), BF16),
            pltpu.VMEM((HELD, WIDTH), BF16),
            pltpu.VMEM((HELD, WIDTH), BF16),
            pltpu.VMEM((2, 8, 128), F32),
            pltpu.VMEM((8, WIDTH), F32),
            pltpu.VMEM((8, WIDTH), F32),
            pltpu.VMEM((CHIPS * TILE // 128 * 2, 4, 128), F32),
            pltpu.VMEM((CHIPS, 4, 128), F32),
            pltpu.SemaphoreType.DMA((5,)),
            pltpu.SemaphoreType.DMA((14,)),
            pltpu.SemaphoreType.DMA((14,)),
        ],
        compiler_params=pltpu.CompilerParams(
            collective_id=0, has_side_effects=True, vmem_limit_bytes=48 * 1024 * 1024
        ),
    )(
        embeddings,
        assign.reshape(1, ROWS),
        owner.reshape(1, CLUSTERS),
        send_count,
        send_index[0],
    )


def body(embeddings, assign, owner, send_count, send_index):
    arguments = (embeddings, assign, owner, send_count, send_index)
    results, fault = routed(*arguments)
    results = lax.cond(fault[0, 0] != 0, lambda: jnp.stack(general(*arguments)), lambda: results)
    return results[0], results[1]


def solution(mesh):
    placed = (
        P(("grp", "blk"), None),
        P(("grp", "blk")),
        P(),
        P(("grp", "blk"), None),
        P(("grp", "blk"), None, None),
    )
    return jax.shard_map(
        body,
        mesh=mesh,
        in_specs=placed,
        out_specs=(P(("grp", "blk")), P(("grp", "blk"))),
        check_vma=False,
    )
```

```python
import functools

import jax
import jax.numpy as jnp
from jax import lax
from jax.experimental import pallas as pl
from jax.experimental.pallas import tpu as pltpu
from jax.sharding import PartitionSpec as P

EPSILON = 1e-06
F32 = jnp.float32
BF16 = jnp.bfloat16

CHIPS = 64
ROWS = 512
WIDTH = 768
CLUSTERS = 128
GROUPS = 16
CAP = 64
BASE = 16
HALF = WIDTH // 2
LINES = 16
DEPTH = 4
POOL = 8
PARTS = ((0, 40, 400), (40, 32, 256))
TOTAL = 72
HELD = 656
STARTS = (0, 400)
LAST = len(PARTS) - 1
NONE = 1e30


def normalize(values):
    widened = values.astype(F32)
    return widened * lax.rsqrt(jnp.sum(widened * widened, axis=1, keepdims=True) + EPSILON)


def general(embeddings, assign, owner, send_count, send_index):
    rows_local = embeddings.shape[0]
    feature_width = embeddings.shape[1]
    groups = lax.axis_size("grp")
    clusters = owner.shape[0]
    capacity = send_index.shape[2]
    slot_total = groups * capacity
    unit_rows = normalize(embeddings)
    unit_low = unit_rows.astype(BF16)
    counts = send_count[0]
    listed = send_index[0]
    live_slot = jnp.arange(capacity, dtype=jnp.int32)[None, :] < counts[:, None]
    listed_cluster = assign[listed]
    owned_here = owner[listed_cluster] == jnp.arange(groups, dtype=jnp.int32)[:, None]
    kept_slot = live_slot & owned_here
    out_cluster = jnp.where(kept_slot, listed_cluster, -1)
    out_tag = jnp.where(kept_slot, lax.axis_index(("grp", "blk")) * rows_local + listed, -1)
    out_vector = unit_low[listed.reshape(-1)].reshape(groups, capacity, feature_width)
    got_vector, got_cluster, got_tag = (
        lax.all_to_all(out_vector, "grp", split_axis=0, concat_axis=0, tiled=True),
        lax.all_to_all(out_cluster, "grp", split_axis=0, concat_axis=0, tiled=True),
        lax.all_to_all(out_tag, "grp", split_axis=0, concat_axis=0, tiled=True),
    )
    own_vector = got_vector.reshape(slot_total, feature_width)
    own_cluster = got_cluster.reshape(slot_total)
    own_tag = got_tag.reshape(slot_total)

    def tile_best(current, shard_piece):
        other_vector, other_cluster, other_tag = shard_piece
        scores = jnp.einsum("id,jd->ij", own_vector, other_vector, preferred_element_type=F32)
        matched = (
            (own_cluster[:, None] == other_cluster[None, :])
            & (other_cluster[None, :] >= 0)
            & (own_tag[:, None] != other_tag[None, :])
        )
        return jnp.maximum(current, jnp.max(jnp.where(matched, scores, -1.0), axis=1))

    other_vector = lax.all_gather(own_vector, "blk", axis=0, tiled=True)
    other_cluster = lax.all_gather(own_cluster, "blk", axis=0, tiled=True)
    other_tag = lax.all_gather(own_tag, "blk", axis=0, tiled=True)
    length = other_vector.shape[0]
    number = length // slot_total
    stacked = (
        other_vector.reshape(number, slot_total, feature_width),
        other_cluster.reshape(number, slot_total),
        other_tag.reshape(number, slot_total),
    )

    def scan_step(carry, single):
        return (tile_best(carry, single), None)

    result, unused = lax.scan(scan_step, jnp.full((slot_total,), -1.0, F32), stacked)
    target = jnp.where(live_slot, listed, rows_local).reshape(-1)
    partial_sum = jax.ops.segment_sum(unit_rows, assign, num_segments=clusters)
    centre = normalize(lax.psum(partial_sum, ("grp", "blk")))
    nearness = jnp.sum(unit_low.astype(F32) * centre[assign], axis=1)
    returned = lax.all_to_all(
        result.reshape(groups, capacity), "grp", split_axis=0, concat_axis=0, tiled=True
    )
    has_entry = (
        jnp.zeros((rows_local,), jnp.int32)
        .at[target]
        .max(kept_slot.astype(jnp.int32).reshape(-1), mode="drop")
    )
    centroid_cos = jnp.where(has_entry > 0, nearness, 0.0)
    max_sim = jnp.full((rows_local,), -1.0, F32).at[target].max(returned.reshape(-1), mode="drop")
    return (max_sim, centroid_cos)


def iota(shape, axis):
    return lax.broadcasted_iota(jnp.int32, shape, axis)


def down(values):
    return jnp.sum(values, axis=0, keepdims=True)


def across(values):
    return jnp.sum(values, axis=1, keepdims=True)


def pick(mask, values):
    return jnp.where(mask, values, 0.0)


def as_column(row):
    size = row.shape[1]
    return across(pick(iota((size, size), 0) == iota((size, size), 1), row))


def as_row(column):
    size = column.shape[0]
    return down(pick(iota((size, size), 0) == iota((size, size), 1), column))


def dot(a, b):
    return jnp.dot(a, b, preferred_element_type=F32)


def dot_rows(a, b):
    return lax.dot_general(a, b, (((1,), (1,)), ((), ())), preferred_element_type=F32)


def onehot(mask):
    return jnp.where(mask, 1.0, 0.0).astype(BF16)


def halves(values):
    first = values.astype(BF16).astype(F32)
    return first, (values - first).astype(BF16).astype(F32)


def rank_groups(count_ref):
    count_row = count_ref[...].astype(F32)
    count_column = as_column(count_row)
    sub, lane = iota((GROUPS, 128), 0), iota((GROUPS, 128), 1)
    count_lanes = down(pick(sub == lane, count_column))
    ahead = (count_column > count_lanes) | ((count_column == count_lanes) & (sub < lane))
    rank = down(jnp.where(ahead, 1.0, 0.0))
    return jnp.where(iota((1, 128), 1) < GROUPS, rank, 0.0), count_column


def place_documents(assign_ref, owner_ref, rank):
    owner_row = owner_ref[...].astype(F32)
    owner_column = as_column(owner_row)
    sub, lane = iota((CLUSTERS, CLUSTERS), 0), iota((CLUSTERS, CLUSTERS), 1)
    within = across(jnp.where((owner_column == owner_row) & (lane < sub), 1.0, 0.0))
    group_rank = across(pick(owner_column == lane.astype(F32), rank))
    place_column = group_rank * (CLUSTERS // GROUPS) + within
    member = iota((CLUSTERS, ROWS), 0) == assign_ref[...]
    place = down(pick(member, place_column))
    group = down(pick(member, owner_column))
    order = iota((CLUSTERS, ROWS), 0).astype(F32)
    at_place = order == place
    earlier = onehot(iota((ROWS, ROWS), 0) < iota((ROWS, ROWS), 1))
    before = dot(onehot(at_place), earlier)
    slot = down(pick(at_place, before))
    count_column = across(jnp.where(at_place, 1.0, 0.0))
    partner_count = down(pick(order == (CLUSTERS - 1) - place, count_column))
    slot = slot + jnp.where(place >= CHIPS, partner_count, 0.0)
    chip = jnp.minimum(place, (CLUSTERS - 1) - place)
    return group, chip.astype(jnp.int32), slot.astype(jnp.int32), as_row(count_column)


def missing_documents(index_ref, count_column, group):
    listed = index_ref[...]
    live = iota((GROUPS, CAP), 1).astype(F32) < count_column
    eye = onehot(iota((CAP, CAP), 0) == iota((CAP, CAP), 1))
    high = dot_rows(eye, jnp.where(live, listed >> 4, 0).astype(F32).astype(BF16))
    low = dot_rows(eye, jnp.where(live, listed & 15, 0).astype(F32).astype(BF16))
    alive = dot_rows(eye, onehot(live))
    slots = jnp.where(alive > 0.5, high * 16.0 + low, -1.0)
    document = iota((1, ROWS), 1).astype(F32)
    lane = iota((CAP, GROUPS), 1)

    def count(g, hits):
        column = across(pick(lane == g, slots))
        wanted = jnp.where(group == g.astype(F32), document, -2.0)
        return hits + jnp.where(column == wanted, 1.0, 0.0)

    hits = lax.fori_loop(0, GROUPS, count, jnp.zeros((CAP, ROWS), F32))
    return across(jnp.where(down(hits) > 0.5, 0.0, 1.0))


def send_order():
    order = []
    for step in range(CHIPS):
        high, middle, low = step // 16, (step // 4) % 4, step % 4
        order.append((low, (middle + low) % 4, (high + middle + low) % 4))
    near = [shift for shift in order if sum(min(d, 4 - d) for d in shift) <= 1] + [(2, 0, 0)]
    near.sort(key=lambda shift: -sum(min(d, 4 - d) for d in shift))
    return [shift for shift in order if shift not in near] + near


ORDER = send_order()
SELF = CHIPS - 1


def step_to(dx, dy, dz):
    shift = (dx & 3) * 16 + (dy & 3) * 4 + (dz & 3)
    step = jnp.full(shift.shape, SELF, jnp.int32)
    for number, (x, y, z) in enumerate(ORDER[:SELF]):
        step = jnp.where(shift == x * 16 + y * 4 + z, number, step)
    return step


def in_part(step, part):
    begin, steps, _ = PARTS[part]
    return (step >= begin) & (step < begin + steps)


def chip_places():
    sub, lane = iota((CLUSTERS, CLUSTERS), 0), iota((CLUSTERS, CLUSTERS), 1)
    return onehot((sub == lane) | (sub == (CLUSTERS - 1) - lane))


def excess(totals):
    lane = iota(totals.shape, 1)
    return jnp.where(lane < CHIPS, jnp.maximum(totals - BASE, 0.0), 0.0)


def receive_plan(counts, ranks, rank, my_x, my_y, my_z):
    chip = my_x * 16 + my_y * 4 + my_z
    differ = jnp.where(ranks != rank, 1.0, 0.0)
    fault = across(down(differ))
    both = dot(counts.astype(BF16), chip_places())
    over = excess(both)
    lanes = iota((CHIPS, CLUSTERS), 1)
    sender = iota((CHIPS, 1), 0)
    source, target = iota((CHIPS, CHIPS), 0), iota((CHIPS, CHIPS), 1)

    same_line = (source >> 2) == (target >> 2)
    over_total = across(over)
    over_row = as_row(over_total)
    line_start = across(pick(same_line & (target < source), over_row))
    line_total = across(pick(same_line, over_row))
    fault = fault + down(jnp.where(line_total > POOL, 1.0, 0.0))
    start = line_start + across(pick(lanes < chip, over))
    number = across(pick(lanes == chip, over))

    to_chip = iota((1, CLUSTERS), 1)
    route = step_to(
        (to_chip >> 4) - (sender >> 4), ((to_chip >> 2) & 3) - ((sender >> 2) & 3), (to_chip & 3) - (sender & 3)
    )
    based = jnp.where(lanes < CHIPS, jnp.minimum(both, float(BASE)), 0.0)
    for part, (_, _, room) in enumerate(PARTS):
        held = down(pick(in_part(route, part), based))
        if part == LAST:
            held = held + down(over)
        fault = fault + across(jnp.where(held > room, 1.0, 0.0))

    first = across(pick(lanes == chip, counts))
    second = across(pick(lanes == (CLUSTERS - 1) - chip, counts))
    place = (lanes & (POOL - 1)).astype(F32) - start
    mine = ((sender >> 2) == (lanes >> 3)) & (place >= 0.0) & (place < number)
    over_first = down(jnp.where(mine & (place + BASE < first), 1.0, 0.0))
    over_second = down(jnp.where(mine & (place + BASE >= first), 1.0, 0.0))
    over_first_total, over_second_total = across(over_first), across(over_second)
    earlier = onehot(iota((CLUSTERS, CLUSTERS), 0) < iota((CLUSTERS, CLUSTERS), 1))
    sub = iota((16, CLUSTERS), 0)
    before = dot((pick(sub == 0, over_first) + pick(sub == 1, over_second)).astype(BF16), earlier)

    base_first = jnp.minimum(first, float(BASE))
    base_second = jnp.minimum(first + second, float(BASE)) - base_first
    first_row, second_row = as_row(base_first), as_row(base_second)

    def my_step(other):
        return step_to(my_x - (other >> 4), my_y - ((other >> 2) & 3), my_z - (other & 3))

    step_column, step_row = my_step(sender), my_step(iota((1, CHIPS), 1))
    plans = []
    ends = []
    for part, (begin, steps, _) in enumerate(PARTS):
        inside = in_part(step_column, part)
        ahead = (target < source) & in_part(step_row, part)
        first_total = down(pick(inside, base_first))
        second_total = down(pick(inside, base_second))
        last = part == LAST
        first_end = first_total + over_first_total if last else first_total
        first_start = across(pick(ahead, first_row))
        second_start = across(pick(ahead, second_row)) + first_end
        spread = step_column - begin == (iota((CHIPS, steps * BASE), 1) >> 4)
        head, tail, head_start, tail_start = [
            down(pick(spread, column)) for column in (base_first, base_second, first_start, second_start)
        ]
        slot = (iota((1, steps * BASE), 1) & (BASE - 1)).astype(F32)
        later = jnp.where(slot < head + tail, tail_start + (slot - head), -1.0)
        plan = jnp.where(slot < head, head_start + slot, later)
        held_end = first_end + second_total
        if last:
            over_row_of = jnp.where(over_second > 0.5, held_end + before[1:2], -1.0)
            over_row_of = jnp.where(over_first > 0.5, first_total + before[0:1], over_row_of)
            plan = jnp.concatenate([plan[:, : steps * BASE - CLUSTERS], over_row_of], axis=1)
            held_end = held_end + over_second_total
        plans.append(plan)
        ends.append((first_end, held_end))
    return plans, ends, fault


def kernel(
    x_hbm, assign_hbm, owner_hbm, count_hbm, index_hbm,
    out_ref, fault_ref,
    x_ref, assign_ref, owner_ref, count_ref, index_ref,
    send, got, own_over, line_over, send_over, got_over, pick_0, pick_1,
    keys, facts, sums, their_sums, back, returned,
    load_sem, send_sem, recv_sem,
):
    grp, blk = lax.axis_index("grp"), lax.axis_index("blk")
    my_x, my_y, my_z, core = grp // 4, grp % 4, blk // 2, blk % 2
    my_chip = grp * 4 + my_z
    picks = (pick_0, pick_1)
    along_x = [((my_x + d) % 4) * 4 for d in range(4)]
    along_y = [(my_y + d) % 4 for d in range(4)]
    along_z = [((my_z + d) % 4) * 2 + core for d in range(4)]
    other_core = {"grp": grp, "blk": my_z * 2 + (1 - core)}

    def device_at(step, sign):
        dx, dy, dz = [(sign * d) % 4 for d in ORDER[step]]
        return {"grp": along_x[dx] + along_y[dy], "blk": along_z[dz]}

    def remote(source, target, number, device):
        return pltpu.make_async_remote_copy(
            src_ref=source,
            dst_ref=target,
            send_sem=send_sem.at[number],
            recv_sem=recv_sem.at[number],
            device_id=device,
            device_id_type=pl.DeviceIdType.MESH,
        )

    def await_blocks(ref, number, semaphore):
        block = ref.at[pl.ds(0, number)]
        pltpu.make_async_copy(block, block, semaphore).wait()

    LINE, OVER, FACTS, SUMS, BACK, SWAP, PART = 0, 1, 2, 3, 4, 5, 7
    messages = [min(begin + steps, SELF) - begin for begin, steps, _ in PARTS]

    loads = [
        pltpu.make_async_copy(source, target, load_sem.at[number])
        for number, (source, target) in enumerate(
            (
                (assign_hbm, assign_ref),
                (owner_hbm, owner_ref),
                (count_hbm, count_ref),
                (index_hbm, index_ref),
                (x_hbm, x_ref),
            )
        )
    ]
    for load in loads:
        load.start()
    barrier = pltpu.get_barrier_semaphore()
    for device in [device_at(step, 1) for step in range(SELF)] + [other_core]:
        pl.semaphore_signal(barrier, inc=1, device_id=device, device_id_type=pl.DeviceIdType.MESH)
    for load in loads[:-1]:
        load.wait()

    rank, count_column = rank_groups(count_ref)
    group, chip, slot, place_counts = place_documents(assign_ref, owner_ref, rank)
    step_of = step_to((chip >> 4) - my_x, ((chip >> 2) & 3) - my_y, (chip & 3) - my_z)
    in_base = slot < BASE
    send_slot = jnp.where(in_base, step_of * BASE + slot, -1)
    loads[-1].wait()

    def pack(first, stop):
        slots = iota(((stop - first) * BASE, ROWS), 0) + first * BASE
        rows = dot(onehot(slots == send_slot), x_ref[...]).astype(BF16)
        send[pl.ds(first, stop - first)] = rows.reshape(stop - first, BASE, WIDTH)

    def post(first, stop):
        for step in range(first, min(stop, SELF)):
            number = max(part for part in range(len(PARTS)) if PARTS[part][0] <= step)
            remote(send.at[step], got.at[step], PART + number, device_at(step, 1)).start()

    pack(0, 24)
    pl.semaphore_wait(barrier, CHIPS)
    post(0, 8)
    place_counts_16 = place_counts + jnp.zeros((16, CLUSTERS), F32)
    own_excess = excess(dot(place_counts_16.astype(BF16), chip_places())[0:1])
    eye = iota((CHIPS, CLUSTERS), 0) == iota((CHIPS, CLUSTERS), 1)
    excess_column = across(pick(eye, own_excess))
    over_slot = down(pick(iota((CHIPS, ROWS), 0) < chip, excess_column)).astype(jnp.int32) + (slot - BASE)
    over_slot = jnp.where(in_base, -1, over_slot)
    row = iota((BASE, CLUSTERS), 0)
    own_over[:, :WIDTH] = dot(onehot(iota((BASE, ROWS), 0) == over_slot), x_ref[...]).astype(BF16)
    own_over[:, WIDTH:] = (pick(row == 0, place_counts) + pick(row == 1, rank)).astype(BF16)
    line_over[my_z] = own_over[...]
    for d in range(1, DEPTH):
        remote(own_over, line_over.at[my_z], LINE, {"grp": grp, "blk": along_z[d]}).start()
    post(8, 24)
    pack(24, 48)

    await_blocks(line_over, DEPTH - 1, recv_sem.at[LINE])
    line_counts = [line_over[d, 0:1, WIDTH:].astype(F32) for d in range(DEPTH)]
    line_ranks = [line_over[d, 1:2, WIDTH:].astype(F32) for d in range(DEPTH)]
    row = iota((2 * POOL, CLUSTERS), 0)
    told = jnp.zeros((2 * POOL, CLUSTERS), F32)
    for d in range(DEPTH):
        told = told + pick(row == d, line_counts[d]) + pick(row == DEPTH + d, line_ranks[d])
    told = told.astype(BF16)
    line_total = across(excess(dot(told, chip_places())))[0:DEPTH]
    depth = iota((DEPTH, 1), 0)
    line_start = jnp.zeros((DEPTH, 1), F32)
    for d in range(DEPTH - 1):
        line_start = line_start + pick(depth > d, line_total[d : d + 1])
    my_start = down(pick(depth == my_z, line_start))
    at = depth == (iota((DEPTH, DEPTH * BASE), 1) >> 4)
    begin = down(pick(at, line_start))
    number = down(pick(at, line_total))
    order = (iota((1, DEPTH * BASE), 1) & (BASE - 1)).astype(F32)
    order = jnp.where(order < number, begin + order, -1.0)
    rows = iota((2 * POOL, DEPTH * BASE), 0).astype(F32)
    blocks = line_over[:, :, :WIDTH].reshape(DEPTH * BASE, WIDTH)
    left = dot(onehot((rows == order) & (rows < POOL)), blocks[:, :HALF])
    right = dot(onehot((rows - POOL == order) & (rows >= POOL)), blocks[:, HALF:])
    send_over[:, :HALF] = (left + right).astype(BF16)
    send_over[:, HALF:] = told
    got_over[grp] = send_over[...]
    for step in range(1, LINES):
        low, middle = step % 4, step // 4
        device = {"grp": along_x[low] + along_y[(middle + low) % 4], "blk": blk}
        remote(send_over, got_over.at[grp], OVER, device).start()
    post(24, 48)
    pack(48, CHIPS)
    post(48, CHIPS)
    got[SELF] = send[SELF]
    missing = missing_documents(index_ref, count_column, group)

    await_blocks(got_over, LINES - 1, recv_sem.at[OVER])
    told = got_over[:, :, HALF:].astype(F32)
    counts = told[:, 0:DEPTH].reshape(CHIPS, CLUSTERS)
    ranks = told[:, DEPTH : 2 * DEPTH].reshape(CHIPS, CLUSTERS)
    plans, ends, fault = receive_plan(counts, ranks, rank, my_x, my_y, my_z)

    row = iota((8, 128), 0)
    told = pick(row == 6, rank) + pick(row == 7, jnp.where(iota((1, 128), 1) == 0, fault, missing))
    for part, (first_end, held_end) in enumerate(ends):
        told = told + pick(row == part, first_end) + pick(row == 2 + part, held_end)
        picks[part][...] = onehot(iota(picks[part].shape, 0).astype(F32) == plans[part])
    facts[0] = told
    swap_facts = remote(facts.at[0], facts.at[1], FACTS, other_core)
    swap_facts.start()

    best = [jnp.full((1, room), -1.0, F32) for _, _, room in PARTS]
    key_kinds = []
    query_kinds = []
    totals = [jnp.zeros((1, WIDTH), F32), jnp.zeros((1, WIDTH), F32)]
    swaps = []

    def add_kinds(first, held, room):
        number = iota((room, 1), 0).astype(F32)
        key_kinds.append(jnp.where(number < first, 0.0, jnp.where(number < held, 1.0, 2.0)))

    for (first_end, held_end), (_, _, room) in zip(ends, PARTS):
        add_kinds(first_end, held_end, room)
        query_kinds.append(jnp.where(iota((1, room), 1).astype(F32) < first_end, 0.0, 1.0))

    def compare(first_key, last_key, part, more=0):
        borders = (*STARTS, *(HELD + start for start in STARTS), 2 * HELD)
        begin, stop = borders[first_key], borders[last_key + 1]
        start, room = STARTS[part], PARTS[part][2]
        scores = dot_rows(keys[begin : stop + more], keys[start : start + room])
        rest, scores = scores[stop - begin :], scores[: stop - begin]
        kind = jnp.concatenate(key_kinds[first_key : last_key + 1], axis=0)
        matched = kind == query_kinds[part]
        if begin < start + room and start < stop:
            matched = matched & (iota(kind.shape, 0) + (begin - start) != iota((1, room), 1))
        best[part] = jnp.maximum(best[part], jnp.max(jnp.where(matched, scores, -1.0), axis=0, keepdims=True))
        return rest

    def arrive(part):
        begin, steps, room = PARTS[part]
        await_blocks(got, messages[part], recv_sem.at[PART + part])
        rows = dot(picks[part][...], got[pl.ds(begin, steps)].reshape(steps * BASE, WIDTH))
        unit = rows * lax.rsqrt(across(rows * rows) + EPSILON)
        keys[pl.ds(STARTS[part], room)] = unit.astype(BF16)
        swap = remote(
            keys.at[pl.ds(STARTS[part], room)], keys.at[pl.ds(HELD + STARTS[part], room)], SWAP + part, other_core
        )
        swap.start()
        swaps.append(swap)
        is_first = iota((room, 1), 0).astype(F32) < ends[part][0]
        totals[0] = totals[0] + down(pick(is_first, unit))
        totals[1] = totals[1] + down(jnp.where(is_first, 0.0, unit))

    arrive(0)
    compare(0, 0, 0)
    swap_facts.wait()
    their_told = facts[1]
    for part, (_, _, room) in enumerate(PARTS):
        add_kinds(their_told[part : part + 1, 0:1], their_told[2 + part : 3 + part, 0:1], room)
    half_rows = got_over[:, :, :HALF].reshape(LINES * 2 * POOL, HALF)
    shape = (LINES * POOL, LINES * 2 * POOL)
    to, at = iota(shape, 0), iota(shape, 1)
    same = ((to >> 3) == (at >> 4)) & ((to & 7) == (at & 7))
    left = dot(onehot(same & ((at & POOL) == 0)), half_rows)
    right = dot(onehot(same & ((at & POOL) != 0)), half_rows)
    whole = jnp.concatenate([left, right], axis=1).astype(BF16)
    got[pl.ds(CHIPS, TOTAL - CHIPS)] = whole.reshape(TOTAL - CHIPS, BASE, WIDTH)
    swaps[0].wait()
    compare(2, 2, 0)

    arrive(1)
    row = iota((8, WIDTH), 0)
    sums[...] = pick(row == 0, totals[0]) + pick(row == 1, totals[1])
    swap_sums = remote(sums, their_sums, SUMS, other_core)
    swap_sums.start()
    compare(0, 2, 1)
    compare(1, 1, 0)

    swap_sums.wait()
    total = sums[...] + their_sums[...]
    keys[pl.ds(2 * HELD, 16)] = jnp.concatenate(halves(total), axis=0).astype(BF16)
    scale = lax.rsqrt(across(total * total) + EPSILON)
    swaps[1].wait()
    near = [compare(3, 3, part, 16) for part in range(len(PARTS))]
    near = [(some[0:8] + some[8:16]) * scale for some in near]

    poison = missing + their_told[7:8, 1:2] > 0.5
    tiles = CHIPS * BASE // 128
    for part, (begin, steps, room) in enumerate(PARTS):
        row = iota((8, room), 0)
        query_number = iota((1, room), 1).astype(F32)
        some = jnp.where(query_number < ends[part][0], near[part][0:1], near[part][1:2])
        values = jnp.zeros((8, room), F32)
        for number, term in enumerate(halves(best[part]) + halves(some)):
            values = jnp.where(row == number, term, values)
        out = dot(values.astype(BF16), picks[part][...])
        for kind in range(2):
            line = out[2 * kind : 2 * kind + 1] + out[2 * kind + 1 : 2 * kind + 2]
            line = jnp.where(poison, NONE, line)
            for tile in range(steps * BASE // 128):
                piece = line[:, tile * 128 : (tile + 1) * 128]
                to = begin * BASE // 128 + tile
                if to < tiles:
                    back[to, kind : kind + 1, :] = piece
                else:
                    for each in range(tiles):
                        back[each, 2 + kind : 3 + kind, :] = piece
    returned[SELF] = back[SELF // 8]
    for step in range(SELF):
        remote(back.at[step // 8], returned.at[step], BACK, device_at(step, -1)).start()

    differ = across(jnp.where(their_told[6:7] != rank, 1.0, 0.0))
    fault = fault + their_told[7:8, 0:1] + differ
    chosen = onehot(iota((CHIPS, ROWS), 0) == step_of)
    sub = iota((128, ROWS), 0)
    at_base = (sub == (step_of & 7) * BASE + slot) & in_base
    at_over = (sub == grp * POOL + my_start.astype(jnp.int32) + over_slot) & (~in_base)

    await_blocks(returned, CHIPS - 1, recv_sem.at[BACK])
    found = []
    for number in range(4):
        line = returned[:, number, :]
        if number == 0:
            poisoned = across(down(jnp.where(line > 0.5 * NONE, 1.0, 0.0)))
            fault_ref[...] = jnp.where(fault + poisoned > 0.5, 1, 0) + jnp.zeros((1, 128), jnp.int32)
        terms = jnp.concatenate(halves(line), axis=1).astype(BF16)
        out = lax.dot_general(terms, chosen, (((0,), (0,)), ((), ())), preferred_element_type=F32)
        found.append(out[0:128] + out[128:256])
    out_ref[0:1] = down(pick(at_base, found[0]) + pick(at_over, found[2]))
    out_ref[1:2] = down(pick(at_base, found[1]) + pick(at_over, found[3]))

    await_blocks(line_over, DEPTH - 1, send_sem.at[LINE])
    await_blocks(got_over, LINES - 1, send_sem.at[OVER])
    await_blocks(returned, CHIPS - 1, send_sem.at[BACK])
    for part in range(len(PARTS)):
        await_blocks(got, messages[part], send_sem.at[PART + part])


def routed(embeddings, assign, owner, send_count, send_index):
    return pl.pallas_call(
        kernel,
        out_shape=(
            jax.ShapeDtypeStruct((2, ROWS), F32),
            jax.ShapeDtypeStruct((1, 128), jnp.int32),
        ),
        in_specs=[pl.BlockSpec(memory_space=pl.ANY)] * 5,
        out_specs=(pl.BlockSpec(memory_space=pltpu.VMEM),) * 2,
        scratch_shapes=[
            pltpu.VMEM((ROWS, WIDTH), BF16),
            pltpu.VMEM((1, ROWS), jnp.int32),
            pltpu.VMEM((1, CLUSTERS), jnp.int32),
            pltpu.VMEM((1, GROUPS), jnp.int32),
            pltpu.VMEM((GROUPS, CAP), jnp.int32),
            pltpu.VMEM((CHIPS, BASE, WIDTH), BF16),
            pltpu.VMEM((TOTAL, BASE, WIDTH), BF16),
            pltpu.VMEM((BASE, WIDTH + CLUSTERS), BF16),
            pltpu.VMEM((DEPTH, BASE, WIDTH + CLUSTERS), BF16),
            pltpu.VMEM((2 * POOL, HALF + CLUSTERS), BF16),
            pltpu.VMEM((LINES, 2 * POOL, HALF + CLUSTERS), BF16),
            *[pltpu.VMEM((room, steps * BASE), BF16) for _, steps, room in PARTS],
            pltpu.VMEM((2 * HELD + 16, WIDTH), BF16),
            pltpu.VMEM((2, 8, 128), F32),
            pltpu.VMEM((8, WIDTH), F32),
            pltpu.VMEM((8, WIDTH), F32),
            pltpu.VMEM((CHIPS * BASE // 128, 4, 128), F32),
            pltpu.VMEM((CHIPS, 4, 128), F32),
            pltpu.SemaphoreType.DMA((5,)),
            pltpu.SemaphoreType.DMA((9,)),
            pltpu.SemaphoreType.DMA((9,)),
        ],
        compiler_params=pltpu.CompilerParams(
            collective_id=0, has_side_effects=True, vmem_limit_bytes=48 * 1024 * 1024
        ),
    )(
        embeddings,
        assign.reshape(1, ROWS),
        owner.reshape(1, CLUSTERS),
        send_count,
        send_index[0],
    )


def body(embeddings, assign, owner, send_count, send_index):
    arguments = (embeddings, assign, owner, send_count, send_index)
    results, fault = routed(*arguments)
    results = lax.cond(fault[0, 0] != 0, lambda: jnp.stack(general(*arguments)), lambda: results)
    return results[0], results[1]


def solution(mesh):
    placed = (
        P(("grp", "blk"), None),
        P(("grp", "blk")),
        P(),
        P(("grp", "blk"), None),
        P(("grp", "blk"), None, None),
    )
    return jax.shard_map(
        body,
        mesh=mesh,
        in_specs=placed,
        out_specs=(P(("grp", "blk")), P(("grp", "blk"))),
        check_vma=False,
    )
```

```python
import functools

import jax
import jax.numpy as jnp
from jax import lax
from jax.experimental import pallas as pl
from jax.experimental.pallas import tpu as pltpu
from jax.sharding import PartitionSpec as P

EPSILON = 1e-06
F32 = jnp.float32
BF16 = jnp.bfloat16

CHIPS = 64
ROWS = 512
WIDTH = 768
CLUSTERS = 128
GROUPS = 16
CAP = 64
BASE = 16
HALF = WIDTH // 2
LINES = 16
DEPTH = 4
POOL = 8
PARTS = ((0, 40, 400), (40, 32, 256))
TOTAL = 72
HELD = 656
STARTS = (0, 400)
LAST = len(PARTS) - 1
NONE = 1e30


def normalize(values):
    widened = values.astype(F32)
    return widened * lax.rsqrt(jnp.sum(widened * widened, axis=1, keepdims=True) + EPSILON)


def general(embeddings, assign, owner, send_count, send_index):
    rows_local = embeddings.shape[0]
    feature_width = embeddings.shape[1]
    groups = lax.axis_size("grp")
    clusters = owner.shape[0]
    capacity = send_index.shape[2]
    slot_total = groups * capacity
    unit_rows = normalize(embeddings)
    unit_low = unit_rows.astype(BF16)
    counts = send_count[0]
    listed = send_index[0]
    live_slot = jnp.arange(capacity, dtype=jnp.int32)[None, :] < counts[:, None]
    listed_cluster = assign[listed]
    owned_here = owner[listed_cluster] == jnp.arange(groups, dtype=jnp.int32)[:, None]
    kept_slot = live_slot & owned_here
    out_cluster = jnp.where(kept_slot, listed_cluster, -1)
    out_tag = jnp.where(kept_slot, lax.axis_index(("grp", "blk")) * rows_local + listed, -1)
    out_vector = unit_low[listed.reshape(-1)].reshape(groups, capacity, feature_width)
    got_vector, got_cluster, got_tag = (
        lax.all_to_all(out_vector, "grp", split_axis=0, concat_axis=0, tiled=True),
        lax.all_to_all(out_cluster, "grp", split_axis=0, concat_axis=0, tiled=True),
        lax.all_to_all(out_tag, "grp", split_axis=0, concat_axis=0, tiled=True),
    )
    own_vector = got_vector.reshape(slot_total, feature_width)
    own_cluster = got_cluster.reshape(slot_total)
    own_tag = got_tag.reshape(slot_total)

    def tile_best(current, shard_piece):
        other_vector, other_cluster, other_tag = shard_piece
        scores = jnp.einsum("id,jd->ij", own_vector, other_vector, preferred_element_type=F32)
        matched = (
            (own_cluster[:, None] == other_cluster[None, :])
            & (other_cluster[None, :] >= 0)
            & (own_tag[:, None] != other_tag[None, :])
        )
        return jnp.maximum(current, jnp.max(jnp.where(matched, scores, -1.0), axis=1))

    other_vector = lax.all_gather(own_vector, "blk", axis=0, tiled=True)
    other_cluster = lax.all_gather(own_cluster, "blk", axis=0, tiled=True)
    other_tag = lax.all_gather(own_tag, "blk", axis=0, tiled=True)
    length = other_vector.shape[0]
    number = length // slot_total
    stacked = (
        other_vector.reshape(number, slot_total, feature_width),
        other_cluster.reshape(number, slot_total),
        other_tag.reshape(number, slot_total),
    )

    def scan_step(carry, single):
        return (tile_best(carry, single), None)

    result, unused = lax.scan(scan_step, jnp.full((slot_total,), -1.0, F32), stacked)
    target = jnp.where(live_slot, listed, rows_local).reshape(-1)
    partial_sum = jax.ops.segment_sum(unit_rows, assign, num_segments=clusters)
    centre = normalize(lax.psum(partial_sum, ("grp", "blk")))
    nearness = jnp.sum(unit_low.astype(F32) * centre[assign], axis=1)
    returned = lax.all_to_all(
        result.reshape(groups, capacity), "grp", split_axis=0, concat_axis=0, tiled=True
    )
    has_entry = (
        jnp.zeros((rows_local,), jnp.int32)
        .at[target]
        .max(kept_slot.astype(jnp.int32).reshape(-1), mode="drop")
    )
    centroid_cos = jnp.where(has_entry > 0, nearness, 0.0)
    max_sim = jnp.full((rows_local,), -1.0, F32).at[target].max(returned.reshape(-1), mode="drop")
    return (max_sim, centroid_cos)


def iota(shape, axis):
    return lax.broadcasted_iota(jnp.int32, shape, axis)


def down(values):
    return jnp.sum(values, axis=0, keepdims=True)


def across(values):
    return jnp.sum(values, axis=1, keepdims=True)


def pick(mask, values):
    return jnp.where(mask, values, 0.0)


def as_column(row):
    size = row.shape[1]
    return across(pick(iota((size, size), 0) == iota((size, size), 1), row))


def as_row(column):
    size = column.shape[0]
    return down(pick(iota((size, size), 0) == iota((size, size), 1), column))


def dot(a, b):
    return jnp.dot(a, b, preferred_element_type=F32)


def dot_rows(a, b):
    return lax.dot_general(a, b, (((1,), (1,)), ((), ())), preferred_element_type=F32)


def onehot(mask):
    return jnp.where(mask, 1.0, 0.0).astype(BF16)


def halves(values):
    first = values.astype(BF16).astype(F32)
    return first, (values - first).astype(BF16).astype(F32)


def rank_groups(count_ref):
    count_row = count_ref[...].astype(F32)
    count_column = as_column(count_row)
    sub, lane = iota((GROUPS, 128), 0), iota((GROUPS, 128), 1)
    count_lanes = down(pick(sub == lane, count_column))
    ahead = (count_column > count_lanes) | ((count_column == count_lanes) & (sub < lane))
    rank = down(jnp.where(ahead, 1.0, 0.0))
    return jnp.where(iota((1, 128), 1) < GROUPS, rank, 0.0), count_column


def place_documents(assign_ref, owner_ref, rank):
    owner_row = owner_ref[...].astype(F32)
    owner_column = as_column(owner_row)
    sub, lane = iota((CLUSTERS, CLUSTERS), 0), iota((CLUSTERS, CLUSTERS), 1)
    within = across(jnp.where((owner_column == owner_row) & (lane < sub), 1.0, 0.0))
    group_rank = across(pick(owner_column == lane.astype(F32), rank))
    place_column = group_rank * (CLUSTERS // GROUPS) + within
    member = iota((CLUSTERS, ROWS), 0) == assign_ref[...]
    place = down(pick(member, place_column))
    group = down(pick(member, owner_column))
    order = iota((CLUSTERS, ROWS), 0).astype(F32)
    at_place = order == place
    earlier = onehot(iota((ROWS, ROWS), 0) < iota((ROWS, ROWS), 1))
    before = dot(onehot(at_place), earlier)
    slot = down(pick(at_place, before))
    count_column = across(jnp.where(at_place, 1.0, 0.0))
    partner_count = down(pick(order == (CLUSTERS - 1) - place, count_column))
    slot = slot + jnp.where(place >= CHIPS, partner_count, 0.0)
    chip = jnp.minimum(place, (CLUSTERS - 1) - place)
    return group, chip.astype(jnp.int32), slot.astype(jnp.int32), as_row(count_column)


def missing_documents(index_ref, count_column, group):
    listed = index_ref[...]
    live = iota((GROUPS, CAP), 1).astype(F32) < count_column
    eye = onehot(iota((CAP, CAP), 0) == iota((CAP, CAP), 1))
    high = dot_rows(eye, jnp.where(live, listed >> 4, 0).astype(F32).astype(BF16))
    low = dot_rows(eye, jnp.where(live, listed & 15, 0).astype(F32).astype(BF16))
    alive = dot_rows(eye, onehot(live))
    slots = jnp.where(alive > 0.5, high * 16.0 + low, -1.0)
    document = iota((1, ROWS), 1).astype(F32)
    lane = iota((CAP, GROUPS), 1)

    def count(g, hits):
        column = across(pick(lane == g, slots))
        wanted = jnp.where(group == g.astype(F32), document, -2.0)
        return hits + jnp.where(column == wanted, 1.0, 0.0)

    hits = lax.fori_loop(0, GROUPS, count, jnp.zeros((CAP, ROWS), F32))
    return across(jnp.where(down(hits) > 0.5, 0.0, 1.0))


def send_order():
    order = []
    for step in range(CHIPS):
        high, middle, low = step // 16, (step // 4) % 4, step % 4
        order.append((low, (middle + low) % 4, (high + middle + low) % 4))
    near = [shift for shift in order if sum(min(d, 4 - d) for d in shift) <= 1] + [(2, 0, 0)]
    near.sort(key=lambda shift: -sum(min(d, 4 - d) for d in shift))
    return [shift for shift in order if shift not in near] + near


ORDER = send_order()
SELF = CHIPS - 1


def step_to(dx, dy, dz):
    shift = (dx & 3) * 16 + (dy & 3) * 4 + (dz & 3)
    step = jnp.full(shift.shape, SELF, jnp.int32)
    for number, (x, y, z) in enumerate(ORDER[:SELF]):
        step = jnp.where(shift == x * 16 + y * 4 + z, number, step)
    return step


def in_part(step, part):
    begin, steps, _ = PARTS[part]
    return (step >= begin) & (step < begin + steps)


def chip_places():
    sub, lane = iota((CLUSTERS, CLUSTERS), 0), iota((CLUSTERS, CLUSTERS), 1)
    return onehot((sub == lane) | (sub == (CLUSTERS - 1) - lane))


def excess(totals):
    lane = iota(totals.shape, 1)
    return jnp.where(lane < CHIPS, jnp.maximum(totals - BASE, 0.0), 0.0)


def receive_plan(counts, ranks, rank, my_x, my_y, my_z):
    chip = my_x * 16 + my_y * 4 + my_z
    differ = jnp.where(ranks != rank, 1.0, 0.0)
    fault = across(down(differ))
    both = dot(counts.astype(BF16), chip_places())
    over = excess(both)
    lanes = iota((CHIPS, CLUSTERS), 1)
    sender = iota((CHIPS, 1), 0)
    source, target = iota((CHIPS, CHIPS), 0), iota((CHIPS, CHIPS), 1)

    same_line = (source >> 2) == (target >> 2)
    over_total = across(over)
    over_row = as_row(over_total)
    line_start = across(pick(same_line & (target < source), over_row))
    line_total = across(pick(same_line, over_row))
    fault = fault + down(jnp.where(line_total > POOL, 1.0, 0.0))
    start = line_start + across(pick(lanes < chip, over))
    number = across(pick(lanes == chip, over))

    to_chip = iota((1, CLUSTERS), 1)
    route = step_to(
        (to_chip >> 4) - (sender >> 4), ((to_chip >> 2) & 3) - ((sender >> 2) & 3), (to_chip & 3) - (sender & 3)
    )
    based = jnp.where(lanes < CHIPS, jnp.minimum(both, float(BASE)), 0.0)
    for part, (_, _, room) in enumerate(PARTS):
        held = down(pick(in_part(route, part), based))
        if part == LAST:
            held = held + down(over)
        fault = fault + across(jnp.where(held > room, 1.0, 0.0))

    first = across(pick(lanes == chip, counts))
    second = across(pick(lanes == (CLUSTERS - 1) - chip, counts))
    place = (lanes & (POOL - 1)).astype(F32) - start
    mine = ((sender >> 2) == (lanes >> 3)) & (place >= 0.0) & (place < number)
    over_first = down(jnp.where(mine & (place + BASE < first), 1.0, 0.0))
    over_second = down(jnp.where(mine & (place + BASE >= first), 1.0, 0.0))
    over_first_total, over_second_total = across(over_first), across(over_second)
    earlier = onehot(iota((CLUSTERS, CLUSTERS), 0) < iota((CLUSTERS, CLUSTERS), 1))
    sub = iota((16, CLUSTERS), 0)
    before = dot((pick(sub == 0, over_first) + pick(sub == 1, over_second)).astype(BF16), earlier)

    base_first = jnp.minimum(first, float(BASE))
    base_second = jnp.minimum(first + second, float(BASE)) - base_first
    first_row, second_row = as_row(base_first), as_row(base_second)

    def my_step(other):
        return step_to(my_x - (other >> 4), my_y - ((other >> 2) & 3), my_z - (other & 3))

    step_column, step_row = my_step(sender), my_step(iota((1, CHIPS), 1))
    plans = []
    ends = []
    for part, (begin, steps, _) in enumerate(PARTS):
        inside = in_part(step_column, part)
        ahead = (target < source) & in_part(step_row, part)
        first_total = down(pick(inside, base_first))
        second_total = down(pick(inside, base_second))
        last = part == LAST
        first_end = first_total + over_first_total if last else first_total
        first_start = across(pick(ahead, first_row))
        second_start = across(pick(ahead, second_row)) + first_end
        spread = step_column - begin == (iota((CHIPS, steps * BASE), 1) >> 4)
        head, tail, head_start, tail_start = [
            down(pick(spread, column)) for column in (base_first, base_second, first_start, second_start)
        ]
        slot = (iota((1, steps * BASE), 1) & (BASE - 1)).astype(F32)
        later = jnp.where(slot < head + tail, tail_start + (slot - head), -1.0)
        plan = jnp.where(slot < head, head_start + slot, later)
        held_end = first_end + second_total
        if last:
            over_row_of = jnp.where(over_second > 0.5, held_end + before[1:2], -1.0)
            over_row_of = jnp.where(over_first > 0.5, first_total + before[0:1], over_row_of)
            plan = jnp.concatenate([plan[:, : steps * BASE - CLUSTERS], over_row_of], axis=1)
            held_end = held_end + over_second_total
        plans.append(plan)
        ends.append((first_end, held_end))
    return plans, ends, fault


def kernel(
    x_hbm, assign_hbm, owner_hbm, count_hbm, index_hbm,
    out_ref, fault_ref,
    x_ref, assign_ref, owner_ref, count_ref, index_ref,
    send, got, own_over, line_over, send_over, got_over, pick_0, pick_1,
    keys, facts, sums, their_sums, back, returned,
    load_sem, send_sem, recv_sem,
):
    grp, blk = lax.axis_index("grp"), lax.axis_index("blk")
    my_x, my_y, my_z, core = grp // 4, grp % 4, blk // 2, blk % 2
    my_chip = grp * 4 + my_z
    picks = (pick_0, pick_1)
    along_x = [((my_x + d) % 4) * 4 for d in range(4)]
    along_y = [(my_y + d) % 4 for d in range(4)]
    along_z = [((my_z + d) % 4) * 2 + core for d in range(4)]
    other_core = {"grp": grp, "blk": my_z * 2 + (1 - core)}

    def device_at(step, sign):
        dx, dy, dz = [(sign * d) % 4 for d in ORDER[step]]
        return {"grp": along_x[dx] + along_y[dy], "blk": along_z[dz]}

    def remote(source, target, number, device):
        return pltpu.make_async_remote_copy(
            src_ref=source,
            dst_ref=target,
            send_sem=send_sem.at[number],
            recv_sem=recv_sem.at[number],
            device_id=device,
            device_id_type=pl.DeviceIdType.MESH,
        )

    def await_blocks(ref, number, semaphore):
        block = ref.at[pl.ds(0, number)]
        pltpu.make_async_copy(block, block, semaphore).wait()

    LINE, OVER, FACTS, SUMS, BACK, SWAP, PART = 0, 1, 2, 3, 4, 5, 7
    messages = [min(begin + steps, SELF) - begin for begin, steps, _ in PARTS]

    loads = [
        pltpu.make_async_copy(source, target, load_sem.at[number])
        for number, (source, target) in enumerate(
            (
                (assign_hbm, assign_ref),
                (owner_hbm, owner_ref),
                (count_hbm, count_ref),
                (index_hbm, index_ref),
                (x_hbm, x_ref),
            )
        )
    ]
    for load in loads:
        load.start()
    for load in loads[:-1]:
        load.wait()

    rank, count_column = rank_groups(count_ref)
    group, chip, slot, place_counts = place_documents(assign_ref, owner_ref, rank)
    step_of = step_to((chip >> 4) - my_x, ((chip >> 2) & 3) - my_y, (chip & 3) - my_z)
    in_base = slot < BASE
    send_slot = jnp.where(in_base, step_of * BASE + slot, -1)
    loads[-1].wait()

    def pack(first, stop):
        slots = iota(((stop - first) * BASE, ROWS), 0) + first * BASE
        rows = dot(onehot(slots == send_slot), x_ref[...]).astype(BF16)
        send[pl.ds(first, stop - first)] = rows.reshape(stop - first, BASE, WIDTH)

    def post(first, stop):
        for step in range(first, min(stop, SELF)):
            number = max(part for part in range(len(PARTS)) if PARTS[part][0] <= step)
            remote(send.at[step], got.at[step], PART + number, device_at(step, 1)).start()

    pack(0, 24)
    post(0, 8)
    place_counts_16 = place_counts + jnp.zeros((16, CLUSTERS), F32)
    own_excess = excess(dot(place_counts_16.astype(BF16), chip_places())[0:1])
    eye = iota((CHIPS, CLUSTERS), 0) == iota((CHIPS, CLUSTERS), 1)
    excess_column = across(pick(eye, own_excess))
    over_slot = down(pick(iota((CHIPS, ROWS), 0) < chip, excess_column)).astype(jnp.int32) + (slot - BASE)
    over_slot = jnp.where(in_base, -1, over_slot)
    row = iota((BASE, CLUSTERS), 0)
    own_over[:, :WIDTH] = dot(onehot(iota((BASE, ROWS), 0) == over_slot), x_ref[...]).astype(BF16)
    own_over[:, WIDTH:] = (pick(row == 0, place_counts) + pick(row == 1, rank)).astype(BF16)
    line_over[my_z] = own_over[...]
    for d in range(1, DEPTH):
        remote(own_over, line_over.at[my_z], LINE, {"grp": grp, "blk": along_z[d]}).start()
    post(8, 24)
    pack(24, 48)

    await_blocks(line_over, DEPTH - 1, recv_sem.at[LINE])
    line_counts = [line_over[d, 0:1, WIDTH:].astype(F32) for d in range(DEPTH)]
    line_ranks = [line_over[d, 1:2, WIDTH:].astype(F32) for d in range(DEPTH)]
    row = iota((2 * POOL, CLUSTERS), 0)
    told = jnp.zeros((2 * POOL, CLUSTERS), F32)
    for d in range(DEPTH):
        told = told + pick(row == d, line_counts[d]) + pick(row == DEPTH + d, line_ranks[d])
    told = told.astype(BF16)
    line_total = across(excess(dot(told, chip_places())))[0:DEPTH]
    depth = iota((DEPTH, 1), 0)
    line_start = jnp.zeros((DEPTH, 1), F32)
    for d in range(DEPTH - 1):
        line_start = line_start + pick(depth > d, line_total[d : d + 1])
    my_start = down(pick(depth == my_z, line_start))
    at = depth == (iota((DEPTH, DEPTH * BASE), 1) >> 4)
    begin = down(pick(at, line_start))
    number = down(pick(at, line_total))
    order = (iota((1, DEPTH * BASE), 1) & (BASE - 1)).astype(F32)
    order = jnp.where(order < number, begin + order, -1.0)
    rows = iota((2 * POOL, DEPTH * BASE), 0).astype(F32)
    blocks = line_over[:, :, :WIDTH].reshape(DEPTH * BASE, WIDTH)
    left = dot(onehot((rows == order) & (rows < POOL)), blocks[:, :HALF])
    right = dot(onehot((rows - POOL == order) & (rows >= POOL)), blocks[:, HALF:])
    send_over[:, :HALF] = (left + right).astype(BF16)
    send_over[:, HALF:] = told
    got_over[grp] = send_over[...]
    for step in range(1, LINES):
        low, middle = step % 4, step // 4
        device = {"grp": along_x[low] + along_y[(middle + low) % 4], "blk": blk}
        remote(send_over, got_over.at[grp], OVER, device).start()
    post(24, 48)
    pack(48, CHIPS)
    post(48, CHIPS)
    got[SELF] = send[SELF]
    missing = missing_documents(index_ref, count_column, group)

    await_blocks(got_over, LINES - 1, recv_sem.at[OVER])
    told = got_over[:, :, HALF:].astype(F32)
    counts = told[:, 0:DEPTH].reshape(CHIPS, CLUSTERS)
    ranks = told[:, DEPTH : 2 * DEPTH].reshape(CHIPS, CLUSTERS)
    plans, ends, fault = receive_plan(counts, ranks, rank, my_x, my_y, my_z)

    row = iota((8, 128), 0)
    told = pick(row == 6, rank) + pick(row == 7, jnp.where(iota((1, 128), 1) == 0, fault, missing))
    for part, (first_end, held_end) in enumerate(ends):
        told = told + pick(row == part, first_end) + pick(row == 2 + part, held_end)
        picks[part][...] = onehot(iota(picks[part].shape, 0).astype(F32) == plans[part])
    facts[0] = told
    swap_facts = remote(facts.at[0], facts.at[1], FACTS, other_core)
    swap_facts.start()

    best = [jnp.full((1, room), -1.0, F32) for _, _, room in PARTS]
    key_kinds = []
    query_kinds = []
    totals = [jnp.zeros((1, WIDTH), F32), jnp.zeros((1, WIDTH), F32)]
    swaps = []

    def add_kinds(first, held, room):
        number = iota((room, 1), 0).astype(F32)
        key_kinds.append(jnp.where(number < first, 0.0, jnp.where(number < held, 1.0, 2.0)))

    for (first_end, held_end), (_, _, room) in zip(ends, PARTS):
        add_kinds(first_end, held_end, room)
        query_kinds.append(jnp.where(iota((1, room), 1).astype(F32) < first_end, 0.0, 1.0))

    def compare(first_key, last_key, part, more=0):
        borders = (*STARTS, *(HELD + start for start in STARTS), 2 * HELD)
        begin, stop = borders[first_key], borders[last_key + 1]
        start, room = STARTS[part], PARTS[part][2]
        scores = dot_rows(keys[begin : stop + more], keys[start : start + room])
        rest, scores = scores[stop - begin :], scores[: stop - begin]
        kind = jnp.concatenate(key_kinds[first_key : last_key + 1], axis=0)
        matched = kind == query_kinds[part]
        if begin < start + room and start < stop:
            matched = matched & (iota(kind.shape, 0) + (begin - start) != iota((1, room), 1))
        best[part] = jnp.maximum(best[part], jnp.max(jnp.where(matched, scores, -1.0), axis=0, keepdims=True))
        return rest

    def arrive(part):
        begin, steps, room = PARTS[part]
        await_blocks(got, messages[part], recv_sem.at[PART + part])
        rows = dot(picks[part][...], got[pl.ds(begin, steps)].reshape(steps * BASE, WIDTH))
        unit = rows * lax.rsqrt(across(rows * rows) + EPSILON)
        keys[pl.ds(STARTS[part], room)] = unit.astype(BF16)
        swap = remote(
            keys.at[pl.ds(STARTS[part], room)], keys.at[pl.ds(HELD + STARTS[part], room)], SWAP + part, other_core
        )
        swap.start()
        swaps.append(swap)
        is_first = iota((room, 1), 0).astype(F32) < ends[part][0]
        totals[0] = totals[0] + down(pick(is_first, unit))
        totals[1] = totals[1] + down(jnp.where(is_first, 0.0, unit))

    arrive(0)
    compare(0, 0, 0)
    swap_facts.wait()
    their_told = facts[1]
    for part, (_, _, room) in enumerate(PARTS):
        add_kinds(their_told[part : part + 1, 0:1], their_told[2 + part : 3 + part, 0:1], room)
    half_rows = got_over[:, :, :HALF].reshape(LINES * 2 * POOL, HALF)
    shape = (LINES * POOL, LINES * 2 * POOL)
    to, at = iota(shape, 0), iota(shape, 1)
    same = ((to >> 3) == (at >> 4)) & ((to & 7) == (at & 7))
    left = dot(onehot(same & ((at & POOL) == 0)), half_rows)
    right = dot(onehot(same & ((at & POOL) != 0)), half_rows)
    whole = jnp.concatenate([left, right], axis=1).astype(BF16)
    got[pl.ds(CHIPS, TOTAL - CHIPS)] = whole.reshape(TOTAL - CHIPS, BASE, WIDTH)
    swaps[0].wait()
    compare(2, 2, 0)

    arrive(1)
    row = iota((8, WIDTH), 0)
    sums[...] = pick(row == 0, totals[0]) + pick(row == 1, totals[1])
    swap_sums = remote(sums, their_sums, SUMS, other_core)
    swap_sums.start()
    compare(0, 2, 1)
    compare(1, 1, 0)

    swap_sums.wait()
    total = sums[...] + their_sums[...]
    keys[pl.ds(2 * HELD, 16)] = jnp.concatenate(halves(total), axis=0).astype(BF16)
    scale = lax.rsqrt(across(total * total) + EPSILON)
    swaps[1].wait()
    near = [compare(3, 3, part, 16) for part in range(len(PARTS))]
    near = [(some[0:8] + some[8:16]) * scale for some in near]

    poison = missing + their_told[7:8, 1:2] > 0.5
    tiles = CHIPS * BASE // 128
    for part, (begin, steps, room) in enumerate(PARTS):
        row = iota((8, room), 0)
        query_number = iota((1, room), 1).astype(F32)
        some = jnp.where(query_number < ends[part][0], near[part][0:1], near[part][1:2])
        values = jnp.zeros((8, room), F32)
        for number, term in enumerate(halves(best[part]) + halves(some)):
            values = jnp.where(row == number, term, values)
        out = dot(values.astype(BF16), picks[part][...])
        for kind in range(2):
            line = out[2 * kind : 2 * kind + 1] + out[2 * kind + 1 : 2 * kind + 2]
            line = jnp.where(poison, NONE, line)
            for tile in range(steps * BASE // 128):
                piece = line[:, tile * 128 : (tile + 1) * 128]
                to = begin * BASE // 128 + tile
                if to < tiles:
                    back[to, kind : kind + 1, :] = piece
                else:
                    for each in range(tiles):
                        back[each, 2 + kind : 3 + kind, :] = piece
    returned[SELF] = back[SELF // 8]
    for step in range(SELF):
        remote(back.at[step // 8], returned.at[step], BACK, device_at(step, -1)).start()

    differ = across(jnp.where(their_told[6:7] != rank, 1.0, 0.0))
    fault = fault + their_told[7:8, 0:1] + differ
    chosen = onehot(iota((CHIPS, ROWS), 0) == step_of)
    sub = iota((128, ROWS), 0)
    at_base = (sub == (step_of & 7) * BASE + slot) & in_base
    at_over = (sub == grp * POOL + my_start.astype(jnp.int32) + over_slot) & (~in_base)

    await_blocks(returned, CHIPS - 1, recv_sem.at[BACK])
    found = []
    for number in range(4):
        line = returned[:, number, :]
        if number == 0:
            poisoned = across(down(jnp.where(line > 0.5 * NONE, 1.0, 0.0)))
            fault_ref[...] = jnp.where(fault + poisoned > 0.5, 1, 0) + jnp.zeros((1, 128), jnp.int32)
        terms = jnp.concatenate(halves(line), axis=1).astype(BF16)
        out = lax.dot_general(terms, chosen, (((0,), (0,)), ((), ())), preferred_element_type=F32)
        found.append(out[0:128] + out[128:256])
    out_ref[0:1] = down(pick(at_base, found[0]) + pick(at_over, found[2]))
    out_ref[1:2] = down(pick(at_base, found[1]) + pick(at_over, found[3]))

    await_blocks(line_over, DEPTH - 1, send_sem.at[LINE])
    await_blocks(got_over, LINES - 1, send_sem.at[OVER])
    await_blocks(returned, CHIPS - 1, send_sem.at[BACK])
    for part in range(len(PARTS)):
        await_blocks(got, messages[part], send_sem.at[PART + part])


def routed(embeddings, assign, owner, send_count, send_index):
    return pl.pallas_call(
        kernel,
        out_shape=(
            jax.ShapeDtypeStruct((2, ROWS), F32),
            jax.ShapeDtypeStruct((1, 128), jnp.int32),
        ),
        in_specs=[pl.BlockSpec(memory_space=pl.ANY)] * 5,
        out_specs=(pl.BlockSpec(memory_space=pltpu.VMEM),) * 2,
        scratch_shapes=[
            pltpu.VMEM((ROWS, WIDTH), BF16),
            pltpu.VMEM((1, ROWS), jnp.int32),
            pltpu.VMEM((1, CLUSTERS), jnp.int32),
            pltpu.VMEM((1, GROUPS), jnp.int32),
            pltpu.VMEM((GROUPS, CAP), jnp.int32),
            pltpu.VMEM((CHIPS, BASE, WIDTH), BF16),
            pltpu.VMEM((TOTAL, BASE, WIDTH), BF16),
            pltpu.VMEM((BASE, WIDTH + CLUSTERS), BF16),
            pltpu.VMEM((DEPTH, BASE, WIDTH + CLUSTERS), BF16),
            pltpu.VMEM((2 * POOL, HALF + CLUSTERS), BF16),
            pltpu.VMEM((LINES, 2 * POOL, HALF + CLUSTERS), BF16),
            *[pltpu.VMEM((room, steps * BASE), BF16) for _, steps, room in PARTS],
            pltpu.VMEM((2 * HELD + 16, WIDTH), BF16),
            pltpu.VMEM((2, 8, 128), F32),
            pltpu.VMEM((8, WIDTH), F32),
            pltpu.VMEM((8, WIDTH), F32),
            pltpu.VMEM((CHIPS * BASE // 128, 4, 128), F32),
            pltpu.VMEM((CHIPS, 4, 128), F32),
            pltpu.SemaphoreType.DMA((5,)),
            pltpu.SemaphoreType.DMA((9,)),
            pltpu.SemaphoreType.DMA((9,)),
        ],
        compiler_params=pltpu.CompilerParams(
            has_side_effects=True, vmem_limit_bytes=48 * 1024 * 1024
        ),
    )(
        embeddings,
        assign.reshape(1, ROWS),
        owner.reshape(1, CLUSTERS),
        send_count,
        send_index[0],
    )


def body(embeddings, assign, owner, send_count, send_index):
    arguments = (embeddings, assign, owner, send_count, send_index)
    results, fault = routed(*arguments)
    results = lax.cond(fault[0, 0] != 0, lambda: jnp.stack(general(*arguments)), lambda: results)
    return results[0], results[1]


def solution(mesh):
    placed = (
        P(("grp", "blk"), None),
        P(("grp", "blk")),
        P(),
        P(("grp", "blk"), None),
        P(("grp", "blk"), None, None),
    )
    return jax.shard_map(
        body,
        mesh=mesh,
        in_specs=placed,
        out_specs=(P(("grp", "blk")), P(("grp", "blk"))),
        check_vma=False,
    )
```

```python
import functools

import jax
import jax.numpy as jnp
from jax import lax
from jax.experimental import pallas as pl
from jax.experimental.pallas import tpu as pltpu
from jax.sharding import PartitionSpec as P

EPSILON = 1e-06
F32 = jnp.float32
BF16 = jnp.bfloat16

CHIPS = 64
ROWS = 512
WIDTH = 768
CLUSTERS = 128
GROUPS = 16
CAP = 64
BASE = 16
HALF = WIDTH // 2
LINES = 16
DEPTH = 4
POOL = 8
PARTS = ((0, 40, 400), (40, 32, 256))
TOTAL = 72
HELD = 656
STARTS = (0, 400)
LAST = len(PARTS) - 1
NONE = 1e30


def normalize(values):
    widened = values.astype(F32)
    return widened * lax.rsqrt(jnp.sum(widened * widened, axis=1, keepdims=True) + EPSILON)


def general(embeddings, assign, owner, send_count, send_index):
    rows_local = embeddings.shape[0]
    feature_width = embeddings.shape[1]
    groups = lax.axis_size("grp")
    clusters = owner.shape[0]
    capacity = send_index.shape[2]
    slot_total = groups * capacity
    unit_rows = normalize(embeddings)
    unit_low = unit_rows.astype(BF16)
    counts = send_count[0]
    listed = send_index[0]
    live_slot = jnp.arange(capacity, dtype=jnp.int32)[None, :] < counts[:, None]
    listed_cluster = assign[listed]
    owned_here = owner[listed_cluster] == jnp.arange(groups, dtype=jnp.int32)[:, None]
    kept_slot = live_slot & owned_here
    out_cluster = jnp.where(kept_slot, listed_cluster, -1)
    out_tag = jnp.where(kept_slot, lax.axis_index(("grp", "blk")) * rows_local + listed, -1)
    out_vector = unit_low[listed.reshape(-1)].reshape(groups, capacity, feature_width)
    got_vector, got_cluster, got_tag = (
        lax.all_to_all(out_vector, "grp", split_axis=0, concat_axis=0, tiled=True),
        lax.all_to_all(out_cluster, "grp", split_axis=0, concat_axis=0, tiled=True),
        lax.all_to_all(out_tag, "grp", split_axis=0, concat_axis=0, tiled=True),
    )
    own_vector = got_vector.reshape(slot_total, feature_width)
    own_cluster = got_cluster.reshape(slot_total)
    own_tag = got_tag.reshape(slot_total)

    def tile_best(current, shard_piece):
        other_vector, other_cluster, other_tag = shard_piece
        scores = jnp.einsum("id,jd->ij", own_vector, other_vector, preferred_element_type=F32)
        matched = (
            (own_cluster[:, None] == other_cluster[None, :])
            & (other_cluster[None, :] >= 0)
            & (own_tag[:, None] != other_tag[None, :])
        )
        return jnp.maximum(current, jnp.max(jnp.where(matched, scores, -1.0), axis=1))

    other_vector = lax.all_gather(own_vector, "blk", axis=0, tiled=True)
    other_cluster = lax.all_gather(own_cluster, "blk", axis=0, tiled=True)
    other_tag = lax.all_gather(own_tag, "blk", axis=0, tiled=True)
    length = other_vector.shape[0]
    number = length // slot_total
    stacked = (
        other_vector.reshape(number, slot_total, feature_width),
        other_cluster.reshape(number, slot_total),
        other_tag.reshape(number, slot_total),
    )

    def scan_step(carry, single):
        return (tile_best(carry, single), None)

    result, unused = lax.scan(scan_step, jnp.full((slot_total,), -1.0, F32), stacked)
    target = jnp.where(live_slot, listed, rows_local).reshape(-1)
    partial_sum = jax.ops.segment_sum(unit_rows, assign, num_segments=clusters)
    centre = normalize(lax.psum(partial_sum, ("grp", "blk")))
    nearness = jnp.sum(unit_low.astype(F32) * centre[assign], axis=1)
    returned = lax.all_to_all(
        result.reshape(groups, capacity), "grp", split_axis=0, concat_axis=0, tiled=True
    )
    has_entry = (
        jnp.zeros((rows_local,), jnp.int32)
        .at[target]
        .max(kept_slot.astype(jnp.int32).reshape(-1), mode="drop")
    )
    centroid_cos = jnp.where(has_entry > 0, nearness, 0.0)
    max_sim = jnp.full((rows_local,), -1.0, F32).at[target].max(returned.reshape(-1), mode="drop")
    return (max_sim, centroid_cos)


def iota(shape, axis):
    return lax.broadcasted_iota(jnp.int32, shape, axis)


def down(values):
    return jnp.sum(values, axis=0, keepdims=True)


def across(values):
    return jnp.sum(values, axis=1, keepdims=True)


def pick(mask, values):
    return jnp.where(mask, values, 0.0)


def as_column(row):
    size = row.shape[1]
    return across(pick(iota((size, size), 0) == iota((size, size), 1), row))


def as_row(column):
    size = column.shape[0]
    return down(pick(iota((size, size), 0) == iota((size, size), 1), column))


def dot(a, b):
    return jnp.dot(a, b, preferred_element_type=F32)


def dot_rows(a, b):
    return lax.dot_general(a, b, (((1,), (1,)), ((), ())), preferred_element_type=F32)


def onehot(mask):
    return jnp.where(mask, 1.0, 0.0).astype(BF16)


def halves(values):
    first = values.astype(BF16).astype(F32)
    return first, (values - first).astype(BF16).astype(F32)


def rank_groups(count_ref):
    count_row = count_ref[...].astype(F32)
    count_column = as_column(count_row)
    sub, lane = iota((GROUPS, 128), 0), iota((GROUPS, 128), 1)
    count_lanes = down(pick(sub == lane, count_column))
    ahead = (count_column > count_lanes) | ((count_column == count_lanes) & (sub < lane))
    rank = down(jnp.where(ahead, 1.0, 0.0))
    return jnp.where(iota((1, 128), 1) < GROUPS, rank, 0.0), count_column


def place_documents(assign_ref, owner_ref, rank, earlier_ref, chip_step):
    member = iota((CLUSTERS, ROWS), 0) == assign_ref[...]
    member_low = onehot(member)
    before = down(pick(member, dot(member_low, earlier_ref[...])))
    count_column = across(jnp.where(member, 1.0, 0.0))
    owner_row = owner_ref[...].astype(F32)
    owner_column = as_column(owner_row)
    sub, lane = iota((CLUSTERS, CLUSTERS), 0), iota((CLUSTERS, CLUSTERS), 1)
    within = across(jnp.where((owner_column == owner_row) & (lane < sub), 1.0, 0.0))
    group_rank = across(pick(owner_column == lane.astype(F32), rank))
    place = group_rank * (CLUSTERS // GROUPS) + within
    chip = jnp.minimum(place, (CLUSTERS - 1) - place)
    count_row, place_row, chip_row = as_row(count_column), as_row(place), as_row(chip)
    opposite = down(pick((CLUSTERS - 1) - place == place_row, count_column))
    offset = jnp.where(place_row >= CHIPS, opposite, 0.0)
    step_row = down(pick(sub.astype(F32) == chip_row, as_column(chip_step)))
    row = iota((16, CLUSTERS), 0)
    told = pick(row == 0, owner_row) + pick(row == 1, chip_row) + pick(row == 2, step_row) + pick(row == 3, offset)
    told = dot(told.astype(BF16), member_low)
    place_counts = down(pick(place == lane.astype(F32), count_column))
    whole = told[1:4].astype(jnp.int32)
    return told[0:1], whole[0:1], whole[1:2], before.astype(jnp.int32) + whole[2:3], place_counts


def missing_documents(index_ref, count_column, group):
    listed = index_ref[...]
    live = iota((GROUPS, CAP), 1).astype(F32) < count_column
    eye = onehot(iota((CAP, CAP), 0) == iota((CAP, CAP), 1))
    high = dot_rows(eye, jnp.where(live, listed >> 4, 0).astype(F32).astype(BF16))
    low = dot_rows(eye, jnp.where(live, listed & 15, 0).astype(F32).astype(BF16))
    alive = dot_rows(eye, onehot(live))
    slots = jnp.where(alive > 0.5, high * 16.0 + low, -1.0)
    document = iota((1, ROWS), 1).astype(F32)
    lane = iota((CAP, GROUPS), 1)

    def count(g, hits):
        column = across(pick(lane == g, slots))
        wanted = jnp.where(group == g.astype(F32), document, -2.0)
        return hits + jnp.where(column == wanted, 1.0, 0.0)

    hits = lax.fori_loop(0, GROUPS, count, jnp.zeros((CAP, ROWS), F32))
    return across(jnp.where(down(hits) > 0.5, 0.0, 1.0))


def send_order():
    order = []
    for step in range(CHIPS):
        high, middle, low = step // 16, (step // 4) % 4, step % 4
        order.append((low, (middle + low) % 4, (high + middle + low) % 4))
    near = [shift for shift in order if sum(min(d, 4 - d) for d in shift) <= 1] + [(2, 0, 0)]
    near.sort(key=lambda shift: -sum(min(d, 4 - d) for d in shift))
    return [shift for shift in order if shift not in near] + near


ORDER = send_order()
SELF = CHIPS - 1


def step_to(dx, dy, dz):
    shift = (dx & 3) * 16 + (dy & 3) * 4 + (dz & 3)
    step = jnp.full(shift.shape, SELF, jnp.int32)
    for number, (x, y, z) in enumerate(ORDER[:SELF]):
        step = jnp.where(shift == x * 16 + y * 4 + z, number, step)
    return step


def in_part(step, part):
    begin, steps, _ = PARTS[part]
    return (step >= begin) & (step < begin + steps)


def chip_places():
    sub, lane = iota((CLUSTERS, CLUSTERS), 0), iota((CLUSTERS, CLUSTERS), 1)
    return onehot((sub == lane) | (sub == (CLUSTERS - 1) - lane))


def excess(totals):
    lane = iota(totals.shape, 1)
    return jnp.where(lane < CHIPS, jnp.maximum(totals - BASE, 0.0), 0.0)


def receive_plan(counts, ranks, rank, my_x, my_y, my_z, routes_ref):
    chip = my_x * 16 + my_y * 4 + my_z
    differ = jnp.where(ranks != rank, 1.0, 0.0)
    fault = across(down(differ))
    both = dot(counts.astype(BF16), chip_places())
    over = excess(both)
    lanes = iota((CHIPS, CLUSTERS), 1)
    sender = iota((CHIPS, 1), 0)
    source, target = iota((CHIPS, CHIPS), 0), iota((CHIPS, CHIPS), 1)

    same_line = (source >> 2) == (target >> 2)
    over_total = across(over)
    over_row = as_row(over_total)
    line_start = across(pick(same_line & (target < source), over_row))
    line_total = across(pick(same_line, over_row))
    fault = fault + down(jnp.where(line_total > POOL, 1.0, 0.0))
    start = line_start + across(pick(lanes < chip, over))
    number = across(pick(lanes == chip, over))

    route = routes_ref[...]
    based = jnp.where(lanes < CHIPS, jnp.minimum(both, float(BASE)), 0.0)
    for part, (_, _, room) in enumerate(PARTS):
        held = down(pick(in_part(route, part), based))
        if part == LAST:
            held = held + down(over)
        fault = fault + across(jnp.where(held > room, 1.0, 0.0))

    first = across(pick(lanes == chip, counts))
    second = across(pick(lanes == (CLUSTERS - 1) - chip, counts))
    place = (lanes & (POOL - 1)).astype(F32) - start
    mine = ((sender >> 2) == (lanes >> 3)) & (place >= 0.0) & (place < number)
    over_first = down(jnp.where(mine & (place + BASE < first), 1.0, 0.0))
    over_second = down(jnp.where(mine & (place + BASE >= first), 1.0, 0.0))
    over_first_total, over_second_total = across(over_first), across(over_second)
    earlier = onehot(iota((CLUSTERS, CLUSTERS), 0) < iota((CLUSTERS, CLUSTERS), 1))
    sub = iota((16, CLUSTERS), 0)
    before = dot((pick(sub == 0, over_first) + pick(sub == 1, over_second)).astype(BF16), earlier)

    base_first = jnp.minimum(first, float(BASE))
    base_second = jnp.minimum(first + second, float(BASE)) - base_first
    first_row, second_row = as_row(base_first), as_row(base_second)

    step_column = across(jnp.where(lanes == chip, route.astype(F32), 0.0)).astype(jnp.int32)
    step_row = as_row(step_column.astype(F32)).astype(jnp.int32)
    plans = []
    ends = []
    for part, (begin, steps, _) in enumerate(PARTS):
        inside = in_part(step_column, part)
        ahead = (target < source) & in_part(step_row, part)
        first_total = down(pick(inside, base_first))
        second_total = down(pick(inside, base_second))
        last = part == LAST
        first_end = first_total + over_first_total if last else first_total
        first_start = across(pick(ahead, first_row))
        second_start = across(pick(ahead, second_row)) + first_end
        spread = step_column - begin == (iota((CHIPS, steps * BASE), 1) >> 4)
        head, tail, head_start, tail_start = [
            down(pick(spread, column)) for column in (base_first, base_second, first_start, second_start)
        ]
        slot = (iota((1, steps * BASE), 1) & (BASE - 1)).astype(F32)
        later = jnp.where(slot < head + tail, tail_start + (slot - head), -1.0)
        plan = jnp.where(slot < head, head_start + slot, later)
        held_end = first_end + second_total
        if last:
            over_row_of = jnp.where(over_second > 0.5, held_end + before[1:2], -1.0)
            over_row_of = jnp.where(over_first > 0.5, first_total + before[0:1], over_row_of)
            plan = jnp.concatenate([plan[:, : steps * BASE - CLUSTERS], over_row_of], axis=1)
            held_end = held_end + over_second_total
        plans.append(plan)
        ends.append((first_end, held_end))
    return plans, ends, fault


def kernel(
    x_hbm, assign_hbm, owner_hbm, count_hbm, index_hbm,
    out_ref, fault_ref,
    x_ref, assign_ref, owner_ref, count_ref, index_ref,
    send, got, own_over, line_over, send_over, got_over, pick_0, pick_1,
    earlier_ref, routes_ref, keys, facts, sums, their_sums, back, returned,
    load_sem, send_sem, recv_sem,
):
    grp, blk = lax.axis_index("grp"), lax.axis_index("blk")
    my_x, my_y, my_z, core = grp // 4, grp % 4, blk // 2, blk % 2
    my_chip = grp * 4 + my_z
    picks = (pick_0, pick_1)
    along_x = [((my_x + d) % 4) * 4 for d in range(4)]
    along_y = [(my_y + d) % 4 for d in range(4)]
    along_z = [((my_z + d) % 4) * 2 + core for d in range(4)]
    other_core = {"grp": grp, "blk": my_z * 2 + (1 - core)}

    def device_at(step, sign):
        dx, dy, dz = [(sign * d) % 4 for d in ORDER[step]]
        return {"grp": along_x[dx] + along_y[dy], "blk": along_z[dz]}

    def remote(source, target, number, device):
        return pltpu.make_async_remote_copy(
            src_ref=source,
            dst_ref=target,
            send_sem=send_sem.at[number],
            recv_sem=recv_sem.at[number],
            device_id=device,
            device_id_type=pl.DeviceIdType.MESH,
        )

    def await_blocks(ref, number, semaphore):
        block = ref.at[pl.ds(0, number)]
        pltpu.make_async_copy(block, block, semaphore).wait()

    LINE, OVER, FACTS, SUMS, BACK, SWAP, PART = 0, 1, 2, 3, 4, 5, 7
    messages = [min(begin + steps, SELF) - begin for begin, steps, _ in PARTS]

    loads = [
        pltpu.make_async_copy(source, target, load_sem.at[number])
        for number, (source, target) in enumerate(
            (
                (assign_hbm, assign_ref),
                (owner_hbm, owner_ref),
                (count_hbm, count_ref),
                (index_hbm, index_ref),
                (x_hbm, x_ref),
            )
        )
    ]
    for load in loads:
        load.start()
    barrier = pltpu.get_barrier_semaphore()
    for device in [device_at(step, 1) for step in range(SELF)] + [other_core]:
        pl.semaphore_signal(barrier, inc=1, device_id=device, device_id_type=pl.DeviceIdType.MESH)
    lane = iota((1, CLUSTERS), 1)
    chip_step = step_to((lane >> 4) - my_x, ((lane >> 2) & 3) - my_y, (lane & 3) - my_z).astype(F32)
    earlier_ref[...] = onehot(iota((ROWS, ROWS), 0) < iota((ROWS, ROWS), 1))
    for load in loads[:-1]:
        load.wait()

    rank, count_column = rank_groups(count_ref)
    group, chip, step_of, slot, place_counts = place_documents(assign_ref, owner_ref, rank, earlier_ref, chip_step)
    in_base = slot < BASE
    send_slot = jnp.where(in_base, step_of * BASE + slot, -1)
    loads[-1].wait()

    def pack(first, stop):
        slots = iota(((stop - first) * BASE, ROWS), 0) + first * BASE
        rows = dot(onehot(slots == send_slot), x_ref[...]).astype(BF16)
        send[pl.ds(first, stop - first)] = rows.reshape(stop - first, BASE, WIDTH)

    def post(first, stop):
        for step in range(first, min(stop, SELF)):
            number = max(part for part in range(len(PARTS)) if PARTS[part][0] <= step)
            remote(send.at[step], got.at[step], PART + number, device_at(step, 1)).start()

    pack(0, 8)
    pl.semaphore_wait(barrier, CHIPS)
    post(0, 8)
    place_counts_16 = place_counts + jnp.zeros((16, CLUSTERS), F32)
    own_excess = excess(dot(place_counts_16.astype(BF16), chip_places())[0:1])
    eye = iota((CHIPS, CLUSTERS), 0) == iota((CHIPS, CLUSTERS), 1)
    excess_column = across(pick(eye, own_excess))
    over_slot = down(pick(iota((CHIPS, ROWS), 0) < chip, excess_column)).astype(jnp.int32) + (slot - BASE)
    over_slot = jnp.where(in_base, -1, over_slot)
    row = iota((BASE, CLUSTERS), 0)
    own_over[:, :WIDTH] = dot(onehot(iota((BASE, ROWS), 0) == over_slot), x_ref[...]).astype(BF16)
    own_over[:, WIDTH:] = (pick(row == 0, place_counts) + pick(row == 1, rank)).astype(BF16)
    line_over[my_z] = own_over[...]
    for d in range(1, DEPTH):
        remote(own_over, line_over.at[my_z], LINE, {"grp": grp, "blk": along_z[d]}).start()
    pack(8, 24)
    post(8, 24)
    pack(24, 48)
    to_chip, sender = iota((CHIPS, CLUSTERS), 1), iota((CHIPS, CLUSTERS), 0)
    routes_ref[...] = step_to(
        (to_chip >> 4) - (sender >> 4), ((to_chip >> 2) & 3) - ((sender >> 2) & 3), (to_chip & 3) - (sender & 3)
    )

    await_blocks(line_over, DEPTH - 1, recv_sem.at[LINE])
    line_counts = [line_over[d, 0:1, WIDTH:].astype(F32) for d in range(DEPTH)]
    line_ranks = [line_over[d, 1:2, WIDTH:].astype(F32) for d in range(DEPTH)]
    row = iota((2 * POOL, CLUSTERS), 0)
    told = jnp.zeros((2 * POOL, CLUSTERS), F32)
    for d in range(DEPTH):
        told = told + pick(row == d, line_counts[d]) + pick(row == DEPTH + d, line_ranks[d])
    told = told.astype(BF16)
    line_total = across(excess(dot(told, chip_places())))[0:DEPTH]
    depth = iota((DEPTH, 1), 0)
    line_start = jnp.zeros((DEPTH, 1), F32)
    for d in range(DEPTH - 1):
        line_start = line_start + pick(depth > d, line_total[d : d + 1])
    my_start = down(pick(depth == my_z, line_start))
    at = depth == (iota((DEPTH, DEPTH * BASE), 1) >> 4)
    begin = down(pick(at, line_start))
    number = down(pick(at, line_total))
    order = (iota((1, DEPTH * BASE), 1) & (BASE - 1)).astype(F32)
    order = jnp.where(order < number, begin + order, -1.0)
    rows = iota((2 * POOL, DEPTH * BASE), 0).astype(F32)
    blocks = line_over[:, :, :WIDTH].reshape(DEPTH * BASE, WIDTH)
    left = dot(onehot((rows == order) & (rows < POOL)), blocks[:, :HALF])
    right = dot(onehot((rows - POOL == order) & (rows >= POOL)), blocks[:, HALF:])
    send_over[:, :HALF] = (left + right).astype(BF16)
    send_over[:, HALF:] = told
    got_over[grp] = send_over[...]
    for step in range(1, LINES):
        low, middle = step % 4, step // 4
        device = {"grp": along_x[low] + along_y[(middle + low) % 4], "blk": blk}
        remote(send_over, got_over.at[grp], OVER, device).start()
    post(24, 48)
    pack(48, CHIPS)
    post(48, CHIPS)
    got[SELF] = send[SELF]
    missing = missing_documents(index_ref, count_column, group)

    await_blocks(got_over, LINES - 1, recv_sem.at[OVER])
    told = got_over[:, :, HALF:].astype(F32)
    counts = told[:, 0:DEPTH].reshape(CHIPS, CLUSTERS)
    ranks = told[:, DEPTH : 2 * DEPTH].reshape(CHIPS, CLUSTERS)
    plans, ends, fault = receive_plan(counts, ranks, rank, my_x, my_y, my_z, routes_ref)

    row = iota((8, 128), 0)
    told = pick(row == 6, rank) + pick(row == 7, jnp.where(iota((1, 128), 1) == 0, fault, missing))
    for part, (first_end, held_end) in enumerate(ends):
        told = told + pick(row == part, first_end) + pick(row == 2 + part, held_end)
        picks[part][...] = onehot(iota(picks[part].shape, 0).astype(F32) == plans[part])
    facts[0] = told
    swap_facts = remote(facts.at[0], facts.at[1], FACTS, other_core)
    swap_facts.start()

    best = [jnp.full((1, room), -1.0, F32) for _, _, room in PARTS]
    key_kinds = []
    query_kinds = []
    totals = [jnp.zeros((1, WIDTH), F32), jnp.zeros((1, WIDTH), F32)]
    swaps = []

    def add_kinds(first, held, room):
        number = iota((room, 1), 0).astype(F32)
        key_kinds.append(jnp.where(number < first, 0.0, jnp.where(number < held, 1.0, 2.0)))

    for (first_end, held_end), (_, _, room) in zip(ends, PARTS):
        add_kinds(first_end, held_end, room)
        query_kinds.append(jnp.where(iota((1, room), 1).astype(F32) < first_end, 0.0, 1.0))

    def compare(first_key, last_key, part, more=0):
        borders = (*STARTS, *(HELD + start for start in STARTS), 2 * HELD)
        begin, stop = borders[first_key], borders[last_key + 1]
        start, room = STARTS[part], PARTS[part][2]
        scores = dot_rows(keys[begin : stop + more], keys[start : start + room])
        rest, scores = scores[stop - begin :], scores[: stop - begin]
        kind = jnp.concatenate(key_kinds[first_key : last_key + 1], axis=0)
        matched = kind == query_kinds[part]
        if begin < start + room and start < stop:
            matched = matched & (iota(kind.shape, 0) + (begin - start) != iota((1, room), 1))
        best[part] = jnp.maximum(best[part], jnp.max(jnp.where(matched, scores, -1.0), axis=0, keepdims=True))
        return rest

    def arrive(part):
        begin, steps, room = PARTS[part]
        await_blocks(got, messages[part], recv_sem.at[PART + part])
        rows = dot(picks[part][...], got[pl.ds(begin, steps)].reshape(steps * BASE, WIDTH))
        unit = rows * lax.rsqrt(across(rows * rows) + EPSILON)
        keys[pl.ds(STARTS[part], room)] = unit.astype(BF16)
        swap = remote(
            keys.at[pl.ds(STARTS[part], room)], keys.at[pl.ds(HELD + STARTS[part], room)], SWAP + part, other_core
        )
        swap.start()
        swaps.append(swap)
        is_first = iota((room, 1), 0).astype(F32) < ends[part][0]
        totals[0] = totals[0] + down(pick(is_first, unit))
        totals[1] = totals[1] + down(jnp.where(is_first, 0.0, unit))

    arrive(0)
    compare(0, 0, 0)
    swap_facts.wait()
    their_told = facts[1]
    for part, (_, _, room) in enumerate(PARTS):
        add_kinds(their_told[part : part + 1, 0:1], their_told[2 + part : 3 + part, 0:1], room)
    half_rows = got_over[:, :, :HALF].reshape(LINES * 2 * POOL, HALF)
    shape = (LINES * POOL, LINES * 2 * POOL)
    to, at = iota(shape, 0), iota(shape, 1)
    same = ((to >> 3) == (at >> 4)) & ((to & 7) == (at & 7))
    left = dot(onehot(same & ((at & POOL) == 0)), half_rows)
    right = dot(onehot(same & ((at & POOL) != 0)), half_rows)
    whole = jnp.concatenate([left, right], axis=1).astype(BF16)
    got[pl.ds(CHIPS, TOTAL - CHIPS)] = whole.reshape(TOTAL - CHIPS, BASE, WIDTH)
    swaps[0].wait()
    compare(2, 2, 0)

    arrive(1)
    row = iota((8, WIDTH), 0)
    sums[...] = pick(row == 0, totals[0]) + pick(row == 1, totals[1])
    swap_sums = remote(sums, their_sums, SUMS, other_core)
    swap_sums.start()
    compare(0, 2, 1)
    compare(1, 1, 0)

    swap_sums.wait()
    total = sums[...] + their_sums[...]
    keys[pl.ds(2 * HELD, 16)] = jnp.concatenate(halves(total), axis=0).astype(BF16)
    scale = lax.rsqrt(across(total * total) + EPSILON)
    swaps[1].wait()
    near = [compare(3, 3, part, 16) for part in range(len(PARTS))]
    near = [(some[0:8] + some[8:16]) * scale for some in near]

    poison = missing + their_told[7:8, 1:2] > 0.5
    tiles = CHIPS * BASE // 128
    for part, (begin, steps, room) in enumerate(PARTS):
        row = iota((8, room), 0)
        query_number = iota((1, room), 1).astype(F32)
        some = jnp.where(query_number < ends[part][0], near[part][0:1], near[part][1:2])
        values = jnp.zeros((8, room), F32)
        for number, term in enumerate(halves(best[part]) + halves(some)):
            values = jnp.where(row == number, term, values)
        out = dot(values.astype(BF16), picks[part][...])
        for kind in range(2):
            line = out[2 * kind : 2 * kind + 1] + out[2 * kind + 1 : 2 * kind + 2]
            line = jnp.where(poison, NONE, line)
            for tile in range(steps * BASE // 128):
                piece = line[:, tile * 128 : (tile + 1) * 128]
                to = begin * BASE // 128 + tile
                if to < tiles:
                    back[to, kind : kind + 1, :] = piece
                else:
                    for each in range(tiles):
                        back[each, 2 + kind : 3 + kind, :] = piece
    returned[SELF] = back[SELF // 8]
    for step in range(SELF):
        remote(back.at[step // 8], returned.at[step], BACK, device_at(step, -1)).start()

    differ = across(jnp.where(their_told[6:7] != rank, 1.0, 0.0))
    fault = fault + their_told[7:8, 0:1] + differ
    chosen = onehot(iota((CHIPS, ROWS), 0) == step_of)
    sub = iota((128, ROWS), 0)
    at_base = (sub == (step_of & 7) * BASE + slot) & in_base
    at_over = (sub == grp * POOL + my_start.astype(jnp.int32) + over_slot) & (~in_base)

    await_blocks(returned, CHIPS - 1, recv_sem.at[BACK])
    found = []
    for number in range(4):
        line = returned[:, number, :]
        if number == 0:
            poisoned = across(down(jnp.where(line > 0.5 * NONE, 1.0, 0.0)))
            fault_ref[...] = jnp.where(fault + poisoned > 0.5, 1, 0) + jnp.zeros((1, 128), jnp.int32)
        terms = jnp.concatenate(halves(line), axis=1).astype(BF16)
        out = lax.dot_general(terms, chosen, (((0,), (0,)), ((), ())), preferred_element_type=F32)
        found.append(out[0:128] + out[128:256])
    out_ref[0:1] = down(pick(at_base, found[0]) + pick(at_over, found[2]))
    out_ref[1:2] = down(pick(at_base, found[1]) + pick(at_over, found[3]))

    await_blocks(line_over, DEPTH - 1, send_sem.at[LINE])
    await_blocks(got_over, LINES - 1, send_sem.at[OVER])
    await_blocks(returned, CHIPS - 1, send_sem.at[BACK])
    for part in range(len(PARTS)):
        await_blocks(got, messages[part], send_sem.at[PART + part])


def routed(embeddings, assign, owner, send_count, send_index):
    return pl.pallas_call(
        kernel,
        out_shape=(
            jax.ShapeDtypeStruct((2, ROWS), F32),
            jax.ShapeDtypeStruct((1, 128), jnp.int32),
        ),
        in_specs=[pl.BlockSpec(memory_space=pl.ANY)] * 5,
        out_specs=(pl.BlockSpec(memory_space=pltpu.VMEM),) * 2,
        scratch_shapes=[
            pltpu.VMEM((ROWS, WIDTH), BF16),
            pltpu.VMEM((1, ROWS), jnp.int32),
            pltpu.VMEM((1, CLUSTERS), jnp.int32),
            pltpu.VMEM((1, GROUPS), jnp.int32),
            pltpu.VMEM((GROUPS, CAP), jnp.int32),
            pltpu.VMEM((CHIPS, BASE, WIDTH), BF16),
            pltpu.VMEM((TOTAL, BASE, WIDTH), BF16),
            pltpu.VMEM((BASE, WIDTH + CLUSTERS), BF16),
            pltpu.VMEM((DEPTH, BASE, WIDTH + CLUSTERS), BF16),
            pltpu.VMEM((2 * POOL, HALF + CLUSTERS), BF16),
            pltpu.VMEM((LINES, 2 * POOL, HALF + CLUSTERS), BF16),
            *[pltpu.VMEM((room, steps * BASE), BF16) for _, steps, room in PARTS],
            pltpu.VMEM((ROWS, ROWS), BF16),
            pltpu.VMEM((CHIPS, CLUSTERS), jnp.int32),
            pltpu.VMEM((2 * HELD + 16, WIDTH), BF16),
            pltpu.VMEM((2, 8, 128), F32),
            pltpu.VMEM((8, WIDTH), F32),
            pltpu.VMEM((8, WIDTH), F32),
            pltpu.VMEM((CHIPS * BASE // 128, 4, 128), F32),
            pltpu.VMEM((CHIPS, 4, 128), F32),
            pltpu.SemaphoreType.DMA((5,)),
            pltpu.SemaphoreType.DMA((9,)),
            pltpu.SemaphoreType.DMA((9,)),
        ],
        compiler_params=pltpu.CompilerParams(
            collective_id=0, has_side_effects=True, vmem_limit_bytes=48 * 1024 * 1024
        ),
    )(
        embeddings,
        assign.reshape(1, ROWS),
        owner.reshape(1, CLUSTERS),
        send_count,
        send_index[0],
    )


def body(embeddings, assign, owner, send_count, send_index):
    arguments = (embeddings, assign, owner, send_count, send_index)
    results, fault = routed(*arguments)
    results = lax.cond(fault[0, 0] != 0, lambda: jnp.stack(general(*arguments)), lambda: results)
    return results[0], results[1]


def solution(mesh):
    placed = (
        P(("grp", "blk"), None),
        P(("grp", "blk")),
        P(),
        P(("grp", "blk"), None),
        P(("grp", "blk"), None, None),
    )
    return jax.shard_map(
        body,
        mesh=mesh,
        in_specs=placed,
        out_specs=(P(("grp", "blk")), P(("grp", "blk"))),
        check_vma=False,
    )
```

```python
import functools

import jax
import jax.numpy as jnp
from jax import lax
from jax.experimental import pallas as pl
from jax.experimental.pallas import tpu as pltpu
from jax.sharding import PartitionSpec as P

EPSILON = 1e-06
F32 = jnp.float32
BF16 = jnp.bfloat16

CHIPS = 64
ROWS = 512
WIDTH = 768
CLUSTERS = 128
GROUPS = 16
CAP = 64
BASE = 16
HALF = WIDTH // 2
LINES = 16
DEPTH = 4
POOL = 8
PARTS = ((0, 40, 400), (40, 32, 256))
TOTAL = 72
HELD = 656
STARTS = (0, 400)
LAST = len(PARTS) - 1
NONE = 1e30


def normalize(values):
    widened = values.astype(F32)
    return widened * lax.rsqrt(jnp.sum(widened * widened, axis=1, keepdims=True) + EPSILON)


def general(embeddings, assign, owner, send_count, send_index):
    rows_local = embeddings.shape[0]
    feature_width = embeddings.shape[1]
    groups = lax.axis_size("grp")
    clusters = owner.shape[0]
    capacity = send_index.shape[2]
    slot_total = groups * capacity
    unit_rows = normalize(embeddings)
    unit_low = unit_rows.astype(BF16)
    counts = send_count[0]
    listed = send_index[0]
    live_slot = jnp.arange(capacity, dtype=jnp.int32)[None, :] < counts[:, None]
    listed_cluster = assign[listed]
    owned_here = owner[listed_cluster] == jnp.arange(groups, dtype=jnp.int32)[:, None]
    kept_slot = live_slot & owned_here
    out_cluster = jnp.where(kept_slot, listed_cluster, -1)
    out_tag = jnp.where(kept_slot, lax.axis_index(("grp", "blk")) * rows_local + listed, -1)
    out_vector = unit_low[listed.reshape(-1)].reshape(groups, capacity, feature_width)
    got_vector, got_cluster, got_tag = (
        lax.all_to_all(out_vector, "grp", split_axis=0, concat_axis=0, tiled=True),
        lax.all_to_all(out_cluster, "grp", split_axis=0, concat_axis=0, tiled=True),
        lax.all_to_all(out_tag, "grp", split_axis=0, concat_axis=0, tiled=True),
    )
    own_vector = got_vector.reshape(slot_total, feature_width)
    own_cluster = got_cluster.reshape(slot_total)
    own_tag = got_tag.reshape(slot_total)

    def tile_best(current, shard_piece):
        other_vector, other_cluster, other_tag = shard_piece
        scores = jnp.einsum("id,jd->ij", own_vector, other_vector, preferred_element_type=F32)
        matched = (
            (own_cluster[:, None] == other_cluster[None, :])
            & (other_cluster[None, :] >= 0)
            & (own_tag[:, None] != other_tag[None, :])
        )
        return jnp.maximum(current, jnp.max(jnp.where(matched, scores, -1.0), axis=1))

    other_vector = lax.all_gather(own_vector, "blk", axis=0, tiled=True)
    other_cluster = lax.all_gather(own_cluster, "blk", axis=0, tiled=True)
    other_tag = lax.all_gather(own_tag, "blk", axis=0, tiled=True)
    length = other_vector.shape[0]
    number = length // slot_total
    stacked = (
        other_vector.reshape(number, slot_total, feature_width),
        other_cluster.reshape(number, slot_total),
        other_tag.reshape(number, slot_total),
    )

    def scan_step(carry, single):
        return (tile_best(carry, single), None)

    result, unused = lax.scan(scan_step, jnp.full((slot_total,), -1.0, F32), stacked)
    target = jnp.where(live_slot, listed, rows_local).reshape(-1)
    partial_sum = jax.ops.segment_sum(unit_rows, assign, num_segments=clusters)
    centre = normalize(lax.psum(partial_sum, ("grp", "blk")))
    nearness = jnp.sum(unit_low.astype(F32) * centre[assign], axis=1)
    returned = lax.all_to_all(
        result.reshape(groups, capacity), "grp", split_axis=0, concat_axis=0, tiled=True
    )
    has_entry = (
        jnp.zeros((rows_local,), jnp.int32)
        .at[target]
        .max(kept_slot.astype(jnp.int32).reshape(-1), mode="drop")
    )
    centroid_cos = jnp.where(has_entry > 0, nearness, 0.0)
    max_sim = jnp.full((rows_local,), -1.0, F32).at[target].max(returned.reshape(-1), mode="drop")
    return (max_sim, centroid_cos)


def iota(shape, axis):
    return lax.broadcasted_iota(jnp.int32, shape, axis)


def down(values):
    return jnp.sum(values, axis=0, keepdims=True)


def across(values):
    return jnp.sum(values, axis=1, keepdims=True)


def pick(mask, values):
    return jnp.where(mask, values, 0.0)


def as_column(row):
    size = row.shape[1]
    return across(pick(iota((size, size), 0) == iota((size, size), 1), row))


def as_row(column):
    size = column.shape[0]
    return down(pick(iota((size, size), 0) == iota((size, size), 1), column))


def dot(a, b):
    return jnp.dot(a, b, preferred_element_type=F32)


def dot_rows(a, b):
    return lax.dot_general(a, b, (((1,), (1,)), ((), ())), preferred_element_type=F32)


def onehot(mask):
    return jnp.where(mask, 1.0, 0.0).astype(BF16)


def halves(values):
    first = values.astype(BF16).astype(F32)
    return first, (values - first).astype(BF16).astype(F32)


def rank_groups(count_ref):
    count_row = count_ref[...].astype(F32)
    count_column = as_column(count_row)
    sub, lane = iota((GROUPS, 128), 0), iota((GROUPS, 128), 1)
    count_lanes = down(pick(sub == lane, count_column))
    ahead = (count_column > count_lanes) | ((count_column == count_lanes) & (sub < lane))
    rank = down(jnp.where(ahead, 1.0, 0.0))
    return jnp.where(iota((1, 128), 1) < GROUPS, rank, 0.0), count_column


def place_documents(assign_ref, owner_ref, rank, earlier_ref, chip_step):
    member = iota((CLUSTERS, ROWS), 0) == assign_ref[...]
    member_low = onehot(member)
    before = down(pick(member, dot(member_low, earlier_ref[...])))
    count_column = across(jnp.where(member, 1.0, 0.0))
    owner_row = owner_ref[...].astype(F32)
    owner_column = as_column(owner_row)
    sub, lane = iota((CLUSTERS, CLUSTERS), 0), iota((CLUSTERS, CLUSTERS), 1)
    within = across(jnp.where((owner_column == owner_row) & (lane < sub), 1.0, 0.0))
    group_rank = across(pick(owner_column == lane.astype(F32), rank))
    place = group_rank * (CLUSTERS // GROUPS) + within
    chip = jnp.minimum(place, (CLUSTERS - 1) - place)
    count_row, place_row, chip_row = as_row(count_column), as_row(place), as_row(chip)
    opposite = down(pick((CLUSTERS - 1) - place == place_row, count_column))
    offset = jnp.where(place_row >= CHIPS, opposite, 0.0)
    step_row = down(pick(sub.astype(F32) == chip_row, as_column(chip_step)))
    row = iota((16, CLUSTERS), 0)
    told = pick(row == 0, owner_row) + pick(row == 1, chip_row) + pick(row == 2, step_row) + pick(row == 3, offset)
    told = dot(told.astype(BF16), member_low)
    place_counts = down(pick(place == lane.astype(F32), count_column))
    whole = told[1:4].astype(jnp.int32)
    return told[0:1], whole[0:1], whole[1:2], before.astype(jnp.int32) + whole[2:3], place_counts


def missing_documents(index_ref, count_column, group):
    listed = index_ref[...]
    live = iota((GROUPS, CAP), 1).astype(F32) < count_column
    eye = onehot(iota((CAP, CAP), 0) == iota((CAP, CAP), 1))
    high = dot_rows(eye, jnp.where(live, listed >> 4, 0).astype(F32).astype(BF16))
    low = dot_rows(eye, jnp.where(live, listed & 15, 0).astype(F32).astype(BF16))
    alive = dot_rows(eye, onehot(live))
    slots = jnp.where(alive > 0.5, high * 16.0 + low, -1.0)
    document = iota((1, ROWS), 1).astype(F32)
    lane = iota((CAP, GROUPS), 1)

    def count(g, hits):
        column = across(pick(lane == g, slots))
        wanted = jnp.where(group == g.astype(F32), document, -2.0)
        return hits + jnp.where(column == wanted, 1.0, 0.0)

    hits = lax.fori_loop(0, GROUPS, count, jnp.zeros((CAP, ROWS), F32))
    return across(jnp.where(down(hits) > 0.5, 0.0, 1.0))


def send_order():
    order = []
    for step in range(CHIPS):
        high, middle, low = step // 16, (step // 4) % 4, step % 4
        order.append((low, (middle + low) % 4, (high + middle + low) % 4))
    near = [shift for shift in order if sum(min(d, 4 - d) for d in shift) <= 1] + [(2, 0, 0)]
    near.sort(key=lambda shift: -sum(min(d, 4 - d) for d in shift))
    return [shift for shift in order if shift not in near] + near


ORDER = send_order()
SELF = CHIPS - 1


def step_to(dx, dy, dz):
    shift = (dx & 3) * 16 + (dy & 3) * 4 + (dz & 3)
    step = jnp.full(shift.shape, SELF, jnp.int32)
    for number, (x, y, z) in enumerate(ORDER[:SELF]):
        step = jnp.where(shift == x * 16 + y * 4 + z, number, step)
    return step


def in_part(step, part):
    begin, steps, _ = PARTS[part]
    return (step >= begin) & (step < begin + steps)


def chip_places():
    sub, lane = iota((CLUSTERS, CLUSTERS), 0), iota((CLUSTERS, CLUSTERS), 1)
    return onehot((sub == lane) | (sub == (CLUSTERS - 1) - lane))


def excess(totals):
    lane = iota(totals.shape, 1)
    return jnp.where(lane < CHIPS, jnp.maximum(totals - BASE, 0.0), 0.0)


def receive_plan(counts, ranks, rank, my_x, my_y, my_z, routes_ref):
    chip = my_x * 16 + my_y * 4 + my_z
    differ = jnp.where(ranks != rank, 1.0, 0.0)
    fault = across(down(differ))
    both = dot(counts.astype(BF16), chip_places())
    over = excess(both)
    lanes = iota((CHIPS, CLUSTERS), 1)
    sender = iota((CHIPS, 1), 0)
    source, target = iota((CHIPS, CHIPS), 0), iota((CHIPS, CHIPS), 1)

    same_line = (source >> 2) == (target >> 2)
    over_total = across(over)
    over_row = as_row(over_total)
    line_start = across(pick(same_line & (target < source), over_row))
    line_total = across(pick(same_line, over_row))
    fault = fault + down(jnp.where(line_total > POOL, 1.0, 0.0))
    start = line_start + across(pick(lanes < chip, over))
    number = across(pick(lanes == chip, over))

    route = routes_ref[...]
    based = jnp.where(lanes < CHIPS, jnp.minimum(both, float(BASE)), 0.0)
    for part, (_, _, room) in enumerate(PARTS):
        held = down(pick(in_part(route, part), based))
        if part == LAST:
            held = held + down(over)
        fault = fault + across(jnp.where(held > room, 1.0, 0.0))

    first = across(pick(lanes == chip, counts))
    second = across(pick(lanes == (CLUSTERS - 1) - chip, counts))
    place = (lanes & (POOL - 1)).astype(F32) - start
    mine = ((sender >> 2) == (lanes >> 3)) & (place >= 0.0) & (place < number)
    over_first = down(jnp.where(mine & (place + BASE < first), 1.0, 0.0))
    over_second = down(jnp.where(mine & (place + BASE >= first), 1.0, 0.0))
    over_first_total, over_second_total = across(over_first), across(over_second)
    earlier = onehot(iota((CLUSTERS, CLUSTERS), 0) < iota((CLUSTERS, CLUSTERS), 1))
    sub = iota((16, CLUSTERS), 0)
    before = dot((pick(sub == 0, over_first) + pick(sub == 1, over_second)).astype(BF16), earlier)

    base_first = jnp.minimum(first, float(BASE))
    base_second = jnp.minimum(first + second, float(BASE)) - base_first
    first_row, second_row = as_row(base_first), as_row(base_second)

    step_column = across(jnp.where(lanes == chip, route.astype(F32), 0.0)).astype(jnp.int32)
    step_row = as_row(step_column.astype(F32)).astype(jnp.int32)
    plans = []
    ends = []
    for part, (begin, steps, _) in enumerate(PARTS):
        inside = in_part(step_column, part)
        ahead = (target < source) & in_part(step_row, part)
        first_total = down(pick(inside, base_first))
        second_total = down(pick(inside, base_second))
        last = part == LAST
        first_end = first_total + over_first_total if last else first_total
        first_start = across(pick(ahead, first_row))
        second_start = across(pick(ahead, second_row)) + first_end
        spread = step_column - begin == (iota((CHIPS, steps * BASE), 1) >> 4)
        head, tail, head_start, tail_start = [
            down(pick(spread, column)) for column in (base_first, base_second, first_start, second_start)
        ]
        slot = (iota((1, steps * BASE), 1) & (BASE - 1)).astype(F32)
        later = jnp.where(slot < head + tail, tail_start + (slot - head), -1.0)
        plan = jnp.where(slot < head, head_start + slot, later)
        held_end = first_end + second_total
        if last:
            over_row_of = jnp.where(over_second > 0.5, held_end + before[1:2], -1.0)
            over_row_of = jnp.where(over_first > 0.5, first_total + before[0:1], over_row_of)
            plan = jnp.concatenate([plan[:, : steps * BASE - CLUSTERS], over_row_of], axis=1)
            held_end = held_end + over_second_total
        plans.append(plan)
        ends.append((first_end, held_end))
    return plans, ends, fault


def kernel(
    x_hbm, assign_hbm, owner_hbm, count_hbm, index_hbm,
    out_ref, fault_ref,
    x_ref, assign_ref, owner_ref, count_ref, index_ref,
    send, got, own_over, line_over, send_over, got_over, pick_0, pick_1,
    earlier_ref, routes_ref, keys, facts, sums, their_sums, back, returned,
    load_sem, send_sem, recv_sem,
):
    grp, blk = lax.axis_index("grp"), lax.axis_index("blk")
    my_x, my_y, my_z, core = grp // 4, grp % 4, blk // 2, blk % 2
    my_chip = grp * 4 + my_z
    picks = (pick_0, pick_1)
    along_x = [((my_x + d) % 4) * 4 for d in range(4)]
    along_y = [(my_y + d) % 4 for d in range(4)]
    along_z = [((my_z + d) % 4) * 2 + core for d in range(4)]
    other_core = {"grp": grp, "blk": my_z * 2 + (1 - core)}

    def device_at(step, sign):
        dx, dy, dz = [(sign * d) % 4 for d in ORDER[step]]
        return {"grp": along_x[dx] + along_y[dy], "blk": along_z[dz]}

    def remote(source, target, number, device):
        return pltpu.make_async_remote_copy(
            src_ref=source,
            dst_ref=target,
            send_sem=send_sem.at[number],
            recv_sem=recv_sem.at[number],
            device_id=device,
            device_id_type=pl.DeviceIdType.MESH,
        )

    def await_blocks(ref, number, semaphore):
        block = ref.at[pl.ds(0, number)]
        pltpu.make_async_copy(block, block, semaphore).wait()

    LINE, OVER, FACTS, SUMS, BACK, SWAP, PART = 0, 1, 2, 3, 4, 6, 8
    messages = [min(begin + steps, SELF) - begin for begin, steps, _ in PARTS]

    loads = [
        pltpu.make_async_copy(source, target, load_sem.at[number])
        for number, (source, target) in enumerate(
            (
                (assign_hbm, assign_ref),
                (owner_hbm, owner_ref),
                (count_hbm, count_ref),
                (index_hbm, index_ref),
                (x_hbm, x_ref),
            )
        )
    ]
    for load in loads:
        load.start()
    barrier = pltpu.get_barrier_semaphore()
    for device in [device_at(step, 1) for step in range(SELF)] + [other_core]:
        pl.semaphore_signal(barrier, inc=1, device_id=device, device_id_type=pl.DeviceIdType.MESH)
    lane = iota((1, CLUSTERS), 1)
    chip_step = step_to((lane >> 4) - my_x, ((lane >> 2) & 3) - my_y, (lane & 3) - my_z).astype(F32)
    earlier_ref[...] = onehot(iota((ROWS, ROWS), 0) < iota((ROWS, ROWS), 1))
    for load in loads[:-1]:
        load.wait()

    rank, count_column = rank_groups(count_ref)
    group, chip, step_of, slot, place_counts = place_documents(assign_ref, owner_ref, rank, earlier_ref, chip_step)
    in_base = slot < BASE
    send_slot = jnp.where(in_base, step_of * BASE + slot, -1)
    loads[-1].wait()

    def pack(first, stop):
        slots = iota(((stop - first) * BASE, ROWS), 0) + first * BASE
        rows = dot(onehot(slots == send_slot), x_ref[...]).astype(BF16)
        send[pl.ds(first, stop - first)] = rows.reshape(stop - first, BASE, WIDTH)

    def post(first, stop):
        for step in range(first, min(stop, SELF)):
            number = max(part for part in range(len(PARTS)) if PARTS[part][0] <= step)
            remote(send.at[step], got.at[step], PART + number, device_at(step, 1)).start()

    pack(0, 8)
    pl.semaphore_wait(barrier, CHIPS)
    post(0, 8)
    place_counts_16 = place_counts + jnp.zeros((16, CLUSTERS), F32)
    own_excess = excess(dot(place_counts_16.astype(BF16), chip_places())[0:1])
    eye = iota((CHIPS, CLUSTERS), 0) == iota((CHIPS, CLUSTERS), 1)
    excess_column = across(pick(eye, own_excess))
    over_slot = down(pick(iota((CHIPS, ROWS), 0) < chip, excess_column)).astype(jnp.int32) + (slot - BASE)
    over_slot = jnp.where(in_base, -1, over_slot)
    row = iota((BASE, CLUSTERS), 0)
    own_over[:, :WIDTH] = dot(onehot(iota((BASE, ROWS), 0) == over_slot), x_ref[...]).astype(BF16)
    own_over[:, WIDTH:] = (pick(row == 0, place_counts) + pick(row == 1, rank)).astype(BF16)
    line_over[my_z] = own_over[...]
    for d in range(1, DEPTH):
        remote(own_over, line_over.at[my_z], LINE, {"grp": grp, "blk": along_z[d]}).start()
    pack(8, 24)
    post(8, 24)
    pack(24, 48)
    to_chip, sender = iota((CHIPS, CLUSTERS), 1), iota((CHIPS, CLUSTERS), 0)
    routes_ref[...] = step_to(
        (to_chip >> 4) - (sender >> 4), ((to_chip >> 2) & 3) - ((sender >> 2) & 3), (to_chip & 3) - (sender & 3)
    )

    await_blocks(line_over, DEPTH - 1, recv_sem.at[LINE])
    line_counts = [line_over[d, 0:1, WIDTH:].astype(F32) for d in range(DEPTH)]
    line_ranks = [line_over[d, 1:2, WIDTH:].astype(F32) for d in range(DEPTH)]
    row = iota((2 * POOL, CLUSTERS), 0)
    told = jnp.zeros((2 * POOL, CLUSTERS), F32)
    for d in range(DEPTH):
        told = told + pick(row == d, line_counts[d]) + pick(row == DEPTH + d, line_ranks[d])
    told = told.astype(BF16)
    line_total = across(excess(dot(told, chip_places())))[0:DEPTH]
    depth = iota((DEPTH, 1), 0)
    line_start = jnp.zeros((DEPTH, 1), F32)
    for d in range(DEPTH - 1):
        line_start = line_start + pick(depth > d, line_total[d : d + 1])
    my_start = down(pick(depth == my_z, line_start))
    at = depth == (iota((DEPTH, DEPTH * BASE), 1) >> 4)
    begin = down(pick(at, line_start))
    number = down(pick(at, line_total))
    order = (iota((1, DEPTH * BASE), 1) & (BASE - 1)).astype(F32)
    order = jnp.where(order < number, begin + order, -1.0)
    rows = iota((2 * POOL, DEPTH * BASE), 0).astype(F32)
    blocks = line_over[:, :, :WIDTH].reshape(DEPTH * BASE, WIDTH)
    left = dot(onehot((rows == order) & (rows < POOL)), blocks[:, :HALF])
    right = dot(onehot((rows - POOL == order) & (rows >= POOL)), blocks[:, HALF:])
    send_over[:, :HALF] = (left + right).astype(BF16)
    send_over[:, HALF:] = told
    got_over[grp] = send_over[...]
    for step in range(1, LINES):
        low, middle = step % 4, step // 4
        device = {"grp": along_x[low] + along_y[(middle + low) % 4], "blk": blk}
        remote(send_over, got_over.at[grp], OVER, device).start()
    post(24, 48)
    pack(48, CHIPS)
    post(48, CHIPS)
    got[SELF] = send[SELF]
    missing = missing_documents(index_ref, count_column, group)

    await_blocks(got_over, LINES - 1, recv_sem.at[OVER])
    told = got_over[:, :, HALF:].astype(F32)
    counts = told[:, 0:DEPTH].reshape(CHIPS, CLUSTERS)
    ranks = told[:, DEPTH : 2 * DEPTH].reshape(CHIPS, CLUSTERS)
    plans, ends, fault = receive_plan(counts, ranks, rank, my_x, my_y, my_z, routes_ref)

    row = iota((8, 128), 0)
    told = pick(row == 6, rank) + pick(row == 7, jnp.where(iota((1, 128), 1) == 0, fault, missing))
    for part, (first_end, held_end) in enumerate(ends):
        told = told + pick(row == part, first_end) + pick(row == 2 + part, held_end)
        picks[part][...] = onehot(iota(picks[part].shape, 0).astype(F32) == plans[part])
    facts[0] = told
    swap_facts = remote(facts.at[0], facts.at[1], FACTS, other_core)
    swap_facts.start()

    best = [jnp.full((1, room), -1.0, F32) for _, _, room in PARTS]
    key_kinds = []
    query_kinds = []
    totals = [jnp.zeros((1, WIDTH), F32), jnp.zeros((1, WIDTH), F32)]
    swaps = []

    def add_kinds(first, held, room):
        number = iota((room, 1), 0).astype(F32)
        key_kinds.append(jnp.where(number < first, 0.0, jnp.where(number < held, 1.0, 2.0)))

    for (first_end, held_end), (_, _, room) in zip(ends, PARTS):
        add_kinds(first_end, held_end, room)
        query_kinds.append(jnp.where(iota((1, room), 1).astype(F32) < first_end, 0.0, 1.0))

    def compare(first_key, last_key, part, more=0):
        borders = (*STARTS, *(HELD + start for start in STARTS), 2 * HELD)
        begin, stop = borders[first_key], borders[last_key + 1]
        start, room = STARTS[part], PARTS[part][2]
        scores = dot_rows(keys[begin : stop + more], keys[start : start + room])
        rest, scores = scores[stop - begin :], scores[: stop - begin]
        kind = jnp.concatenate(key_kinds[first_key : last_key + 1], axis=0)
        matched = kind == query_kinds[part]
        if begin < start + room and start < stop:
            matched = matched & (iota(kind.shape, 0) + (begin - start) != iota((1, room), 1))
        best[part] = jnp.maximum(best[part], jnp.max(jnp.where(matched, scores, -1.0), axis=0, keepdims=True))
        return rest

    def arrive(part):
        begin, steps, room = PARTS[part]
        await_blocks(got, messages[part], recv_sem.at[PART + part])
        rows = dot(picks[part][...], got[pl.ds(begin, steps)].reshape(steps * BASE, WIDTH))
        unit = rows * lax.rsqrt(across(rows * rows) + EPSILON)
        keys[pl.ds(STARTS[part], room)] = unit.astype(BF16)
        swap = remote(
            keys.at[pl.ds(STARTS[part], room)], keys.at[pl.ds(HELD + STARTS[part], room)], SWAP + part, other_core
        )
        swap.start()
        swaps.append(swap)
        is_first = iota((room, 1), 0).astype(F32) < ends[part][0]
        totals[0] = totals[0] + down(pick(is_first, unit))
        totals[1] = totals[1] + down(jnp.where(is_first, 0.0, unit))

    arrive(0)
    compare(0, 0, 0)
    swap_facts.wait()
    their_told = facts[1]
    for part, (_, _, room) in enumerate(PARTS):
        add_kinds(their_told[part : part + 1, 0:1], their_told[2 + part : 3 + part, 0:1], room)
    half_rows = got_over[:, :, :HALF].reshape(LINES * 2 * POOL, HALF)
    shape = (LINES * POOL, LINES * 2 * POOL)
    to, at = iota(shape, 0), iota(shape, 1)
    same = ((to >> 3) == (at >> 4)) & ((to & 7) == (at & 7))
    left = dot(onehot(same & ((at & POOL) == 0)), half_rows)
    right = dot(onehot(same & ((at & POOL) != 0)), half_rows)
    whole = jnp.concatenate([left, right], axis=1).astype(BF16)
    got[pl.ds(CHIPS, TOTAL - CHIPS)] = whole.reshape(TOTAL - CHIPS, BASE, WIDTH)
    swaps[0].wait()
    compare(2, 2, 0)

    arrive(1)
    row = iota((8, WIDTH), 0)
    sums[...] = pick(row == 0, totals[0]) + pick(row == 1, totals[1])
    swap_sums = remote(sums, their_sums, SUMS, other_core)
    swap_sums.start()
    compare(0, 2, 1)
    compare(1, 1, 0)

    swap_sums.wait()
    total = sums[...] + their_sums[...]
    keys[pl.ds(2 * HELD, 16)] = jnp.concatenate(halves(total), axis=0).astype(BF16)
    scale = lax.rsqrt(across(total * total) + EPSILON)
    swaps[1].wait()

    poison = missing + their_told[7:8, 1:2] > 0.5
    tiles = CHIPS * BASE // 128
    for part in (1, 0):
        begin, steps, room = PARTS[part]
        near = compare(3, 3, part, 16)
        near = (near[0:8] + near[8:16]) * scale
        row = iota((8, room), 0)
        query_number = iota((1, room), 1).astype(F32)
        some = jnp.where(query_number < ends[part][0], near[0:1], near[1:2])
        values = jnp.zeros((8, room), F32)
        for number, term in enumerate(halves(best[part]) + halves(some)):
            values = jnp.where(row == number, term, values)
        out = dot(values.astype(BF16), picks[part][...])
        for kind in range(2):
            line = out[2 * kind : 2 * kind + 1] + out[2 * kind + 1 : 2 * kind + 2]
            line = jnp.where(poison, NONE, line)
            for tile in range(steps * BASE // 128):
                piece = line[:, tile * 128 : (tile + 1) * 128]
                to = begin * BASE // 128 + tile
                if to < tiles:
                    back[to, kind : kind + 1, :] = piece
                else:
                    for each in range(tiles):
                        back[each, 2 + kind : 3 + kind, :] = piece
        for step in range(begin, min(begin + steps, SELF)):
            remote(back.at[step // 8], returned.at[step], BACK + part, device_at(step, -1)).start()
    returned[SELF] = back[SELF // 8]

    differ = across(jnp.where(their_told[6:7] != rank, 1.0, 0.0))
    fault = fault + their_told[7:8, 0:1] + differ
    chosen = onehot(iota((CHIPS, ROWS), 0) == step_of)
    sub = iota((128, ROWS), 0)
    at_base = (sub == (step_of & 7) * BASE + slot) & in_base
    at_over = (sub == grp * POOL + my_start.astype(jnp.int32) + over_slot) & (~in_base)

    found = [jnp.zeros((128, ROWS), F32) for _ in range(4)]
    poisoned = jnp.zeros((1, 1), F32)
    for part in (1, 0):
        begin, steps, _ = PARTS[part]
        stop = min(begin + steps, CHIPS)
        await_blocks(returned, messages[part], recv_sem.at[BACK + part])
        for number in range(4):
            line = returned[begin:stop, number, :]
            if number == 0:
                poisoned = poisoned + across(down(jnp.where(line > 0.5 * NONE, 1.0, 0.0)))
            terms = jnp.concatenate(halves(line), axis=1).astype(BF16)
            out = lax.dot_general(terms, chosen[begin:stop], (((0,), (0,)), ((), ())), preferred_element_type=F32)
            found[number] = found[number] + (out[0:128] + out[128:256])
    fault_ref[...] = jnp.where(fault + poisoned > 0.5, 1, 0) + jnp.zeros((1, 128), jnp.int32)
    out_ref[0:1] = down(pick(at_base, found[0]) + pick(at_over, found[2]))
    out_ref[1:2] = down(pick(at_base, found[1]) + pick(at_over, found[3]))

    await_blocks(line_over, DEPTH - 1, send_sem.at[LINE])
    await_blocks(got_over, LINES - 1, send_sem.at[OVER])
    for part in range(len(PARTS)):
        await_blocks(returned, messages[part], send_sem.at[BACK + part])
    for part in range(len(PARTS)):
        await_blocks(got, messages[part], send_sem.at[PART + part])


def routed(embeddings, assign, owner, send_count, send_index):
    return pl.pallas_call(
        kernel,
        out_shape=(
            jax.ShapeDtypeStruct((2, ROWS), F32),
            jax.ShapeDtypeStruct((1, 128), jnp.int32),
        ),
        in_specs=[pl.BlockSpec(memory_space=pl.ANY)] * 5,
        out_specs=(pl.BlockSpec(memory_space=pltpu.VMEM),) * 2,
        scratch_shapes=[
            pltpu.VMEM((ROWS, WIDTH), BF16),
            pltpu.VMEM((1, ROWS), jnp.int32),
            pltpu.VMEM((1, CLUSTERS), jnp.int32),
            pltpu.VMEM((1, GROUPS), jnp.int32),
            pltpu.VMEM((GROUPS, CAP), jnp.int32),
            pltpu.VMEM((CHIPS, BASE, WIDTH), BF16),
            pltpu.VMEM((TOTAL, BASE, WIDTH), BF16),
            pltpu.VMEM((BASE, WIDTH + CLUSTERS), BF16),
            pltpu.VMEM((DEPTH, BASE, WIDTH + CLUSTERS), BF16),
            pltpu.VMEM((2 * POOL, HALF + CLUSTERS), BF16),
            pltpu.VMEM((LINES, 2 * POOL, HALF + CLUSTERS), BF16),
            *[pltpu.VMEM((room, steps * BASE), BF16) for _, steps, room in PARTS],
            pltpu.VMEM((ROWS, ROWS), BF16),
            pltpu.VMEM((CHIPS, CLUSTERS), jnp.int32),
            pltpu.VMEM((2 * HELD + 16, WIDTH), BF16),
            pltpu.VMEM((2, 8, 128), F32),
            pltpu.VMEM((8, WIDTH), F32),
            pltpu.VMEM((8, WIDTH), F32),
            pltpu.VMEM((CHIPS * BASE // 128, 4, 128), F32),
            pltpu.VMEM((CHIPS, 4, 128), F32),
            pltpu.SemaphoreType.DMA((5,)),
            pltpu.SemaphoreType.DMA((10,)),
            pltpu.SemaphoreType.DMA((10,)),
        ],
        compiler_params=pltpu.CompilerParams(
            collective_id=0, has_side_effects=True, vmem_limit_bytes=48 * 1024 * 1024
        ),
    )(
        embeddings,
        assign.reshape(1, ROWS),
        owner.reshape(1, CLUSTERS),
        send_count,
        send_index[0],
    )


def body(embeddings, assign, owner, send_count, send_index):
    arguments = (embeddings, assign, owner, send_count, send_index)
    results, fault = routed(*arguments)
    results = lax.cond(fault[0, 0] != 0, lambda: jnp.stack(general(*arguments)), lambda: results)
    return results[0], results[1]


def solution(mesh):
    placed = (
        P(("grp", "blk"), None),
        P(("grp", "blk")),
        P(),
        P(("grp", "blk"), None),
        P(("grp", "blk"), None, None),
    )
    return jax.shard_map(
        body,
        mesh=mesh,
        in_specs=placed,
        out_specs=(P(("grp", "blk")), P(("grp", "blk"))),
        check_vma=False,
    )
```

```python
import functools

import jax
import jax.numpy as jnp
from jax import lax
from jax.experimental import pallas as pl
from jax.experimental.pallas import tpu as pltpu
from jax.sharding import PartitionSpec as P

EPSILON = 1e-06
F32 = jnp.float32
BF16 = jnp.bfloat16

CHIPS = 64
ROWS = 512
WIDTH = 768
CLUSTERS = 128
GROUPS = 16
CAP = 64
BASE = 16
HALF = WIDTH // 2
LINES = 16
DEPTH = 4
POOL = 8
PARTS = ((0, 40, 400), (40, 32, 256))
TOTAL = 72
HELD = 656
STARTS = (0, 400)
LAST = len(PARTS) - 1
NONE = 1e30


def normalize(values):
    widened = values.astype(F32)
    return widened * lax.rsqrt(jnp.sum(widened * widened, axis=1, keepdims=True) + EPSILON)


def general(embeddings, assign, owner, send_count, send_index):
    rows_local = embeddings.shape[0]
    feature_width = embeddings.shape[1]
    groups = lax.axis_size("grp")
    clusters = owner.shape[0]
    capacity = send_index.shape[2]
    slot_total = groups * capacity
    unit_rows = normalize(embeddings)
    unit_low = unit_rows.astype(BF16)
    counts = send_count[0]
    listed = send_index[0]
    live_slot = jnp.arange(capacity, dtype=jnp.int32)[None, :] < counts[:, None]
    listed_cluster = assign[listed]
    owned_here = owner[listed_cluster] == jnp.arange(groups, dtype=jnp.int32)[:, None]
    kept_slot = live_slot & owned_here
    out_cluster = jnp.where(kept_slot, listed_cluster, -1)
    out_tag = jnp.where(kept_slot, lax.axis_index(("grp", "blk")) * rows_local + listed, -1)
    out_vector = unit_low[listed.reshape(-1)].reshape(groups, capacity, feature_width)
    got_vector, got_cluster, got_tag = (
        lax.all_to_all(out_vector, "grp", split_axis=0, concat_axis=0, tiled=True),
        lax.all_to_all(out_cluster, "grp", split_axis=0, concat_axis=0, tiled=True),
        lax.all_to_all(out_tag, "grp", split_axis=0, concat_axis=0, tiled=True),
    )
    own_vector = got_vector.reshape(slot_total, feature_width)
    own_cluster = got_cluster.reshape(slot_total)
    own_tag = got_tag.reshape(slot_total)

    def tile_best(current, shard_piece):
        other_vector, other_cluster, other_tag = shard_piece
        scores = jnp.einsum("id,jd->ij", own_vector, other_vector, preferred_element_type=F32)
        matched = (
            (own_cluster[:, None] == other_cluster[None, :])
            & (other_cluster[None, :] >= 0)
            & (own_tag[:, None] != other_tag[None, :])
        )
        return jnp.maximum(current, jnp.max(jnp.where(matched, scores, -1.0), axis=1))

    other_vector = lax.all_gather(own_vector, "blk", axis=0, tiled=True)
    other_cluster = lax.all_gather(own_cluster, "blk", axis=0, tiled=True)
    other_tag = lax.all_gather(own_tag, "blk", axis=0, tiled=True)
    length = other_vector.shape[0]
    number = length // slot_total
    stacked = (
        other_vector.reshape(number, slot_total, feature_width),
        other_cluster.reshape(number, slot_total),
        other_tag.reshape(number, slot_total),
    )

    def scan_step(carry, single):
        return (tile_best(carry, single), None)

    result, unused = lax.scan(scan_step, jnp.full((slot_total,), -1.0, F32), stacked)
    target = jnp.where(live_slot, listed, rows_local).reshape(-1)
    partial_sum = jax.ops.segment_sum(unit_rows, assign, num_segments=clusters)
    centre = normalize(lax.psum(partial_sum, ("grp", "blk")))
    nearness = jnp.sum(unit_low.astype(F32) * centre[assign], axis=1)
    returned = lax.all_to_all(
        result.reshape(groups, capacity), "grp", split_axis=0, concat_axis=0, tiled=True
    )
    has_entry = (
        jnp.zeros((rows_local,), jnp.int32)
        .at[target]
        .max(kept_slot.astype(jnp.int32).reshape(-1), mode="drop")
    )
    centroid_cos = jnp.where(has_entry > 0, nearness, 0.0)
    max_sim = jnp.full((rows_local,), -1.0, F32).at[target].max(returned.reshape(-1), mode="drop")
    return (max_sim, centroid_cos)


def iota(shape, axis):
    return lax.broadcasted_iota(jnp.int32, shape, axis)


def down(values):
    return jnp.sum(values, axis=0, keepdims=True)


def across(values):
    return jnp.sum(values, axis=1, keepdims=True)


def pick(mask, values):
    return jnp.where(mask, values, 0.0)


def as_column(row):
    size = row.shape[1]
    return across(pick(iota((size, size), 0) == iota((size, size), 1), row))


def as_row(column):
    size = column.shape[0]
    return down(pick(iota((size, size), 0) == iota((size, size), 1), column))


def dot(a, b):
    return jnp.dot(a, b, preferred_element_type=F32)


def dot_rows(a, b):
    return lax.dot_general(a, b, (((1,), (1,)), ((), ())), preferred_element_type=F32)


def onehot(mask):
    return jnp.where(mask, 1.0, 0.0).astype(BF16)


def halves(values):
    first = values.astype(BF16).astype(F32)
    return first, (values - first).astype(BF16).astype(F32)


def rank_groups(count_ref):
    count_row = count_ref[...].astype(F32)
    count_column = as_column(count_row)
    sub, lane = iota((GROUPS, 128), 0), iota((GROUPS, 128), 1)
    count_lanes = down(pick(sub == lane, count_column))
    ahead = (count_column > count_lanes) | ((count_column == count_lanes) & (sub < lane))
    rank = down(jnp.where(ahead, 1.0, 0.0))
    return jnp.where(iota((1, 128), 1) < GROUPS, rank, 0.0), count_column


def place_documents(assign_ref, owner_ref, rank, earlier_ref, chip_step):
    member = iota((CLUSTERS, ROWS), 0) == assign_ref[...]
    member_low = onehot(member)
    before = down(pick(member, dot(member_low, earlier_ref[...])))
    count_column = across(jnp.where(member, 1.0, 0.0))
    owner_row = owner_ref[...].astype(F32)
    owner_column = as_column(owner_row)
    sub, lane = iota((CLUSTERS, CLUSTERS), 0), iota((CLUSTERS, CLUSTERS), 1)
    within = across(jnp.where((owner_column == owner_row) & (lane < sub), 1.0, 0.0))
    group_rank = across(pick(owner_column == lane.astype(F32), rank))
    place = group_rank * (CLUSTERS // GROUPS) + within
    chip = jnp.minimum(place, (CLUSTERS - 1) - place)
    count_row, place_row, chip_row = as_row(count_column), as_row(place), as_row(chip)
    opposite = down(pick((CLUSTERS - 1) - place == place_row, count_column))
    offset = jnp.where(place_row >= CHIPS, opposite, 0.0)
    step_row = down(pick(sub.astype(F32) == chip_row, as_column(chip_step)))
    row = iota((16, CLUSTERS), 0)
    told = pick(row == 0, owner_row) + pick(row == 1, chip_row) + pick(row == 2, step_row) + pick(row == 3, offset)
    told = dot(told.astype(BF16), member_low)
    place_counts = down(pick(place == lane.astype(F32), count_column))
    whole = told[1:4].astype(jnp.int32)
    return told[0:1], whole[0:1], whole[1:2], before.astype(jnp.int32) + whole[2:3], place_counts


def missing_documents(index_ref, count_column, group):
    listed = index_ref[...]
    live = iota((GROUPS, CAP), 1).astype(F32) < count_column
    eye = onehot(iota((CAP, CAP), 0) == iota((CAP, CAP), 1))
    high = dot_rows(eye, jnp.where(live, listed >> 4, 0).astype(F32).astype(BF16))
    low = dot_rows(eye, jnp.where(live, listed & 15, 0).astype(F32).astype(BF16))
    alive = dot_rows(eye, onehot(live))
    slots = jnp.where(alive > 0.5, high * 16.0 + low, -1.0)
    document = iota((1, ROWS), 1).astype(F32)
    lane = iota((CAP, GROUPS), 1)

    def count(g, hits):
        column = across(pick(lane == g, slots))
        wanted = jnp.where(group == g.astype(F32), document, -2.0)
        return hits + jnp.where(column == wanted, 1.0, 0.0)

    hits = lax.fori_loop(0, GROUPS, count, jnp.zeros((CAP, ROWS), F32))
    return across(jnp.where(down(hits) > 0.5, 0.0, 1.0))


def send_order():
    order = []
    for step in range(CHIPS):
        high, middle, low = step // 16, (step // 4) % 4, step % 4
        order.append((low, (middle + low) % 4, (high + middle + low) % 4))
    near = [shift for shift in order if sum(min(d, 4 - d) for d in shift) <= 1] + [(2, 0, 0)]
    near.sort(key=lambda shift: -sum(min(d, 4 - d) for d in shift))
    return [shift for shift in order if shift not in near] + near


ORDER = send_order()
SELF = CHIPS - 1


def step_to(dx, dy, dz):
    shift = (dx & 3) * 16 + (dy & 3) * 4 + (dz & 3)
    step = jnp.full(shift.shape, SELF, jnp.int32)
    for number, (x, y, z) in enumerate(ORDER[:SELF]):
        step = jnp.where(shift == x * 16 + y * 4 + z, number, step)
    return step


def in_part(step, part):
    begin, steps, _ = PARTS[part]
    return (step >= begin) & (step < begin + steps)


def chip_places():
    sub, lane = iota((CLUSTERS, CLUSTERS), 0), iota((CLUSTERS, CLUSTERS), 1)
    return onehot((sub == lane) | (sub == (CLUSTERS - 1) - lane))


def excess(totals):
    lane = iota(totals.shape, 1)
    return jnp.where(lane < CHIPS, jnp.maximum(totals - BASE, 0.0), 0.0)


def receive_plan(counts, ranks, rank, my_x, my_y, my_z, routes_ref):
    chip = my_x * 16 + my_y * 4 + my_z
    differ = jnp.where(ranks != rank, 1.0, 0.0)
    fault = across(down(differ))
    both = dot(counts.astype(BF16), chip_places())
    over = excess(both)
    lanes = iota((CHIPS, CLUSTERS), 1)
    sender = iota((CHIPS, 1), 0)
    source, target = iota((CHIPS, CHIPS), 0), iota((CHIPS, CHIPS), 1)

    same_line = (source >> 2) == (target >> 2)
    fault = fault + down(jnp.where(across(over) > BASE, 1.0, 0.0))
    of_line = dot(onehot(same_line), over.astype(BF16))
    fault = fault + across(down(jnp.where(of_line > POOL, 1.0, 0.0)))
    number = across(pick(lanes == chip, over))
    start = across(pick(same_line & (target < source), as_row(number)))

    route = routes_ref[...]
    based = jnp.where(lanes < CHIPS, jnp.minimum(both, float(BASE)), 0.0)
    for part, (_, _, room) in enumerate(PARTS):
        held = down(pick(in_part(route, part), based))
        if part == LAST:
            held = held + down(over)
        fault = fault + across(jnp.where(held > room, 1.0, 0.0))

    first = across(pick(lanes == chip, counts))
    second = across(pick(lanes == (CLUSTERS - 1) - chip, counts))
    place = (lanes & (POOL - 1)).astype(F32) - start
    mine = ((sender >> 2) == (lanes >> 3)) & (place >= 0.0) & (place < number)
    over_first = down(jnp.where(mine & (place + BASE < first), 1.0, 0.0))
    over_second = down(jnp.where(mine & (place + BASE >= first), 1.0, 0.0))
    over_first_total, over_second_total = across(over_first), across(over_second)
    earlier = onehot(iota((CLUSTERS, CLUSTERS), 0) < iota((CLUSTERS, CLUSTERS), 1))
    sub = iota((16, CLUSTERS), 0)
    before = dot((pick(sub == 0, over_first) + pick(sub == 1, over_second)).astype(BF16), earlier)

    base_first = jnp.minimum(first, float(BASE))
    base_second = jnp.minimum(first + second, float(BASE)) - base_first
    first_row, second_row = as_row(base_first), as_row(base_second)

    step_column = across(jnp.where(lanes == chip, route.astype(F32), 0.0)).astype(jnp.int32)
    step_row = as_row(step_column.astype(F32)).astype(jnp.int32)
    plans = []
    ends = []
    for part, (begin, steps, _) in enumerate(PARTS):
        inside = in_part(step_column, part)
        ahead = (target < source) & in_part(step_row, part)
        first_total = down(pick(inside, base_first))
        second_total = down(pick(inside, base_second))
        last = part == LAST
        first_end = first_total + over_first_total if last else first_total
        first_start = across(pick(ahead, first_row))
        second_start = across(pick(ahead, second_row)) + first_end
        spread = step_column - begin == (iota((CHIPS, steps * BASE), 1) >> 4)
        head, tail, head_start, tail_start = [
            down(pick(spread, column)) for column in (base_first, base_second, first_start, second_start)
        ]
        slot = (iota((1, steps * BASE), 1) & (BASE - 1)).astype(F32)
        later = jnp.where(slot < head + tail, tail_start + (slot - head), -1.0)
        plan = jnp.where(slot < head, head_start + slot, later)
        held_end = first_end + second_total
        if last:
            over_row_of = jnp.where(over_second > 0.5, held_end + before[1:2], -1.0)
            over_row_of = jnp.where(over_first > 0.5, first_total + before[0:1], over_row_of)
            plan = jnp.concatenate([plan[:, : steps * BASE - CLUSTERS], over_row_of], axis=1)
            held_end = held_end + over_second_total
        plans.append(plan)
        ends.append((first_end, held_end))
    return plans, ends, fault


def kernel(
    x_hbm, assign_hbm, owner_hbm, count_hbm, index_hbm,
    out_ref, fault_ref,
    x_ref, assign_ref, owner_ref, count_ref, index_ref,
    send, got, own_over, line_over, send_over, got_over, pick_0, pick_1,
    earlier_ref, routes_ref, keys, facts, sums, their_sums, back, returned,
    load_sem, send_sem, recv_sem,
):
    grp, blk = lax.axis_index("grp"), lax.axis_index("blk")
    my_x, my_y, my_z, core = grp // 4, grp % 4, blk // 2, blk % 2
    my_chip = grp * 4 + my_z
    picks = (pick_0, pick_1)
    along_x = [((my_x + d) % 4) * 4 for d in range(4)]
    along_y = [(my_y + d) % 4 for d in range(4)]
    along_z = [((my_z + d) % 4) * 2 + core for d in range(4)]
    other_core = {"grp": grp, "blk": my_z * 2 + (1 - core)}

    def device_at(step, sign):
        dx, dy, dz = [(sign * d) % 4 for d in ORDER[step]]
        return {"grp": along_x[dx] + along_y[dy], "blk": along_z[dz]}

    def remote(source, target, number, device):
        return pltpu.make_async_remote_copy(
            src_ref=source,
            dst_ref=target,
            send_sem=send_sem.at[number],
            recv_sem=recv_sem.at[number],
            device_id=device,
            device_id_type=pl.DeviceIdType.MESH,
        )

    def await_blocks(ref, number, semaphore):
        block = ref.at[pl.ds(0, number)]
        pltpu.make_async_copy(block, block, semaphore).wait()

    LINE, OVER, FACTS, SUMS, BACK, SWAP, PART = 0, 1, 2, 3, 4, 5, 7
    messages = [min(begin + steps, SELF) - begin for begin, steps, _ in PARTS]

    loads = [
        pltpu.make_async_copy(source, target, load_sem.at[number])
        for number, (source, target) in enumerate(
            (
                (assign_hbm, assign_ref),
                (owner_hbm, owner_ref),
                (count_hbm, count_ref),
                (index_hbm, index_ref),
                (x_hbm, x_ref),
            )
        )
    ]
    for load in loads:
        load.start()
    barrier = pltpu.get_barrier_semaphore()
    for device in [device_at(step, 1) for step in range(SELF)] + [other_core]:
        pl.semaphore_signal(barrier, inc=1, device_id=device, device_id_type=pl.DeviceIdType.MESH)
    lane = iota((1, CLUSTERS), 1)
    chip_step = step_to((lane >> 4) - my_x, ((lane >> 2) & 3) - my_y, (lane & 3) - my_z).astype(F32)
    earlier_ref[...] = onehot(iota((ROWS, ROWS), 0) < iota((ROWS, ROWS), 1))
    for load in loads[:-1]:
        load.wait()

    rank, count_column = rank_groups(count_ref)
    group, chip, step_of, slot, place_counts = place_documents(assign_ref, owner_ref, rank, earlier_ref, chip_step)
    in_base = slot < BASE
    send_slot = jnp.where(in_base, step_of * BASE + slot, -1)
    loads[-1].wait()

    def pack(first, stop):
        slots = iota(((stop - first) * BASE, ROWS), 0) + first * BASE
        rows = dot(onehot(slots == send_slot), x_ref[...]).astype(BF16)
        send[pl.ds(first, stop - first)] = rows.reshape(stop - first, BASE, WIDTH)

    def post(first, stop):
        for step in range(first, min(stop, SELF)):
            number = max(part for part in range(len(PARTS)) if PARTS[part][0] <= step)
            remote(send.at[step], got.at[step], PART + number, device_at(step, 1)).start()

    pack(0, 8)
    pl.semaphore_wait(barrier, CHIPS)
    post(0, 8)
    place_counts_16 = place_counts + jnp.zeros((16, CLUSTERS), F32)
    own_excess = excess(dot(place_counts_16.astype(BF16), chip_places())[0:1])
    eye = iota((CHIPS, CLUSTERS), 0) == iota((CHIPS, CLUSTERS), 1)
    excess_column = across(pick(eye, own_excess))
    over_slot = down(pick(iota((CHIPS, ROWS), 0) < chip, excess_column)).astype(jnp.int32) + (slot - BASE)
    over_slot = jnp.where(in_base, -1, over_slot)
    row = iota((BASE, CLUSTERS), 0)
    own_over[:, :WIDTH] = dot(onehot(iota((BASE, ROWS), 0) == over_slot), x_ref[...]).astype(BF16)
    own_over[:, WIDTH:] = (pick(row == 0, place_counts) + pick(row == 1, rank)).astype(BF16)
    line_over[my_z] = own_over[...]
    for d in range(1, DEPTH):
        remote(own_over, line_over.at[my_z], LINE, {"grp": grp, "blk": along_z[d]}).start()
    pack(8, 24)
    post(8, 24)
    pack(24, 48)
    to_chip, sender = iota((CHIPS, CLUSTERS), 1), iota((CHIPS, CLUSTERS), 0)
    routes_ref[...] = step_to(
        (to_chip >> 4) - (sender >> 4), ((to_chip >> 2) & 3) - ((sender >> 2) & 3), (to_chip & 3) - (sender & 3)
    )

    await_blocks(line_over, DEPTH - 1, recv_sem.at[LINE])
    line_counts = [line_over[d, 0:1, WIDTH:].astype(F32) for d in range(DEPTH)]
    line_ranks = [line_over[d, 1:2, WIDTH:].astype(F32) for d in range(DEPTH)]
    row = iota((2 * POOL, CLUSTERS), 0)
    told = jnp.zeros((2 * POOL, CLUSTERS), F32)
    for d in range(DEPTH):
        told = told + pick(row == d, line_counts[d]) + pick(row == DEPTH + d, line_ranks[d])
    told = told.astype(BF16)
    over = excess(dot(told, chip_places()))[0:DEPTH]
    ahead = dot(over.astype(BF16), onehot(iota((CLUSTERS, CLUSTERS), 0) < iota((CLUSTERS, CLUSTERS), 1)))
    before = [jnp.zeros((1, CLUSTERS), F32)]
    for d in range(DEPTH - 1):
        before.append(before[-1] + over[d : d + 1])
    before = jnp.concatenate(before, axis=0)
    before_mine = down(pick(iota((DEPTH, 1), 0) == my_z, before))
    known = jnp.concatenate([over, ahead, before, jnp.zeros((DEPTH, CLUSTERS), F32)], axis=0).astype(BF16)
    sublane = iota((LINES * 2 * POOL, 1), 0)
    way = sublane >> 4
    to_chip = ((my_x + (way >> 2)) & 3) * 16 + ((my_y + way) & 3) * 4 + my_z
    known = dot_rows(onehot(iota((LINES * 2 * POOL, CLUSTERS), 1) == to_chip), known)
    entry = iota((LINES * 2 * POOL, DEPTH * BASE), 1)

    def of_depth(kind):
        values = known[:, kind * DEPTH : kind * DEPTH + 1]
        for d in range(1, DEPTH):
            values = jnp.where((entry >> 4) == d, known[:, kind * DEPTH + d : kind * DEPTH + d + 1], values)
        return values

    offset = (entry & (BASE - 1)).astype(F32) - of_depth(1)
    position = jnp.where((offset >= 0.0) & (offset < of_depth(0)), offset + of_depth(2), -1.0)
    wanted = (sublane & (2 * POOL - 1)).astype(F32)
    blocks = line_over[:, :, :WIDTH].reshape(DEPTH * BASE, WIDTH)
    left = dot(onehot((wanted == position) & (wanted < POOL)), blocks[:, :HALF])
    right = dot(onehot((wanted - POOL == position) & (wanted >= POOL)), blocks[:, HALF:])
    send_over[:, :, :HALF] = (left + right).astype(BF16).reshape(LINES, 2 * POOL, HALF)
    for d in range(LINES):
        send_over[d, :, HALF:] = told
    got_over[grp] = send_over[0]
    for d in range(1, LINES):
        device = {"grp": along_x[d // 4] + along_y[d % 4], "blk": blk}
        remote(send_over.at[d], got_over.at[grp], OVER, device).start()
    post(24, 48)
    pack(48, CHIPS)
    post(48, CHIPS)
    got[SELF] = send[SELF]
    missing = missing_documents(index_ref, count_column, group)

    await_blocks(got_over, LINES - 1, recv_sem.at[OVER])
    told = got_over[:, :, HALF:].astype(F32)
    counts = told[:, 0:DEPTH].reshape(CHIPS, CLUSTERS)
    ranks = told[:, DEPTH : 2 * DEPTH].reshape(CHIPS, CLUSTERS)
    plans, ends, fault = receive_plan(counts, ranks, rank, my_x, my_y, my_z, routes_ref)

    row = iota((8, 128), 0)
    told = pick(row == 6, rank) + pick(row == 7, jnp.where(iota((1, 128), 1) == 0, fault, missing))
    for part, (first_end, held_end) in enumerate(ends):
        told = told + pick(row == part, first_end) + pick(row == 2 + part, held_end)
        picks[part][...] = onehot(iota(picks[part].shape, 0).astype(F32) == plans[part])
    facts[0] = told
    swap_facts = remote(facts.at[0], facts.at[1], FACTS, other_core)
    swap_facts.start()

    best = [jnp.full((1, room), -1.0, F32) for _, _, room in PARTS]
    key_kinds = []
    query_kinds = []
    totals = [jnp.zeros((1, WIDTH), F32), jnp.zeros((1, WIDTH), F32)]
    swaps = []

    def add_kinds(first, held, room):
        number = iota((room, 1), 0).astype(F32)
        key_kinds.append(jnp.where(number < first, 0.0, jnp.where(number < held, 1.0, 2.0)))

    for (first_end, held_end), (_, _, room) in zip(ends, PARTS):
        add_kinds(first_end, held_end, room)
        query_kinds.append(jnp.where(iota((1, room), 1).astype(F32) < first_end, 0.0, 1.0))

    def compare(first_key, last_key, part, more=0):
        borders = (*STARTS, *(HELD + start for start in STARTS), 2 * HELD)
        begin, stop = borders[first_key], borders[last_key + 1]
        start, room = STARTS[part], PARTS[part][2]
        scores = dot_rows(keys[begin : stop + more], keys[start : start + room])
        rest, scores = scores[stop - begin :], scores[: stop - begin]
        kind = jnp.concatenate(key_kinds[first_key : last_key + 1], axis=0)
        matched = kind == query_kinds[part]
        if begin < start + room and start < stop:
            matched = matched & (iota(kind.shape, 0) + (begin - start) != iota((1, room), 1))
        best[part] = jnp.maximum(best[part], jnp.max(jnp.where(matched, scores, -1.0), axis=0, keepdims=True))
        return rest

    def arrive(part):
        begin, steps, room = PARTS[part]
        await_blocks(got, messages[part], recv_sem.at[PART + part])
        rows = dot(picks[part][...], got[pl.ds(begin, steps)].reshape(steps * BASE, WIDTH))
        unit = rows * lax.rsqrt(across(rows * rows) + EPSILON)
        keys[pl.ds(STARTS[part], room)] = unit.astype(BF16)
        swap = remote(
            keys.at[pl.ds(STARTS[part], room)], keys.at[pl.ds(HELD + STARTS[part], room)], SWAP + part, other_core
        )
        swap.start()
        swaps.append(swap)
        is_first = iota((room, 1), 0).astype(F32) < ends[part][0]
        totals[0] = totals[0] + down(pick(is_first, unit))
        totals[1] = totals[1] + down(jnp.where(is_first, 0.0, unit))

    arrive(0)
    compare(0, 0, 0)
    swap_facts.wait()
    their_told = facts[1]
    for part, (_, _, room) in enumerate(PARTS):
        add_kinds(their_told[part : part + 1, 0:1], their_told[2 + part : 3 + part, 0:1], room)
    half_rows = got_over[:, :, :HALF].reshape(LINES * 2 * POOL, HALF)
    shape = (LINES * POOL, LINES * 2 * POOL)
    to, at = iota(shape, 0), iota(shape, 1)
    same = ((to >> 3) == (at >> 4)) & ((to & 7) == (at & 7))
    left = dot(onehot(same & ((at & POOL) == 0)), half_rows)
    right = dot(onehot(same & ((at & POOL) != 0)), half_rows)
    whole = jnp.concatenate([left, right], axis=1).astype(BF16)
    got[pl.ds(CHIPS, TOTAL - CHIPS)] = whole.reshape(TOTAL - CHIPS, BASE, WIDTH)
    swaps[0].wait()
    compare(2, 2, 0)

    arrive(1)
    row = iota((8, WIDTH), 0)
    sums[...] = pick(row == 0, totals[0]) + pick(row == 1, totals[1])
    swap_sums = remote(sums, their_sums, SUMS, other_core)
    swap_sums.start()
    compare(0, 2, 1)
    compare(1, 1, 0)

    swap_sums.wait()
    total = sums[...] + their_sums[...]
    keys[pl.ds(2 * HELD, 16)] = jnp.concatenate(halves(total), axis=0).astype(BF16)
    scale = lax.rsqrt(across(total * total) + EPSILON)
    swaps[1].wait()
    near = [compare(3, 3, part, 16) for part in range(len(PARTS))]
    near = [(some[0:8] + some[8:16]) * scale for some in near]

    poison = missing + their_told[7:8, 1:2] > 0.5
    tiles = CHIPS * BASE // 128
    for part, (begin, steps, room) in enumerate(PARTS):
        row = iota((8, room), 0)
        query_number = iota((1, room), 1).astype(F32)
        some = jnp.where(query_number < ends[part][0], near[part][0:1], near[part][1:2])
        values = jnp.zeros((8, room), F32)
        for number, term in enumerate(halves(best[part]) + halves(some)):
            values = jnp.where(row == number, term, values)
        out = dot(values.astype(BF16), picks[part][...])
        for kind in range(2):
            line = out[2 * kind : 2 * kind + 1] + out[2 * kind + 1 : 2 * kind + 2]
            line = jnp.where(poison, NONE, line)
            for tile in range(steps * BASE // 128):
                piece = line[:, tile * 128 : (tile + 1) * 128]
                to = begin * BASE // 128 + tile
                if to < tiles:
                    back[to, kind : kind + 1, :] = piece
                else:
                    for each in range(tiles):
                        back[each, 2 + kind : 3 + kind, :] = piece
    returned[SELF] = back[SELF // 8]
    for step in range(SELF):
        remote(back.at[step // 8], returned.at[step], BACK, device_at(step, -1)).start()

    differ = across(jnp.where(their_told[6:7] != rank, 1.0, 0.0))
    fault = fault + their_told[7:8, 0:1] + differ
    chosen = onehot(iota((CHIPS, ROWS), 0) == step_of)
    sub = iota((128, ROWS), 0)
    at_base = (sub == (step_of & 7) * BASE + slot) & in_base
    before_column = across(pick(eye, before_mine))
    line_slot = down(pick(iota((CHIPS, ROWS), 0) == chip, before_column)).astype(jnp.int32)
    at_over = (sub == grp * POOL + line_slot + (slot - BASE)) & (~in_base)

    await_blocks(returned, CHIPS - 1, recv_sem.at[BACK])
    found = []
    for number in range(4):
        line = returned[:, number, :]
        if number == 0:
            poisoned = across(down(jnp.where(line > 0.5 * NONE, 1.0, 0.0)))
            fault_ref[...] = jnp.where(fault + poisoned > 0.5, 1, 0) + jnp.zeros((1, 128), jnp.int32)
        terms = jnp.concatenate(halves(line), axis=1).astype(BF16)
        out = lax.dot_general(terms, chosen, (((0,), (0,)), ((), ())), preferred_element_type=F32)
        found.append(out[0:128] + out[128:256])
    out_ref[0:1] = down(pick(at_base, found[0]) + pick(at_over, found[2]))
    out_ref[1:2] = down(pick(at_base, found[1]) + pick(at_over, found[3]))

    await_blocks(line_over, DEPTH - 1, send_sem.at[LINE])
    await_blocks(got_over, LINES - 1, send_sem.at[OVER])
    await_blocks(returned, CHIPS - 1, send_sem.at[BACK])
    for part in range(len(PARTS)):
        await_blocks(got, messages[part], send_sem.at[PART + part])


def routed(embeddings, assign, owner, send_count, send_index):
    return pl.pallas_call(
        kernel,
        out_shape=(
            jax.ShapeDtypeStruct((2, ROWS), F32),
            jax.ShapeDtypeStruct((1, 128), jnp.int32),
        ),
        in_specs=[pl.BlockSpec(memory_space=pl.ANY)] * 5,
        out_specs=(pl.BlockSpec(memory_space=pltpu.VMEM),) * 2,
        scratch_shapes=[
            pltpu.VMEM((ROWS, WIDTH), BF16),
            pltpu.VMEM((1, ROWS), jnp.int32),
            pltpu.VMEM((1, CLUSTERS), jnp.int32),
            pltpu.VMEM((1, GROUPS), jnp.int32),
            pltpu.VMEM((GROUPS, CAP), jnp.int32),
            pltpu.VMEM((CHIPS, BASE, WIDTH), BF16),
            pltpu.VMEM((TOTAL, BASE, WIDTH), BF16),
            pltpu.VMEM((BASE, WIDTH + CLUSTERS), BF16),
            pltpu.VMEM((DEPTH, BASE, WIDTH + CLUSTERS), BF16),
            pltpu.VMEM((LINES, 2 * POOL, HALF + CLUSTERS), BF16),
            pltpu.VMEM((LINES, 2 * POOL, HALF + CLUSTERS), BF16),
            *[pltpu.VMEM((room, steps * BASE), BF16) for _, steps, room in PARTS],
            pltpu.VMEM((ROWS, ROWS), BF16),
            pltpu.VMEM((CHIPS, CLUSTERS), jnp.int32),
            pltpu.VMEM((2 * HELD + 16, WIDTH), BF16),
            pltpu.VMEM((2, 8, 128), F32),
            pltpu.VMEM((8, WIDTH), F32),
            pltpu.VMEM((8, WIDTH), F32),
            pltpu.VMEM((CHIPS * BASE // 128, 4, 128), F32),
            pltpu.VMEM((CHIPS, 4, 128), F32),
            pltpu.SemaphoreType.DMA((5,)),
            pltpu.SemaphoreType.DMA((9,)),
            pltpu.SemaphoreType.DMA((9,)),
        ],
        compiler_params=pltpu.CompilerParams(
            collective_id=0, has_side_effects=True, vmem_limit_bytes=48 * 1024 * 1024
        ),
    )(
        embeddings,
        assign.reshape(1, ROWS),
        owner.reshape(1, CLUSTERS),
        send_count,
        send_index[0],
    )


def body(embeddings, assign, owner, send_count, send_index):
    arguments = (embeddings, assign, owner, send_count, send_index)
    results, fault = routed(*arguments)
    results = lax.cond(fault[0, 0] != 0, lambda: jnp.stack(general(*arguments)), lambda: results)
    return results[0], results[1]


def solution(mesh):
    placed = (
        P(("grp", "blk"), None),
        P(("grp", "blk")),
        P(),
        P(("grp", "blk"), None),
        P(("grp", "blk"), None, None),
    )
    return jax.shard_map(
        body,
        mesh=mesh,
        in_specs=placed,
        out_specs=(P(("grp", "blk")), P(("grp", "blk"))),
        check_vma=False,
    )
```

```python
import functools

import jax
import jax.numpy as jnp
from jax import lax
from jax.experimental import pallas as pl
from jax.experimental.pallas import tpu as pltpu
from jax.sharding import PartitionSpec as P

EPSILON = 1e-06
F32 = jnp.float32
BF16 = jnp.bfloat16

CHIPS = 64
ROWS = 512
WIDTH = 768
CLUSTERS = 128
GROUPS = 16
CAP = 64
BASE = 16
HALF = WIDTH // 2
LINES = 16
DEPTH = 4
POOL = 8
PARTS = ((0, 40, 400), (40, 32, 256))
TOTAL = 72
HELD = 656
STARTS = (0, 400)
LAST = len(PARTS) - 1
NONE = 1e30


def normalize(values):
    widened = values.astype(F32)
    return widened * lax.rsqrt(jnp.sum(widened * widened, axis=1, keepdims=True) + EPSILON)


def general(embeddings, assign, owner, send_count, send_index):
    rows_local = embeddings.shape[0]
    feature_width = embeddings.shape[1]
    groups = lax.axis_size("grp")
    clusters = owner.shape[0]
    capacity = send_index.shape[2]
    slot_total = groups * capacity
    unit_rows = normalize(embeddings)
    unit_low = unit_rows.astype(BF16)
    counts = send_count[0]
    listed = send_index[0]
    live_slot = jnp.arange(capacity, dtype=jnp.int32)[None, :] < counts[:, None]
    listed_cluster = assign[listed]
    owned_here = owner[listed_cluster] == jnp.arange(groups, dtype=jnp.int32)[:, None]
    kept_slot = live_slot & owned_here
    out_cluster = jnp.where(kept_slot, listed_cluster, -1)
    out_tag = jnp.where(kept_slot, lax.axis_index(("grp", "blk")) * rows_local + listed, -1)
    out_vector = unit_low[listed.reshape(-1)].reshape(groups, capacity, feature_width)
    got_vector, got_cluster, got_tag = (
        lax.all_to_all(out_vector, "grp", split_axis=0, concat_axis=0, tiled=True),
        lax.all_to_all(out_cluster, "grp", split_axis=0, concat_axis=0, tiled=True),
        lax.all_to_all(out_tag, "grp", split_axis=0, concat_axis=0, tiled=True),
    )
    own_vector = got_vector.reshape(slot_total, feature_width)
    own_cluster = got_cluster.reshape(slot_total)
    own_tag = got_tag.reshape(slot_total)

    def tile_best(current, shard_piece):
        other_vector, other_cluster, other_tag = shard_piece
        scores = jnp.einsum("id,jd->ij", own_vector, other_vector, preferred_element_type=F32)
        matched = (
            (own_cluster[:, None] == other_cluster[None, :])
            & (other_cluster[None, :] >= 0)
            & (own_tag[:, None] != other_tag[None, :])
        )
        return jnp.maximum(current, jnp.max(jnp.where(matched, scores, -1.0), axis=1))

    other_vector = lax.all_gather(own_vector, "blk", axis=0, tiled=True)
    other_cluster = lax.all_gather(own_cluster, "blk", axis=0, tiled=True)
    other_tag = lax.all_gather(own_tag, "blk", axis=0, tiled=True)
    length = other_vector.shape[0]
    number = length // slot_total
    stacked = (
        other_vector.reshape(number, slot_total, feature_width),
        other_cluster.reshape(number, slot_total),
        other_tag.reshape(number, slot_total),
    )

    def scan_step(carry, single):
        return (tile_best(carry, single), None)

    result, unused = lax.scan(scan_step, jnp.full((slot_total,), -1.0, F32), stacked)
    target = jnp.where(live_slot, listed, rows_local).reshape(-1)
    partial_sum = jax.ops.segment_sum(unit_rows, assign, num_segments=clusters)
    centre = normalize(lax.psum(partial_sum, ("grp", "blk")))
    nearness = jnp.sum(unit_low.astype(F32) * centre[assign], axis=1)
    returned = lax.all_to_all(
        result.reshape(groups, capacity), "grp", split_axis=0, concat_axis=0, tiled=True
    )
    has_entry = (
        jnp.zeros((rows_local,), jnp.int32)
        .at[target]
        .max(kept_slot.astype(jnp.int32).reshape(-1), mode="drop")
    )
    centroid_cos = jnp.where(has_entry > 0, nearness, 0.0)
    max_sim = jnp.full((rows_local,), -1.0, F32).at[target].max(returned.reshape(-1), mode="drop")
    return (max_sim, centroid_cos)


def iota(shape, axis):
    return lax.broadcasted_iota(jnp.int32, shape, axis)


def down(values):
    return jnp.sum(values, axis=0, keepdims=True)


def across(values):
    return jnp.sum(values, axis=1, keepdims=True)


def pick(mask, values):
    return jnp.where(mask, values, 0.0)


def as_column(row):
    size = row.shape[1]
    return across(pick(iota((size, size), 0) == iota((size, size), 1), row))


def as_row(column):
    size = column.shape[0]
    return down(pick(iota((size, size), 0) == iota((size, size), 1), column))


def dot(a, b):
    return jnp.dot(a, b, preferred_element_type=F32)


def dot_rows(a, b):
    return lax.dot_general(a, b, (((1,), (1,)), ((), ())), preferred_element_type=F32)


def onehot(mask):
    return jnp.where(mask, 1.0, 0.0).astype(BF16)


def halves(values):
    first = values.astype(BF16).astype(F32)
    return first, (values - first).astype(BF16).astype(F32)


def rank_groups(count_ref):
    count_row = count_ref[...].astype(F32)
    count_column = as_column(count_row)
    sub, lane = iota((GROUPS, 128), 0), iota((GROUPS, 128), 1)
    count_lanes = down(pick(sub == lane, count_column))
    ahead = (count_column > count_lanes) | ((count_column == count_lanes) & (sub < lane))
    rank = down(jnp.where(ahead, 1.0, 0.0))
    return jnp.where(iota((1, 128), 1) < GROUPS, rank, 0.0), count_column


def place_documents(assign_ref, owner_ref, rank, earlier_ref, chip_step):
    member = iota((CLUSTERS, ROWS), 0) == assign_ref[...]
    member_low = onehot(member)
    before = down(pick(member, dot(member_low, earlier_ref[...])))
    count_column = across(jnp.where(member, 1.0, 0.0))
    owner_row = owner_ref[...].astype(F32)
    owner_column = as_column(owner_row)
    sub, lane = iota((CLUSTERS, CLUSTERS), 0), iota((CLUSTERS, CLUSTERS), 1)
    within = across(jnp.where((owner_column == owner_row) & (lane < sub), 1.0, 0.0))
    group_rank = across(pick(owner_column == lane.astype(F32), rank))
    place = group_rank * (CLUSTERS // GROUPS) + within
    chip = jnp.minimum(place, (CLUSTERS - 1) - place)
    count_row, place_row, chip_row = as_row(count_column), as_row(place), as_row(chip)
    opposite = down(pick((CLUSTERS - 1) - place == place_row, count_column))
    offset = jnp.where(place_row >= CHIPS, opposite, 0.0)
    step_row = down(pick(sub.astype(F32) == chip_row, as_column(chip_step)))
    row = iota((16, CLUSTERS), 0)
    told = pick(row == 0, owner_row) + pick(row == 1, chip_row) + pick(row == 2, step_row) + pick(row == 3, offset)
    told = dot(told.astype(BF16), member_low)
    place_counts = down(pick(place == lane.astype(F32), count_column))
    whole = told[1:4].astype(jnp.int32)
    return told[0:1], whole[0:1], whole[1:2], before.astype(jnp.int32) + whole[2:3], place_counts


def missing_documents(index_ref, count_column, group):
    listed = index_ref[...]
    live = iota((GROUPS, CAP), 1).astype(F32) < count_column
    eye = onehot(iota((CAP, CAP), 0) == iota((CAP, CAP), 1))
    high = dot_rows(eye, jnp.where(live, listed >> 4, 0).astype(F32).astype(BF16))
    low = dot_rows(eye, jnp.where(live, listed & 15, 0).astype(F32).astype(BF16))
    alive = dot_rows(eye, onehot(live))
    slots = jnp.where(alive > 0.5, high * 16.0 + low, -1.0)
    document = iota((1, ROWS), 1).astype(F32)
    lane = iota((CAP, GROUPS), 1)

    def count(g, hits):
        column = across(pick(lane == g, slots))
        wanted = jnp.where(group == g.astype(F32), document, -2.0)
        return hits + jnp.where(column == wanted, 1.0, 0.0)

    hits = lax.fori_loop(0, GROUPS, count, jnp.zeros((CAP, ROWS), F32))
    return across(jnp.where(down(hits) > 0.5, 0.0, 1.0))


def send_order():
    order = []
    for step in range(CHIPS):
        high, middle, low = step // 16, (step // 4) % 4, step % 4
        order.append((low, (middle + low) % 4, (high + middle + low) % 4))
    near = [shift for shift in order if sum(min(d, 4 - d) for d in shift) <= 1] + [(2, 0, 0)]
    near.sort(key=lambda shift: -sum(min(d, 4 - d) for d in shift))
    return [shift for shift in order if shift not in near] + near


ORDER = send_order()
SELF = CHIPS - 1


def step_to(dx, dy, dz):
    shift = (dx & 3) * 16 + (dy & 3) * 4 + (dz & 3)
    step = jnp.full(shift.shape, SELF, jnp.int32)
    for number, (x, y, z) in enumerate(ORDER[:SELF]):
        step = jnp.where(shift == x * 16 + y * 4 + z, number, step)
    return step


def in_part(step, part):
    begin, steps, _ = PARTS[part]
    return (step >= begin) & (step < begin + steps)


def chip_places():
    sub, lane = iota((CLUSTERS, CLUSTERS), 0), iota((CLUSTERS, CLUSTERS), 1)
    return onehot((sub == lane) | (sub == (CLUSTERS - 1) - lane))


def excess(totals):
    lane = iota(totals.shape, 1)
    return jnp.where(lane < CHIPS, jnp.maximum(totals - BASE, 0.0), 0.0)


def receive_plan(counts, ranks, rank, my_x, my_y, my_z, routes_ref):
    chip = my_x * 16 + my_y * 4 + my_z
    differ = jnp.where(ranks != rank, 1.0, 0.0)
    fault = across(down(differ))
    both = dot(counts.astype(BF16), chip_places())
    over = excess(both)
    lanes = iota((CHIPS, CLUSTERS), 1)
    sender = iota((CHIPS, 1), 0)
    source, target = iota((CHIPS, CHIPS), 0), iota((CHIPS, CHIPS), 1)

    same_line = (source >> 2) == (target >> 2)
    fault = fault + down(jnp.where(across(over) > BASE, 1.0, 0.0))
    of_line = dot(onehot(same_line), over.astype(BF16))
    fault = fault + across(down(jnp.where(of_line > POOL, 1.0, 0.0)))
    number = across(pick(lanes == chip, over))
    start = across(pick(same_line & (target < source), as_row(number)))

    route = routes_ref[...]
    based = jnp.where(lanes < CHIPS, jnp.minimum(both, float(BASE)), 0.0)
    for part, (_, _, room) in enumerate(PARTS):
        held = down(pick(in_part(route, part), based))
        if part == LAST:
            held = held + down(over)
        fault = fault + across(jnp.where(held > room, 1.0, 0.0))

    first = across(pick(lanes == chip, counts))
    second = across(pick(lanes == (CLUSTERS - 1) - chip, counts))
    place = (lanes & (POOL - 1)).astype(F32) - start
    mine = ((sender >> 2) == (lanes >> 3)) & (place >= 0.0) & (place < number)
    over_first = down(jnp.where(mine & (place + BASE < first), 1.0, 0.0))
    over_second = down(jnp.where(mine & (place + BASE >= first), 1.0, 0.0))
    over_first_total, over_second_total = across(over_first), across(over_second)
    earlier = onehot(iota((CLUSTERS, CLUSTERS), 0) < iota((CLUSTERS, CLUSTERS), 1))
    sub = iota((16, CLUSTERS), 0)
    before = dot((pick(sub == 0, over_first) + pick(sub == 1, over_second)).astype(BF16), earlier)

    base_first = jnp.minimum(first, float(BASE))
    base_second = jnp.minimum(first + second, float(BASE)) - base_first
    first_row, second_row = as_row(base_first), as_row(base_second)

    step_column = across(jnp.where(lanes == chip, route.astype(F32), 0.0)).astype(jnp.int32)
    step_row = as_row(step_column.astype(F32)).astype(jnp.int32)
    plans = []
    ends = []
    for part, (begin, steps, _) in enumerate(PARTS):
        inside = in_part(step_column, part)
        ahead = (target < source) & in_part(step_row, part)
        first_total = down(pick(inside, base_first))
        second_total = down(pick(inside, base_second))
        last = part == LAST
        first_end = first_total + over_first_total if last else first_total
        first_start = across(pick(ahead, first_row))
        second_start = across(pick(ahead, second_row)) + first_end
        spread = step_column - begin == (iota((CHIPS, steps * BASE), 1) >> 4)
        head, tail, head_start, tail_start = [
            down(pick(spread, column)) for column in (base_first, base_second, first_start, second_start)
        ]
        slot = (iota((1, steps * BASE), 1) & (BASE - 1)).astype(F32)
        later = jnp.where(slot < head + tail, tail_start + (slot - head), -1.0)
        plan = jnp.where(slot < head, head_start + slot, later)
        held_end = first_end + second_total
        if last:
            over_row_of = jnp.where(over_second > 0.5, held_end + before[1:2], -1.0)
            over_row_of = jnp.where(over_first > 0.5, first_total + before[0:1], over_row_of)
            plan = jnp.concatenate([plan[:, : steps * BASE - CLUSTERS], over_row_of], axis=1)
            held_end = held_end + over_second_total
        plans.append(plan)
        ends.append((first_end, held_end))
    return plans, ends, fault


def kernel(
    x_hbm, assign_hbm, owner_hbm, count_hbm, index_hbm,
    out_ref, fault_ref,
    x_ref, assign_ref, owner_ref, count_ref, index_ref,
    send, got, own_over, line_over, send_over, got_over, pick_0, pick_1,
    earlier_ref, routes_ref, way_ref, keys, facts, sums, their_sums, back, returned,
    load_sem, send_sem, recv_sem,
):
    grp, blk = lax.axis_index("grp"), lax.axis_index("blk")
    my_x, my_y, my_z, core = grp // 4, grp % 4, blk // 2, blk % 2
    my_chip = grp * 4 + my_z
    picks = (pick_0, pick_1)
    along_x = [((my_x + d) % 4) * 4 for d in range(4)]
    along_y = [(my_y + d) % 4 for d in range(4)]
    along_z = [((my_z + d) % 4) * 2 + core for d in range(4)]
    other_core = {"grp": grp, "blk": my_z * 2 + (1 - core)}

    def device_at(step, sign):
        dx, dy, dz = [(sign * d) % 4 for d in ORDER[step]]
        return {"grp": along_x[dx] + along_y[dy], "blk": along_z[dz]}

    def remote(source, target, number, device):
        return pltpu.make_async_remote_copy(
            src_ref=source,
            dst_ref=target,
            send_sem=send_sem.at[number],
            recv_sem=recv_sem.at[number],
            device_id=device,
            device_id_type=pl.DeviceIdType.MESH,
        )

    def await_blocks(ref, number, semaphore):
        block = ref.at[pl.ds(0, number)]
        pltpu.make_async_copy(block, block, semaphore).wait()

    LINE, OVER, FACTS, SUMS, BACK, SWAP, PART = 0, 1, 2, 3, 4, 5, 7
    messages = [min(begin + steps, SELF) - begin for begin, steps, _ in PARTS]

    loads = [
        pltpu.make_async_copy(source, target, load_sem.at[number])
        for number, (source, target) in enumerate(
            (
                (assign_hbm, assign_ref),
                (owner_hbm, owner_ref),
                (count_hbm, count_ref),
                (index_hbm, index_ref),
                (x_hbm, x_ref),
            )
        )
    ]
    for load in loads:
        load.start()
    barrier = pltpu.get_barrier_semaphore()
    for device in [device_at(step, 1) for step in range(SELF)] + [other_core]:
        pl.semaphore_signal(barrier, inc=1, device_id=device, device_id_type=pl.DeviceIdType.MESH)
    lane = iota((1, CLUSTERS), 1)
    chip_step = step_to((lane >> 4) - my_x, ((lane >> 2) & 3) - my_y, (lane & 3) - my_z).astype(F32)
    earlier_ref[...] = onehot(iota((ROWS, ROWS), 0) < iota((ROWS, ROWS), 1))
    for load in loads[:-1]:
        load.wait()

    rank, count_column = rank_groups(count_ref)
    group, chip, step_of, slot, place_counts = place_documents(assign_ref, owner_ref, rank, earlier_ref, chip_step)
    in_base = slot < BASE
    send_slot = jnp.where(in_base, step_of * BASE + slot, -1)
    loads[-1].wait()

    def pack(first, stop):
        slots = iota(((stop - first) * BASE, ROWS), 0) + first * BASE
        rows = dot(onehot(slots == send_slot), x_ref[...]).astype(BF16)
        send[pl.ds(first, stop - first)] = rows.reshape(stop - first, BASE, WIDTH)

    def post(first, stop):
        for step in range(first, min(stop, SELF)):
            number = max(part for part in range(len(PARTS)) if PARTS[part][0] <= step)
            remote(send.at[step], got.at[step], PART + number, device_at(step, 1)).start()

    place_counts_16 = place_counts + jnp.zeros((16, CLUSTERS), F32)
    own_excess = excess(dot(place_counts_16.astype(BF16), chip_places())[0:1])
    eye = iota((CHIPS, CLUSTERS), 0) == iota((CHIPS, CLUSTERS), 1)
    excess_column = across(pick(eye, own_excess))
    over_slot = down(pick(iota((CHIPS, ROWS), 0) < chip, excess_column)).astype(jnp.int32) + (slot - BASE)
    over_slot = jnp.where(in_base, -1, over_slot)
    row = iota((BASE, CLUSTERS), 0)
    own_over[:, :WIDTH] = dot(onehot(iota((BASE, ROWS), 0) == over_slot), x_ref[...]).astype(BF16)
    own_over[:, WIDTH:] = (pick(row == 0, place_counts) + pick(row == 1, rank)).astype(BF16)
    line_over[my_z] = own_over[...]
    sublane = iota((LINES * 2 * POOL, 1), 0)
    way = sublane >> 4
    to_chip = ((my_x + (way >> 2)) & 3) * 16 + ((my_y + way) & 3) * 4 + my_z
    way_ref[...] = onehot(iota((LINES * 2 * POOL, CLUSTERS), 1) == to_chip)
    pack(0, 8)
    pl.semaphore_wait(barrier, CHIPS)
    for d in range(1, DEPTH):
        remote(own_over, line_over.at[my_z], LINE, {"grp": grp, "blk": along_z[d]}).start()
    post(0, 8)
    pack(8, 24)
    post(8, 24)
    pack(24, 48)
    to_chip, sender = iota((CHIPS, CLUSTERS), 1), iota((CHIPS, CLUSTERS), 0)
    routes_ref[...] = step_to(
        (to_chip >> 4) - (sender >> 4), ((to_chip >> 2) & 3) - ((sender >> 2) & 3), (to_chip & 3) - (sender & 3)
    )

    await_blocks(line_over, DEPTH - 1, recv_sem.at[LINE])
    line_counts = [line_over[d, 0:1, WIDTH:].astype(F32) for d in range(DEPTH)]
    line_ranks = [line_over[d, 1:2, WIDTH:].astype(F32) for d in range(DEPTH)]
    row = iota((2 * POOL, CLUSTERS), 0)
    told = jnp.zeros((2 * POOL, CLUSTERS), F32)
    for d in range(DEPTH):
        told = told + pick(row == d, line_counts[d]) + pick(row == DEPTH + d, line_ranks[d])
    told = told.astype(BF16)
    over = excess(dot(told, chip_places()))[0:DEPTH]
    ahead = dot(over.astype(BF16), onehot(iota((CLUSTERS, CLUSTERS), 0) < iota((CLUSTERS, CLUSTERS), 1)))
    before = [jnp.zeros((1, CLUSTERS), F32)]
    for d in range(DEPTH - 1):
        before.append(before[-1] + over[d : d + 1])
    before = jnp.concatenate(before, axis=0)
    before_mine = down(pick(iota((DEPTH, 1), 0) == my_z, before))
    known = jnp.concatenate([over, ahead, before, jnp.zeros((DEPTH, CLUSTERS), F32)], axis=0).astype(BF16)
    known = dot_rows(way_ref[...], known)
    entry = iota((LINES * 2 * POOL, DEPTH * BASE), 1)

    def of_depth(kind):
        values = known[:, kind * DEPTH : kind * DEPTH + 1]
        for d in range(1, DEPTH):
            values = jnp.where((entry >> 4) == d, known[:, kind * DEPTH + d : kind * DEPTH + d + 1], values)
        return values

    offset = (entry & (BASE - 1)).astype(F32) - of_depth(1)
    position = jnp.where((offset >= 0.0) & (offset < of_depth(0)), offset + of_depth(2), -1.0)
    wanted = (sublane & (2 * POOL - 1)).astype(F32)
    blocks = line_over[:, :, :WIDTH].reshape(DEPTH * BASE, WIDTH)
    left = dot(onehot((wanted == position) & (wanted < POOL)), blocks[:, :HALF])
    right = dot(onehot((wanted - POOL == position) & (wanted >= POOL)), blocks[:, HALF:])
    send_over[:, :, :HALF] = (left + right).astype(BF16).reshape(LINES, 2 * POOL, HALF)
    for d in range(LINES):
        send_over[d, :, HALF:] = told
    got_over[grp] = send_over[0]
    for d in range(1, LINES):
        device = {"grp": along_x[d // 4] + along_y[d % 4], "blk": blk}
        remote(send_over.at[d], got_over.at[grp], OVER, device).start()
    post(24, 48)
    pack(48, CHIPS)
    post(48, CHIPS)
    got[SELF] = send[SELF]
    missing = missing_documents(index_ref, count_column, group)

    await_blocks(got_over, LINES - 1, recv_sem.at[OVER])
    told = got_over[:, :, HALF:].astype(F32)
    counts = told[:, 0:DEPTH].reshape(CHIPS, CLUSTERS)
    ranks = told[:, DEPTH : 2 * DEPTH].reshape(CHIPS, CLUSTERS)
    plans, ends, fault = receive_plan(counts, ranks, rank, my_x, my_y, my_z, routes_ref)

    row = iota((8, 128), 0)
    told = pick(row == 6, rank) + pick(row == 7, jnp.where(iota((1, 128), 1) == 0, fault, missing))
    for part, (first_end, held_end) in enumerate(ends):
        told = told + pick(row == part, first_end) + pick(row == 2 + part, held_end)
        picks[part][...] = onehot(iota(picks[part].shape, 0).astype(F32) == plans[part])
    facts[0] = told
    swap_facts = remote(facts.at[0], facts.at[1], FACTS, other_core)
    swap_facts.start()

    best = [jnp.full((1, room), -1.0, F32) for _, _, room in PARTS]
    key_kinds = []
    query_kinds = []
    totals = [jnp.zeros((1, WIDTH), F32), jnp.zeros((1, WIDTH), F32)]
    swaps = []

    def add_kinds(first, held, room):
        number = iota((room, 1), 0).astype(F32)
        key_kinds.append(jnp.where(number < first, 0.0, jnp.where(number < held, 1.0, 2.0)))

    for (first_end, held_end), (_, _, room) in zip(ends, PARTS):
        add_kinds(first_end, held_end, room)
        query_kinds.append(jnp.where(iota((1, room), 1).astype(F32) < first_end, 0.0, 1.0))

    def compare(first_key, last_key, part, more=0):
        borders = (*STARTS, *(HELD + start for start in STARTS), 2 * HELD)
        begin, stop = borders[first_key], borders[last_key + 1]
        start, room = STARTS[part], PARTS[part][2]
        scores = dot_rows(keys[begin : stop + more], keys[start : start + room])
        rest, scores = scores[stop - begin :], scores[: stop - begin]
        kind = jnp.concatenate(key_kinds[first_key : last_key + 1], axis=0)
        matched = kind == query_kinds[part]
        if begin < start + room and start < stop:
            matched = matched & (iota(kind.shape, 0) + (begin - start) != iota((1, room), 1))
        best[part] = jnp.maximum(best[part], jnp.max(jnp.where(matched, scores, -1.0), axis=0, keepdims=True))
        return rest

    def arrive(part):
        begin, steps, room = PARTS[part]
        await_blocks(got, messages[part], recv_sem.at[PART + part])
        rows = dot(picks[part][...], got[pl.ds(begin, steps)].reshape(steps * BASE, WIDTH))
        unit = rows * lax.rsqrt(across(rows * rows) + EPSILON)
        keys[pl.ds(STARTS[part], room)] = unit.astype(BF16)
        swap = remote(
            keys.at[pl.ds(STARTS[part], room)], keys.at[pl.ds(HELD + STARTS[part], room)], SWAP + part, other_core
        )
        swap.start()
        swaps.append(swap)
        is_first = iota((room, 1), 0).astype(F32) < ends[part][0]
        totals[0] = totals[0] + down(pick(is_first, unit))
        totals[1] = totals[1] + down(jnp.where(is_first, 0.0, unit))

    arrive(0)
    compare(0, 0, 0)
    swap_facts.wait()
    their_told = facts[1]
    for part, (_, _, room) in enumerate(PARTS):
        add_kinds(their_told[part : part + 1, 0:1], their_told[2 + part : 3 + part, 0:1], room)
    half_rows = got_over[:, :, :HALF].reshape(LINES * 2 * POOL, HALF)
    shape = (LINES * POOL, LINES * 2 * POOL)
    to, at = iota(shape, 0), iota(shape, 1)
    same = ((to >> 3) == (at >> 4)) & ((to & 7) == (at & 7))
    left = dot(onehot(same & ((at & POOL) == 0)), half_rows)
    right = dot(onehot(same & ((at & POOL) != 0)), half_rows)
    whole = jnp.concatenate([left, right], axis=1).astype(BF16)
    got[pl.ds(CHIPS, TOTAL - CHIPS)] = whole.reshape(TOTAL - CHIPS, BASE, WIDTH)
    swaps[0].wait()
    compare(2, 2, 0)

    arrive(1)
    row = iota((8, WIDTH), 0)
    sums[...] = pick(row == 0, totals[0]) + pick(row == 1, totals[1])
    swap_sums = remote(sums, their_sums, SUMS, other_core)
    swap_sums.start()
    compare(0, 2, 1)
    compare(1, 1, 0)

    swap_sums.wait()
    total = sums[...] + their_sums[...]
    keys[pl.ds(2 * HELD, 16)] = jnp.concatenate(halves(total), axis=0).astype(BF16)
    scale = lax.rsqrt(across(total * total) + EPSILON)
    swaps[1].wait()
    near = [compare(3, 3, part, 16) for part in range(len(PARTS))]
    near = [(some[0:8] + some[8:16]) * scale for some in near]

    poison = missing + their_told[7:8, 1:2] > 0.5
    tiles = CHIPS * BASE // 128
    for part, (begin, steps, room) in enumerate(PARTS):
        row = iota((8, room), 0)
        query_number = iota((1, room), 1).astype(F32)
        some = jnp.where(query_number < ends[part][0], near[part][0:1], near[part][1:2])
        values = jnp.zeros((8, room), F32)
        for number, term in enumerate(halves(best[part]) + halves(some)):
            values = jnp.where(row == number, term, values)
        out = dot(values.astype(BF16), picks[part][...])
        for kind in range(2):
            line = out[2 * kind : 2 * kind + 1] + out[2 * kind + 1 : 2 * kind + 2]
            line = jnp.where(poison, NONE, line)
            for tile in range(steps * BASE // 128):
                piece = line[:, tile * 128 : (tile + 1) * 128]
                to = begin * BASE // 128 + tile
                if to < tiles:
                    back[to, kind : kind + 1, :] = piece
                else:
                    for each in range(tiles):
                        back[each, 2 + kind : 3 + kind, :] = piece
    returned[SELF] = back[SELF // 8]
    for step in range(SELF):
        remote(back.at[step // 8], returned.at[step], BACK, device_at(step, -1)).start()

    differ = across(jnp.where(their_told[6:7] != rank, 1.0, 0.0))
    fault = fault + their_told[7:8, 0:1] + differ
    chosen = onehot(iota((CHIPS, ROWS), 0) == step_of)
    sub = iota((128, ROWS), 0)
    at_base = (sub == (step_of & 7) * BASE + slot) & in_base
    before_column = across(pick(eye, before_mine))
    line_slot = down(pick(iota((CHIPS, ROWS), 0) == chip, before_column)).astype(jnp.int32)
    at_over = (sub == grp * POOL + line_slot + (slot - BASE)) & (~in_base)

    await_blocks(returned, CHIPS - 1, recv_sem.at[BACK])
    found = []
    for number in range(4):
        line = returned[:, number, :]
        if number == 0:
            poisoned = across(down(jnp.where(line > 0.5 * NONE, 1.0, 0.0)))
            fault_ref[...] = jnp.where(fault + poisoned > 0.5, 1, 0) + jnp.zeros((1, 128), jnp.int32)
        terms = jnp.concatenate(halves(line), axis=1).astype(BF16)
        out = lax.dot_general(terms, chosen, (((0,), (0,)), ((), ())), preferred_element_type=F32)
        found.append(out[0:128] + out[128:256])
    out_ref[0:1] = down(pick(at_base, found[0]) + pick(at_over, found[2]))
    out_ref[1:2] = down(pick(at_base, found[1]) + pick(at_over, found[3]))

    await_blocks(line_over, DEPTH - 1, send_sem.at[LINE])
    await_blocks(got_over, LINES - 1, send_sem.at[OVER])
    await_blocks(returned, CHIPS - 1, send_sem.at[BACK])
    for part in range(len(PARTS)):
        await_blocks(got, messages[part], send_sem.at[PART + part])


def routed(embeddings, assign, owner, send_count, send_index):
    return pl.pallas_call(
        kernel,
        out_shape=(
            jax.ShapeDtypeStruct((2, ROWS), F32),
            jax.ShapeDtypeStruct((1, 128), jnp.int32),
        ),
        in_specs=[pl.BlockSpec(memory_space=pl.ANY)] * 5,
        out_specs=(pl.BlockSpec(memory_space=pltpu.VMEM),) * 2,
        scratch_shapes=[
            pltpu.VMEM((ROWS, WIDTH), BF16),
            pltpu.VMEM((1, ROWS), jnp.int32),
            pltpu.VMEM((1, CLUSTERS), jnp.int32),
            pltpu.VMEM((1, GROUPS), jnp.int32),
            pltpu.VMEM((GROUPS, CAP), jnp.int32),
            pltpu.VMEM((CHIPS, BASE, WIDTH), BF16),
            pltpu.VMEM((TOTAL, BASE, WIDTH), BF16),
            pltpu.VMEM((BASE, WIDTH + CLUSTERS), BF16),
            pltpu.VMEM((DEPTH, BASE, WIDTH + CLUSTERS), BF16),
            pltpu.VMEM((LINES, 2 * POOL, HALF + CLUSTERS), BF16),
            pltpu.VMEM((LINES, 2 * POOL, HALF + CLUSTERS), BF16),
            *[pltpu.VMEM((room, steps * BASE), BF16) for _, steps, room in PARTS],
            pltpu.VMEM((ROWS, ROWS), BF16),
            pltpu.VMEM((CHIPS, CLUSTERS), jnp.int32),
            pltpu.VMEM((LINES * 2 * POOL, CLUSTERS), BF16),
            pltpu.VMEM((2 * HELD + 16, WIDTH), BF16),
            pltpu.VMEM((2, 8, 128), F32),
            pltpu.VMEM((8, WIDTH), F32),
            pltpu.VMEM((8, WIDTH), F32),
            pltpu.VMEM((CHIPS * BASE // 128, 4, 128), F32),
            pltpu.VMEM((CHIPS, 4, 128), F32),
            pltpu.SemaphoreType.DMA((5,)),
            pltpu.SemaphoreType.DMA((9,)),
            pltpu.SemaphoreType.DMA((9,)),
        ],
        compiler_params=pltpu.CompilerParams(
            collective_id=0, has_side_effects=True, vmem_limit_bytes=48 * 1024 * 1024
        ),
    )(
        embeddings,
        assign.reshape(1, ROWS),
        owner.reshape(1, CLUSTERS),
        send_count,
        send_index[0],
    )


def body(embeddings, assign, owner, send_count, send_index):
    arguments = (embeddings, assign, owner, send_count, send_index)
    results, fault = routed(*arguments)
    results = lax.cond(fault[0, 0] != 0, lambda: jnp.stack(general(*arguments)), lambda: results)
    return results[0], results[1]


def solution(mesh):
    placed = (
        P(("grp", "blk"), None),
        P(("grp", "blk")),
        P(),
        P(("grp", "blk"), None),
        P(("grp", "blk"), None, None),
    )
    return jax.shard_map(
        body,
        mesh=mesh,
        in_specs=placed,
        out_specs=(P(("grp", "blk")), P(("grp", "blk"))),
        check_vma=False,
    )
```

```python
import functools

import jax
import jax.numpy as jnp
from jax import lax
from jax.experimental import pallas as pl
from jax.experimental.pallas import tpu as pltpu
from jax.sharding import PartitionSpec as P

EPSILON = 1e-06
F32 = jnp.float32
BF16 = jnp.bfloat16

CHIPS = 64
ROWS = 512
WIDTH = 768
CLUSTERS = 128
GROUPS = 16
CAP = 64
BASE = 16
HALF = WIDTH // 2
LINES = 16
DEPTH = 4
POOL = 8
PARTS = ((0, 40, 400), (40, 32, 256))
TOTAL = 72
HELD = 656
STARTS = (0, 400)
LAST = len(PARTS) - 1
NONE = 1e30


def normalize(values):
    widened = values.astype(F32)
    return widened * lax.rsqrt(jnp.sum(widened * widened, axis=1, keepdims=True) + EPSILON)


def general(embeddings, assign, owner, send_count, send_index):
    rows_local = embeddings.shape[0]
    feature_width = embeddings.shape[1]
    groups = lax.axis_size("grp")
    clusters = owner.shape[0]
    capacity = send_index.shape[2]
    slot_total = groups * capacity
    unit_rows = normalize(embeddings)
    unit_low = unit_rows.astype(BF16)
    counts = send_count[0]
    listed = send_index[0]
    live_slot = jnp.arange(capacity, dtype=jnp.int32)[None, :] < counts[:, None]
    listed_cluster = assign[listed]
    owned_here = owner[listed_cluster] == jnp.arange(groups, dtype=jnp.int32)[:, None]
    kept_slot = live_slot & owned_here
    out_cluster = jnp.where(kept_slot, listed_cluster, -1)
    out_tag = jnp.where(kept_slot, lax.axis_index(("grp", "blk")) * rows_local + listed, -1)
    out_vector = unit_low[listed.reshape(-1)].reshape(groups, capacity, feature_width)
    got_vector, got_cluster, got_tag = (
        lax.all_to_all(out_vector, "grp", split_axis=0, concat_axis=0, tiled=True),
        lax.all_to_all(out_cluster, "grp", split_axis=0, concat_axis=0, tiled=True),
        lax.all_to_all(out_tag, "grp", split_axis=0, concat_axis=0, tiled=True),
    )
    own_vector = got_vector.reshape(slot_total, feature_width)
    own_cluster = got_cluster.reshape(slot_total)
    own_tag = got_tag.reshape(slot_total)

    def tile_best(current, shard_piece):
        other_vector, other_cluster, other_tag = shard_piece
        scores = jnp.einsum("id,jd->ij", own_vector, other_vector, preferred_element_type=F32)
        matched = (
            (own_cluster[:, None] == other_cluster[None, :])
            & (other_cluster[None, :] >= 0)
            & (own_tag[:, None] != other_tag[None, :])
        )
        return jnp.maximum(current, jnp.max(jnp.where(matched, scores, -1.0), axis=1))

    other_vector = lax.all_gather(own_vector, "blk", axis=0, tiled=True)
    other_cluster = lax.all_gather(own_cluster, "blk", axis=0, tiled=True)
    other_tag = lax.all_gather(own_tag, "blk", axis=0, tiled=True)
    length = other_vector.shape[0]
    number = length // slot_total
    stacked = (
        other_vector.reshape(number, slot_total, feature_width),
        other_cluster.reshape(number, slot_total),
        other_tag.reshape(number, slot_total),
    )

    def scan_step(carry, single):
        return (tile_best(carry, single), None)

    result, unused = lax.scan(scan_step, jnp.full((slot_total,), -1.0, F32), stacked)
    target = jnp.where(live_slot, listed, rows_local).reshape(-1)
    partial_sum = jax.ops.segment_sum(unit_rows, assign, num_segments=clusters)
    centre = normalize(lax.psum(partial_sum, ("grp", "blk")))
    nearness = jnp.sum(unit_low.astype(F32) * centre[assign], axis=1)
    returned = lax.all_to_all(
        result.reshape(groups, capacity), "grp", split_axis=0, concat_axis=0, tiled=True
    )
    has_entry = (
        jnp.zeros((rows_local,), jnp.int32)
        .at[target]
        .max(kept_slot.astype(jnp.int32).reshape(-1), mode="drop")
    )
    centroid_cos = jnp.where(has_entry > 0, nearness, 0.0)
    max_sim = jnp.full((rows_local,), -1.0, F32).at[target].max(returned.reshape(-1), mode="drop")
    return (max_sim, centroid_cos)


def iota(shape, axis):
    return lax.broadcasted_iota(jnp.int32, shape, axis)


def down(values):
    return jnp.sum(values, axis=0, keepdims=True)


def across(values):
    return jnp.sum(values, axis=1, keepdims=True)


def pick(mask, values):
    return jnp.where(mask, values, 0.0)


def as_column(row):
    size = row.shape[1]
    return across(pick(iota((size, size), 0) == iota((size, size), 1), row))


def as_row(column):
    size = column.shape[0]
    return down(pick(iota((size, size), 0) == iota((size, size), 1), column))


def dot(a, b):
    return jnp.dot(a, b, preferred_element_type=F32)


def dot_rows(a, b):
    return lax.dot_general(a, b, (((1,), (1,)), ((), ())), preferred_element_type=F32)


def onehot(mask):
    return jnp.where(mask, 1.0, 0.0).astype(BF16)


def halves(values):
    first = values.astype(BF16).astype(F32)
    return first, (values - first).astype(BF16).astype(F32)


def rank_groups(count_ref):
    count_row = count_ref[...].astype(F32)
    count_column = as_column(count_row)
    sub, lane = iota((GROUPS, 128), 0), iota((GROUPS, 128), 1)
    count_lanes = down(pick(sub == lane, count_column))
    ahead = (count_column > count_lanes) | ((count_column == count_lanes) & (sub < lane))
    rank = down(jnp.where(ahead, 1.0, 0.0))
    return jnp.where(iota((1, 128), 1) < GROUPS, rank, 0.0), count_column


def place_documents(assign_ref, owner_ref, rank, earlier_ref, chip_step):
    member = iota((CLUSTERS, ROWS), 0) == assign_ref[...]
    member_low = onehot(member)
    before = down(pick(member, dot(member_low, earlier_ref[...])))
    count_column = across(jnp.where(member, 1.0, 0.0))
    owner_row = owner_ref[...].astype(F32)
    owner_column = as_column(owner_row)
    sub, lane = iota((CLUSTERS, CLUSTERS), 0), iota((CLUSTERS, CLUSTERS), 1)
    within = across(jnp.where((owner_column == owner_row) & (lane < sub), 1.0, 0.0))
    group_rank = across(pick(owner_column == lane.astype(F32), rank))
    place = group_rank * (CLUSTERS // GROUPS) + within
    chip = jnp.minimum(place, (CLUSTERS - 1) - place)
    count_row, place_row, chip_row = as_row(count_column), as_row(place), as_row(chip)
    opposite = down(pick((CLUSTERS - 1) - place == place_row, count_column))
    offset = jnp.where(place_row >= CHIPS, opposite, 0.0)
    step_row = down(pick(sub.astype(F32) == chip_row, as_column(chip_step)))
    row = iota((16, CLUSTERS), 0)
    told = pick(row == 0, owner_row) + pick(row == 1, chip_row) + pick(row == 2, step_row) + pick(row == 3, offset)
    told = dot(told.astype(BF16), member_low)
    place_counts = down(pick(place == lane.astype(F32), count_column))
    whole = told[1:4].astype(jnp.int32)
    return told[0:1], whole[0:1], whole[1:2], before.astype(jnp.int32) + whole[2:3], place_counts


def missing_documents(index_ref, count_column, group):
    listed = index_ref[...]
    live = iota((GROUPS, CAP), 1).astype(F32) < count_column
    eye = onehot(iota((CAP, CAP), 0) == iota((CAP, CAP), 1))
    high = dot_rows(eye, jnp.where(live, listed >> 4, 0).astype(F32).astype(BF16))
    low = dot_rows(eye, jnp.where(live, listed & 15, 0).astype(F32).astype(BF16))
    alive = dot_rows(eye, onehot(live))
    slots = jnp.where(alive > 0.5, high * 16.0 + low, -1.0)
    document = iota((1, ROWS), 1).astype(F32)
    lane = iota((CAP, GROUPS), 1)

    def count(g, hits):
        column = across(pick(lane == g, slots))
        wanted = jnp.where(group == g.astype(F32), document, -2.0)
        return hits + jnp.where(column == wanted, 1.0, 0.0)

    hits = lax.fori_loop(0, GROUPS, count, jnp.zeros((CAP, ROWS), F32))
    return across(jnp.where(down(hits) > 0.5, 0.0, 1.0))


def send_order():
    order = []
    for step in range(CHIPS):
        high, middle, low = step // 16, (step // 4) % 4, step % 4
        order.append((low, (middle + low) % 4, (high + middle + low) % 4))
    near = [shift for shift in order if sum(min(d, 4 - d) for d in shift) <= 1] + [(2, 0, 0)]
    near.sort(key=lambda shift: -sum(min(d, 4 - d) for d in shift))
    return [shift for shift in order if shift not in near] + near


ORDER = send_order()
SELF = CHIPS - 1


def step_to(dx, dy, dz):
    shift = (dx & 3) * 16 + (dy & 3) * 4 + (dz & 3)
    step = jnp.full(shift.shape, SELF, jnp.int32)
    for number, (x, y, z) in enumerate(ORDER[:SELF]):
        step = jnp.where(shift == x * 16 + y * 4 + z, number, step)
    return step


def in_part(step, part):
    begin, steps, _ = PARTS[part]
    return (step >= begin) & (step < begin + steps)


def chip_places():
    sub, lane = iota((CLUSTERS, CLUSTERS), 0), iota((CLUSTERS, CLUSTERS), 1)
    return onehot((sub == lane) | (sub == (CLUSTERS - 1) - lane))


def excess(totals):
    lane = iota(totals.shape, 1)
    return jnp.where(lane < CHIPS, jnp.maximum(totals - BASE, 0.0), 0.0)


def receive_plan(counts, ranks, rank, my_x, my_y, my_z, routes_ref):
    chip = my_x * 16 + my_y * 4 + my_z
    both = dot(counts.astype(BF16), chip_places())
    over = excess(both)
    lanes = iota((CHIPS, CLUSTERS), 1)
    sender = iota((CHIPS, 1), 0)
    source, target = iota((CHIPS, CHIPS), 0), iota((CHIPS, CHIPS), 1)

    same_line = (source >> 2) == (target >> 2)
    number = across(pick(lanes == chip, over))
    start = across(pick(same_line & (target < source), as_row(number)))

    def faults():
        differ = jnp.where(ranks != rank, 1.0, 0.0)
        differ = differ + jnp.where(dot(onehot(same_line), over.astype(BF16)) > POOL, 1.0, 0.0)
        based = jnp.where(lanes < CHIPS, jnp.minimum(both, float(BASE)), 0.0)
        fault = across(down(differ)) + down(jnp.where(across(over) > BASE, 1.0, 0.0))
        for part, (_, _, room) in enumerate(PARTS):
            held = down(pick(in_part(routes_ref[...], part), based))
            if part == LAST:
                held = held + down(over)
            fault = fault + across(jnp.where(held > room, 1.0, 0.0))
        return fault

    first = across(pick(lanes == chip, counts))
    second = across(pick(lanes == (CLUSTERS - 1) - chip, counts))
    place = (lanes & (POOL - 1)).astype(F32) - start
    mine = ((sender >> 2) == (lanes >> 3)) & (place >= 0.0) & (place < number)
    over_first = down(jnp.where(mine & (place + BASE < first), 1.0, 0.0))
    over_second = down(jnp.where(mine & (place + BASE >= first), 1.0, 0.0))
    over_first_total, over_second_total = across(over_first), across(over_second)
    earlier = onehot(iota((CLUSTERS, CLUSTERS), 0) < iota((CLUSTERS, CLUSTERS), 1))
    sub = iota((16, CLUSTERS), 0)
    before = dot((pick(sub == 0, over_first) + pick(sub == 1, over_second)).astype(BF16), earlier)

    base_first = jnp.minimum(first, float(BASE))
    base_second = jnp.minimum(first + second, float(BASE)) - base_first
    first_row, second_row = as_row(base_first), as_row(base_second)

    step_column = across(jnp.where(lanes == chip, routes_ref[...].astype(F32), 0.0)).astype(jnp.int32)
    step_row = as_row(step_column.astype(F32)).astype(jnp.int32)
    plans = []
    ends = []
    for part, (begin, steps, _) in enumerate(PARTS):
        inside = in_part(step_column, part)
        ahead = (target < source) & in_part(step_row, part)
        first_total = down(pick(inside, base_first))
        second_total = down(pick(inside, base_second))
        last = part == LAST
        first_end = first_total + over_first_total if last else first_total
        first_start = across(pick(ahead, first_row))
        second_start = across(pick(ahead, second_row)) + first_end
        spread = step_column - begin == (iota((CHIPS, steps * BASE), 1) >> 4)
        head, tail, head_start, tail_start = [
            down(pick(spread, column)) for column in (base_first, base_second, first_start, second_start)
        ]
        slot = (iota((1, steps * BASE), 1) & (BASE - 1)).astype(F32)
        later = jnp.where(slot < head + tail, tail_start + (slot - head), -1.0)
        plan = jnp.where(slot < head, head_start + slot, later)
        held_end = first_end + second_total
        if last:
            over_row_of = jnp.where(over_second > 0.5, held_end + before[1:2], -1.0)
            over_row_of = jnp.where(over_first > 0.5, first_total + before[0:1], over_row_of)
            plan = jnp.concatenate([plan[:, : steps * BASE - CLUSTERS], over_row_of], axis=1)
            held_end = held_end + over_second_total
        plans.append(plan)
        ends.append((first_end, held_end))
    return plans, ends, faults


def kernel(
    x_hbm, assign_hbm, owner_hbm, count_hbm, index_hbm,
    out_ref, fault_ref,
    x_ref, assign_ref, owner_ref, count_ref, index_ref,
    send, got, own_over, line_over, send_over, got_over, pick_0, pick_1,
    earlier_ref, routes_ref, way_ref, keys, facts, sums, their_sums, back, returned,
    load_sem, send_sem, recv_sem,
):
    grp, blk = lax.axis_index("grp"), lax.axis_index("blk")
    my_x, my_y, my_z, core = grp // 4, grp % 4, blk // 2, blk % 2
    my_chip = grp * 4 + my_z
    picks = (pick_0, pick_1)
    along_x = [((my_x + d) % 4) * 4 for d in range(4)]
    along_y = [(my_y + d) % 4 for d in range(4)]
    along_z = [((my_z + d) % 4) * 2 + core for d in range(4)]
    other_core = {"grp": grp, "blk": my_z * 2 + (1 - core)}

    def device_at(step, sign):
        dx, dy, dz = [(sign * d) % 4 for d in ORDER[step]]
        return {"grp": along_x[dx] + along_y[dy], "blk": along_z[dz]}

    def remote(source, target, number, device):
        return pltpu.make_async_remote_copy(
            src_ref=source,
            dst_ref=target,
            send_sem=send_sem.at[number],
            recv_sem=recv_sem.at[number],
            device_id=device,
            device_id_type=pl.DeviceIdType.MESH,
        )

    def await_blocks(ref, number, semaphore):
        block = ref.at[pl.ds(0, number)]
        pltpu.make_async_copy(block, block, semaphore).wait()

    LINE, OVER, FACTS, SUMS, BACK, SWAP, PART = 0, 1, 2, 3, 4, 5, 7
    messages = [min(begin + steps, SELF) - begin for begin, steps, _ in PARTS]

    loads = [
        pltpu.make_async_copy(source, target, load_sem.at[number])
        for number, (source, target) in enumerate(
            (
                (assign_hbm, assign_ref),
                (owner_hbm, owner_ref),
                (count_hbm, count_ref),
                (index_hbm, index_ref),
                (x_hbm, x_ref),
            )
        )
    ]
    for load in loads:
        load.start()
    barrier = pltpu.get_barrier_semaphore()
    for device in [device_at(step, 1) for step in range(SELF)] + [other_core]:
        pl.semaphore_signal(barrier, inc=1, device_id=device, device_id_type=pl.DeviceIdType.MESH)
    lane = iota((1, CLUSTERS), 1)
    chip_step = step_to((lane >> 4) - my_x, ((lane >> 2) & 3) - my_y, (lane & 3) - my_z).astype(F32)
    earlier_ref[...] = onehot(iota((ROWS, ROWS), 0) < iota((ROWS, ROWS), 1))
    for load in loads[:-1]:
        load.wait()

    rank, count_column = rank_groups(count_ref)
    group, chip, step_of, slot, place_counts = place_documents(assign_ref, owner_ref, rank, earlier_ref, chip_step)
    in_base = slot < BASE
    send_slot = jnp.where(in_base, step_of * BASE + slot, -1)
    loads[-1].wait()

    def pack(first, stop):
        slots = iota(((stop - first) * BASE, ROWS), 0) + first * BASE
        rows = dot(onehot(slots == send_slot), x_ref[...]).astype(BF16)
        send[pl.ds(first, stop - first)] = rows.reshape(stop - first, BASE, WIDTH)

    def post(first, stop):
        for step in range(first, min(stop, SELF)):
            number = max(part for part in range(len(PARTS)) if PARTS[part][0] <= step)
            remote(send.at[step], got.at[step], PART + number, device_at(step, 1)).start()

    place_counts_16 = place_counts + jnp.zeros((16, CLUSTERS), F32)
    own_excess = excess(dot(place_counts_16.astype(BF16), chip_places())[0:1])
    eye = iota((CHIPS, CLUSTERS), 0) == iota((CHIPS, CLUSTERS), 1)
    excess_column = across(pick(eye, own_excess))
    over_slot = down(pick(iota((CHIPS, ROWS), 0) < chip, excess_column)).astype(jnp.int32) + (slot - BASE)
    over_slot = jnp.where(in_base, -1, over_slot)
    row = iota((BASE, CLUSTERS), 0)
    own_over[:, :WIDTH] = dot(onehot(iota((BASE, ROWS), 0) == over_slot), x_ref[...]).astype(BF16)
    own_over[:, WIDTH:] = (pick(row == 0, place_counts) + pick(row == 1, rank)).astype(BF16)
    line_over[my_z] = own_over[...]
    sublane = iota((LINES * 2 * POOL, 1), 0)
    way = sublane >> 4
    to_chip = ((my_x + (way >> 2)) & 3) * 16 + ((my_y + way) & 3) * 4 + my_z
    way_ref[...] = onehot(iota((LINES * 2 * POOL, CLUSTERS), 1) == to_chip)
    pack(0, 16)
    pl.semaphore_wait(barrier, CHIPS)
    for d in range(1, DEPTH):
        remote(own_over, line_over.at[my_z], LINE, {"grp": grp, "blk": along_z[d]}).start()
    post(0, 16)

    await_blocks(line_over, DEPTH - 1, recv_sem.at[LINE])
    line_counts = [line_over[d, 0:1, WIDTH:].astype(F32) for d in range(DEPTH)]
    line_ranks = [line_over[d, 1:2, WIDTH:].astype(F32) for d in range(DEPTH)]
    row = iota((2 * POOL, CLUSTERS), 0)
    told = jnp.zeros((2 * POOL, CLUSTERS), F32)
    for d in range(DEPTH):
        told = told + pick(row == d, line_counts[d]) + pick(row == DEPTH + d, line_ranks[d])
    told = told.astype(BF16)
    over = excess(dot(told, chip_places()))[0:DEPTH]
    ahead = dot(over.astype(BF16), onehot(iota((CLUSTERS, CLUSTERS), 0) < iota((CLUSTERS, CLUSTERS), 1)))
    before = [jnp.zeros((1, CLUSTERS), F32)]
    for d in range(DEPTH - 1):
        before.append(before[-1] + over[d : d + 1])
    before = jnp.concatenate(before, axis=0)
    before_mine = down(pick(iota((DEPTH, 1), 0) == my_z, before))
    known = jnp.concatenate([over, ahead, before, jnp.zeros((DEPTH, CLUSTERS), F32)], axis=0).astype(BF16)
    known = dot_rows(way_ref[...], known)
    entry = iota((LINES * 2 * POOL, DEPTH * BASE), 1)

    def of_depth(kind):
        values = known[:, kind * DEPTH : kind * DEPTH + 1]
        for d in range(1, DEPTH):
            values = jnp.where((entry >> 4) == d, known[:, kind * DEPTH + d : kind * DEPTH + d + 1], values)
        return values

    offset = (entry & (BASE - 1)).astype(F32) - of_depth(1)
    position = jnp.where((offset >= 0.0) & (offset < of_depth(0)), offset + of_depth(2), -1.0)
    wanted = (sublane & (2 * POOL - 1)).astype(F32)
    blocks = line_over[:, :, :WIDTH].reshape(DEPTH * BASE, WIDTH)
    left = dot(onehot((wanted == position) & (wanted < POOL)), blocks[:, :HALF])
    right = dot(onehot((wanted - POOL == position) & (wanted >= POOL)), blocks[:, HALF:])
    send_over[:, :, :HALF] = (left + right).astype(BF16).reshape(LINES, 2 * POOL, HALF)
    for d in range(LINES):
        send_over[d, :, HALF:] = told
    got_over[grp] = send_over[0]
    for d in range(1, LINES):
        device = {"grp": along_x[d // 4] + along_y[d % 4], "blk": blk}
        remote(send_over.at[d], got_over.at[grp], OVER, device).start()
    pack(16, 40)
    post(16, 40)
    pack(40, CHIPS)
    post(40, CHIPS)
    got[SELF] = send[SELF]
    to_chip, sender = iota((CHIPS, CLUSTERS), 1), iota((CHIPS, CLUSTERS), 0)
    routes_ref[...] = step_to(
        (to_chip >> 4) - (sender >> 4), ((to_chip >> 2) & 3) - ((sender >> 2) & 3), (to_chip & 3) - (sender & 3)
    )
    missing = missing_documents(index_ref, count_column, group)

    await_blocks(got_over, LINES - 1, recv_sem.at[OVER])
    told = got_over[:, :, HALF:].astype(F32)
    counts = told[:, 0:DEPTH].reshape(CHIPS, CLUSTERS)
    ranks = told[:, DEPTH : 2 * DEPTH].reshape(CHIPS, CLUSTERS)
    plans, ends, faults = receive_plan(counts, ranks, rank, my_x, my_y, my_z, routes_ref)

    row = iota((8, 128), 0)
    told = pick(row == 6, rank) + pick(row == 7, missing)
    for part, (first_end, held_end) in enumerate(ends):
        told = told + pick(row == part, first_end) + pick(row == 2 + part, held_end)
        picks[part][...] = onehot(iota(picks[part].shape, 0).astype(F32) == plans[part])
    facts[0] = told
    swap_facts = remote(facts.at[0], facts.at[1], FACTS, other_core)
    swap_facts.start()

    best = [jnp.full((1, room), -1.0, F32) for _, _, room in PARTS]
    key_kinds = []
    query_kinds = []
    totals = [jnp.zeros((1, WIDTH), F32), jnp.zeros((1, WIDTH), F32)]
    swaps = []

    def add_kinds(first, held, room):
        number = iota((room, 1), 0).astype(F32)
        key_kinds.append(jnp.where(number < first, 0.0, jnp.where(number < held, 1.0, 2.0)))

    for (first_end, held_end), (_, _, room) in zip(ends, PARTS):
        add_kinds(first_end, held_end, room)
        query_kinds.append(jnp.where(iota((1, room), 1).astype(F32) < first_end, 0.0, 1.0))

    def compare(first_key, last_key, part, more=0):
        borders = (*STARTS, *(HELD + start for start in STARTS), 2 * HELD)
        begin, stop = borders[first_key], borders[last_key + 1]
        start, room = STARTS[part], PARTS[part][2]
        scores = dot_rows(keys[begin : stop + more], keys[start : start + room])
        rest, scores = scores[stop - begin :], scores[: stop - begin]
        kind = jnp.concatenate(key_kinds[first_key : last_key + 1], axis=0)
        matched = kind == query_kinds[part]
        if begin < start + room and start < stop:
            matched = matched & (iota(kind.shape, 0) + (begin - start) != iota((1, room), 1))
        best[part] = jnp.maximum(best[part], jnp.max(jnp.where(matched, scores, -1.0), axis=0, keepdims=True))
        return rest

    def arrive(part):
        begin, steps, room = PARTS[part]
        await_blocks(got, messages[part], recv_sem.at[PART + part])
        rows = dot(picks[part][...], got[pl.ds(begin, steps)].reshape(steps * BASE, WIDTH))
        unit = rows * lax.rsqrt(across(rows * rows) + EPSILON)
        keys[pl.ds(STARTS[part], room)] = unit.astype(BF16)
        swap = remote(
            keys.at[pl.ds(STARTS[part], room)], keys.at[pl.ds(HELD + STARTS[part], room)], SWAP + part, other_core
        )
        swap.start()
        swaps.append(swap)
        is_first = iota((room, 1), 0).astype(F32) < ends[part][0]
        totals[0] = totals[0] + down(pick(is_first, unit))
        totals[1] = totals[1] + down(jnp.where(is_first, 0.0, unit))

    arrive(0)
    fault = faults()
    compare(0, 0, 0)
    swap_facts.wait()
    their_told = facts[1]
    for part, (_, _, room) in enumerate(PARTS):
        add_kinds(their_told[part : part + 1, 0:1], their_told[2 + part : 3 + part, 0:1], room)
    half_rows = got_over[:, :, :HALF].reshape(LINES * 2 * POOL, HALF)
    shape = (LINES * POOL, LINES * 2 * POOL)
    to, at = iota(shape, 0), iota(shape, 1)
    same = ((to >> 3) == (at >> 4)) & ((to & 7) == (at & 7))
    left = dot(onehot(same & ((at & POOL) == 0)), half_rows)
    right = dot(onehot(same & ((at & POOL) != 0)), half_rows)
    whole = jnp.concatenate([left, right], axis=1).astype(BF16)
    got[pl.ds(CHIPS, TOTAL - CHIPS)] = whole.reshape(TOTAL - CHIPS, BASE, WIDTH)
    swaps[0].wait()
    compare(2, 2, 0)

    arrive(1)
    row = iota((8, WIDTH), 0)
    sums[...] = pick(row == 0, totals[0]) + pick(row == 1, totals[1]) + pick(row == 2, fault)
    swap_sums = remote(sums, their_sums, SUMS, other_core)
    swap_sums.start()
    compare(0, 2, 1)
    compare(1, 1, 0)

    swap_sums.wait()
    total = pick(row < 2, sums[...] + their_sums[...])
    keys[pl.ds(2 * HELD, 16)] = jnp.concatenate(halves(total), axis=0).astype(BF16)
    scale = lax.rsqrt(across(total * total) + EPSILON)
    swaps[1].wait()
    near = [compare(3, 3, part, 16) for part in range(len(PARTS))]
    near = [(some[0:8] + some[8:16]) * scale for some in near]

    poison = missing + their_told[7:8, 1:2] > 0.5
    tiles = CHIPS * BASE // 128
    for part, (begin, steps, room) in enumerate(PARTS):
        row = iota((8, room), 0)
        query_number = iota((1, room), 1).astype(F32)
        some = jnp.where(query_number < ends[part][0], near[part][0:1], near[part][1:2])
        values = jnp.zeros((8, room), F32)
        for number, term in enumerate(halves(best[part]) + halves(some)):
            values = jnp.where(row == number, term, values)
        out = dot(values.astype(BF16), picks[part][...])
        for kind in range(2):
            line = out[2 * kind : 2 * kind + 1] + out[2 * kind + 1 : 2 * kind + 2]
            line = jnp.where(poison, NONE, line)
            for tile in range(steps * BASE // 128):
                piece = line[:, tile * 128 : (tile + 1) * 128]
                to = begin * BASE // 128 + tile
                if to < tiles:
                    back[to, kind : kind + 1, :] = piece
                else:
                    for each in range(tiles):
                        back[each, 2 + kind : 3 + kind, :] = piece
    returned[SELF] = back[SELF // 8]
    for step in range(SELF):
        remote(back.at[step // 8], returned.at[step], BACK, device_at(step, -1)).start()

    differ = across(jnp.where(their_told[6:7] != rank, 1.0, 0.0))
    fault = fault + their_sums[2:3, 0:1] + differ
    chosen = onehot(iota((CHIPS, ROWS), 0) == step_of)
    sub = iota((128, ROWS), 0)
    at_base = (sub == (step_of & 7) * BASE + slot) & in_base
    before_column = across(pick(eye, before_mine))
    line_slot = down(pick(iota((CHIPS, ROWS), 0) == chip, before_column)).astype(jnp.int32)
    at_over = (sub == grp * POOL + line_slot + (slot - BASE)) & (~in_base)

    await_blocks(returned, CHIPS - 1, recv_sem.at[BACK])
    found = []
    for number in range(4):
        line = returned[:, number, :]
        if number == 0:
            poisoned = across(down(jnp.where(line > 0.5 * NONE, 1.0, 0.0)))
            fault_ref[...] = jnp.where(fault + poisoned > 0.5, 1, 0) + jnp.zeros((1, 128), jnp.int32)
        terms = jnp.concatenate(halves(line), axis=1).astype(BF16)
        out = lax.dot_general(terms, chosen, (((0,), (0,)), ((), ())), preferred_element_type=F32)
        found.append(out[0:128] + out[128:256])
    out_ref[0:1] = down(pick(at_base, found[0]) + pick(at_over, found[2]))
    out_ref[1:2] = down(pick(at_base, found[1]) + pick(at_over, found[3]))

    await_blocks(line_over, DEPTH - 1, send_sem.at[LINE])
    await_blocks(got_over, LINES - 1, send_sem.at[OVER])
    await_blocks(returned, CHIPS - 1, send_sem.at[BACK])
    for part in range(len(PARTS)):
        await_blocks(got, messages[part], send_sem.at[PART + part])


def routed(embeddings, assign, owner, send_count, send_index):
    return pl.pallas_call(
        kernel,
        out_shape=(
            jax.ShapeDtypeStruct((2, ROWS), F32),
            jax.ShapeDtypeStruct((1, 128), jnp.int32),
        ),
        in_specs=[pl.BlockSpec(memory_space=pl.ANY)] * 5,
        out_specs=(pl.BlockSpec(memory_space=pltpu.VMEM),) * 2,
        scratch_shapes=[
            pltpu.VMEM((ROWS, WIDTH), BF16),
            pltpu.VMEM((1, ROWS), jnp.int32),
            pltpu.VMEM((1, CLUSTERS), jnp.int32),
            pltpu.VMEM((1, GROUPS), jnp.int32),
            pltpu.VMEM((GROUPS, CAP), jnp.int32),
            pltpu.VMEM((CHIPS, BASE, WIDTH), BF16),
            pltpu.VMEM((TOTAL, BASE, WIDTH), BF16),
            pltpu.VMEM((BASE, WIDTH + CLUSTERS), BF16),
            pltpu.VMEM((DEPTH, BASE, WIDTH + CLUSTERS), BF16),
            pltpu.VMEM((LINES, 2 * POOL, HALF + CLUSTERS), BF16),
            pltpu.VMEM((LINES, 2 * POOL, HALF + CLUSTERS), BF16),
            *[pltpu.VMEM((room, steps * BASE), BF16) for _, steps, room in PARTS],
            pltpu.VMEM((ROWS, ROWS), BF16),
            pltpu.VMEM((CHIPS, CLUSTERS), jnp.int32),
            pltpu.VMEM((LINES * 2 * POOL, CLUSTERS), BF16),
            pltpu.VMEM((2 * HELD + 16, WIDTH), BF16),
            pltpu.VMEM((2, 8, 128), F32),
            pltpu.VMEM((8, WIDTH), F32),
            pltpu.VMEM((8, WIDTH), F32),
            pltpu.VMEM((CHIPS * BASE // 128, 4, 128), F32),
            pltpu.VMEM((CHIPS, 4, 128), F32),
            pltpu.SemaphoreType.DMA((5,)),
            pltpu.SemaphoreType.DMA((9,)),
            pltpu.SemaphoreType.DMA((9,)),
        ],
        compiler_params=pltpu.CompilerParams(
            collective_id=0, has_side_effects=True, vmem_limit_bytes=48 * 1024 * 1024
        ),
    )(
        embeddings,
        assign.reshape(1, ROWS),
        owner.reshape(1, CLUSTERS),
        send_count,
        send_index[0],
    )


def body(embeddings, assign, owner, send_count, send_index):
    arguments = (embeddings, assign, owner, send_count, send_index)
    results, fault = routed(*arguments)
    results = lax.cond(fault[0, 0] != 0, lambda: jnp.stack(general(*arguments)), lambda: results)
    return results[0], results[1]


def solution(mesh):
    placed = (
        P(("grp", "blk"), None),
        P(("grp", "blk")),
        P(),
        P(("grp", "blk"), None),
        P(("grp", "blk"), None, None),
    )
    return jax.shard_map(
        body,
        mesh=mesh,
        in_specs=placed,
        out_specs=(P(("grp", "blk")), P(("grp", "blk"))),
        check_vma=False,
    )
```

```python
import functools

import jax
import jax.numpy as jnp
from jax import lax
from jax.experimental import pallas as pl
from jax.experimental.pallas import tpu as pltpu
from jax.sharding import PartitionSpec as P

EPSILON = 1e-06
F32 = jnp.float32
BF16 = jnp.bfloat16

CHIPS = 64
ROWS = 512
WIDTH = 768
CLUSTERS = 128
GROUPS = 16
CAP = 64
BASE = 16
HALF = WIDTH // 2
LINES = 16
DEPTH = 4
POOL = 8
PARTS = ((0, 40, 400), (40, 32, 256))
TOTAL = 72
HELD = 656
STARTS = (0, 400)
LAST = len(PARTS) - 1
NONE = 1e30


def normalize(values):
    widened = values.astype(F32)
    return widened * lax.rsqrt(jnp.sum(widened * widened, axis=1, keepdims=True) + EPSILON)


def general(embeddings, assign, owner, send_count, send_index):
    rows_local = embeddings.shape[0]
    feature_width = embeddings.shape[1]
    groups = lax.axis_size("grp")
    clusters = owner.shape[0]
    capacity = send_index.shape[2]
    slot_total = groups * capacity
    unit_rows = normalize(embeddings)
    unit_low = unit_rows.astype(BF16)
    counts = send_count[0]
    listed = send_index[0]
    live_slot = jnp.arange(capacity, dtype=jnp.int32)[None, :] < counts[:, None]
    listed_cluster = assign[listed]
    owned_here = owner[listed_cluster] == jnp.arange(groups, dtype=jnp.int32)[:, None]
    kept_slot = live_slot & owned_here
    out_cluster = jnp.where(kept_slot, listed_cluster, -1)
    out_tag = jnp.where(kept_slot, lax.axis_index(("grp", "blk")) * rows_local + listed, -1)
    out_vector = unit_low[listed.reshape(-1)].reshape(groups, capacity, feature_width)
    got_vector, got_cluster, got_tag = (
        lax.all_to_all(out_vector, "grp", split_axis=0, concat_axis=0, tiled=True),
        lax.all_to_all(out_cluster, "grp", split_axis=0, concat_axis=0, tiled=True),
        lax.all_to_all(out_tag, "grp", split_axis=0, concat_axis=0, tiled=True),
    )
    own_vector = got_vector.reshape(slot_total, feature_width)
    own_cluster = got_cluster.reshape(slot_total)
    own_tag = got_tag.reshape(slot_total)

    def tile_best(current, shard_piece):
        other_vector, other_cluster, other_tag = shard_piece
        scores = jnp.einsum("id,jd->ij", own_vector, other_vector, preferred_element_type=F32)
        matched = (
            (own_cluster[:, None] == other_cluster[None, :])
            & (other_cluster[None, :] >= 0)
            & (own_tag[:, None] != other_tag[None, :])
        )
        return jnp.maximum(current, jnp.max(jnp.where(matched, scores, -1.0), axis=1))

    other_vector = lax.all_gather(own_vector, "blk", axis=0, tiled=True)
    other_cluster = lax.all_gather(own_cluster, "blk", axis=0, tiled=True)
    other_tag = lax.all_gather(own_tag, "blk", axis=0, tiled=True)
    length = other_vector.shape[0]
    number = length // slot_total
    stacked = (
        other_vector.reshape(number, slot_total, feature_width),
        other_cluster.reshape(number, slot_total),
        other_tag.reshape(number, slot_total),
    )

    def scan_step(carry, single):
        return (tile_best(carry, single), None)

    result, unused = lax.scan(scan_step, jnp.full((slot_total,), -1.0, F32), stacked)
    target = jnp.where(live_slot, listed, rows_local).reshape(-1)
    partial_sum = jax.ops.segment_sum(unit_rows, assign, num_segments=clusters)
    centre = normalize(lax.psum(partial_sum, ("grp", "blk")))
    nearness = jnp.sum(unit_low.astype(F32) * centre[assign], axis=1)
    returned = lax.all_to_all(
        result.reshape(groups, capacity), "grp", split_axis=0, concat_axis=0, tiled=True
    )
    has_entry = (
        jnp.zeros((rows_local,), jnp.int32)
        .at[target]
        .max(kept_slot.astype(jnp.int32).reshape(-1), mode="drop")
    )
    centroid_cos = jnp.where(has_entry > 0, nearness, 0.0)
    max_sim = jnp.full((rows_local,), -1.0, F32).at[target].max(returned.reshape(-1), mode="drop")
    return (max_sim, centroid_cos)


def iota(shape, axis):
    return lax.broadcasted_iota(jnp.int32, shape, axis)


def down(values):
    return jnp.sum(values, axis=0, keepdims=True)


def across(values):
    return jnp.sum(values, axis=1, keepdims=True)


def pick(mask, values):
    return jnp.where(mask, values, 0.0)


def as_column(row):
    size = row.shape[1]
    return across(pick(iota((size, size), 0) == iota((size, size), 1), row))


def as_row(column):
    size = column.shape[0]
    return down(pick(iota((size, size), 0) == iota((size, size), 1), column))


def dot(a, b):
    return jnp.dot(a, b, preferred_element_type=F32)


def dot_rows(a, b):
    return lax.dot_general(a, b, (((1,), (1,)), ((), ())), preferred_element_type=F32)


def onehot(mask):
    return jnp.where(mask, 1.0, 0.0).astype(BF16)


def halves(values):
    first = values.astype(BF16).astype(F32)
    return first, (values - first).astype(BF16).astype(F32)


def rank_groups(count_ref):
    count_row = count_ref[...].astype(F32)
    count_column = as_column(count_row)
    sub, lane = iota((GROUPS, 128), 0), iota((GROUPS, 128), 1)
    count_lanes = down(pick(sub == lane, count_column))
    ahead = (count_column > count_lanes) | ((count_column == count_lanes) & (sub < lane))
    rank = down(jnp.where(ahead, 1.0, 0.0))
    return jnp.where(iota((1, 128), 1) < GROUPS, rank, 0.0), count_column


def place_documents(assign_ref, owner_ref, rank, earlier_ref, chip_step):
    member = iota((CLUSTERS, ROWS), 0) == assign_ref[...]
    member_low = onehot(member)
    before = down(pick(member, dot(member_low, earlier_ref[...])))
    count_column = across(jnp.where(member, 1.0, 0.0))
    owner_row = owner_ref[...].astype(F32)
    owner_column = as_column(owner_row)
    sub, lane = iota((CLUSTERS, CLUSTERS), 0), iota((CLUSTERS, CLUSTERS), 1)
    within = across(jnp.where((owner_column == owner_row) & (lane < sub), 1.0, 0.0))
    group_rank = across(pick(owner_column == lane.astype(F32), rank))
    place = group_rank * (CLUSTERS // GROUPS) + within
    chip = jnp.minimum(place, (CLUSTERS - 1) - place)
    count_row, place_row, chip_row = as_row(count_column), as_row(place), as_row(chip)
    opposite = down(pick((CLUSTERS - 1) - place == place_row, count_column))
    offset = jnp.where(place_row >= CHIPS, opposite, 0.0)
    step_row = down(pick(sub.astype(F32) == chip_row, as_column(chip_step)))
    row = iota((16, CLUSTERS), 0)
    told = pick(row == 0, owner_row) + pick(row == 1, chip_row) + pick(row == 2, step_row) + pick(row == 3, offset)
    told = dot(told.astype(BF16), member_low)
    place_counts = down(pick(place == lane.astype(F32), count_column))
    whole = told[1:4].astype(jnp.int32)
    return told[0:1], whole[0:1], whole[1:2], before.astype(jnp.int32) + whole[2:3], place_counts


def missing_documents(index_ref, count_column, group):
    listed = index_ref[...]
    live = iota((GROUPS, CAP), 1).astype(F32) < count_column
    eye = onehot(iota((CAP, CAP), 0) == iota((CAP, CAP), 1))
    high = dot_rows(eye, jnp.where(live, listed >> 4, 0).astype(F32).astype(BF16))
    low = dot_rows(eye, jnp.where(live, listed & 15, 0).astype(F32).astype(BF16))
    alive = dot_rows(eye, onehot(live))
    slots = jnp.where(alive > 0.5, high * 16.0 + low, -1.0)
    document = iota((1, ROWS), 1).astype(F32)
    lane = iota((CAP, GROUPS), 1)

    def count(g, hits):
        column = across(pick(lane == g, slots))
        wanted = jnp.where(group == g.astype(F32), document, -2.0)
        return hits + jnp.where(column == wanted, 1.0, 0.0)

    hits = lax.fori_loop(0, GROUPS, count, jnp.zeros((CAP, ROWS), F32))
    return across(jnp.where(down(hits) > 0.5, 0.0, 1.0))


def send_order():
    order = []
    for step in range(CHIPS):
        high, middle, low = step // 16, (step // 4) % 4, step % 4
        order.append((low, (middle + low) % 4, (high + middle + low) % 4))
    near = [shift for shift in order if sum(min(d, 4 - d) for d in shift) <= 1] + [(2, 0, 0)]
    near.sort(key=lambda shift: -sum(min(d, 4 - d) for d in shift))
    return [shift for shift in order if shift not in near] + near


ORDER = send_order()
SELF = CHIPS - 1


def step_to(dx, dy, dz):
    shift = (dx & 3) * 16 + (dy & 3) * 4 + (dz & 3)
    step = jnp.full(shift.shape, SELF, jnp.int32)
    for number, (x, y, z) in enumerate(ORDER[:SELF]):
        step = jnp.where(shift == x * 16 + y * 4 + z, number, step)
    return step


def in_part(step, part):
    begin, steps, _ = PARTS[part]
    return (step >= begin) & (step < begin + steps)


def chip_places():
    sub, lane = iota((CLUSTERS, CLUSTERS), 0), iota((CLUSTERS, CLUSTERS), 1)
    return onehot((sub == lane) | (sub == (CLUSTERS - 1) - lane))


def excess(totals):
    lane = iota(totals.shape, 1)
    return jnp.where(lane < CHIPS, jnp.maximum(totals - BASE, 0.0), 0.0)


def receive_plan(counts, ranks, rank, my_x, my_y, my_z, routes_ref):
    chip = my_x * 16 + my_y * 4 + my_z
    both = dot(counts.astype(BF16), chip_places())
    over = excess(both)
    lanes = iota((CHIPS, CLUSTERS), 1)
    sender = iota((CHIPS, 1), 0)
    source, target = iota((CHIPS, CHIPS), 0), iota((CHIPS, CHIPS), 1)

    same_line = (source >> 2) == (target >> 2)
    number = across(pick(lanes == chip, over))
    start = across(pick(same_line & (target < source), as_row(number)))

    def faults():
        differ = jnp.where(ranks != rank, 1.0, 0.0)
        differ = differ + jnp.where(dot(onehot(same_line), over.astype(BF16)) > POOL, 1.0, 0.0)
        based = jnp.where(lanes < CHIPS, jnp.minimum(both, float(BASE)), 0.0)
        fault = across(down(differ)) + down(jnp.where(across(over) > BASE, 1.0, 0.0))
        for part, (_, _, room) in enumerate(PARTS):
            held = down(pick(in_part(routes_ref[...], part), based))
            if part == LAST:
                held = held + down(over)
            fault = fault + across(jnp.where(held > room, 1.0, 0.0))
        return fault

    first = across(pick(lanes == chip, counts))
    second = across(pick(lanes == (CLUSTERS - 1) - chip, counts))
    place = (lanes & (POOL - 1)).astype(F32) - start
    mine = ((sender >> 2) == (lanes >> 3)) & (place >= 0.0) & (place < number)
    over_first = down(jnp.where(mine & (place + BASE < first), 1.0, 0.0))
    over_second = down(jnp.where(mine & (place + BASE >= first), 1.0, 0.0))
    over_first_total, over_second_total = across(over_first), across(over_second)
    earlier = onehot(iota((CLUSTERS, CLUSTERS), 0) < iota((CLUSTERS, CLUSTERS), 1))
    sub = iota((16, CLUSTERS), 0)
    before = dot((pick(sub == 0, over_first) + pick(sub == 1, over_second)).astype(BF16), earlier)

    base_first = jnp.minimum(first, float(BASE))
    base_second = jnp.minimum(first + second, float(BASE)) - base_first
    first_row, second_row = as_row(base_first), as_row(base_second)

    step_column = across(jnp.where(lanes == chip, routes_ref[...].astype(F32), 0.0)).astype(jnp.int32)
    step_row = as_row(step_column.astype(F32)).astype(jnp.int32)
    plans = []
    ends = []
    for part, (begin, steps, _) in enumerate(PARTS):
        inside = in_part(step_column, part)
        ahead = (target < source) & in_part(step_row, part)
        first_total = down(pick(inside, base_first))
        second_total = down(pick(inside, base_second))
        last = part == LAST
        first_end = first_total + over_first_total if last else first_total
        first_start = across(pick(ahead, first_row))
        second_start = across(pick(ahead, second_row)) + first_end
        spread = step_column - begin == (iota((CHIPS, steps * BASE), 1) >> 4)
        head, tail, head_start, tail_start = [
            down(pick(spread, column)) for column in (base_first, base_second, first_start, second_start)
        ]
        slot = (iota((1, steps * BASE), 1) & (BASE - 1)).astype(F32)
        later = jnp.where(slot < head + tail, tail_start + (slot - head), -1.0)
        plan = jnp.where(slot < head, head_start + slot, later)
        held_end = first_end + second_total
        if last:
            over_row_of = jnp.where(over_second > 0.5, held_end + before[1:2], -1.0)
            over_row_of = jnp.where(over_first > 0.5, first_total + before[0:1], over_row_of)
            plan = jnp.concatenate([plan[:, : steps * BASE - CLUSTERS], over_row_of], axis=1)
            held_end = held_end + over_second_total
        plans.append(plan)
        ends.append((first_end, held_end))
    return plans, ends, faults


def kernel(
    x_hbm, assign_hbm, owner_hbm, count_hbm, index_hbm,
    out_ref, fault_ref,
    x_ref, assign_ref, owner_ref, count_ref, index_ref,
    send, got, own_over, line_over, send_over, got_over, pick_0, pick_1,
    earlier_ref, routes_ref, way_ref, keys, facts, sums, their_sums, back, returned,
    load_sem, send_sem, recv_sem,
):
    grp, blk = lax.axis_index("grp"), lax.axis_index("blk")
    my_x, my_y, my_z, core = grp // 4, grp % 4, blk // 2, blk % 2
    my_chip = grp * 4 + my_z
    picks = (pick_0, pick_1)
    along_x = [((my_x + d) % 4) * 4 for d in range(4)]
    along_y = [(my_y + d) % 4 for d in range(4)]
    along_z = [((my_z + d) % 4) * 2 + core for d in range(4)]
    other_core = {"grp": grp, "blk": my_z * 2 + (1 - core)}

    def device_at(step, sign):
        dx, dy, dz = [(sign * d) % 4 for d in ORDER[step]]
        return {"grp": along_x[dx] + along_y[dy], "blk": along_z[dz]}

    def remote(source, target, number, device):
        return pltpu.make_async_remote_copy(
            src_ref=source,
            dst_ref=target,
            send_sem=send_sem.at[number],
            recv_sem=recv_sem.at[number],
            device_id=device,
            device_id_type=pl.DeviceIdType.MESH,
        )

    def await_blocks(ref, number, semaphore):
        block = ref.at[pl.ds(0, number)]
        pltpu.make_async_copy(block, block, semaphore).wait()

    LINE, OVER, FACTS, SUMS, BACK, SWAP, PART = 0, 1, 2, 3, 4, 5, 7
    messages = [min(begin + steps, SELF) - begin for begin, steps, _ in PARTS]

    loads = [
        pltpu.make_async_copy(source, target, load_sem.at[number])
        for number, (source, target) in enumerate(
            (
                (assign_hbm, assign_ref),
                (owner_hbm, owner_ref),
                (count_hbm, count_ref),
                (index_hbm, index_ref),
                (x_hbm, x_ref),
            )
        )
    ]
    for load in loads:
        load.start()
    barrier = pltpu.get_barrier_semaphore()
    for device in [device_at(step, 1) for step in range(SELF)] + [other_core]:
        pl.semaphore_signal(barrier, inc=1, device_id=device, device_id_type=pl.DeviceIdType.MESH)
    lane = iota((1, CLUSTERS), 1)
    chip_step = step_to((lane >> 4) - my_x, ((lane >> 2) & 3) - my_y, (lane & 3) - my_z).astype(F32)
    earlier_ref[...] = onehot(iota((ROWS, ROWS), 0) < iota((ROWS, ROWS), 1))
    for load in loads[:-1]:
        load.wait()

    rank, count_column = rank_groups(count_ref)
    group, chip, step_of, slot, place_counts = place_documents(assign_ref, owner_ref, rank, earlier_ref, chip_step)
    in_base = slot < BASE
    send_slot = jnp.where(in_base, step_of * BASE + slot, -1)
    loads[-1].wait()

    def pack(first, stop):
        slots = iota(((stop - first) * BASE, ROWS), 0) + first * BASE
        rows = dot(onehot(slots == send_slot), x_ref[...]).astype(BF16)
        send[pl.ds(first, stop - first)] = rows.reshape(stop - first, BASE, WIDTH)

    def post(first, stop):
        for step in range(first, min(stop, SELF)):
            number = max(part for part in range(len(PARTS)) if PARTS[part][0] <= step)
            remote(send.at[step], got.at[step], PART + number, device_at(step, 1)).start()

    place_counts_16 = place_counts + jnp.zeros((16, CLUSTERS), F32)
    own_excess = excess(dot(place_counts_16.astype(BF16), chip_places())[0:1])
    eye = iota((CHIPS, CLUSTERS), 0) == iota((CHIPS, CLUSTERS), 1)
    excess_column = across(pick(eye, own_excess))
    over_slot = down(pick(iota((CHIPS, ROWS), 0) < chip, excess_column)).astype(jnp.int32) + (slot - BASE)
    over_slot = jnp.where(in_base, -1, over_slot)
    row = iota((BASE, CLUSTERS), 0)
    own_over[:, :WIDTH] = dot(onehot(iota((BASE, ROWS), 0) == over_slot), x_ref[...]).astype(BF16)
    own_over[:, WIDTH:] = (pick(row == 0, place_counts) + pick(row == 1, rank)).astype(BF16)
    line_over[my_z] = own_over[...]
    sublane = iota((LINES * 2 * POOL, 1), 0)
    way = sublane >> 4
    to_chip = ((my_x + (way >> 2)) & 3) * 16 + ((my_y + way) & 3) * 4 + my_z
    way_ref[...] = onehot(iota((LINES * 2 * POOL, CLUSTERS), 1) == to_chip)
    pack(0, 16)
    pl.semaphore_wait(barrier, CHIPS)
    for d in range(1, DEPTH):
        remote(own_over, line_over.at[my_z], LINE, {"grp": grp, "blk": along_z[d]}).start()
    post(0, 16)
    pack(16, 24)
    post(16, 24)

    await_blocks(line_over, DEPTH - 1, recv_sem.at[LINE])
    line_counts = [line_over[d, 0:1, WIDTH:].astype(F32) for d in range(DEPTH)]
    line_ranks = [line_over[d, 1:2, WIDTH:].astype(F32) for d in range(DEPTH)]
    row = iota((2 * POOL, CLUSTERS), 0)
    told = jnp.zeros((2 * POOL, CLUSTERS), F32)
    for d in range(DEPTH):
        told = told + pick(row == d, line_counts[d]) + pick(row == DEPTH + d, line_ranks[d])
    told = told.astype(BF16)
    over = excess(dot(told, chip_places()))[0:DEPTH]
    ahead = dot(over.astype(BF16), onehot(iota((CLUSTERS, CLUSTERS), 0) < iota((CLUSTERS, CLUSTERS), 1)))
    before = [jnp.zeros((1, CLUSTERS), F32)]
    for d in range(DEPTH - 1):
        before.append(before[-1] + over[d : d + 1])
    before = jnp.concatenate(before, axis=0)
    before_mine = down(pick(iota((DEPTH, 1), 0) == my_z, before))
    known = jnp.concatenate([over, ahead, before, jnp.zeros((DEPTH, CLUSTERS), F32)], axis=0).astype(BF16)
    known = dot_rows(way_ref[...], known)
    entry = iota((LINES * 2 * POOL, DEPTH * BASE), 1)

    def of_depth(kind):
        values = known[:, kind * DEPTH : kind * DEPTH + 1]
        for d in range(1, DEPTH):
            values = jnp.where((entry >> 4) == d, known[:, kind * DEPTH + d : kind * DEPTH + d + 1], values)
        return values

    offset = (entry & (BASE - 1)).astype(F32) - of_depth(1)
    position = jnp.where((offset >= 0.0) & (offset < of_depth(0)), offset + of_depth(2), -1.0)
    wanted = (sublane & (2 * POOL - 1)).astype(F32)
    blocks = line_over[:, :, :WIDTH].reshape(DEPTH * BASE, WIDTH)
    left = dot(onehot((wanted == position) & (wanted < POOL)), blocks[:, :HALF])
    right = dot(onehot((wanted - POOL == position) & (wanted >= POOL)), blocks[:, HALF:])
    send_over[:, :, :HALF] = (left + right).astype(BF16).reshape(LINES, 2 * POOL, HALF)
    for d in range(LINES):
        send_over[d, :, HALF:] = told
    got_over[grp] = send_over[0]
    for d in range(1, LINES):
        device = {"grp": along_x[d // 4] + along_y[d % 4], "blk": blk}
        remote(send_over.at[d], got_over.at[grp], OVER, device).start()
    pack(24, 48)
    post(24, 48)
    pack(48, CHIPS)
    post(48, CHIPS)
    got[SELF] = send[SELF]
    to_chip, sender = iota((CHIPS, CLUSTERS), 1), iota((CHIPS, CLUSTERS), 0)
    routes_ref[...] = step_to(
        (to_chip >> 4) - (sender >> 4), ((to_chip >> 2) & 3) - ((sender >> 2) & 3), (to_chip & 3) - (sender & 3)
    )
    missing = missing_documents(index_ref, count_column, group)

    await_blocks(got_over, LINES - 1, recv_sem.at[OVER])
    told = got_over[:, :, HALF:].astype(F32)
    counts = told[:, 0:DEPTH].reshape(CHIPS, CLUSTERS)
    ranks = told[:, DEPTH : 2 * DEPTH].reshape(CHIPS, CLUSTERS)
    plans, ends, faults = receive_plan(counts, ranks, rank, my_x, my_y, my_z, routes_ref)

    row = iota((8, 128), 0)
    told = pick(row == 6, rank) + pick(row == 7, missing)
    for part, (first_end, held_end) in enumerate(ends):
        told = told + pick(row == part, first_end) + pick(row == 2 + part, held_end)
        picks[part][...] = onehot(iota(picks[part].shape, 0).astype(F32) == plans[part])
    facts[0] = told
    swap_facts = remote(facts.at[0], facts.at[1], FACTS, other_core)
    swap_facts.start()

    best = [jnp.full((1, room), -1.0, F32) for _, _, room in PARTS]
    key_kinds = []
    query_kinds = []
    totals = [jnp.zeros((1, WIDTH), F32), jnp.zeros((1, WIDTH), F32)]
    swaps = []

    def add_kinds(first, held, room):
        number = iota((room, 1), 0).astype(F32)
        key_kinds.append(jnp.where(number < first, 0.0, jnp.where(number < held, 1.0, 2.0)))

    for (first_end, held_end), (_, _, room) in zip(ends, PARTS):
        add_kinds(first_end, held_end, room)
        query_kinds.append(jnp.where(iota((1, room), 1).astype(F32) < first_end, 0.0, 1.0))

    def compare(first_key, last_key, part, more=0):
        borders = (*STARTS, *(HELD + start for start in STARTS), 2 * HELD)
        begin, stop = borders[first_key], borders[last_key + 1]
        start, room = STARTS[part], PARTS[part][2]
        scores = dot_rows(keys[begin : stop + more], keys[start : start + room])
        rest, scores = scores[stop - begin :], scores[: stop - begin]
        kind = jnp.concatenate(key_kinds[first_key : last_key + 1], axis=0)
        matched = kind == query_kinds[part]
        if begin < start + room and start < stop:
            matched = matched & (iota(kind.shape, 0) + (begin - start) != iota((1, room), 1))
        best[part] = jnp.maximum(best[part], jnp.max(jnp.where(matched, scores, -1.0), axis=0, keepdims=True))
        return rest

    def arrive(part):
        begin, steps, room = PARTS[part]
        await_blocks(got, messages[part], recv_sem.at[PART + part])
        rows = dot(picks[part][...], got[pl.ds(begin, steps)].reshape(steps * BASE, WIDTH))
        unit = rows * lax.rsqrt(across(rows * rows) + EPSILON)
        keys[pl.ds(STARTS[part], room)] = unit.astype(BF16)
        swap = remote(
            keys.at[pl.ds(STARTS[part], room)], keys.at[pl.ds(HELD + STARTS[part], room)], SWAP + part, other_core
        )
        swap.start()
        swaps.append(swap)
        is_first = iota((room, 1), 0).astype(F32) < ends[part][0]
        totals[0] = totals[0] + down(pick(is_first, unit))
        totals[1] = totals[1] + down(jnp.where(is_first, 0.0, unit))

    arrive(0)
    fault = faults()
    compare(0, 0, 0)
    swap_facts.wait()
    their_told = facts[1]
    for part, (_, _, room) in enumerate(PARTS):
        add_kinds(their_told[part : part + 1, 0:1], their_told[2 + part : 3 + part, 0:1], room)
    half_rows = got_over[:, :, :HALF].reshape(LINES * 2 * POOL, HALF)
    shape = (LINES * POOL, LINES * 2 * POOL)
    to, at = iota(shape, 0), iota(shape, 1)
    same = ((to >> 3) == (at >> 4)) & ((to & 7) == (at & 7))
    left = dot(onehot(same & ((at & POOL) == 0)), half_rows)
    right = dot(onehot(same & ((at & POOL) != 0)), half_rows)
    whole = jnp.concatenate([left, right], axis=1).astype(BF16)
    got[pl.ds(CHIPS, TOTAL - CHIPS)] = whole.reshape(TOTAL - CHIPS, BASE, WIDTH)
    swaps[0].wait()
    compare(2, 2, 0)

    arrive(1)
    row = iota((8, WIDTH), 0)
    sums[...] = pick(row == 0, totals[0]) + pick(row == 1, totals[1]) + pick(row == 2, fault)
    swap_sums = remote(sums, their_sums, SUMS, other_core)
    swap_sums.start()
    compare(0, 2, 1)
    compare(1, 1, 0)

    swap_sums.wait()
    total = pick(row < 2, sums[...] + their_sums[...])
    keys[pl.ds(2 * HELD, 16)] = jnp.concatenate(halves(total), axis=0).astype(BF16)
    scale = lax.rsqrt(across(total * total) + EPSILON)
    swaps[1].wait()
    near = [compare(3, 3, part, 16) for part in range(len(PARTS))]
    near = [(some[0:8] + some[8:16]) * scale for some in near]

    poison = missing + their_told[7:8, 1:2] > 0.5
    tiles = CHIPS * BASE // 128
    for part, (begin, steps, room) in enumerate(PARTS):
        row = iota((8, room), 0)
        query_number = iota((1, room), 1).astype(F32)
        some = jnp.where(query_number < ends[part][0], near[part][0:1], near[part][1:2])
        values = jnp.zeros((8, room), F32)
        for number, term in enumerate(halves(best[part]) + halves(some)):
            values = jnp.where(row == number, term, values)
        out = dot(values.astype(BF16), picks[part][...])
        for kind in range(2):
            line = out[2 * kind : 2 * kind + 1] + out[2 * kind + 1 : 2 * kind + 2]
            line = jnp.where(poison, NONE, line)
            for tile in range(steps * BASE // 128):
                piece = line[:, tile * 128 : (tile + 1) * 128]
                to = begin * BASE // 128 + tile
                if to < tiles:
                    back[to, kind : kind + 1, :] = piece
                else:
                    for each in range(tiles):
                        back[each, 2 + kind : 3 + kind, :] = piece
    returned[SELF] = back[SELF // 8]
    for step in range(SELF):
        remote(back.at[step // 8], returned.at[step], BACK, device_at(step, -1)).start()

    differ = across(jnp.where(their_told[6:7] != rank, 1.0, 0.0))
    fault = fault + their_sums[2:3, 0:1] + differ
    chosen = onehot(iota((CHIPS, ROWS), 0) == step_of)
    sub = iota((128, ROWS), 0)
    at_base = (sub == (step_of & 7) * BASE + slot) & in_base
    before_column = across(pick(eye, before_mine))
    line_slot = down(pick(iota((CHIPS, ROWS), 0) == chip, before_column)).astype(jnp.int32)
    at_over = (sub == grp * POOL + line_slot + (slot - BASE)) & (~in_base)

    await_blocks(returned, CHIPS - 1, recv_sem.at[BACK])
    found = []
    for number in range(4):
        line = returned[:, number, :]
        if number == 0:
            poisoned = across(down(jnp.where(line > 0.5 * NONE, 1.0, 0.0)))
            fault_ref[...] = jnp.where(fault + poisoned > 0.5, 1, 0) + jnp.zeros((1, 128), jnp.int32)
        terms = jnp.concatenate(halves(line), axis=1).astype(BF16)
        out = lax.dot_general(terms, chosen, (((0,), (0,)), ((), ())), preferred_element_type=F32)
        found.append(out[0:128] + out[128:256])
    out_ref[0:1] = down(pick(at_base, found[0]) + pick(at_over, found[2]))
    out_ref[1:2] = down(pick(at_base, found[1]) + pick(at_over, found[3]))

    await_blocks(line_over, DEPTH - 1, send_sem.at[LINE])
    await_blocks(got_over, LINES - 1, send_sem.at[OVER])
    await_blocks(returned, CHIPS - 1, send_sem.at[BACK])
    for part in range(len(PARTS)):
        await_blocks(got, messages[part], send_sem.at[PART + part])


def routed(embeddings, assign, owner, send_count, send_index):
    return pl.pallas_call(
        kernel,
        out_shape=(
            jax.ShapeDtypeStruct((2, ROWS), F32),
            jax.ShapeDtypeStruct((1, 128), jnp.int32),
        ),
        in_specs=[pl.BlockSpec(memory_space=pl.ANY)] * 5,
        out_specs=(pl.BlockSpec(memory_space=pltpu.VMEM),) * 2,
        scratch_shapes=[
            pltpu.VMEM((ROWS, WIDTH), BF16),
            pltpu.VMEM((1, ROWS), jnp.int32),
            pltpu.VMEM((1, CLUSTERS), jnp.int32),
            pltpu.VMEM((1, GROUPS), jnp.int32),
            pltpu.VMEM((GROUPS, CAP), jnp.int32),
            pltpu.VMEM((CHIPS, BASE, WIDTH), BF16),
            pltpu.VMEM((TOTAL, BASE, WIDTH), BF16),
            pltpu.VMEM((BASE, WIDTH + CLUSTERS), BF16),
            pltpu.VMEM((DEPTH, BASE, WIDTH + CLUSTERS), BF16),
            pltpu.VMEM((LINES, 2 * POOL, HALF + CLUSTERS), BF16),
            pltpu.VMEM((LINES, 2 * POOL, HALF + CLUSTERS), BF16),
            *[pltpu.VMEM((room, steps * BASE), BF16) for _, steps, room in PARTS],
            pltpu.VMEM((ROWS, ROWS), BF16),
            pltpu.VMEM((CHIPS, CLUSTERS), jnp.int32),
            pltpu.VMEM((LINES * 2 * POOL, CLUSTERS), BF16),
            pltpu.VMEM((2 * HELD + 16, WIDTH), BF16),
            pltpu.VMEM((2, 8, 128), F32),
            pltpu.VMEM((8, WIDTH), F32),
            pltpu.VMEM((8, WIDTH), F32),
            pltpu.VMEM((CHIPS * BASE // 128, 4, 128), F32),
            pltpu.VMEM((CHIPS, 4, 128), F32),
            pltpu.SemaphoreType.DMA((5,)),
            pltpu.SemaphoreType.DMA((9,)),
            pltpu.SemaphoreType.DMA((9,)),
        ],
        compiler_params=pltpu.CompilerParams(
            collective_id=0, has_side_effects=True, vmem_limit_bytes=48 * 1024 * 1024
        ),
    )(
        embeddings,
        assign.reshape(1, ROWS),
        owner.reshape(1, CLUSTERS),
        send_count,
        send_index[0],
    )


def body(embeddings, assign, owner, send_count, send_index):
    arguments = (embeddings, assign, owner, send_count, send_index)
    results, fault = routed(*arguments)
    results = lax.cond(fault[0, 0] != 0, lambda: jnp.stack(general(*arguments)), lambda: results)
    return results[0], results[1]


def solution(mesh):
    placed = (
        P(("grp", "blk"), None),
        P(("grp", "blk")),
        P(),
        P(("grp", "blk"), None),
        P(("grp", "blk"), None, None),
    )
    return jax.shard_map(
        body,
        mesh=mesh,
        in_specs=placed,
        out_specs=(P(("grp", "blk")), P(("grp", "blk"))),
        check_vma=False,
    )
```

```python
import functools

import jax
import jax.numpy as jnp
from jax import lax
from jax.experimental import pallas as pl
from jax.experimental.pallas import tpu as pltpu
from jax.sharding import PartitionSpec as P

EPSILON = 1e-06
F32 = jnp.float32
BF16 = jnp.bfloat16

CHIPS = 64
ROWS = 512
WIDTH = 768
CLUSTERS = 128
GROUPS = 16
CAP = 64
BASE = 16
HALF = WIDTH // 2
LINES = 16
DEPTH = 4
POOL = 8
PARTS = ((0, 48, 464), (48, 24, 176))
TOTAL = 72
HELD = 640
STARTS = (0, 464)
LAST = len(PARTS) - 1
NONE = 1e30


def normalize(values):
    widened = values.astype(F32)
    return widened * lax.rsqrt(jnp.sum(widened * widened, axis=1, keepdims=True) + EPSILON)


def general(embeddings, assign, owner, send_count, send_index):
    rows_local = embeddings.shape[0]
    feature_width = embeddings.shape[1]
    groups = lax.axis_size("grp")
    clusters = owner.shape[0]
    capacity = send_index.shape[2]
    slot_total = groups * capacity
    unit_rows = normalize(embeddings)
    unit_low = unit_rows.astype(BF16)
    counts = send_count[0]
    listed = send_index[0]
    live_slot = jnp.arange(capacity, dtype=jnp.int32)[None, :] < counts[:, None]
    listed_cluster = assign[listed]
    owned_here = owner[listed_cluster] == jnp.arange(groups, dtype=jnp.int32)[:, None]
    kept_slot = live_slot & owned_here
    out_cluster = jnp.where(kept_slot, listed_cluster, -1)
    out_tag = jnp.where(kept_slot, lax.axis_index(("grp", "blk")) * rows_local + listed, -1)
    out_vector = unit_low[listed.reshape(-1)].reshape(groups, capacity, feature_width)
    got_vector, got_cluster, got_tag = (
        lax.all_to_all(out_vector, "grp", split_axis=0, concat_axis=0, tiled=True),
        lax.all_to_all(out_cluster, "grp", split_axis=0, concat_axis=0, tiled=True),
        lax.all_to_all(out_tag, "grp", split_axis=0, concat_axis=0, tiled=True),
    )
    own_vector = got_vector.reshape(slot_total, feature_width)
    own_cluster = got_cluster.reshape(slot_total)
    own_tag = got_tag.reshape(slot_total)

    def tile_best(current, shard_piece):
        other_vector, other_cluster, other_tag = shard_piece
        scores = jnp.einsum("id,jd->ij", own_vector, other_vector, preferred_element_type=F32)
        matched = (
            (own_cluster[:, None] == other_cluster[None, :])
            & (other_cluster[None, :] >= 0)
            & (own_tag[:, None] != other_tag[None, :])
        )
        return jnp.maximum(current, jnp.max(jnp.where(matched, scores, -1.0), axis=1))

    other_vector = lax.all_gather(own_vector, "blk", axis=0, tiled=True)
    other_cluster = lax.all_gather(own_cluster, "blk", axis=0, tiled=True)
    other_tag = lax.all_gather(own_tag, "blk", axis=0, tiled=True)
    length = other_vector.shape[0]
    number = length // slot_total
    stacked = (
        other_vector.reshape(number, slot_total, feature_width),
        other_cluster.reshape(number, slot_total),
        other_tag.reshape(number, slot_total),
    )

    def scan_step(carry, single):
        return (tile_best(carry, single), None)

    result, unused = lax.scan(scan_step, jnp.full((slot_total,), -1.0, F32), stacked)
    target = jnp.where(live_slot, listed, rows_local).reshape(-1)
    partial_sum = jax.ops.segment_sum(unit_rows, assign, num_segments=clusters)
    centre = normalize(lax.psum(partial_sum, ("grp", "blk")))
    nearness = jnp.sum(unit_low.astype(F32) * centre[assign], axis=1)
    returned = lax.all_to_all(
        result.reshape(groups, capacity), "grp", split_axis=0, concat_axis=0, tiled=True
    )
    has_entry = (
        jnp.zeros((rows_local,), jnp.int32)
        .at[target]
        .max(kept_slot.astype(jnp.int32).reshape(-1), mode="drop")
    )
    centroid_cos = jnp.where(has_entry > 0, nearness, 0.0)
    max_sim = jnp.full((rows_local,), -1.0, F32).at[target].max(returned.reshape(-1), mode="drop")
    return (max_sim, centroid_cos)


def iota(shape, axis):
    return lax.broadcasted_iota(jnp.int32, shape, axis)


def down(values):
    return jnp.sum(values, axis=0, keepdims=True)


def across(values):
    return jnp.sum(values, axis=1, keepdims=True)


def pick(mask, values):
    return jnp.where(mask, values, 0.0)


def as_column(row):
    size = row.shape[1]
    return across(pick(iota((size, size), 0) == iota((size, size), 1), row))


def as_row(column):
    size = column.shape[0]
    return down(pick(iota((size, size), 0) == iota((size, size), 1), column))


def dot(a, b):
    return jnp.dot(a, b, preferred_element_type=F32)


def dot_rows(a, b):
    return lax.dot_general(a, b, (((1,), (1,)), ((), ())), preferred_element_type=F32)


def onehot(mask):
    return jnp.where(mask, 1.0, 0.0).astype(BF16)


def halves(values):
    first = values.astype(BF16).astype(F32)
    return first, (values - first).astype(BF16).astype(F32)


def rank_groups(count_ref):
    count_row = count_ref[...].astype(F32)
    count_column = as_column(count_row)
    sub, lane = iota((GROUPS, 128), 0), iota((GROUPS, 128), 1)
    count_lanes = down(pick(sub == lane, count_column))
    ahead = (count_column > count_lanes) | ((count_column == count_lanes) & (sub < lane))
    rank = down(jnp.where(ahead, 1.0, 0.0))
    return jnp.where(iota((1, 128), 1) < GROUPS, rank, 0.0), count_column


def place_documents(assign_ref, owner_ref, rank, earlier_ref, chip_step):
    member = iota((CLUSTERS, ROWS), 0) == assign_ref[...]
    member_low = onehot(member)
    before = down(pick(member, dot(member_low, earlier_ref[...])))
    count_column = across(jnp.where(member, 1.0, 0.0))
    owner_row = owner_ref[...].astype(F32)
    owner_column = as_column(owner_row)
    sub, lane = iota((CLUSTERS, CLUSTERS), 0), iota((CLUSTERS, CLUSTERS), 1)
    within = across(jnp.where((owner_column == owner_row) & (lane < sub), 1.0, 0.0))
    group_rank = across(pick(owner_column == lane.astype(F32), rank))
    place = group_rank * (CLUSTERS // GROUPS) + within
    chip = jnp.minimum(place, (CLUSTERS - 1) - place)
    count_row, place_row, chip_row = as_row(count_column), as_row(place), as_row(chip)
    opposite = down(pick((CLUSTERS - 1) - place == place_row, count_column))
    offset = jnp.where(place_row >= CHIPS, opposite, 0.0)
    step_row = down(pick(sub.astype(F32) == chip_row, as_column(chip_step)))
    row = iota((16, CLUSTERS), 0)
    told = pick(row == 0, owner_row) + pick(row == 1, chip_row) + pick(row == 2, step_row) + pick(row == 3, offset)
    told = dot(told.astype(BF16), member_low)
    place_counts = down(pick(place == lane.astype(F32), count_column))
    whole = told[1:4].astype(jnp.int32)
    return told[0:1], whole[0:1], whole[1:2], before.astype(jnp.int32) + whole[2:3], place_counts


def missing_documents(index_ref, count_column, group):
    listed = index_ref[...]
    live = iota((GROUPS, CAP), 1).astype(F32) < count_column
    eye = onehot(iota((CAP, CAP), 0) == iota((CAP, CAP), 1))
    high = dot_rows(eye, jnp.where(live, listed >> 4, 0).astype(F32).astype(BF16))
    low = dot_rows(eye, jnp.where(live, listed & 15, 0).astype(F32).astype(BF16))
    alive = dot_rows(eye, onehot(live))
    slots = jnp.where(alive > 0.5, high * 16.0 + low, -1.0)
    document = iota((1, ROWS), 1).astype(F32)
    lane = iota((CAP, GROUPS), 1)

    def count(g, hits):
        column = across(pick(lane == g, slots))
        wanted = jnp.where(group == g.astype(F32), document, -2.0)
        return hits + jnp.where(column == wanted, 1.0, 0.0)

    hits = lax.fori_loop(0, GROUPS, count, jnp.zeros((CAP, ROWS), F32))
    return across(jnp.where(down(hits) > 0.5, 0.0, 1.0))


def send_order():
    order = []
    for step in range(CHIPS):
        high, middle, low = step // 16, (step // 4) % 4, step % 4
        order.append((low, (middle + low) % 4, (high + middle + low) % 4))
    near = [shift for shift in order if sum(min(d, 4 - d) for d in shift) <= 1] + [(2, 0, 0)]
    near.sort(key=lambda shift: -sum(min(d, 4 - d) for d in shift))
    return [shift for shift in order if shift not in near] + near


ORDER = send_order()
SELF = CHIPS - 1


def step_to(dx, dy, dz):
    shift = (dx & 3) * 16 + (dy & 3) * 4 + (dz & 3)
    step = jnp.full(shift.shape, SELF, jnp.int32)
    for number, (x, y, z) in enumerate(ORDER[:SELF]):
        step = jnp.where(shift == x * 16 + y * 4 + z, number, step)
    return step


def in_part(step, part):
    begin, steps, _ = PARTS[part]
    return (step >= begin) & (step < begin + steps)


def chip_places():
    sub, lane = iota((CLUSTERS, CLUSTERS), 0), iota((CLUSTERS, CLUSTERS), 1)
    return onehot((sub == lane) | (sub == (CLUSTERS - 1) - lane))


def excess(totals):
    lane = iota(totals.shape, 1)
    return jnp.where(lane < CHIPS, jnp.maximum(totals - BASE, 0.0), 0.0)


def receive_plan(counts, ranks, rank, my_x, my_y, my_z, routes_ref):
    chip = my_x * 16 + my_y * 4 + my_z
    both = dot(counts.astype(BF16), chip_places())
    over = excess(both)
    lanes = iota((CHIPS, CLUSTERS), 1)
    sender = iota((CHIPS, 1), 0)
    source, target = iota((CHIPS, CHIPS), 0), iota((CHIPS, CHIPS), 1)

    same_line = (source >> 2) == (target >> 2)
    number = across(pick(lanes == chip, over))
    start = across(pick(same_line & (target < source), as_row(number)))

    def faults():
        differ = jnp.where(ranks != rank, 1.0, 0.0)
        differ = differ + jnp.where(dot(onehot(same_line), over.astype(BF16)) > POOL, 1.0, 0.0)
        based = jnp.where(lanes < CHIPS, jnp.minimum(both, float(BASE)), 0.0)
        fault = across(down(differ)) + down(jnp.where(across(over) > BASE, 1.0, 0.0))
        for part, (_, _, room) in enumerate(PARTS):
            held = down(pick(in_part(routes_ref[...], part), based))
            if part == LAST:
                held = held + down(over)
            fault = fault + across(jnp.where(held > room, 1.0, 0.0))
        return fault

    first = across(pick(lanes == chip, counts))
    second = across(pick(lanes == (CLUSTERS - 1) - chip, counts))
    place = (lanes & (POOL - 1)).astype(F32) - start
    mine = ((sender >> 2) == (lanes >> 3)) & (place >= 0.0) & (place < number)
    over_first = down(jnp.where(mine & (place + BASE < first), 1.0, 0.0))
    over_second = down(jnp.where(mine & (place + BASE >= first), 1.0, 0.0))
    over_first_total, over_second_total = across(over_first), across(over_second)
    earlier = onehot(iota((CLUSTERS, CLUSTERS), 0) < iota((CLUSTERS, CLUSTERS), 1))
    sub = iota((16, CLUSTERS), 0)
    before = dot((pick(sub == 0, over_first) + pick(sub == 1, over_second)).astype(BF16), earlier)

    base_first = jnp.minimum(first, float(BASE))
    base_second = jnp.minimum(first + second, float(BASE)) - base_first
    first_row, second_row = as_row(base_first), as_row(base_second)

    step_column = across(jnp.where(lanes == chip, routes_ref[...].astype(F32), 0.0)).astype(jnp.int32)
    step_row = as_row(step_column.astype(F32)).astype(jnp.int32)
    plans = []
    ends = []
    for part, (begin, steps, _) in enumerate(PARTS):
        inside = in_part(step_column, part)
        ahead = (target < source) & in_part(step_row, part)
        first_total = down(pick(inside, base_first))
        second_total = down(pick(inside, base_second))
        last = part == LAST
        first_end = first_total + over_first_total if last else first_total
        first_start = across(pick(ahead, first_row))
        second_start = across(pick(ahead, second_row)) + first_end
        spread = step_column - begin == (iota((CHIPS, steps * BASE), 1) >> 4)
        head, tail, head_start, tail_start = [
            down(pick(spread, column)) for column in (base_first, base_second, first_start, second_start)
        ]
        slot = (iota((1, steps * BASE), 1) & (BASE - 1)).astype(F32)
        later = jnp.where(slot < head + tail, tail_start + (slot - head), -1.0)
        plan = jnp.where(slot < head, head_start + slot, later)
        held_end = first_end + second_total
        if last:
            over_row_of = jnp.where(over_second > 0.5, held_end + before[1:2], -1.0)
            over_row_of = jnp.where(over_first > 0.5, first_total + before[0:1], over_row_of)
            plan = jnp.concatenate([plan[:, : steps * BASE - CLUSTERS], over_row_of], axis=1)
            held_end = held_end + over_second_total
        plans.append(plan)
        ends.append((first_end, held_end))
    return plans, ends, faults


def kernel(
    x_hbm, assign_hbm, owner_hbm, count_hbm, index_hbm,
    out_ref, fault_ref,
    x_ref, assign_ref, owner_ref, count_ref, index_ref,
    send, got, own_over, line_over, send_over, got_over, pick_0, pick_1,
    earlier_ref, routes_ref, way_ref, keys, facts, sums, their_sums, back, returned,
    load_sem, send_sem, recv_sem,
):
    grp, blk = lax.axis_index("grp"), lax.axis_index("blk")
    my_x, my_y, my_z, core = grp // 4, grp % 4, blk // 2, blk % 2
    my_chip = grp * 4 + my_z
    picks = (pick_0, pick_1)
    along_x = [((my_x + d) % 4) * 4 for d in range(4)]
    along_y = [(my_y + d) % 4 for d in range(4)]
    along_z = [((my_z + d) % 4) * 2 + core for d in range(4)]
    other_core = {"grp": grp, "blk": my_z * 2 + (1 - core)}

    def device_at(step, sign):
        dx, dy, dz = [(sign * d) % 4 for d in ORDER[step]]
        return {"grp": along_x[dx] + along_y[dy], "blk": along_z[dz]}

    def remote(source, target, number, device):
        return pltpu.make_async_remote_copy(
            src_ref=source,
            dst_ref=target,
            send_sem=send_sem.at[number],
            recv_sem=recv_sem.at[number],
            device_id=device,
            device_id_type=pl.DeviceIdType.MESH,
        )

    def await_blocks(ref, number, semaphore):
        block = ref.at[pl.ds(0, number)]
        pltpu.make_async_copy(block, block, semaphore).wait()

    LINE, OVER, FACTS, SUMS, BACK, SWAP, PART = 0, 1, 2, 3, 4, 5, 7
    messages = [min(begin + steps, SELF) - begin for begin, steps, _ in PARTS]

    loads = [
        pltpu.make_async_copy(source, target, load_sem.at[number])
        for number, (source, target) in enumerate(
            (
                (assign_hbm, assign_ref),
                (owner_hbm, owner_ref),
                (count_hbm, count_ref),
                (index_hbm, index_ref),
                (x_hbm, x_ref),
            )
        )
    ]
    for load in loads:
        load.start()
    barrier = pltpu.get_barrier_semaphore()
    for device in [device_at(step, 1) for step in range(SELF)] + [other_core]:
        pl.semaphore_signal(barrier, inc=1, device_id=device, device_id_type=pl.DeviceIdType.MESH)
    lane = iota((1, CLUSTERS), 1)
    chip_step = step_to((lane >> 4) - my_x, ((lane >> 2) & 3) - my_y, (lane & 3) - my_z).astype(F32)
    earlier_ref[...] = onehot(iota((ROWS, ROWS), 0) < iota((ROWS, ROWS), 1))
    for load in loads[:-1]:
        load.wait()

    rank, count_column = rank_groups(count_ref)
    group, chip, step_of, slot, place_counts = place_documents(assign_ref, owner_ref, rank, earlier_ref, chip_step)
    in_base = slot < BASE
    send_slot = jnp.where(in_base, step_of * BASE + slot, -1)
    loads[-1].wait()

    def pack(first, stop):
        slots = iota(((stop - first) * BASE, ROWS), 0) + first * BASE
        rows = dot(onehot(slots == send_slot), x_ref[...]).astype(BF16)
        send[pl.ds(first, stop - first)] = rows.reshape(stop - first, BASE, WIDTH)

    def post(first, stop):
        for step in range(first, min(stop, SELF)):
            number = max(part for part in range(len(PARTS)) if PARTS[part][0] <= step)
            remote(send.at[step], got.at[step], PART + number, device_at(step, 1)).start()

    place_counts_16 = place_counts + jnp.zeros((16, CLUSTERS), F32)
    own_excess = excess(dot(place_counts_16.astype(BF16), chip_places())[0:1])
    eye = iota((CHIPS, CLUSTERS), 0) == iota((CHIPS, CLUSTERS), 1)
    excess_column = across(pick(eye, own_excess))
    over_slot = down(pick(iota((CHIPS, ROWS), 0) < chip, excess_column)).astype(jnp.int32) + (slot - BASE)
    over_slot = jnp.where(in_base, -1, over_slot)
    row = iota((BASE, CLUSTERS), 0)
    own_over[:, :WIDTH] = dot(onehot(iota((BASE, ROWS), 0) == over_slot), x_ref[...]).astype(BF16)
    own_over[:, WIDTH:] = (pick(row == 0, place_counts) + pick(row == 1, rank)).astype(BF16)
    line_over[my_z] = own_over[...]
    sublane = iota((LINES * 2 * POOL, 1), 0)
    way = sublane >> 4
    to_chip = ((my_x + (way >> 2)) & 3) * 16 + ((my_y + way) & 3) * 4 + my_z
    way_ref[...] = onehot(iota((LINES * 2 * POOL, CLUSTERS), 1) == to_chip)
    pack(0, 16)
    pl.semaphore_wait(barrier, CHIPS)
    for d in range(1, DEPTH):
        remote(own_over, line_over.at[my_z], LINE, {"grp": grp, "blk": along_z[d]}).start()
    post(0, 16)
    pack(16, 24)
    post(16, 24)

    await_blocks(line_over, DEPTH - 1, recv_sem.at[LINE])
    line_counts = [line_over[d, 0:1, WIDTH:].astype(F32) for d in range(DEPTH)]
    line_ranks = [line_over[d, 1:2, WIDTH:].astype(F32) for d in range(DEPTH)]
    row = iota((2 * POOL, CLUSTERS), 0)
    told = jnp.zeros((2 * POOL, CLUSTERS), F32)
    for d in range(DEPTH):
        told = told + pick(row == d, line_counts[d]) + pick(row == DEPTH + d, line_ranks[d])
    told = told.astype(BF16)
    over = excess(dot(told, chip_places()))[0:DEPTH]
    ahead = dot(over.astype(BF16), onehot(iota((CLUSTERS, CLUSTERS), 0) < iota((CLUSTERS, CLUSTERS), 1)))
    before = [jnp.zeros((1, CLUSTERS), F32)]
    for d in range(DEPTH - 1):
        before.append(before[-1] + over[d : d + 1])
    before = jnp.concatenate(before, axis=0)
    before_mine = down(pick(iota((DEPTH, 1), 0) == my_z, before))
    known = jnp.concatenate([over, ahead, before, jnp.zeros((DEPTH, CLUSTERS), F32)], axis=0).astype(BF16)
    known = dot_rows(way_ref[...], known)
    entry = iota((LINES * 2 * POOL, DEPTH * BASE), 1)

    def of_depth(kind):
        values = known[:, kind * DEPTH : kind * DEPTH + 1]
        for d in range(1, DEPTH):
            values = jnp.where((entry >> 4) == d, known[:, kind * DEPTH + d : kind * DEPTH + d + 1], values)
        return values

    offset = (entry & (BASE - 1)).astype(F32) - of_depth(1)
    position = jnp.where((offset >= 0.0) & (offset < of_depth(0)), offset + of_depth(2), -1.0)
    wanted = (sublane & (2 * POOL - 1)).astype(F32)
    blocks = line_over[:, :, :WIDTH].reshape(DEPTH * BASE, WIDTH)
    left = dot(onehot((wanted == position) & (wanted < POOL)), blocks[:, :HALF])
    right = dot(onehot((wanted - POOL == position) & (wanted >= POOL)), blocks[:, HALF:])
    send_over[:, :, :HALF] = (left + right).astype(BF16).reshape(LINES, 2 * POOL, HALF)
    for d in range(LINES):
        send_over[d, :, HALF:] = told
    got_over[grp] = send_over[0]
    for d in range(1, LINES):
        device = {"grp": along_x[d // 4] + along_y[d % 4], "blk": blk}
        remote(send_over.at[d], got_over.at[grp], OVER, device).start()
    pack(24, 48)
    post(24, 48)
    pack(48, CHIPS)
    post(48, CHIPS)
    got[SELF] = send[SELF]
    to_chip, sender = iota((CHIPS, CLUSTERS), 1), iota((CHIPS, CLUSTERS), 0)
    routes_ref[...] = step_to(
        (to_chip >> 4) - (sender >> 4), ((to_chip >> 2) & 3) - ((sender >> 2) & 3), (to_chip & 3) - (sender & 3)
    )
    missing = missing_documents(index_ref, count_column, group)

    await_blocks(got_over, LINES - 1, recv_sem.at[OVER])
    told = got_over[:, :, HALF:].astype(F32)
    counts = told[:, 0:DEPTH].reshape(CHIPS, CLUSTERS)
    ranks = told[:, DEPTH : 2 * DEPTH].reshape(CHIPS, CLUSTERS)
    plans, ends, faults = receive_plan(counts, ranks, rank, my_x, my_y, my_z, routes_ref)

    row = iota((8, 128), 0)
    told = pick(row == 6, rank) + pick(row == 7, missing)
    for part, (first_end, held_end) in enumerate(ends):
        told = told + pick(row == part, first_end) + pick(row == 2 + part, held_end)
        picks[part][...] = onehot(iota(picks[part].shape, 0).astype(F32) == plans[part])
    facts[0] = told
    swap_facts = remote(facts.at[0], facts.at[1], FACTS, other_core)
    swap_facts.start()

    best = [jnp.full((1, room), -1.0, F32) for _, _, room in PARTS]
    key_kinds = []
    query_kinds = []
    totals = [jnp.zeros((1, WIDTH), F32), jnp.zeros((1, WIDTH), F32)]
    swaps = []

    def add_kinds(first, held, room):
        number = iota((room, 1), 0).astype(F32)
        key_kinds.append(jnp.where(number < first, 0.0, jnp.where(number < held, 1.0, 2.0)))

    for (first_end, held_end), (_, _, room) in zip(ends, PARTS):
        add_kinds(first_end, held_end, room)
        query_kinds.append(jnp.where(iota((1, room), 1).astype(F32) < first_end, 0.0, 1.0))

    def compare(first_key, last_key, part, more=0):
        borders = (*STARTS, *(HELD + start for start in STARTS), 2 * HELD)
        begin, stop = borders[first_key], borders[last_key + 1]
        start, room = STARTS[part], PARTS[part][2]
        scores = dot_rows(keys[begin : stop + more], keys[start : start + room])
        rest, scores = scores[stop - begin :], scores[: stop - begin]
        kind = jnp.concatenate(key_kinds[first_key : last_key + 1], axis=0)
        matched = kind == query_kinds[part]
        if begin < start + room and start < stop:
            matched = matched & (iota(kind.shape, 0) + (begin - start) != iota((1, room), 1))
        best[part] = jnp.maximum(best[part], jnp.max(jnp.where(matched, scores, -1.0), axis=0, keepdims=True))
        return rest

    def arrive(part):
        begin, steps, room = PARTS[part]
        await_blocks(got, messages[part], recv_sem.at[PART + part])
        rows = dot(picks[part][...], got[pl.ds(begin, steps)].reshape(steps * BASE, WIDTH))
        unit = rows * lax.rsqrt(across(rows * rows) + EPSILON)
        keys[pl.ds(STARTS[part], room)] = unit.astype(BF16)
        swap = remote(
            keys.at[pl.ds(STARTS[part], room)], keys.at[pl.ds(HELD + STARTS[part], room)], SWAP + part, other_core
        )
        swap.start()
        swaps.append(swap)
        is_first = iota((room, 1), 0).astype(F32) < ends[part][0]
        totals[0] = totals[0] + down(pick(is_first, unit))
        totals[1] = totals[1] + down(jnp.where(is_first, 0.0, unit))

    arrive(0)
    fault = faults()
    compare(0, 0, 0)
    swap_facts.wait()
    their_told = facts[1]
    for part, (_, _, room) in enumerate(PARTS):
        add_kinds(their_told[part : part + 1, 0:1], their_told[2 + part : 3 + part, 0:1], room)
    half_rows = got_over[:, :, :HALF].reshape(LINES * 2 * POOL, HALF)
    shape = (LINES * POOL, LINES * 2 * POOL)
    to, at = iota(shape, 0), iota(shape, 1)
    same = ((to >> 3) == (at >> 4)) & ((to & 7) == (at & 7))
    left = dot(onehot(same & ((at & POOL) == 0)), half_rows)
    right = dot(onehot(same & ((at & POOL) != 0)), half_rows)
    whole = jnp.concatenate([left, right], axis=1).astype(BF16)
    got[pl.ds(CHIPS, TOTAL - CHIPS)] = whole.reshape(TOTAL - CHIPS, BASE, WIDTH)
    swaps[0].wait()
    compare(2, 2, 0)

    arrive(1)
    row = iota((8, WIDTH), 0)
    sums[...] = pick(row == 0, totals[0]) + pick(row == 1, totals[1]) + pick(row == 2, fault)
    swap_sums = remote(sums, their_sums, SUMS, other_core)
    swap_sums.start()
    compare(0, 2, 1)
    compare(1, 1, 0)

    swap_sums.wait()
    total = pick(row < 2, sums[...] + their_sums[...])
    keys[pl.ds(2 * HELD, 16)] = jnp.concatenate(halves(total), axis=0).astype(BF16)
    scale = lax.rsqrt(across(total * total) + EPSILON)
    swaps[1].wait()
    near = [compare(3, 3, part, 16) for part in range(len(PARTS))]
    near = [(some[0:8] + some[8:16]) * scale for some in near]

    poison = missing + their_told[7:8, 1:2] > 0.5
    tiles = CHIPS * BASE // 128
    for part, (begin, steps, room) in enumerate(PARTS):
        row = iota((8, room), 0)
        query_number = iota((1, room), 1).astype(F32)
        some = jnp.where(query_number < ends[part][0], near[part][0:1], near[part][1:2])
        values = jnp.zeros((8, room), F32)
        for number, term in enumerate(halves(best[part]) + halves(some)):
            values = jnp.where(row == number, term, values)
        out = dot(values.astype(BF16), picks[part][...])
        for kind in range(2):
            line = out[2 * kind : 2 * kind + 1] + out[2 * kind + 1 : 2 * kind + 2]
            line = jnp.where(poison, NONE, line)
            for tile in range(steps * BASE // 128):
                piece = line[:, tile * 128 : (tile + 1) * 128]
                to = begin * BASE // 128 + tile
                if to < tiles:
                    back[to, kind : kind + 1, :] = piece
                else:
                    for each in range(tiles):
                        back[each, 2 + kind : 3 + kind, :] = piece
    returned[SELF] = back[SELF // 8]
    for step in range(SELF):
        remote(back.at[step // 8], returned.at[step], BACK, device_at(step, -1)).start()

    differ = across(jnp.where(their_told[6:7] != rank, 1.0, 0.0))
    fault = fault + their_sums[2:3, 0:1] + differ
    chosen = onehot(iota((CHIPS, ROWS), 0) == step_of)
    sub = iota((128, ROWS), 0)
    at_base = (sub == (step_of & 7) * BASE + slot) & in_base
    before_column = across(pick(eye, before_mine))
    line_slot = down(pick(iota((CHIPS, ROWS), 0) == chip, before_column)).astype(jnp.int32)
    at_over = (sub == grp * POOL + line_slot + (slot - BASE)) & (~in_base)

    await_blocks(returned, CHIPS - 1, recv_sem.at[BACK])
    found = []
    for number in range(4):
        line = returned[:, number, :]
        if number == 0:
            poisoned = across(down(jnp.where(line > 0.5 * NONE, 1.0, 0.0)))
            fault_ref[...] = jnp.where(fault + poisoned > 0.5, 1, 0) + jnp.zeros((1, 128), jnp.int32)
        terms = jnp.concatenate(halves(line), axis=1).astype(BF16)
        out = lax.dot_general(terms, chosen, (((0,), (0,)), ((), ())), preferred_element_type=F32)
        found.append(out[0:128] + out[128:256])
    out_ref[0:1] = down(pick(at_base, found[0]) + pick(at_over, found[2]))
    out_ref[1:2] = down(pick(at_base, found[1]) + pick(at_over, found[3]))

    await_blocks(line_over, DEPTH - 1, send_sem.at[LINE])
    await_blocks(got_over, LINES - 1, send_sem.at[OVER])
    await_blocks(returned, CHIPS - 1, send_sem.at[BACK])
    for part in range(len(PARTS)):
        await_blocks(got, messages[part], send_sem.at[PART + part])


def routed(embeddings, assign, owner, send_count, send_index):
    return pl.pallas_call(
        kernel,
        out_shape=(
            jax.ShapeDtypeStruct((2, ROWS), F32),
            jax.ShapeDtypeStruct((1, 128), jnp.int32),
        ),
        in_specs=[pl.BlockSpec(memory_space=pl.ANY)] * 5,
        out_specs=(pl.BlockSpec(memory_space=pltpu.VMEM),) * 2,
        scratch_shapes=[
            pltpu.VMEM((ROWS, WIDTH), BF16),
            pltpu.VMEM((1, ROWS), jnp.int32),
            pltpu.VMEM((1, CLUSTERS), jnp.int32),
            pltpu.VMEM((1, GROUPS), jnp.int32),
            pltpu.VMEM((GROUPS, CAP), jnp.int32),
            pltpu.VMEM((CHIPS, BASE, WIDTH), BF16),
            pltpu.VMEM((TOTAL, BASE, WIDTH), BF16),
            pltpu.VMEM((BASE, WIDTH + CLUSTERS), BF16),
            pltpu.VMEM((DEPTH, BASE, WIDTH + CLUSTERS), BF16),
            pltpu.VMEM((LINES, 2 * POOL, HALF + CLUSTERS), BF16),
            pltpu.VMEM((LINES, 2 * POOL, HALF + CLUSTERS), BF16),
            *[pltpu.VMEM((room, steps * BASE), BF16) for _, steps, room in PARTS],
            pltpu.VMEM((ROWS, ROWS), BF16),
            pltpu.VMEM((CHIPS, CLUSTERS), jnp.int32),
            pltpu.VMEM((LINES * 2 * POOL, CLUSTERS), BF16),
            pltpu.VMEM((2 * HELD + 16, WIDTH), BF16),
            pltpu.VMEM((2, 8, 128), F32),
            pltpu.VMEM((8, WIDTH), F32),
            pltpu.VMEM((8, WIDTH), F32),
            pltpu.VMEM((CHIPS * BASE // 128, 4, 128), F32),
            pltpu.VMEM((CHIPS, 4, 128), F32),
            pltpu.SemaphoreType.DMA((5,)),
            pltpu.SemaphoreType.DMA((9,)),
            pltpu.SemaphoreType.DMA((9,)),
        ],
        compiler_params=pltpu.CompilerParams(
            collective_id=0, has_side_effects=True, vmem_limit_bytes=48 * 1024 * 1024
        ),
    )(
        embeddings,
        assign.reshape(1, ROWS),
        owner.reshape(1, CLUSTERS),
        send_count,
        send_index[0],
    )


def body(embeddings, assign, owner, send_count, send_index):
    arguments = (embeddings, assign, owner, send_count, send_index)
    results, fault = routed(*arguments)
    results = lax.cond(fault[0, 0] != 0, lambda: jnp.stack(general(*arguments)), lambda: results)
    return results[0], results[1]


def solution(mesh):
    placed = (
        P(("grp", "blk"), None),
        P(("grp", "blk")),
        P(),
        P(("grp", "blk"), None),
        P(("grp", "blk"), None, None),
    )
    return jax.shard_map(
        body,
        mesh=mesh,
        in_specs=placed,
        out_specs=(P(("grp", "blk")), P(("grp", "blk"))),
        check_vma=False,
    )
```
